32 devices in a mesh: fsdp: 4 (over y, core), ctx: 8 (over z, x).
Axes of the slice: x: 2, y: 2, z: 4, core: 2. Of those that a mesh axis runs over, the one named last changes fastest.
Arguments:
- hidden_in: bfloat16 [4, 1024, 2048], P('fsdp', 'ctx'), may hold values from -6 to 6
- segments: int32 [4, 1024], P('fsdp', 'ctx'), may hold values from -1 to 9, as said below
- block_pairs: int32 [16], replicated, may hold values from 0 to 15, as said below
- routes: int32 [4, 1024, 4], P('fsdp', 'ctx'), may hold values from 0 to 7, all different within a row; in each aligned block of 128 rows (0 to 127, 128 to 255, ..., all dimensions but the last counted through in order) at most 128 rows name the same one
- out_grad: bfloat16 [4, 1024, 2048], P('fsdp', 'ctx'), may hold values from -6 to 6
- norm_gain_attn: bfloat16 [2048], P(('fsdp', 'ctx')), may hold values from 0.5 to 1.5
- qkv_weight: bfloat16 [2048, 6144], P(('fsdp', 'ctx')), may hold values from -0.1875 to 0.1875
- qkv_bias: bfloat16 [6144], P(('fsdp', 'ctx')), may hold values from -1 to 1
- out_weight: bfloat16 [2048, 2048], P(('fsdp', 'ctx')), may hold values from -0.75 to 0.75
- norm_gain_ffn: bfloat16 [2048], P(('fsdp', 'ctx')), may hold values from 0.5 to 1.5
- router_weight: bfloat16 [2048, 8], P(('fsdp', 'ctx')), may hold values from -0.0625 to 0.0625
- shared_gate_weight: bfloat16 [2048], P(('fsdp', 'ctx')), may hold values from -0.125 to 0.125
- shared_in_weight: bfloat16 [2048, 11264], P(('fsdp', 'ctx')), may hold values from -0.125 to 0.125
- shared_out_weight: bfloat16 [5632, 2048], P(('fsdp', 'ctx')), may hold values from -0.15625 to 0.15625
- expert_in_weight: bfloat16 [8, 2048, 2816], P('ctx', 'fsdp'), may hold values from -0.125 to 0.125
- expert_out_weight: bfloat16 [8, 1408, 2048], P('ctx', 'fsdp'), may hold values from -0.875 to 0.875
Outputs:
- hidden_out: bfloat16 [4, 1024, 2048], P('fsdp', 'ctx')
- hidden_grad: float32 [4, 1024, 2048], P('fsdp', 'ctx')
- grad_norm_gain_attn: float32 [2048], P(('fsdp', 'ctx'))
- grad_qkv_weight: float32 [2048, 6144], P(('fsdp', 'ctx'))
- grad_qkv_bias: float32 [6144], P(('fsdp', 'ctx'))
- grad_out_weight: float32 [2048, 2048], P(('fsdp', 'ctx'))
- grad_norm_gain_ffn: float32 [2048], P(('fsdp', 'ctx'))
- grad_router_weight: float32 [2048, 8], P(('fsdp', 'ctx'))
- grad_shared_gate_weight: float32 [2048], P(('fsdp', 'ctx'))
- grad_shared_in_weight: float32 [2048, 11264], P(('fsdp', 'ctx'))
- grad_shared_out_weight: float32 [5632, 2048], P(('fsdp', 'ctx'))
- grad_expert_in_weight: float32 [8, 2048, 2816], P('ctx', 'fsdp')
- grad_expert_out_weight: float32 [8, 1408, 2048], P('ctx', 'fsdp')
The draws below stay inside these ranges and needn't reach their ends.
Inputs may be any that keep to these rules, and one draw needn't show every extreme that they name: `segments`: read in the order of positions that block_pairs gives, the segment numbers of a row start at 0 and never fall; -1 marks padding, which ends every row. `block_pairs`: device c of ctx holds, in this order, the row blocks numbered by entries 2 c and 2 c + 1, each 64 consecutive positions; every block number appears once. `routes`: each token names 4 different experts; among the tokens of one device (aligned blocks of 128 tokens of the array) no expert is named more than 128 times.
All inputs are finite; a program needn't handle non-finite values.
Results may differ from the reference program's by a relative error of at most 0.015.
The reference program's roundings to bfloat16 on the way count: a program that leaves them out, or rounds other values in their place, can miss the bound.
Values may be sent and summed in bfloat16 or wider, within the bound.
A program may use at most 512 MiB of HBM per device.

```python
import math
import jax
import jax.numpy as jnp
import numpy as np
from jax import lax

D = 2048
HEADS = 16
HD = 128
FF = 1408
FS = 5632
TOP = 4
BLOCK = 64
EXPERTS = 8
CAP = 128
LEN = 1024
ROWS = 4
N_CTX = 8


def pair_table(key):
    lower = jax.random.permutation(jax.random.fold_in(key, 101), N_CTX).astype(jnp.int32)
    upper = jax.random.permutation(jax.random.fold_in(key, 102), N_CTX).astype(jnp.int32) + N_CTX
    flips = jax.random.randint(jax.random.fold_in(key, 103), (N_CTX,), 0, 2)
    leading = jnp.where(flips == 1, upper, lower)
    trailing = jnp.where(flips == 1, lower, upper)
    return jnp.stack([leading, trailing], axis=1).reshape(2 * N_CTX).astype(jnp.int32)


def draw_block_pairs(key, part):
    table = pair_table(key)
    return table


def row_segments(row_key):
    first_len = LEN // 2 + jax.random.randint(jax.random.fold_in(row_key, 1), (), 0, LEN // 8 + 1)
    others = jax.random.randint(jax.random.fold_in(row_key, 2), (8,), LEN // 64, LEN // 32 + 1)
    bounds = first_len + jnp.cumsum(others)
    padding = jax.random.randint(jax.random.fold_in(row_key, 3), (), 1, LEN // 16 + 1)
    places = jnp.arange(LEN, dtype=jnp.int32)
    numbers = (places >= first_len).astype(jnp.int32) + jnp.sum((places[:, None] >= bounds[None, :]).astype(jnp.int32), axis=1)
    return jnp.where(places < LEN - padding, numbers, -1).astype(jnp.int32)


def draw_segments(key, part):
    table = pair_table(key)
    key = jax.random.fold_in(key, 2)
    row_keys = jax.random.split(key, ROWS)
    natural = jax.vmap(row_segments)(row_keys)
    order = (table[:, None] * BLOCK + jnp.arange(BLOCK, dtype=jnp.int32)[None, :]).reshape(LEN)
    return natural[:, order].astype(jnp.int32)


def block_levels(key, dims, cuts, low, largest):
    level = 1.0
    for dim, shards_of in cuts:
        draws = jax.random.uniform(jax.random.fold_in(jax.random.fold_in(key, 6), dim), (shards_of,), jnp.float32, low / len(cuts), largest / len(cuts))
        level = level * jnp.repeat(jnp.exp(draws), dims[dim] // shards_of).reshape((-1,) + (1,) * (len(dims) - 1 - dim))
    return level


def assign_block(rng, own, number, rows, count, top, limit, skew):
    ranking = jax.random.permutation(rng, count)
    packed, usual = shares(count, rows * top, limit, skew, True), shares(count, rows * top, limit, skew, False)
    places = jnp.arange(count)

    def named(lengths, offset_by):
        used = int((lengths > 0).sum())
        fixed = max(1, used // 4)
        passed = fixed + (places - fixed + offset_by * (used - fixed)) % max(1, count - fixed)
        return jnp.zeros((count,), jnp.int32).at[ranking[jnp.where(places < fixed, places, passed)]].set(jnp.asarray(lengths, jnp.int32))

    lengths = jnp.where(number % 4 == 0, named(packed, number // 4), named(usual, number - number // 4 - 1))
    mixed = jax.random.permutation(jax.random.fold_in(own, 3), count)
    donor, sink = mixed[0:count // 2 * 2:2], mixed[1:count // 2 * 2:2]
    room = jnp.minimum(lengths[donor] - 1, limit - lengths[sink]) // 2
    room = jnp.where((donor == ranking[0]) | (sink == ranking[0]) | (lengths[sink] == 0), 0, jnp.maximum(room, 0))
    passed = jax.random.randint(jax.random.fold_in(own, 4), (count // 2,), 0, 1 << 20) % (room + 1)
    lengths = lengths.at[donor].add(-passed).at[sink].add(passed)
    labels = jnp.searchsorted(jnp.cumsum(lengths), jnp.arange(rows * top), side="right").astype(jnp.int32)
    listing = labels.reshape(top, rows).T
    listing = listing[jax.random.permutation(jax.random.fold_in(own, 1), rows)]
    offset_by = jax.random.randint(jax.random.fold_in(own, 2), (rows, 1), 0, top)
    return jnp.take_along_axis(listing, (jnp.arange(top)[None, :] + offset_by) % top, axis=1)


def shares(number_of, total, bound, slope, full):
    weights = [(1 << 20) // math.isqrt(grade ** slope) + 1 for grade in range(1, number_of + 1)]
    largest = bound if full else min(bound, max(-(-total // number_of), total * weights[0] // sum(weights)))
    least = 1 if total - largest >= number_of - 1 else 0
    counts, surplus = [largest] + [least] * (number_of - 1), total - largest - least * (number_of - 1)
    while surplus > 0:
        movable = [i for i in range(1, number_of) if counts[i] < largest] or [i for i in range(1, number_of) if counts[i] < bound]
        whole, left = sum([weights[i] for i in movable]), surplus
        for i in movable:
            extra = min(bound - counts[i], max(1, left * weights[i] // whole), surplus)
            counts[i] = counts[i] + extra
            surplus = surplus - extra
    return np.array(counts)


def normal_values(own_key, dims, deviation, bound, pieces=(), kind=jnp.bfloat16):
    array = deviation * jax.random.normal(own_key, dims, jnp.float32)
    if pieces:
        array = array * block_levels(own_key, dims, pieces, -0.22, 0.18)
    return jnp.clip(array, -bound, bound).astype(kind)


def setup_inputs(seed: int = 0) -> dict:
    streams_of = jax.random.split(jax.random.key(seed), 17)
    hidden_in = normal_values(streams_of[0], (ROWS, LEN, D), 1.0, 6.0, ((0, 4), (1, 8)))
    segments = draw_segments(jax.random.fold_in(streams_of[16], 71), 0)
    block_pairs = draw_block_pairs(jax.random.fold_in(streams_of[16], 71), 0)
    routes_keys = jax.random.split(jax.random.fold_in(streams_of[3], 1), ROWS * LEN // (2 * BLOCK))
    routes_turns = jax.random.permutation(jax.random.fold_in(streams_of[3], 3), ROWS * LEN // (2 * BLOCK))
    routes = jax.vmap(lambda own, number: assign_block(jax.random.fold_in(streams_of[3], 2), own, number, 2 * BLOCK, EXPERTS, TOP, CAP, 2))(routes_keys, routes_turns).reshape((ROWS, LEN, TOP))
    out_grad = normal_values(streams_of[4], (ROWS, LEN, D), 1.0, 6.0, ((0, 4), (1, 8)))
    norm_gain_attn = jnp.clip(1.0 + 0.1 * jax.random.normal(streams_of[5], (D,), jnp.float32), 0.5, 1.5).astype(jnp.bfloat16)
    qkv_weight = normal_values(streams_of[6], (D, 3 * HEADS * HD), (D // 2) ** -0.5, 0.1875, ((0, 32),))
    qkv_bias = normal_values(streams_of[7], (3 * HEADS * HD,), 0.2, 1.0, ((0, 32),))
    out_weight = normal_values(streams_of[8], (HEADS * HD, D), (HEADS * HD // 32) ** -0.5, 0.75, ((0, 32),))
    norm_gain_ffn = jnp.clip(1.0 + 0.1 * jax.random.normal(streams_of[9], (D,), jnp.float32), 0.5, 1.5).astype(jnp.bfloat16)
    router_weight = normal_values(streams_of[10], (D, EXPERTS), (4 * D) ** -0.5, 0.0625, ((0, 32),))
    shared_gate_weight = normal_values(streams_of[11], (D,), D ** -0.5, 0.125, ((0, 32),))
    shared_in_weight = normal_values(streams_of[12], (D, 2 * FS), D ** -0.5, 0.125, ((0, 32),))
    shared_out_weight = normal_values(streams_of[13], (FS, D), (FS // 4) ** -0.5, 0.15625, ((0, 32),))
    expert_in_weight = normal_values(streams_of[14], (EXPERTS, D, 2 * FF), D ** -0.5, 0.125, ((0, 8), (1, 4)))
    expert_out_weight = normal_values(streams_of[15], (EXPERTS, FF, D), (max(FF * 9 // (4 * EXPERTS * EXPERTS), 1)) ** -0.5, 0.875, ((0, 8), (1, 4)))
    return {"hidden_in": hidden_in, "segments": segments, "block_pairs": block_pairs, "routes": routes, "out_grad": out_grad, "norm_gain_attn": norm_gain_attn, "qkv_weight": qkv_weight, "qkv_bias": qkv_bias, "out_weight": out_weight, "norm_gain_ffn": norm_gain_ffn, "router_weight": router_weight, "shared_gate_weight": shared_gate_weight, "shared_in_weight": shared_in_weight, "shared_out_weight": shared_out_weight, "expert_in_weight": expert_in_weight, "expert_out_weight": expert_out_weight}


@jax.custom_vjp
def low(v):
    return lax.optimization_barrier(v.astype(jnp.bfloat16)).astype(jnp.float32)

@jax.custom_vjp
def low_back(v):
    return v

def low_keep(v):
    return (low(v), None)

def low_pass(kept, grad):
    return (grad,)

def back_keep(v):
    return (v, None)

def back_low(kept, grad):
    return (low(grad),)
low.defvjp(low_keep, low_pass)
low_back.defvjp(back_keep, back_low)
EPSILON = 1e-06
THETA = 1000000.0

def exact_dot(left, right):
    return jnp.dot(left, right, precision=lax.Precision.HIGHEST, preferred_element_type=jnp.float32)

def rms_scale(values, gain_vec):
    return values * lax.rsqrt(lax.optimization_barrier(jnp.mean(values * values, axis=-1, keepdims=True)) + EPSILON) * gain_vec

def rotate(values, positions):
    half_len = values.shape[-1] // 2
    frequency = THETA ** (-jnp.arange(half_len, dtype=jnp.float32) / half_len)
    angles = positions.astype(jnp.float32)[:, None] * frequency[None, :]
    cosine = jnp.cos(angles)[:, None, :]
    sine_part = jnp.sin(angles)[:, None, :]
    first_half = values[..., :half_len]
    second = values[..., half_len:]
    return jnp.concatenate([first_half * cosine - second * sine_part, second * cosine + first_half * sine_part], axis=-1)

def visible(query_pos, query_seg, key_pos, key_seg):
    same_doc = (key_seg[None, :] == query_seg[:, None]) & (query_seg[:, None] >= 0)
    causal = key_pos[None, :] <= query_pos[:, None]
    return same_doc & causal | (key_pos[None, :] == query_pos[:, None])

def attend_row(queries, keys_row, values_row, positions, segments_row):
    span_len = 512 if LEN % 512 == 0 else LEN

    def one_block(offset):
        query_block = lax.dynamic_slice_in_dim(queries, offset, span_len, 0)
        pos_block = lax.dynamic_slice_in_dim(positions, offset, span_len, 0)
        seg_block = lax.dynamic_slice_in_dim(segments_row, offset, span_len, 0)
        scores = low_back(jnp.einsum('qhd,khd->hqk', query_block, keys_row, precision=lax.Precision.HIGHEST))
        scores = jnp.where(visible(pos_block, seg_block, positions, segments_row)[None], scores, -1e+30)
        weights = jax.nn.softmax(scores, axis=-1)
        return jnp.einsum('hqk,khd->qhd', low(weights), values_row, precision=lax.Precision.HIGHEST)
    starts = jnp.arange(LEN // span_len, dtype=jnp.int32) * span_len
    blocks = lax.map(jax.checkpoint(one_block), starts)
    return blocks.reshape(LEN, HEADS * HD)

def slot_places(routes_row):
    flat_routes = routes_row.reshape(N_CTX, 2 * BLOCK * TOP)
    onehot = (flat_routes[:, :, None] == jnp.arange(EXPERTS, dtype=jnp.int32)[None, None, :]).astype(jnp.int32)
    earlier = jnp.cumsum(onehot, axis=1) - onehot
    within = lax.optimization_barrier(jnp.sum(earlier * onehot, axis=2))
    sources = jnp.arange(N_CTX, dtype=jnp.int32)[:, None] * CAP
    return (sources + within).reshape(LEN, TOP).astype(jnp.int32)

def expert_block(operands):
    buffer_rows, inner_weight, outer_weight = operands
    gate_up = low_back(exact_dot(buffer_rows, inner_weight))
    hidden_units = low(jax.nn.silu(gate_up[:, :FF]) * gate_up[:, FF:])
    return low_back(low(exact_dot(hidden_units, outer_weight)))

def layer_row(inputs_row, segments_row, routes_row, positions, params):
    gain_attn, qkv_mat, qkv_shift, out_mat, gain_ffn, router_mat, gate_vec, shared_inner, shared_outer, expert_inner, expert_outer = params
    width_heads = HEADS * HD
    normed = low(rms_scale(inputs_row, gain_attn))
    projected = low_back(exact_dot(normed, qkv_mat) + qkv_shift)
    queries = low(rotate(projected[:, :width_heads].reshape(LEN, HEADS, HD), positions) * HD ** (-0.5))
    keys_row = low(rotate(projected[:, width_heads:2 * width_heads].reshape(LEN, HEADS, HD), positions))
    values_row = low(projected[:, 2 * width_heads:].reshape(LEN, HEADS, HD))
    attended = attend_row(queries, keys_row, values_row, positions, segments_row)
    branch = low_back(exact_dot(low_back(low(attended)), out_mat))
    middle = inputs_row + branch
    normed_ffn = low(rms_scale(middle, gain_ffn))
    logits = low_back(exact_dot(normed_ffn, router_mat))
    router_probs = jax.nn.softmax(logits, axis=-1)
    gate_weights = jnp.take_along_axis(router_probs, routes_row, axis=1)
    shared_gu = low_back(exact_dot(normed_ffn, shared_inner))
    shared_hidden = low(jax.nn.silu(shared_gu[:, :FS]) * shared_gu[:, FS:])
    shared_out = low_back(exact_dot(shared_hidden, shared_outer))
    gate_logit = low_back(exact_dot(normed_ffn, gate_vec))
    places = slot_places(routes_row)
    spread = jnp.broadcast_to(normed_ffn[:, None, :], (LEN, TOP, D))
    buffers = jnp.zeros((EXPERTS, N_CTX * CAP, D), jnp.float32).at[routes_row, places].add(spread)
    buffers = low_back(buffers)
    returned = lax.map(jax.checkpoint(expert_block), (buffers, expert_inner, expert_outer))
    picked = returned[routes_row, places]
    routed = lax.optimization_barrier(jnp.sum(gate_weights[:, :, None] * picked, axis=1))
    return middle + jax.nn.sigmoid(gate_logit)[:, None] * shared_out + routed

def reference(hidden_in, segments, block_pairs, routes, out_grad, norm_gain_attn, qkv_weight, qkv_bias, out_weight, norm_gain_ffn, router_weight, shared_gate_weight, shared_in_weight, shared_out_weight, expert_in_weight, expert_out_weight):
    positions = (block_pairs[:, None] * BLOCK + jnp.arange(BLOCK, dtype=jnp.int32)[None, :]).reshape(LEN).astype(jnp.int32)
    params = (norm_gain_attn.astype(jnp.float32), qkv_weight.astype(jnp.float32), qkv_bias.astype(jnp.float32), out_weight.astype(jnp.float32), norm_gain_ffn.astype(jnp.float32), router_weight.astype(jnp.float32), shared_gate_weight.astype(jnp.float32), shared_in_weight.astype(jnp.float32), shared_out_weight.astype(jnp.float32), expert_in_weight.astype(jnp.float32), expert_out_weight.astype(jnp.float32))
    inputs = hidden_in.astype(jnp.float32)

    def forward(inputs_all, params_all):

        def row_step(carried, operands):
            inputs_row, segments_row, routes_row = operands
            return (carried, layer_row(inputs_row, segments_row, routes_row, positions, params_all))
        unused, outputs = lax.scan(row_step, jnp.float32(0.0), (inputs_all, segments, routes))
        return outputs
    outputs, pull_back = jax.vjp(forward, inputs, params)
    input_grad, param_grads = pull_back(out_grad.astype(jnp.float32))
    return (outputs.astype(jnp.bfloat16), input_grad, param_grads[0], param_grads[1], param_grads[2], param_grads[3], param_grads[4], param_grads[5], param_grads[6], param_grads[7], param_grads[8], param_grads[9], param_grads[10])
```

```python
from functools import partial

import jax
import jax.numpy as jnp
from jax import lax
from jax.sharding import PartitionSpec as P

HD = 128


EPSILON = 1e-06
THETA = 1000000.0
heads_per_group = 4


def rms_scale(values, gain_vec):
    return (
        values * lax.rsqrt(jnp.mean(values * values, axis=-1, keepdims=True) + EPSILON) * gain_vec
    )


def rotate(values, positions):
    half_len = values.shape[-1] // 2
    frequency = THETA ** (-jnp.arange(half_len, dtype=jnp.float32) / half_len)
    angles = positions.astype(jnp.float32)[:, None] * frequency[None, :]
    cosine = jnp.cos(angles)[:, None, :]
    sine_part = jnp.sin(angles)[:, None, :]
    first_half = values[..., :half_len]
    second = values[..., half_len:]
    return jnp.concatenate(
        [first_half * cosine - second * sine_part, second * cosine + first_half * sine_part],
        axis=-1,
    )


def visible(query_pos, query_seg, key_pos, key_seg):
    same_doc = (key_seg[None, :] == query_seg[:, None]) & (query_seg[:, None] >= 0)
    causal = key_pos[None, :] <= query_pos[:, None]
    return same_doc & causal | (key_pos[None, :] == query_pos[:, None])


def swiglu_mix(gate_up, hidden_width):
    return jax.nn.silu(gate_up[..., :hidden_width]) * gate_up[..., hidden_width:]


def matmul_low(left, right):
    return jnp.dot(left, right, preferred_element_type=jnp.float32)


def gathered_plan(
    hidden_in,
    segments,
    block_pairs,
    routes,
    out_grad,
    norm_gain_attn,
    qkv_weight,
    qkv_bias,
    out_weight,
    norm_gain_ffn,
    router_weight,
    shared_gate_weight,
    shared_in_weight,
    shared_out_weight,
    expert_in_weight,
    expert_out_weight,
):
    tokens_dev = hidden_in.shape[1]
    model_width = hidden_in.shape[2]
    block_len = tokens_dev // 2
    inputs = hidden_in.reshape(tokens_dev, model_width).astype(jnp.float32)
    seg_local = segments.reshape(tokens_dev)
    token_routes = routes.reshape(tokens_dev, -1)
    top_count = token_routes.shape[1]
    ctx_count = lax.axis_size("ctx")
    ctx_rank = lax.axis_index("ctx")
    offsets = jnp.arange(block_len, dtype=jnp.int32)
    all_positions = (
        block_pairs.reshape(ctx_count, 2)[:, :, None] * block_len + offsets[None, None, :]
    ).reshape(ctx_count * tokens_dev)
    my_positions = lax.dynamic_slice_in_dim(all_positions, ctx_rank * tokens_dev, tokens_dev, 0)
    gathered = (
        lax.all_gather(norm_gain_attn, ("fsdp", "ctx"), axis=0, tiled=True),
        lax.all_gather(qkv_weight, ("fsdp", "ctx"), axis=0, tiled=True),
        lax.all_gather(qkv_bias, ("fsdp", "ctx"), axis=0, tiled=True),
        lax.all_gather(out_weight, ("fsdp", "ctx"), axis=0, tiled=True),
        lax.all_gather(norm_gain_ffn, ("fsdp", "ctx"), axis=0, tiled=True),
        lax.all_gather(router_weight, ("fsdp", "ctx"), axis=0, tiled=True),
        lax.all_gather(shared_gate_weight, ("fsdp", "ctx"), axis=0, tiled=True),
        lax.all_gather(shared_in_weight, ("fsdp", "ctx"), axis=0, tiled=True),
        lax.all_gather(shared_out_weight, ("fsdp", "ctx"), axis=0, tiled=True),
    )
    (
        gain_attn,
        qkv_full,
        shift_full,
        out_full,
        gain_ffn,
        router_full,
        gate_full,
        inner_full,
        outer_full,
    ) = gathered
    gain_attn = gain_attn.astype(jnp.float32)
    gain_ffn = gain_ffn.astype(jnp.float32)
    heads_width = out_full.shape[0]
    head_count = heads_width // HD
    group_width = heads_per_group * HD
    group_count = head_count // heads_per_group
    normed = rms_scale(inputs, gain_attn).astype(jnp.bfloat16)
    projected = matmul_low(normed, qkv_full) + shift_full.astype(jnp.float32)
    query_pre = projected[:, :heads_width].reshape(tokens_dev, head_count, HD)
    key_pre = projected[:, heads_width : 2 * heads_width].reshape(tokens_dev, head_count, HD)

    def place_heads(query_in, key_in):
        return (rotate(query_in, my_positions) * HD ** (-0.5), rotate(key_in, my_positions))

    query_rot, key_rot = place_heads(query_pre, key_pre)
    query_low = query_rot.reshape(tokens_dev, heads_width).astype(jnp.bfloat16)
    key_low = key_rot.reshape(tokens_dev, heads_width).astype(jnp.bfloat16)
    value_low = projected[:, 2 * heads_width :].astype(jnp.bfloat16)
    keys_all, values_all, segs_all = (
        lax.all_gather(key_low, "ctx", axis=0, tiled=True),
        lax.all_gather(value_low, "ctx", axis=0, tiled=True),
        lax.all_gather(seg_local.astype(jnp.bfloat16), "ctx", axis=0, tiled=True),
    )
    allowed = visible(
        my_positions, seg_local.astype(jnp.float32), all_positions, segs_all.astype(jnp.float32)
    )

    def head_slice(matrix, group_index):
        return lax.dynamic_slice_in_dim(matrix, group_index * group_width, group_width, 1).reshape(
            matrix.shape[0], heads_per_group, HD
        )

    def forward_group(group_index):
        query_part = head_slice(query_low, group_index)
        key_part = head_slice(keys_all, group_index)
        value_part = head_slice(values_all, group_index)
        scores = jnp.einsum(
            "qhd,khd->hqk", query_part, key_part, preferred_element_type=jnp.float32
        )
        scores = jnp.where(allowed[None], scores, -1e30)
        highest = jnp.max(scores, axis=-1, keepdims=True)
        log_total = highest + jnp.log(jnp.sum(jnp.exp(scores - highest), axis=-1, keepdims=True))
        weights = jnp.exp(scores - log_total).astype(jnp.bfloat16)
        mixed = jnp.einsum("hqk,khd->qhd", weights, value_part, preferred_element_type=jnp.float32)
        return (mixed, log_total[..., 0])

    mixed_groups, log_totals = lax.map(forward_group, jnp.arange(group_count, dtype=jnp.int32))
    attended = (
        jnp.moveaxis(mixed_groups, 0, 1).reshape(tokens_dev, heads_width).astype(jnp.bfloat16)
    )
    middle = inputs + matmul_low(attended, out_full)
    normed_ffn = rms_scale(middle, gain_ffn).astype(jnp.bfloat16)
    logits = matmul_low(normed_ffn, router_full)
    router_probs = jax.nn.softmax(logits, axis=-1)
    expert_count = logits.shape[1]
    expert_ids = jnp.arange(expert_count, dtype=jnp.int32)
    chosen = (token_routes[:, :, None] == expert_ids[None, None, :]).astype(jnp.float32)
    gate_weights = jnp.sum(chosen * router_probs[:, None, :], axis=-1)
    capacity = 2 * tokens_dev * top_count // expert_count
    local_experts = expert_in_weight.shape[0]
    assigned = tokens_dev * top_count
    flat_routes = token_routes.reshape(assigned)
    onehot = (flat_routes[:, None] == expert_ids[None, :]).astype(jnp.int32)
    earlier = jnp.cumsum(onehot, axis=0) - onehot
    places = flat_routes * capacity + jnp.sum(earlier * onehot, axis=1)
    slot_source = (
        jnp.full((expert_count * capacity,), assigned, jnp.int32)
        .at[places]
        .set(jnp.arange(assigned, dtype=jnp.int32))
    )
    slot_token = slot_source // top_count
    padded_rows = jnp.concatenate([normed_ffn, jnp.zeros((1, model_width), jnp.bfloat16)], axis=0)
    outgoing = padded_rows[slot_token].reshape(ctx_count, local_experts * capacity, model_width)
    expert_inner, expert_outer = (
        lax.all_gather(expert_in_weight, "fsdp", axis=1, tiled=True),
        lax.all_gather(expert_out_weight, "fsdp", axis=1, tiled=True),
    )
    landed_tokens = lax.all_to_all(outgoing, "ctx", split_axis=0, concat_axis=0, tiled=True)
    incoming = landed_tokens.reshape(ctx_count, local_experts, capacity, model_width)
    expert_gu = jnp.einsum(
        "necd,edf->necf", incoming, expert_inner, preferred_element_type=jnp.float32
    )
    expert_width = expert_outer.shape[1]
    expert_hidden = swiglu_mix(expert_gu, expert_width).astype(jnp.bfloat16)
    expert_result = jnp.einsum(
        "necf,efd->necd", expert_hidden, expert_outer, preferred_element_type=jnp.float32
    ).astype(jnp.bfloat16)
    returned = lax.all_to_all(
        expert_result.reshape(ctx_count, local_experts * capacity, model_width),
        "ctx",
        split_axis=0,
        concat_axis=0,
        tiled=True,
    )
    picked = (
        returned.reshape(expert_count * capacity, model_width)[places]
        .reshape(tokens_dev, top_count, model_width)
        .astype(jnp.float32)
    )
    routed = jnp.sum(gate_weights[:, :, None] * picked, axis=1)
    upstream = out_grad.reshape(tokens_dev, model_width).astype(jnp.float32)
    shared_gu = matmul_low(normed_ffn, inner_full)
    shared_width = outer_full.shape[0]
    shared_hidden = swiglu_mix(shared_gu, shared_width).astype(jnp.bfloat16)
    shared_out = matmul_low(shared_hidden, outer_full)
    gate_value = jax.nn.sigmoid(matmul_low(normed_ffn, gate_full))
    output = middle + gate_value[:, None] * shared_out + routed
    hidden_out = output.astype(jnp.bfloat16).reshape(1, tokens_dev, model_width)
    gain_ffn, router_full, gate_full, inner_full, outer_full = (
        lax.all_gather(norm_gain_ffn, ("fsdp", "ctx"), axis=0, tiled=True),
        lax.all_gather(router_weight, ("fsdp", "ctx"), axis=0, tiled=True),
        lax.all_gather(shared_gate_weight, ("fsdp", "ctx"), axis=0, tiled=True),
        lax.all_gather(shared_in_weight, ("fsdp", "ctx"), axis=0, tiled=True),
        lax.all_gather(shared_out_weight, ("fsdp", "ctx"), axis=0, tiled=True),
    )
    gain_ffn = gain_ffn.astype(jnp.float32)
    grad_shared_out = (gate_value[:, None] * upstream).astype(jnp.bfloat16)
    grad_outer = jnp.einsum(
        "tf,td->fd", shared_hidden, grad_shared_out, preferred_element_type=jnp.float32
    )
    grad_hidden = jnp.einsum(
        "td,fd->tf", grad_shared_out, outer_full, preferred_element_type=jnp.float32
    )
    unused_mix, mix_pull = jax.vjp(partial(swiglu_mix, hidden_width=shared_width), shared_gu)
    grad_shared_gu = mix_pull(grad_hidden)[0].astype(jnp.bfloat16)
    grad_inner = jnp.einsum(
        "td,tf->df", normed_ffn, grad_shared_gu, preferred_element_type=jnp.float32
    )
    grad_normed = jnp.einsum(
        "tf,df->td", grad_shared_gu, inner_full, preferred_element_type=jnp.float32
    )
    grad_gate_logit = (
        gate_value * (1.0 - gate_value) * jnp.sum(upstream * shared_out, axis=1)
    ).astype(jnp.bfloat16)
    grad_gate_vec = jnp.einsum(
        "td,t->d", normed_ffn, grad_gate_logit, preferred_element_type=jnp.float32
    )
    grad_normed = (
        grad_normed
        + grad_gate_logit.astype(jnp.float32)[:, None] * gate_full.astype(jnp.float32)[None, :]
    )
    grad_gates = jnp.sum(upstream[:, None, :] * picked, axis=2)
    grad_choice_probs = jnp.sum(chosen * grad_gates[:, :, None], axis=1)
    grad_logits = (
        router_probs
        * (grad_choice_probs - jnp.sum(router_probs * grad_choice_probs, axis=1, keepdims=True))
    ).astype(jnp.bfloat16)
    grad_router = jnp.einsum(
        "td,te->de", normed_ffn, grad_logits, preferred_element_type=jnp.float32
    )
    grad_normed = grad_normed + jnp.einsum(
        "te,de->td", grad_logits, router_full, preferred_element_type=jnp.float32
    )
    grad_slots = (
        (gate_weights[:, :, None] * upstream[:, None, :])
        .astype(jnp.bfloat16)
        .reshape(assigned, model_width)
    )
    padded_grads = jnp.concatenate([grad_slots, jnp.zeros((1, model_width), jnp.bfloat16)], axis=0)
    grad_outgoing = padded_grads[slot_source].reshape(
        ctx_count, local_experts * capacity, model_width
    )
    grad_incoming = lax.all_to_all(
        grad_outgoing, "ctx", split_axis=0, concat_axis=0, tiled=True
    ).reshape(ctx_count, local_experts, capacity, model_width)
    grad_expert_hidden = jnp.einsum(
        "necd,efd->necf", grad_incoming, expert_outer, preferred_element_type=jnp.float32
    )
    grad_expert_outer = jnp.einsum(
        "necf,necd->efd", expert_hidden, grad_incoming, preferred_element_type=jnp.float32
    )
    unused_mix, expert_pull = jax.vjp(partial(swiglu_mix, hidden_width=expert_width), expert_gu)
    grad_expert_gu = expert_pull(grad_expert_hidden)[0].astype(jnp.bfloat16)
    grad_expert_inner = jnp.einsum(
        "necd,necf->edf", incoming, grad_expert_gu, preferred_element_type=jnp.float32
    )
    grad_expert_rows = jnp.einsum(
        "necf,edf->necd", grad_expert_gu, expert_inner, preferred_element_type=jnp.float32
    ).astype(jnp.bfloat16)
    grad_returned = lax.all_to_all(
        grad_expert_rows.reshape(ctx_count, local_experts * capacity, model_width),
        "ctx",
        split_axis=0,
        concat_axis=0,
        tiled=True,
    )
    grad_picked = grad_returned.reshape(expert_count * capacity, model_width)[places].reshape(
        tokens_dev, top_count, model_width
    )
    grad_normed = grad_normed + jnp.sum(grad_picked.astype(jnp.float32), axis=1)
    sum_expert_inner, sum_expert_outer = (
        lax.psum_scatter(
            grad_expert_inner.astype(jnp.bfloat16), "fsdp", scatter_dimension=1, tiled=True
        ).astype(jnp.float32),
        lax.psum_scatter(
            grad_expert_outer.astype(jnp.bfloat16), "fsdp", scatter_dimension=1, tiled=True
        ).astype(jnp.float32),
    )
    unused_norm, norm_pull = jax.vjp(rms_scale, middle, gain_ffn)
    grad_middle_norm, grad_gain_ffn = norm_pull(grad_normed)
    grad_middle = upstream + grad_middle_norm
    sum_gain_ffn, sum_router, sum_gate_vec, sum_inner, sum_outer = (
        lax.psum_scatter(grad_gain_ffn, ("fsdp", "ctx"), scatter_dimension=0, tiled=True),
        lax.psum_scatter(grad_router, ("fsdp", "ctx"), scatter_dimension=0, tiled=True),
        lax.psum_scatter(grad_gate_vec, ("fsdp", "ctx"), scatter_dimension=0, tiled=True),
        lax.psum_scatter(grad_inner, ("fsdp", "ctx"), scatter_dimension=0, tiled=True),
        lax.psum_scatter(grad_outer, ("fsdp", "ctx"), scatter_dimension=0, tiled=True),
    )
    grad_branch = grad_middle.astype(jnp.bfloat16)
    grad_out_mat = jnp.einsum(
        "tc,td->cd", attended, grad_branch, preferred_element_type=jnp.float32
    )
    grad_attended = jnp.einsum(
        "td,cd->tc", grad_branch, out_full, preferred_element_type=jnp.float32
    ).astype(jnp.bfloat16)
    keys_again, values_again = (
        lax.all_gather(key_low, "ctx", axis=0, tiled=True),
        lax.all_gather(value_low, "ctx", axis=0, tiled=True),
    )

    def backward_group(group_index):
        query_part = head_slice(query_low, group_index)
        key_part = head_slice(keys_again, group_index)
        value_part = head_slice(values_again, group_index)
        grad_part = head_slice(grad_attended, group_index)
        log_total = lax.dynamic_index_in_dim(log_totals, group_index, 0, keepdims=False)
        scores = jnp.einsum(
            "qhd,khd->hqk", query_part, key_part, preferred_element_type=jnp.float32
        )
        scores = jnp.where(allowed[None], scores, -1e30)
        weights = jnp.exp(scores - log_total[..., None])
        grad_weights = jnp.einsum(
            "qhd,khd->hqk", grad_part, value_part, preferred_element_type=jnp.float32
        )
        offset_term = jnp.sum(weights * grad_weights, axis=-1, keepdims=True)
        grad_scores = (weights * (grad_weights - offset_term)).astype(jnp.bfloat16)
        grad_query = jnp.einsum(
            "hqk,khd->qhd", grad_scores, key_part, preferred_element_type=jnp.float32
        )
        grad_key = jnp.einsum(
            "hqk,qhd->khd", grad_scores, query_part, preferred_element_type=jnp.float32
        )
        grad_value = jnp.einsum(
            "hqk,qhd->khd",
            weights.astype(jnp.bfloat16),
            grad_part,
            preferred_element_type=jnp.float32,
        )
        return (grad_query, grad_key, grad_value)

    grad_queries, grad_keys, grad_values = lax.map(
        backward_group, jnp.arange(group_count, dtype=jnp.int32)
    )
    row_total = keys_again.shape[0]
    grad_key_rows = jnp.moveaxis(grad_keys, 0, 1).reshape(row_total, heads_width)
    grad_value_rows = jnp.moveaxis(grad_values, 0, 1).reshape(row_total, heads_width)
    key_share, value_share = (
        lax.psum_scatter(
            grad_key_rows.astype(jnp.bfloat16), "ctx", scatter_dimension=0, tiled=True
        ).astype(jnp.float32),
        lax.psum_scatter(
            grad_value_rows.astype(jnp.bfloat16), "ctx", scatter_dimension=0, tiled=True
        ).astype(jnp.float32),
    )
    grad_query_heads = jnp.moveaxis(grad_queries, 0, 1).reshape(tokens_dev, head_count, HD)
    unused_rot, rotate_pull = jax.vjp(place_heads, query_pre, key_pre)
    grad_query_pre, grad_key_pre = rotate_pull(
        (grad_query_heads, key_share.reshape(tokens_dev, head_count, HD))
    )
    grad_projected = jnp.concatenate(
        [
            grad_query_pre.reshape(tokens_dev, heads_width),
            grad_key_pre.reshape(tokens_dev, heads_width),
            value_share,
        ],
        axis=1,
    ).astype(jnp.bfloat16)
    grad_qkv = jnp.einsum("td,tc->dc", normed, grad_projected, preferred_element_type=jnp.float32)
    grad_shift = jnp.sum(grad_projected.astype(jnp.float32), axis=0)
    grad_normed_attn = jnp.einsum(
        "tc,dc->td", grad_projected, qkv_full, preferred_element_type=jnp.float32
    )
    unused_norm, first_pull = jax.vjp(rms_scale, inputs, gain_attn)
    grad_inputs_norm, grad_gain_attn = first_pull(grad_normed_attn)
    input_grad = grad_middle + grad_inputs_norm
    sum_gain_attn, sum_qkv, sum_shift, sum_out = (
        lax.psum_scatter(grad_gain_attn, ("fsdp", "ctx"), scatter_dimension=0, tiled=True),
        lax.psum_scatter(grad_qkv, ("fsdp", "ctx"), scatter_dimension=0, tiled=True),
        lax.psum_scatter(grad_shift, ("fsdp", "ctx"), scatter_dimension=0, tiled=True),
        lax.psum_scatter(grad_out_mat, ("fsdp", "ctx"), scatter_dimension=0, tiled=True),
    )
    return (
        hidden_out,
        input_grad.reshape(1, tokens_dev, model_width),
        sum_gain_attn,
        sum_qkv,
        sum_shift,
        sum_out,
        sum_gain_ffn,
        sum_router,
        sum_gate_vec,
        sum_inner,
        sum_outer,
        sum_expert_inner,
        sum_expert_outer,
    )


def over(axis, array, dim=0):
    return lax.all_gather(array, axis, axis=dim, tiled=True)


def reduce_over(axis, array, dim=0):
    return lax.psum_scatter(array, axis, scatter_dimension=dim, tiled=True)


def exchange(array):
    return lax.all_to_all(array, "ctx", split_axis=0, concat_axis=0, tiled=True)


def transposed_dot(left, right):
    return lax.dot_general(
        left, right, (((0,), (0,)), ((), ())), preferred_element_type=jnp.float32
    )


def dot_transposed(left, right):
    return lax.dot_general(
        left, right, (((1,), (1,)), ((), ())), preferred_element_type=jnp.float32
    )


def split_plan(
    hidden_in,
    segments,
    block_pairs,
    routes,
    out_grad,
    norm_gain_attn,
    qkv_weight,
    qkv_bias,
    out_weight,
    norm_gain_ffn,
    router_weight,
    shared_gate_weight,
    shared_in_weight,
    shared_out_weight,
    expert_in_weight,
    expert_out_weight,
):
    low = jnp.bfloat16
    full = jnp.float32
    tokens_dev, width = hidden_in.shape[1:]
    block_len = tokens_dev // 2
    ctx_count = lax.axis_size("ctx")
    fsdp_count = lax.axis_size("fsdp")
    ctx_rank = lax.axis_index("ctx")
    dev_count = ctx_count * fsdp_count
    row_len = ctx_count * tokens_dev
    head_count = width // HD
    shard = qkv_weight.shape[0]
    expert_count = router_weight.shape[1]
    shared_shard = shared_out_weight.shape[0]
    shared_width = fsdp_count * shared_shard
    expert_width = expert_out_weight.shape[1] * fsdp_count
    pair_rank = ctx_rank // 2
    side = ctx_rank % 2
    pairs = ctx_count // 2
    head_order = [j + (p * 2 + t) * pairs for j in range(pairs) for p in range(2) for t in range(2)]

    small = jnp.concatenate(
        [
            norm_gain_attn,
            norm_gain_ffn,
            shared_gate_weight,
            router_weight.T.reshape(-1),
            qkv_bias,
        ]
    )[None, :]
    small_all = over(("fsdp", "ctx"), small)
    gain_attn = small_all[:, :shard].reshape(width).astype(full)
    gain_ffn = small_all[:, shard : 2 * shard].reshape(width).astype(full)
    gate_full = small_all[:, 2 * shard : 3 * shard].reshape(width)
    router_t = (
        small_all[:, 3 * shard : (3 + expert_count) * shard]
        .reshape(dev_count, expert_count, shard)
        .transpose(1, 0, 2)
        .reshape(expert_count, width)
    )
    bias_full = small_all[:, (3 + expert_count) * shard :].reshape(3, head_count, HD)
    router_gate = jnp.concatenate([router_t, gate_full[None, :]], axis=0)
    own_routes = routes.reshape(tokens_dev, -1)
    own_seg = segments.reshape(1, tokens_dev)
    numbers = over("ctx", jnp.concatenate([own_routes.T, own_seg], axis=0)[None])
    row_seg = numbers[:, -1].reshape(row_len)
    routed_here = jnp.any(numbers[:, :-1] == ctx_rank, axis=1).reshape(row_len)

    qkv_parts = (
        qkv_weight.reshape(shard, 3, head_count, HD)[:, :, jnp.array(head_order)]
        .reshape(shard, 3, ctx_count, 2 * HD)
        .transpose(2, 0, 1, 3)
        .reshape(ctx_count, shard, 6 * HD)
    )
    qkv_c = over("fsdp", exchange(qkv_parts).reshape(ctx_count * shard, 6 * HD))
    inner_parts = (
        shared_in_weight.reshape(shard, 2, fsdp_count, ctx_count, shared_shard)
        .transpose(3, 0, 1, 2, 4)
        .reshape(ctx_count, shard, 2 * shared_width)
    )
    inner_c = over("fsdp", exchange(inner_parts).reshape(ctx_count * shard, 2 * shared_width))
    outer_c = over("fsdp", shared_out_weight)
    out_full = over(("fsdp", "ctx"), out_weight)
    expert_inner = over("fsdp", expert_in_weight[0])
    expert_outer = over("fsdp", expert_out_weight[0])
    out_heads = out_full.reshape(head_count, HD, width)
    my_heads = [pair_rank + (side * 2 + t) * pairs for t in range(2)]
    out_c = jnp.concatenate(
        [lax.dynamic_index_in_dim(out_heads, h, 0, keepdims=False) for h in my_heads], axis=0
    )
    bias_c = jnp.concatenate(
        [lax.dynamic_index_in_dim(bias_full, h, 1, keepdims=False) for h in my_heads], axis=1
    ).reshape(6 * HD)

    offsets = jnp.arange(block_len, dtype=jnp.int32)
    positions = (block_pairs[:, None] * block_len + offsets[None, :]).reshape(row_len)
    own_inputs = hidden_in.reshape(tokens_dev, width)
    inputs = own_inputs.astype(full)
    row_inputs = over("ctx", own_inputs).astype(full)
    row_upstream = over("ctx", out_grad.reshape(tokens_dev, width))
    row_normed = rms_scale(row_inputs, gain_attn).astype(low)
    projected = matmul_low(row_normed, qkv_c) + bias_c.astype(full)
    query_pre = projected[:, : 2 * HD].reshape(row_len, 2, HD)
    key_pre = projected[:, 2 * HD : 4 * HD].reshape(row_len, 2, HD)

    def place_heads(query_in, key_in):
        return (rotate(query_in, positions) * HD ** (-0.5), rotate(key_in, positions))

    query_rot, key_rot = place_heads(query_pre, key_pre)
    queries = query_rot.astype(low)
    keys = key_rot.astype(low)
    values = projected[:, 4 * HD :].reshape(row_len, 2, HD).astype(low)
    seg_real = row_seg.astype(full)
    allowed = visible(positions, seg_real, positions, seg_real)

    def score_part():
        scores = jnp.einsum("qhd,khd->hqk", queries, keys, preferred_element_type=full)
        return jnp.where(allowed[None], scores, -1e30)

    scores = score_part()
    highest = jnp.max(scores, axis=-1, keepdims=True)
    log_total = highest + jnp.log(jnp.sum(jnp.exp(scores - highest), axis=-1, keepdims=True))
    probs = jnp.exp(scores - log_total)
    attended_row = (
        jnp.einsum("hqk,khd->qhd", probs.astype(low), values, preferred_element_type=full)
        .astype(low)
        .reshape(row_len, 2 * HD)
    )
    landed = exchange(attended_row.reshape(ctx_count, tokens_dev, 2 * HD))
    places_of = [head_order.index(h) for h in range(head_count)]
    attended = jnp.concatenate(
        [landed[p // 2, :, (p % 2) * HD : (p % 2 + 1) * HD] for p in places_of], axis=1
    )
    middle = inputs + matmul_low(attended, out_full)
    normed_ffn = rms_scale(middle, gain_ffn).astype(low)

    row_ffn = over("ctx", normed_ffn)
    row_logits = dot_transposed(row_ffn, router_gate)
    row_probs = jax.nn.softmax(row_logits[:, :expert_count], axis=-1)
    expert_ids = jnp.arange(expert_count, dtype=jnp.int32)
    here = jnp.where(
        routed_here, jnp.sum(jnp.where(expert_ids[None, :] == ctx_rank, row_probs, 0.0), axis=1), 0.0
    )
    row_gate = jax.nn.sigmoid(row_logits[:, expert_count])
    expert_gu = matmul_low(row_ffn, expert_inner)
    expert_hidden = swiglu_mix(expert_gu, expert_width).astype(low)
    expert_result = matmul_low(expert_hidden, expert_outer).astype(low).astype(full)
    shared_gu = matmul_low(row_ffn, inner_c)
    shared_hidden = swiglu_mix(shared_gu, shared_width).astype(low)
    shared_out = matmul_low(shared_hidden, outer_c)
    upstream_row = row_upstream.astype(full)
    out_part = (row_gate[:, None] * shared_out + here[:, None] * expert_result).astype(low)
    gate_dot = jnp.sum(upstream_row * shared_out, axis=1)
    expert_dot = jnp.where(routed_here, jnp.sum(upstream_row * expert_result, axis=1), 0.0)
    own_dots = exchange(
        jnp.stack([gate_dot, expert_dot]).reshape(2, ctx_count, tokens_dev).transpose(1, 0, 2)
    )
    output = middle + reduce_over("ctx", out_part).astype(full)
    hidden_out = output.astype(low).reshape(1, tokens_dev, width)

    grad_shared_out = (row_gate[:, None] * upstream_row).astype(low)
    grad_buffers = (here[:, None] * upstream_row).astype(low)
    grad_hidden = dot_transposed(grad_shared_out, outer_c)
    unused_mix, mix_pull = jax.vjp(partial(swiglu_mix, hidden_width=shared_width), shared_gu)
    grad_shared_gu = mix_pull(grad_hidden)[0].astype(low)
    grad_expert_hidden = dot_transposed(grad_buffers, expert_outer)
    unused_mix, expert_pull = jax.vjp(partial(swiglu_mix, hidden_width=expert_width), expert_gu)
    grad_expert_gu = expert_pull(grad_expert_hidden)[0].astype(low)
    grad_rows = dot_transposed(grad_expert_gu, expert_inner).astype(low).astype(full)
    grad_ffn_part = (dot_transposed(grad_shared_gu, inner_c) + grad_rows).astype(low)
    grad_normed = reduce_over("ctx", grad_ffn_part).astype(full)
    sum_expert_inner = reduce_over("fsdp", transposed_dot(row_ffn, grad_expert_gu).astype(low))
    sum_expert_outer = reduce_over("fsdp", transposed_dot(expert_hidden, grad_buffers).astype(low))
    sum_outer = reduce_over("fsdp", transposed_dot(shared_hidden, grad_shared_out).astype(low))
    sum_inner_c = reduce_over("fsdp", transposed_dot(row_ffn, grad_shared_gu).astype(low))
    sum_inner = (
        exchange(sum_inner_c.reshape(ctx_count, shard, 2 * shared_width))
        .reshape(ctx_count, shard, 2, fsdp_count, shared_shard)
        .transpose(1, 2, 3, 0, 4)
        .reshape(shard, 2 * fsdp_count * ctx_count * shared_shard)
    )

    own_logits = dot_transposed(normed_ffn, router_gate)
    router_probs = jax.nn.softmax(own_logits[:, :expert_count], axis=-1)
    gate_value = jax.nn.sigmoid(own_logits[:, expert_count])
    grad_gate_logit = gate_value * (1.0 - gate_value) * jnp.sum(own_dots[:, 0], axis=0)
    grad_choice = own_dots[:, 1].T
    grad_logits = router_probs * (
        grad_choice - jnp.sum(router_probs * grad_choice, axis=1, keepdims=True)
    )
    grad_small = jnp.concatenate([grad_logits, grad_gate_logit[:, None]], axis=1).astype(low)
    grad_router_gate = transposed_dot(grad_small, normed_ffn)
    grad_normed = grad_normed + matmul_low(grad_small, router_gate)
    unused_norm, norm_pull = jax.vjp(rms_scale, middle, gain_ffn)
    grad_middle_norm, grad_gain_ffn = norm_pull(grad_normed)
    grad_middle = out_grad.reshape(tokens_dev, width).astype(full) + grad_middle_norm

    row_branch = over("ctx", grad_middle.astype(low))
    grad_attended = dot_transposed(row_branch, out_c).astype(low).reshape(row_len, 2, HD)
    grad_out_c = transposed_dot(attended_row, row_branch).astype(low).reshape(2, HD, width)
    padded_out = jnp.concatenate(
        [jnp.where(side == p, grad_out_c, jnp.zeros_like(grad_out_c)) for p in range(2)], axis=0
    )
    pair_out = reduce_over("fsdp", padded_out).reshape(2, shard, width)
    kept = lax.dynamic_index_in_dim(pair_out, side, 0, keepdims=False)
    given = lax.dynamic_index_in_dim(pair_out, 1 - side, 0, keepdims=False)
    taken = lax.ppermute(given, "ctx", [(i, i ^ 1) for i in range(ctx_count)])
    sum_out = kept.astype(full) + taken.astype(full)

    grad_probs = jnp.einsum("qhd,khd->hqk", grad_attended, values, preferred_element_type=full)
    weights = jnp.exp(score_part() - log_total)
    offset_term = jnp.sum(weights * grad_probs, axis=-1, keepdims=True)
    grad_scores = (weights * (grad_probs - offset_term)).astype(low)
    grad_queries = jnp.einsum("hqk,khd->qhd", grad_scores, keys, preferred_element_type=full)
    grad_keys = jnp.einsum("hqk,qhd->khd", grad_scores, queries, preferred_element_type=full)
    grad_values = jnp.einsum(
        "hqk,qhd->khd", weights.astype(low), grad_attended, preferred_element_type=full
    )
    unused_rot, rotate_pull = jax.vjp(place_heads, query_pre, key_pre)
    grad_query_pre, grad_key_pre = rotate_pull((grad_queries, grad_keys))
    grad_projected = jnp.concatenate(
        [
            grad_query_pre.reshape(row_len, 2 * HD),
            grad_key_pre.reshape(row_len, 2 * HD),
            grad_values.reshape(row_len, 2 * HD),
        ],
        axis=1,
    ).astype(low)
    grad_attn_part = dot_transposed(grad_projected, qkv_c).astype(low)
    grad_normed_attn = reduce_over("ctx", grad_attn_part).astype(full)
    sum_qkv_c = reduce_over("fsdp", transposed_dot(row_normed, grad_projected).astype(low))
    sum_qkv = (
        exchange(sum_qkv_c.reshape(ctx_count, shard, 6 * HD))
        .reshape(ctx_count, shard, 3, 2, HD)
        .transpose(1, 2, 0, 3, 4)
        .reshape(shard, 3, head_count, HD)[:, :, jnp.array(places_of)]
        .reshape(shard, 3 * width)
    )
    grad_bias_c = jnp.sum(grad_projected.astype(full), axis=0).reshape(3, 1, 2, HD)
    mine = (jnp.arange(ctx_count) == ctx_rank)[None, :, None, None]
    grad_bias = (
        jnp.where(mine, grad_bias_c, 0.0)
        .reshape(3, head_count, HD)[:, jnp.array(places_of)]
        .reshape(dev_count, -1)
    )
    unused_norm, first_pull = jax.vjp(rms_scale, inputs, gain_attn)
    grad_inputs_norm, grad_gain_attn = first_pull(grad_normed_attn)
    input_grad = grad_middle + grad_inputs_norm
    small_grads = jnp.concatenate(
        [
            grad_gain_attn.reshape(dev_count, shard),
            grad_gain_ffn.reshape(dev_count, shard),
            grad_router_gate.reshape(expert_count + 1, dev_count, shard)
            .transpose(1, 0, 2)
            .reshape(dev_count, (expert_count + 1) * shard),
            grad_bias,
        ],
        axis=1,
    )
    sums = reduce_over(("fsdp", "ctx"), small_grads)[0]
    sum_router = sums[2 * shard : (2 + expert_count) * shard].reshape(expert_count, shard).T
    return (
        hidden_out,
        input_grad.reshape(1, tokens_dev, width),
        sums[:shard],
        sum_qkv.astype(full),
        sums[(3 + expert_count) * shard :],
        sum_out,
        sums[shard : 2 * shard],
        sum_router,
        sums[(2 + expert_count) * shard : (3 + expert_count) * shard],
        sum_inner.astype(full),
        sum_outer.astype(full),
        sum_expert_inner.astype(full)[None],
        sum_expert_outer.astype(full)[None],
    )


def local(*arrays):
    width = arrays[0].shape[2]
    ctx_count = lax.axis_size("ctx")
    shard = arrays[6].shape[0]
    fits = (
        width == 2 * ctx_count * HD
        and 2 * shard == HD
        and ctx_count % 2 == 0
        and lax.axis_size("fsdp") * ctx_count * shard == width
        and arrays[14].shape[0] == 1
    )
    return split_plan(*arrays) if fits else gathered_plan(*arrays)


def solution(mesh):
    in_specs = (
        P("fsdp", "ctx", None),
        P("fsdp", "ctx"),
        P(),
        P("fsdp", "ctx", None),
        P("fsdp", "ctx", None),
        P(("fsdp", "ctx")),
        P(("fsdp", "ctx"), None),
        P(("fsdp", "ctx")),
        P(("fsdp", "ctx"), None),
        P(("fsdp", "ctx")),
        P(("fsdp", "ctx"), None),
        P(("fsdp", "ctx")),
        P(("fsdp", "ctx"), None),
        P(("fsdp", "ctx"), None),
        P("ctx", "fsdp", None),
        P("ctx", "fsdp", None),
    )
    out_specs = (
        P("fsdp", "ctx", None),
        P("fsdp", "ctx", None),
        P(("fsdp", "ctx")),
        P(("fsdp", "ctx"), None),
        P(("fsdp", "ctx")),
        P(("fsdp", "ctx"), None),
        P(("fsdp", "ctx")),
        P(("fsdp", "ctx"), None),
        P(("fsdp", "ctx")),
        P(("fsdp", "ctx"), None),
        P(("fsdp", "ctx"), None),
        P("ctx", "fsdp", None),
        P("ctx", "fsdp", None),
    )
    return jax.shard_map(local, mesh=mesh, in_specs=in_specs, out_specs=out_specs, check_vma=False)
```

```python
import functools

import jax
import jax.numpy as jnp
from jax import lax
from jax.experimental import pallas as pl
from jax.experimental.pallas import tpu as pltpu
from jax.sharding import PartitionSpec as P

HD = 128


EPSILON = 1e-06
THETA = 1000000.0
heads_per_group = 4


def rms_scale(values, gain_vec):
    return (
        values * lax.rsqrt(jnp.mean(values * values, axis=-1, keepdims=True) + EPSILON) * gain_vec
    )


def rotate(values, positions):
    half_len = values.shape[-1] // 2
    frequency = THETA ** (-jnp.arange(half_len, dtype=jnp.float32) / half_len)
    angles = positions.astype(jnp.float32)[:, None] * frequency[None, :]
    cosine = jnp.cos(angles)[:, None, :]
    sine_part = jnp.sin(angles)[:, None, :]
    first_half = values[..., :half_len]
    second = values[..., half_len:]
    return jnp.concatenate(
        [first_half * cosine - second * sine_part, second * cosine + first_half * sine_part],
        axis=-1,
    )


def visible(query_pos, query_seg, key_pos, key_seg):
    same_doc = (key_seg[None, :] == query_seg[:, None]) & (query_seg[:, None] >= 0)
    causal = key_pos[None, :] <= query_pos[:, None]
    return same_doc & causal | (key_pos[None, :] == query_pos[:, None])


def swiglu_mix(gate_up, hidden_width):
    return jax.nn.silu(gate_up[..., :hidden_width]) * gate_up[..., hidden_width:]


def matmul_low(left, right):
    return jnp.dot(left, right, preferred_element_type=jnp.float32)


def gathered_plan(
    hidden_in,
    segments,
    block_pairs,
    routes,
    out_grad,
    norm_gain_attn,
    qkv_weight,
    qkv_bias,
    out_weight,
    norm_gain_ffn,
    router_weight,
    shared_gate_weight,
    shared_in_weight,
    shared_out_weight,
    expert_in_weight,
    expert_out_weight,
):
    tokens_dev = hidden_in.shape[1]
    model_width = hidden_in.shape[2]
    block_len = tokens_dev // 2
    inputs = hidden_in.reshape(tokens_dev, model_width).astype(jnp.float32)
    seg_local = segments.reshape(tokens_dev)
    token_routes = routes.reshape(tokens_dev, -1)
    top_count = token_routes.shape[1]
    ctx_count = lax.axis_size("ctx")
    ctx_rank = lax.axis_index("ctx")
    offsets = jnp.arange(block_len, dtype=jnp.int32)
    all_positions = (
        block_pairs.reshape(ctx_count, 2)[:, :, None] * block_len + offsets[None, None, :]
    ).reshape(ctx_count * tokens_dev)
    my_positions = lax.dynamic_slice_in_dim(all_positions, ctx_rank * tokens_dev, tokens_dev, 0)
    gathered = (
        lax.all_gather(norm_gain_attn, ("fsdp", "ctx"), axis=0, tiled=True),
        lax.all_gather(qkv_weight, ("fsdp", "ctx"), axis=0, tiled=True),
        lax.all_gather(qkv_bias, ("fsdp", "ctx"), axis=0, tiled=True),
        lax.all_gather(out_weight, ("fsdp", "ctx"), axis=0, tiled=True),
        lax.all_gather(norm_gain_ffn, ("fsdp", "ctx"), axis=0, tiled=True),
        lax.all_gather(router_weight, ("fsdp", "ctx"), axis=0, tiled=True),
        lax.all_gather(shared_gate_weight, ("fsdp", "ctx"), axis=0, tiled=True),
        lax.all_gather(shared_in_weight, ("fsdp", "ctx"), axis=0, tiled=True),
        lax.all_gather(shared_out_weight, ("fsdp", "ctx"), axis=0, tiled=True),
    )
    (
        gain_attn,
        qkv_full,
        shift_full,
        out_full,
        gain_ffn,
        router_full,
        gate_full,
        inner_full,
        outer_full,
    ) = gathered
    gain_attn = gain_attn.astype(jnp.float32)
    gain_ffn = gain_ffn.astype(jnp.float32)
    heads_width = out_full.shape[0]
    head_count = heads_width // HD
    group_width = heads_per_group * HD
    group_count = head_count // heads_per_group
    normed = rms_scale(inputs, gain_attn).astype(jnp.bfloat16)
    projected = matmul_low(normed, qkv_full) + shift_full.astype(jnp.float32)
    query_pre = projected[:, :heads_width].reshape(tokens_dev, head_count, HD)
    key_pre = projected[:, heads_width : 2 * heads_width].reshape(tokens_dev, head_count, HD)

    def place_heads(query_in, key_in):
        return (rotate(query_in, my_positions) * HD ** (-0.5), rotate(key_in, my_positions))

    query_rot, key_rot = place_heads(query_pre, key_pre)
    query_low = query_rot.reshape(tokens_dev, heads_width).astype(jnp.bfloat16)
    key_low = key_rot.reshape(tokens_dev, heads_width).astype(jnp.bfloat16)
    value_low = projected[:, 2 * heads_width :].astype(jnp.bfloat16)
    keys_all, values_all, segs_all = (
        lax.all_gather(key_low, "ctx", axis=0, tiled=True),
        lax.all_gather(value_low, "ctx", axis=0, tiled=True),
        lax.all_gather(seg_local.astype(jnp.bfloat16), "ctx", axis=0, tiled=True),
    )
    allowed = visible(
        my_positions, seg_local.astype(jnp.float32), all_positions, segs_all.astype(jnp.float32)
    )

    def head_slice(matrix, group_index):
        return lax.dynamic_slice_in_dim(matrix, group_index * group_width, group_width, 1).reshape(
            matrix.shape[0], heads_per_group, HD
        )

    def forward_group(group_index):
        query_part = head_slice(query_low, group_index)
        key_part = head_slice(keys_all, group_index)
        value_part = head_slice(values_all, group_index)
        scores = jnp.einsum(
            "qhd,khd->hqk", query_part, key_part, preferred_element_type=jnp.float32
        )
        scores = jnp.where(allowed[None], scores, -1e30)
        highest = jnp.max(scores, axis=-1, keepdims=True)
        log_total = highest + jnp.log(jnp.sum(jnp.exp(scores - highest), axis=-1, keepdims=True))
        weights = jnp.exp(scores - log_total).astype(jnp.bfloat16)
        mixed = jnp.einsum("hqk,khd->qhd", weights, value_part, preferred_element_type=jnp.float32)
        return (mixed, log_total[..., 0])

    mixed_groups, log_totals = lax.map(forward_group, jnp.arange(group_count, dtype=jnp.int32))
    attended = (
        jnp.moveaxis(mixed_groups, 0, 1).reshape(tokens_dev, heads_width).astype(jnp.bfloat16)
    )
    middle = inputs + matmul_low(attended, out_full)
    normed_ffn = rms_scale(middle, gain_ffn).astype(jnp.bfloat16)
    logits = matmul_low(normed_ffn, router_full)
    router_probs = jax.nn.softmax(logits, axis=-1)
    expert_count = logits.shape[1]
    expert_ids = jnp.arange(expert_count, dtype=jnp.int32)
    chosen = (token_routes[:, :, None] == expert_ids[None, None, :]).astype(jnp.float32)
    gate_weights = jnp.sum(chosen * router_probs[:, None, :], axis=-1)
    capacity = 2 * tokens_dev * top_count // expert_count
    local_experts = expert_in_weight.shape[0]
    assigned = tokens_dev * top_count
    flat_routes = token_routes.reshape(assigned)
    onehot = (flat_routes[:, None] == expert_ids[None, :]).astype(jnp.int32)
    earlier = jnp.cumsum(onehot, axis=0) - onehot
    places = flat_routes * capacity + jnp.sum(earlier * onehot, axis=1)
    slot_source = (
        jnp.full((expert_count * capacity,), assigned, jnp.int32)
        .at[places]
        .set(jnp.arange(assigned, dtype=jnp.int32))
    )
    slot_token = slot_source // top_count
    padded_rows = jnp.concatenate([normed_ffn, jnp.zeros((1, model_width), jnp.bfloat16)], axis=0)
    outgoing = padded_rows[slot_token].reshape(ctx_count, local_experts * capacity, model_width)
    expert_inner, expert_outer = (
        lax.all_gather(expert_in_weight, "fsdp", axis=1, tiled=True),
        lax.all_gather(expert_out_weight, "fsdp", axis=1, tiled=True),
    )
    landed_tokens = lax.all_to_all(outgoing, "ctx", split_axis=0, concat_axis=0, tiled=True)
    incoming = landed_tokens.reshape(ctx_count, local_experts, capacity, model_width)
    expert_gu = jnp.einsum(
        "necd,edf->necf", incoming, expert_inner, preferred_element_type=jnp.float32
    )
    expert_width = expert_outer.shape[1]
    expert_hidden = swiglu_mix(expert_gu, expert_width).astype(jnp.bfloat16)
    expert_result = jnp.einsum(
        "necf,efd->necd", expert_hidden, expert_outer, preferred_element_type=jnp.float32
    ).astype(jnp.bfloat16)
    returned = lax.all_to_all(
        expert_result.reshape(ctx_count, local_experts * capacity, model_width),
        "ctx",
        split_axis=0,
        concat_axis=0,
        tiled=True,
    )
    picked = (
        returned.reshape(expert_count * capacity, model_width)[places]
        .reshape(tokens_dev, top_count, model_width)
        .astype(jnp.float32)
    )
    routed = jnp.sum(gate_weights[:, :, None] * picked, axis=1)
    upstream = out_grad.reshape(tokens_dev, model_width).astype(jnp.float32)
    shared_gu = matmul_low(normed_ffn, inner_full)
    shared_width = outer_full.shape[0]
    shared_hidden = swiglu_mix(shared_gu, shared_width).astype(jnp.bfloat16)
    shared_out = matmul_low(shared_hidden, outer_full)
    gate_value = jax.nn.sigmoid(matmul_low(normed_ffn, gate_full))
    output = middle + gate_value[:, None] * shared_out + routed
    hidden_out = output.astype(jnp.bfloat16).reshape(1, tokens_dev, model_width)
    gain_ffn, router_full, gate_full, inner_full, outer_full = (
        lax.all_gather(norm_gain_ffn, ("fsdp", "ctx"), axis=0, tiled=True),
        lax.all_gather(router_weight, ("fsdp", "ctx"), axis=0, tiled=True),
        lax.all_gather(shared_gate_weight, ("fsdp", "ctx"), axis=0, tiled=True),
        lax.all_gather(shared_in_weight, ("fsdp", "ctx"), axis=0, tiled=True),
        lax.all_gather(shared_out_weight, ("fsdp", "ctx"), axis=0, tiled=True),
    )
    gain_ffn = gain_ffn.astype(jnp.float32)
    grad_shared_out = (gate_value[:, None] * upstream).astype(jnp.bfloat16)
    grad_outer = jnp.einsum(
        "tf,td->fd", shared_hidden, grad_shared_out, preferred_element_type=jnp.float32
    )
    grad_hidden = jnp.einsum(
        "td,fd->tf", grad_shared_out, outer_full, preferred_element_type=jnp.float32
    )
    unused_mix, mix_pull = jax.vjp(functools.partial(swiglu_mix, hidden_width=shared_width), shared_gu)
    grad_shared_gu = mix_pull(grad_hidden)[0].astype(jnp.bfloat16)
    grad_inner = jnp.einsum(
        "td,tf->df", normed_ffn, grad_shared_gu, preferred_element_type=jnp.float32
    )
    grad_normed = jnp.einsum(
        "tf,df->td", grad_shared_gu, inner_full, preferred_element_type=jnp.float32
    )
    grad_gate_logit = (
        gate_value * (1.0 - gate_value) * jnp.sum(upstream * shared_out, axis=1)
    ).astype(jnp.bfloat16)
    grad_gate_vec = jnp.einsum(
        "td,t->d", normed_ffn, grad_gate_logit, preferred_element_type=jnp.float32
    )
    grad_normed = (
        grad_normed
        + grad_gate_logit.astype(jnp.float32)[:, None] * gate_full.astype(jnp.float32)[None, :]
    )
    grad_gates = jnp.sum(upstream[:, None, :] * picked, axis=2)
    grad_choice_probs = jnp.sum(chosen * grad_gates[:, :, None], axis=1)
    grad_logits = (
        router_probs
        * (grad_choice_probs - jnp.sum(router_probs * grad_choice_probs, axis=1, keepdims=True))
    ).astype(jnp.bfloat16)
    grad_router = jnp.einsum(
        "td,te->de", normed_ffn, grad_logits, preferred_element_type=jnp.float32
    )
    grad_normed = grad_normed + jnp.einsum(
        "te,de->td", grad_logits, router_full, preferred_element_type=jnp.float32
    )
    grad_slots = (
        (gate_weights[:, :, None] * upstream[:, None, :])
        .astype(jnp.bfloat16)
        .reshape(assigned, model_width)
    )
    padded_grads = jnp.concatenate([grad_slots, jnp.zeros((1, model_width), jnp.bfloat16)], axis=0)
    grad_outgoing = padded_grads[slot_source].reshape(
        ctx_count, local_experts * capacity, model_width
    )
    grad_incoming = lax.all_to_all(
        grad_outgoing, "ctx", split_axis=0, concat_axis=0, tiled=True
    ).reshape(ctx_count, local_experts, capacity, model_width)
    grad_expert_hidden = jnp.einsum(
        "necd,efd->necf", grad_incoming, expert_outer, preferred_element_type=jnp.float32
    )
    grad_expert_outer = jnp.einsum(
        "necf,necd->efd", expert_hidden, grad_incoming, preferred_element_type=jnp.float32
    )
    unused_mix, expert_pull = jax.vjp(functools.partial(swiglu_mix, hidden_width=expert_width), expert_gu)
    grad_expert_gu = expert_pull(grad_expert_hidden)[0].astype(jnp.bfloat16)
    grad_expert_inner = jnp.einsum(
        "necd,necf->edf", incoming, grad_expert_gu, preferred_element_type=jnp.float32
    )
    grad_expert_rows = jnp.einsum(
        "necf,edf->necd", grad_expert_gu, expert_inner, preferred_element_type=jnp.float32
    ).astype(jnp.bfloat16)
    grad_returned = lax.all_to_all(
        grad_expert_rows.reshape(ctx_count, local_experts * capacity, model_width),
        "ctx",
        split_axis=0,
        concat_axis=0,
        tiled=True,
    )
    grad_picked = grad_returned.reshape(expert_count * capacity, model_width)[places].reshape(
        tokens_dev, top_count, model_width
    )
    grad_normed = grad_normed + jnp.sum(grad_picked.astype(jnp.float32), axis=1)
    sum_expert_inner, sum_expert_outer = (
        lax.psum_scatter(
            grad_expert_inner.astype(jnp.bfloat16), "fsdp", scatter_dimension=1, tiled=True
        ).astype(jnp.float32),
        lax.psum_scatter(
            grad_expert_outer.astype(jnp.bfloat16), "fsdp", scatter_dimension=1, tiled=True
        ).astype(jnp.float32),
    )
    unused_norm, norm_pull = jax.vjp(rms_scale, middle, gain_ffn)
    grad_middle_norm, grad_gain_ffn = norm_pull(grad_normed)
    grad_middle = upstream + grad_middle_norm
    sum_gain_ffn, sum_router, sum_gate_vec, sum_inner, sum_outer = (
        lax.psum_scatter(grad_gain_ffn, ("fsdp", "ctx"), scatter_dimension=0, tiled=True),
        lax.psum_scatter(grad_router, ("fsdp", "ctx"), scatter_dimension=0, tiled=True),
        lax.psum_scatter(grad_gate_vec, ("fsdp", "ctx"), scatter_dimension=0, tiled=True),
        lax.psum_scatter(grad_inner, ("fsdp", "ctx"), scatter_dimension=0, tiled=True),
        lax.psum_scatter(grad_outer, ("fsdp", "ctx"), scatter_dimension=0, tiled=True),
    )
    grad_branch = grad_middle.astype(jnp.bfloat16)
    grad_out_mat = jnp.einsum(
        "tc,td->cd", attended, grad_branch, preferred_element_type=jnp.float32
    )
    grad_attended = jnp.einsum(
        "td,cd->tc", grad_branch, out_full, preferred_element_type=jnp.float32
    ).astype(jnp.bfloat16)
    keys_again, values_again = (
        lax.all_gather(key_low, "ctx", axis=0, tiled=True),
        lax.all_gather(value_low, "ctx", axis=0, tiled=True),
    )

    def backward_group(group_index):
        query_part = head_slice(query_low, group_index)
        key_part = head_slice(keys_again, group_index)
        value_part = head_slice(values_again, group_index)
        grad_part = head_slice(grad_attended, group_index)
        log_total = lax.dynamic_index_in_dim(log_totals, group_index, 0, keepdims=False)
        scores = jnp.einsum(
            "qhd,khd->hqk", query_part, key_part, preferred_element_type=jnp.float32
        )
        scores = jnp.where(allowed[None], scores, -1e30)
        weights = jnp.exp(scores - log_total[..., None])
        grad_weights = jnp.einsum(
            "qhd,khd->hqk", grad_part, value_part, preferred_element_type=jnp.float32
        )
        offset_term = jnp.sum(weights * grad_weights, axis=-1, keepdims=True)
        grad_scores = (weights * (grad_weights - offset_term)).astype(jnp.bfloat16)
        grad_query = jnp.einsum(
            "hqk,khd->qhd", grad_scores, key_part, preferred_element_type=jnp.float32
        )
        grad_key = jnp.einsum(
            "hqk,qhd->khd", grad_scores, query_part, preferred_element_type=jnp.float32
        )
        grad_value = jnp.einsum(
            "hqk,qhd->khd",
            weights.astype(jnp.bfloat16),
            grad_part,
            preferred_element_type=jnp.float32,
        )
        return (grad_query, grad_key, grad_value)

    grad_queries, grad_keys, grad_values = lax.map(
        backward_group, jnp.arange(group_count, dtype=jnp.int32)
    )
    row_total = keys_again.shape[0]
    grad_key_rows = jnp.moveaxis(grad_keys, 0, 1).reshape(row_total, heads_width)
    grad_value_rows = jnp.moveaxis(grad_values, 0, 1).reshape(row_total, heads_width)
    key_share, value_share = (
        lax.psum_scatter(
            grad_key_rows.astype(jnp.bfloat16), "ctx", scatter_dimension=0, tiled=True
        ).astype(jnp.float32),
        lax.psum_scatter(
            grad_value_rows.astype(jnp.bfloat16), "ctx", scatter_dimension=0, tiled=True
        ).astype(jnp.float32),
    )
    grad_query_heads = jnp.moveaxis(grad_queries, 0, 1).reshape(tokens_dev, head_count, HD)
    unused_rot, rotate_pull = jax.vjp(place_heads, query_pre, key_pre)
    grad_query_pre, grad_key_pre = rotate_pull(
        (grad_query_heads, key_share.reshape(tokens_dev, head_count, HD))
    )
    grad_projected = jnp.concatenate(
        [
            grad_query_pre.reshape(tokens_dev, heads_width),
            grad_key_pre.reshape(tokens_dev, heads_width),
            value_share,
        ],
        axis=1,
    ).astype(jnp.bfloat16)
    grad_qkv = jnp.einsum("td,tc->dc", normed, grad_projected, preferred_element_type=jnp.float32)
    grad_shift = jnp.sum(grad_projected.astype(jnp.float32), axis=0)
    grad_normed_attn = jnp.einsum(
        "tc,dc->td", grad_projected, qkv_full, preferred_element_type=jnp.float32
    )
    unused_norm, first_pull = jax.vjp(rms_scale, inputs, gain_attn)
    grad_inputs_norm, grad_gain_attn = first_pull(grad_normed_attn)
    input_grad = grad_middle + grad_inputs_norm
    sum_gain_attn, sum_qkv, sum_shift, sum_out = (
        lax.psum_scatter(grad_gain_attn, ("fsdp", "ctx"), scatter_dimension=0, tiled=True),
        lax.psum_scatter(grad_qkv, ("fsdp", "ctx"), scatter_dimension=0, tiled=True),
        lax.psum_scatter(grad_shift, ("fsdp", "ctx"), scatter_dimension=0, tiled=True),
        lax.psum_scatter(grad_out_mat, ("fsdp", "ctx"), scatter_dimension=0, tiled=True),
    )
    return (
        hidden_out,
        input_grad.reshape(1, tokens_dev, model_width),
        sum_gain_attn,
        sum_qkv,
        sum_shift,
        sum_out,
        sum_gain_ffn,
        sum_router,
        sum_gate_vec,
        sum_inner,
        sum_outer,
        sum_expert_inner,
        sum_expert_outer,
    )


MESH = pl.DeviceIdType.MESH
ANY = pl.BlockSpec(memory_space=pl.ANY)
VMEM = pl.BlockSpec(memory_space=pltpu.VMEM)


def remote(source, target, send_sem, recv_sem, **place):
    return pltpu.make_async_remote_copy(
        src_ref=source,
        dst_ref=target,
        send_sem=send_sem,
        recv_sem=recv_sem,
        device_id=place,
        device_id_type=MESH,
    )


def line_place():
    here = lax.axis_index("ctx")
    line = here % 2
    return here, here // 2, line, here + 1 - 2 * line


def greet_line(last, here, level, side):
    barrier = pltpu.get_barrier_semaphore()
    pl.semaphore_signal(barrier, inc=1, device_id={"ctx": side}, device_id_type=MESH)

    @pl.when(level < last)
    def up():
        pl.semaphore_signal(barrier, inc=1, device_id={"ctx": here + 2}, device_id_type=MESH)

    @pl.when(level > 0)
    def down():
        pl.semaphore_signal(barrier, inc=1, device_id={"ctx": here - 2}, device_id_type=MESH)

    ends = jnp.where(level < last, 1, 0) + jnp.where(level > 0, 1, 0)
    pl.semaphore_wait(barrier, 1 + ends)


def line_copy(rows_ref, block, way, target, sems, source=None):
    send_sem, recv_sem = sems
    return remote(
        rows_ref.at[block] if source is None else source,
        rows_ref.at[block],
        send_sem.at[block, way],
        recv_sem.at[block],
        ctx=target,
    )


def line_start(rows_ref, own_ref, sems, place, last):
    here, level, line, side = place

    @pl.when(level < last)
    def up():
        line_copy(rows_ref, here, 0, here + 2, sems, own_ref).start()

    @pl.when(level > 0)
    def down():
        line_copy(rows_ref, here, 1, here - 2, sems, own_ref).start()

    line_copy(rows_ref, here, 2, side, sems, own_ref).start()


def line_step(rows_ref, sems, place, last, step):
    here, level, line, side = place

    @pl.when(level >= step)
    def from_below():
        block = here - 2 * step
        line_copy(rows_ref, block, 0, side, sems).wait_recv()

        @pl.when(level < last)
        def on():
            line_copy(rows_ref, block, 0, here + 2, sems).start()

        line_copy(rows_ref, block, 2, side, sems).start()

    @pl.when(level + step <= last)
    def from_above():
        block = here + 2 * step
        line_copy(rows_ref, block, 1, side, sems).wait_recv()

        @pl.when(level > 0)
        def on():
            line_copy(rows_ref, block, 1, here - 2, sems).start()

        line_copy(rows_ref, block, 2, side, sems).start()


def line_finish(rows_ref, sems, place, last):
    here, level, line, side = place
    for other in range(last + 1):
        block = 2 * other + line
        line_copy(rows_ref, 2 * other + 1 - line, 2, side, sems).wait_recv()
        line_copy(rows_ref, block, 2, side, sems).wait_send()

        @pl.when((other <= level) & (level < last))
        def up():
            line_copy(rows_ref, block, 0, side, sems).wait_send()

        @pl.when((other >= level) & (level > 0))
        def down():
            line_copy(rows_ref, block, 1, side, sems).wait_send()


def gather_kernel(last, count, *refs):
    owns, rows = refs[:count], refs[count : 2 * count]
    keep_sem = refs[2 * count]
    place = line_place()
    here, level, line, side = place
    sems = [(refs[2 * count + 1 + 2 * i], refs[2 * count + 2 + 2 * i]) for i in range(count)]
    greet_line(last, here, level, side)
    keeps = [
        pltpu.make_async_copy(owns[i], rows[i].at[here], keep_sem.at[i]) for i in range(count)
    ]
    for i in range(count):
        line_start(rows[i], owns[i], sems[i], place, last)
        keeps[i].start()
    for i in range(count):
        for step in range(1, last + 1):
            line_step(rows[i], sems[i], place, last, step)
    for i in range(count):
        line_finish(rows[i], sems[i], place, last)
        keeps[i].wait()


def line_gather(ctx_count, call_id, *arrays):
    count = len(arrays)
    return pl.pallas_call(
        functools.partial(gather_kernel, ctx_count // 2 - 1, count),
        out_shape=[jax.ShapeDtypeStruct((ctx_count,) + a.shape, a.dtype) for a in arrays],
        in_specs=[ANY] * count,
        out_specs=[ANY] * count,
        scratch_shapes=[pltpu.SemaphoreType.DMA((count,))]
        + [
            pltpu.SemaphoreType.DMA((ctx_count, 3)),
            pltpu.SemaphoreType.DMA((ctx_count,)),
        ]
        * count,
        compiler_params=pltpu.CompilerParams(collective_id=call_id, has_side_effects=True),
        name="line_gather",
    )(*arrays)


ROWS_STEP = 16


def add_rows(target, pieces, row_count):
    def one(index, carry):
        rows = pl.ds(pl.multiple_of(index * ROWS_STEP, ROWS_STEP), ROWS_STEP)
        total = pieces[0][rows, :].astype(jnp.float32)
        for piece in pieces[1:]:
            total = total + piece[rows, :].astype(jnp.float32)
        target[rows, :] = total.astype(target.dtype)
        return carry

    lax.fori_loop(0, row_count // ROWS_STEP, one, 0)


def scatter_turns(last, part, total, crossed, rising, falling, sums, *sems):
    cross_send, cross_recv, move_send, rise_recv, fall_recv = sems
    here, level, line, side = line_place()
    row_count = total.shape[0]

    def turn(k):
        middle = (level > 0) & (level < last)
        swapped = k + jnp.where(middle, (0, 0, 1, -1)[k], 0)
        return jnp.where(level * 2 < last, last - swapped, swapped)

    def cross(goal):
        return remote(
            part.at[2 * goal + 1 - line],
            crossed.at[goal],
            cross_send.at[goal],
            cross_recv.at[goal],
            ctx=side,
        )

    def rise(goal):
        return remote(
            sums.at[goal], rising.at[goal], move_send.at[goal], rise_recv.at[goal], ctx=here + 2
        )

    def fall(goal):
        return remote(
            sums.at[goal], falling.at[goal], move_send.at[goal], fall_recv.at[goal], ctx=here - 2
        )

    for k in range(last + 1):
        cross(turn(k)).start()
    for k in range(last + 1):
        yield k
        goal = turn(k)
        mine = part.at[2 * goal + line]
        cross(goal).wait_recv()

        @pl.when(goal > level)
        def upward():
            @pl.when(level > 0)
            def joined():
                rise(goal).wait_recv()
                add_rows(sums.at[goal], (mine, crossed.at[goal], rising.at[goal]), row_count)

            @pl.when(level == 0)
            def first():
                add_rows(sums.at[goal], (mine, crossed.at[goal]), row_count)

            rise(goal).start()

        @pl.when(goal < level)
        def downward():
            @pl.when(level < last)
            def joined():
                fall(goal).wait_recv()
                add_rows(sums.at[goal], (mine, crossed.at[goal], falling.at[goal]), row_count)

            @pl.when(level == last)
            def first():
                add_rows(sums.at[goal], (mine, crossed.at[goal]), row_count)

            fall(goal).start()

        @pl.when(goal == level)
        def here_at_last():
            @pl.when(level > 0)
            def from_below():
                rise(goal).wait_recv()

            @pl.when(level < last)
            def from_above():
                fall(goal).wait_recv()

            @pl.when(level == 0)
            def bottom():
                add_rows(total, (mine, crossed.at[goal], falling.at[goal]), row_count)

            @pl.when(level == last)
            def top():
                add_rows(total, (mine, crossed.at[goal], rising.at[goal]), row_count)

            @pl.when((level > 0) & (level < last))
            def between():
                add_rows(
                    total,
                    (mine, crossed.at[goal], rising.at[goal], falling.at[goal]),
                    row_count,
                )

    for goal in range(last + 1):
        cross(goal).wait_send()

        @pl.when(goal != level)
        def sent():
            rise(goal).wait_send()


def scatter_kernel(last, count, *refs):
    parts, totals = refs[:count], refs[count : 2 * count]
    slots, sems = refs[2 * count : 6 * count], refs[6 * count :]
    here, level, line, side = line_place()
    greet_line(last, here, level, side)
    turns = [
        scatter_turns(
            last, parts[i], totals[i], *slots[4 * i : 4 * i + 4], *sems[5 * i : 5 * i + 5]
        )
        for i in range(count)
    ]
    for each in turns:
        next(each)
    for each in turns:
        for step in each:
            pass


def line_scatter(ctx_count, call_id, *parts):
    rows, width = parts[0].shape[1:]
    count = len(parts)
    half = ctx_count // 2
    dma = pltpu.SemaphoreType.DMA((half,))
    slots = pltpu.VMEM((half, rows, width), parts[0].dtype)
    return pl.pallas_call(
        functools.partial(scatter_kernel, half - 1, count),
        out_shape=[jax.ShapeDtypeStruct((rows, width), jnp.float32)] * count,
        in_specs=[VMEM] * count,
        out_specs=[VMEM] * count,
        scratch_shapes=[slots] * (4 * count) + [dma] * (5 * count),
        compiler_params=pltpu.CompilerParams(
            collective_id=call_id, has_side_effects=True, vmem_limit_bytes=48 * 2**20
        ),
        name="line_scatter",
    )(*parts)


def fsdp_place():
    here = lax.axis_index("fsdp")
    beside = here + 1 - 2 * (here % 2)
    return here, beside, (here + 2) % 4, (beside + 2) % 4


def greet_all(ctx_count):
    barrier = pltpu.get_barrier_semaphore()
    here = lax.axis_index("ctx")
    group = lax.axis_index("fsdp")
    for k in range(1, ctx_count):
        pl.semaphore_signal(
            barrier, inc=1, device_id={"ctx": (here + k) % ctx_count}, device_id_type=MESH
        )
    for k in range(1, 4):
        pl.semaphore_signal(barrier, inc=1, device_id={"fsdp": (group + k) % 4}, device_id_type=MESH)
    pl.semaphore_wait(barrier, ctx_count + 2)


def share_start(blocks, sems):
    send_sem, recv_sem = sems
    here, beside, across, corner = fsdp_place()
    for way, target in ((0, across), (1, beside)):
        remote(
            blocks.at[here], blocks.at[here], send_sem.at[way], recv_sem.at[here], fsdp=target
        ).start()


def share_step(blocks, sems):
    send_sem, recv_sem = sems
    here, beside, across, corner = fsdp_place()
    copy = remote(
        blocks.at[across], blocks.at[across], send_sem.at[2], recv_sem.at[across], fsdp=beside
    )
    copy.wait_recv()
    copy.start()


def share_finish(blocks, sems):
    send_sem, recv_sem = sems
    here, beside, across, corner = fsdp_place()
    for way, block in ((0, beside), (1, corner)):
        copy = remote(
            blocks.at[block], blocks.at[block], send_sem.at[way], recv_sem.at[block], fsdp=beside
        )
        copy.wait_recv()
        copy.wait_send()
    remote(
        blocks.at[here], blocks.at[here], send_sem.at[2], recv_sem.at[here], fsdp=beside
    ).wait_send()


def spread(pieces, landing, sems, ctx_count):
    send_sem, recv_sem = sems
    here = lax.axis_index("ctx")

    def copy(k, peer, source):
        return remote(pieces(peer), landing(source), send_sem.at[k], recv_sem.at[k], ctx=peer)

    starts = [copy(k, (here + k) % ctx_count, here) for k in range(1, ctx_count)]
    waits = [
        copy(k, (here + k) % ctx_count, (here + ctx_count - k) % ctx_count)
        for k in range(1, ctx_count)
    ]
    return starts, waits


def opening_kernel(
    ctx_count,
    own,
    qkv_own,
    out_own,
    small_own,
    number_own,
    rows,
    qkv,
    out_pair,
    small,
    numbers,
    keep_sem,
    pair_send,
    pair_recv,
    row_send,
    row_recv,
    *sems,
):
    last = ctx_count // 2 - 1
    place = line_place()
    here, level, line, side = place
    group = lax.axis_index("fsdp")
    sems = [(sems[2 * i], sems[2 * i + 1]) for i in range(6)]
    qkv_spread, small_spread, number_spread, qkv_share, out_share, small_share = sems
    row_sems = (row_send, row_recv)
    greet_all(ctx_count)
    qkv_start, qkv_wait = spread(
        lambda peer: qkv_own.at[peer], lambda source: qkv.at[group, source], qkv_spread, ctx_count
    )
    small_start, small_wait = spread(
        lambda peer: small_own, lambda source: small.at[group, source], small_spread, ctx_count
    )
    number_start, number_wait = spread(
        lambda peer: number_own, lambda source: numbers.at[source], number_spread, ctx_count
    )
    for copy in qkv_start + small_start + number_start:
        copy.start()
    line_start(rows, own, row_sems, place, last)
    pair = remote(
        out_own, out_pair.at[group, line], pair_send.at[0], pair_recv.at[0], ctx=side
    )
    pair.start()
    keeps = [
        pltpu.make_async_copy(source, target, keep_sem.at[i])
        for i, (source, target) in enumerate(
            (
                (qkv_own.at[here], qkv.at[group, here]),
                (out_own, out_pair.at[group, line]),
                (small_own, small.at[group, here]),
                (number_own, numbers.at[here]),
                (own, rows.at[here]),
            )
        )
    ]
    for copy in keeps:
        copy.start()
    line_step(rows, row_sems, place, last, 1)
    for copy in small_wait + qkv_wait:
        copy.wait_recv()
    keeps[2].wait()
    keeps[0].wait()
    share_start(small, small_share)
    share_start(qkv, qkv_share)
    remote(
        out_own, out_pair.at[group, 1 - line], pair_send.at[0], pair_recv.at[0], ctx=side
    ).wait_recv()
    keeps[1].wait()
    share_start(out_pair, out_share)
    line_step(rows, row_sems, place, last, 2)
    share_step(small, small_share)
    share_step(qkv, qkv_share)
    for step in range(3, last + 1):
        line_step(rows, row_sems, place, last, step)
    share_step(out_pair, out_share)
    line_finish(rows, row_sems, place, last)
    for copy in number_wait:
        copy.wait_recv()
    for copy in qkv_start + small_start + number_start:
        copy.wait_send()
    pair.wait_send()
    share_finish(small, small_share)
    share_finish(qkv, qkv_share)
    share_finish(out_pair, out_share)
    keeps[3].wait()
    keeps[4].wait()


def opening(ctx_count, call_id, own, qkv_own, out_own, small_own, number_own):
    def out(lead, array):
        return jax.ShapeDtypeStruct(lead + array.shape, array.dtype)

    dma = pltpu.SemaphoreType.DMA
    return pl.pallas_call(
        functools.partial(opening_kernel, ctx_count),
        out_shape=[
            out((ctx_count,), own),
            out((4,), qkv_own),
            out((4, 2), out_own),
            out((4, ctx_count), small_own),
            out((ctx_count,), number_own),
        ],
        in_specs=[ANY] * 5,
        out_specs=[ANY] * 5,
        scratch_shapes=[
            dma((5,)),
            dma((1,)),
            dma((1,)),
            dma((ctx_count, 3)),
            dma((ctx_count,)),
        ]
        + [dma((ctx_count,))] * 6
        + [dma((3,)), dma((4,))] * 3,
        compiler_params=pltpu.CompilerParams(collective_id=call_id, has_side_effects=True),
        name="opening",
    )(own, qkv_own, out_own, small_own, number_own)


def group_reduce(blocks, beside_in, pair_sums, across_in, settled, sems):
    core_send, core_recv, far_send, far_recv = sems
    group, beside, across, corner = fsdp_place()
    rows = settled.shape[0]

    def core_copy(slot, block):
        return remote(
            blocks.at[block],
            beside_in.at[slot],
            core_send.at[slot],
            core_recv.at[slot],
            fsdp=beside,
        )

    far = remote(pair_sums.at[1], across_in, far_send.at[0], far_recv.at[0], fsdp=across)
    core_copy(1, corner).start()
    core_copy(0, beside).start()
    yield
    core_copy(1, corner).wait_recv()
    add_rows(pair_sums.at[1], (blocks.at[across], beside_in.at[1]), rows)
    far.start()
    core_copy(0, beside).wait_recv()
    add_rows(pair_sums.at[0], (blocks.at[group], beside_in.at[0]), rows)
    yield
    far.wait_recv()
    add_rows(settled, (pair_sums.at[0], across_in), rows)
    yield
    core_copy(1, corner).wait_send()
    core_copy(0, beside).wait_send()
    far.wait_send()
    yield


def closing_kernel(ctx_count, part, weight, pair, small, *refs):
    total, landed, pair_total, small_total = refs[:4]
    line_slots, weight_slots, pair_slots = refs[4:8], refs[8:12], refs[12:16]
    pair_in, small_in, small_sums, small_across = refs[16:20]
    line_sems, weight_sems, pair_sems = refs[20:25], refs[25:29], refs[29:33]
    keep_sem, half_send, half_recv = refs[33:36]
    weight_spread, small_spread, (group_send, group_recv) = refs[36:38], refs[38:40], refs[40:42]
    here, level, line, side = line_place()
    group = lax.axis_index("fsdp")
    greet_all(ctx_count)
    turns = scatter_turns(ctx_count // 2 - 1, part, total, *line_slots, *line_sems)
    settled, pair_settled = weight_slots[3], pair_slots[3]
    weight_steps = group_reduce(weight, *weight_slots, weight_sems)
    pair_steps = group_reduce(pair, *pair_slots, pair_sems)
    next(weight_steps)
    next(turns)
    small_start, small_wait = spread(
        lambda peer: small.at[:, peer], lambda source: small_in.at[source], small_spread, ctx_count
    )
    for copy in small_start:
        copy.start()
    next(weight_steps)
    next(pair_steps)
    next(turns)
    next(pair_steps)
    for copy in small_wait:
        copy.wait_recv()
    small_sum = small[:, here]
    for k in range(1, ctx_count):
        small_sum = small_sum + small_in[(here + k) % ctx_count]
    small_sums[...] = small_sum
    group_copies = [
        remote(
            small_sums.at[(group + k) % 4],
            small_across.at[k],
            group_send.at[k],
            group_recv.at[k],
            fsdp=(group + k) % 4,
        )
        for k in range(1, 4)
    ]
    for copy in group_copies:
        copy.start()
    next(weight_steps)
    piece = settled.shape[0] // ctx_count
    weight_start, weight_wait = spread(
        lambda peer: settled.at[pl.ds(pl.multiple_of(peer * piece, piece), piece)],
        lambda source: landed.at[source],
        weight_spread,
        ctx_count,
    )
    for copy in weight_start:
        copy.start()
    keep = pltpu.make_async_copy(
        settled.at[pl.ds(pl.multiple_of(here * piece, piece), piece)],
        landed.at[here],
        keep_sem.at[0],
    )
    keep.start()
    next(turns)
    next(pair_steps)
    half = pair_total.shape[0]
    half_copy = remote(
        pair_settled.at[pl.ds(pl.multiple_of((1 - line) * half, half), half)],
        pair_in,
        half_send.at[0],
        half_recv.at[0],
        ctx=side,
    )
    half_copy.start()
    for copy in group_copies:
        copy.wait_recv()
    small_total[...] = small_sums[group] + small_across[1] + small_across[2] + small_across[3]
    for step in turns:
        pass
    half_copy.wait_recv()
    kept = pair_settled.at[pl.ds(pl.multiple_of(line * half, half), half)]
    add_rows(pair_total, (kept, pair_in), half)
    for copy in weight_wait:
        copy.wait_recv()
    for copy in weight_start + small_start + group_copies:
        copy.wait_send()
    half_copy.wait_send()
    next(weight_steps)
    next(pair_steps)
    keep.wait()


def closing(ctx_count, call_id, part, weight, pair, small):
    rows, width = part.shape[1:]
    half = ctx_count // 2
    dma = pltpu.SemaphoreType.DMA
    slots = pltpu.VMEM((half, rows, width), part.dtype)

    def group_slots(array):
        one = pltpu.VMEM(array.shape[1:], array.dtype)
        two = pltpu.VMEM((2,) + array.shape[1:], array.dtype)
        return [two, two, one, one]

    block, columns = weight.shape[1:]
    pair_half = (pair.shape[1] // 2, pair.shape[2])
    return pl.pallas_call(
        functools.partial(closing_kernel, ctx_count),
        out_shape=[
            jax.ShapeDtypeStruct((rows, width), jnp.float32),
            jax.ShapeDtypeStruct((ctx_count, block // ctx_count, columns), weight.dtype),
            jax.ShapeDtypeStruct(pair_half, jnp.float32),
            jax.ShapeDtypeStruct(small.shape[2:], small.dtype),
        ],
        in_specs=[VMEM] * 4,
        out_specs=[VMEM] * 4,
        scratch_shapes=[slots] * 4
        + group_slots(weight)
        + group_slots(pair)
        + [
            pltpu.VMEM(pair_half, pair.dtype),
            pltpu.VMEM((ctx_count, 4) + small.shape[2:], small.dtype),
            pltpu.VMEM((4,) + small.shape[2:], small.dtype),
            pltpu.VMEM((4,) + small.shape[2:], small.dtype),
        ]
        + [dma((half,))] * 5
        + [dma((2,)), dma((2,)), dma((1,)), dma((1,))] * 2
        + [dma((1,))] * 3
        + [dma((ctx_count,))] * 4
        + [dma((4,))] * 2,
        compiler_params=pltpu.CompilerParams(
            collective_id=call_id, has_side_effects=True, vmem_limit_bytes=48 * 2**20
        ),
        name="closing",
    )(part, weight, pair, small)


def over(axis, array, dim=0):
    return lax.all_gather(array, axis, axis=dim, tiled=True)


def reduce_over(axis, array, dim=0):
    return lax.psum_scatter(array, axis, scatter_dimension=dim, tiled=True)


def exchange(array):
    return lax.all_to_all(array, "ctx", split_axis=0, concat_axis=0, tiled=True)


def transposed_dot(left, right):
    return lax.dot_general(
        left, right, (((0,), (0,)), ((), ())), preferred_element_type=jnp.float32
    )


def dot_transposed(left, right):
    return lax.dot_general(
        left, right, (((1,), (1,)), ((), ())), preferred_element_type=jnp.float32
    )


def split_plan(
    hidden_in,
    segments,
    block_pairs,
    routes,
    out_grad,
    norm_gain_attn,
    qkv_weight,
    qkv_bias,
    out_weight,
    norm_gain_ffn,
    router_weight,
    shared_gate_weight,
    shared_in_weight,
    shared_out_weight,
    expert_in_weight,
    expert_out_weight,
):
    low = jnp.bfloat16
    full = jnp.float32
    tokens_dev, width = hidden_in.shape[1:]
    block_len = tokens_dev // 2
    ctx_count = lax.axis_size("ctx")
    fsdp_count = lax.axis_size("fsdp")
    ctx_rank = lax.axis_index("ctx")
    dev_count = ctx_count * fsdp_count
    row_len = ctx_count * tokens_dev
    head_count = width // HD
    shard = qkv_weight.shape[0]
    expert_count = router_weight.shape[1]
    shared_shard = shared_out_weight.shape[0]
    shared_width = fsdp_count * shared_shard
    expert_width = expert_out_weight.shape[1] * fsdp_count
    pair_rank = ctx_rank // 2
    side = ctx_rank % 2
    pairs = ctx_count // 2
    head_order = [j + (p * 2 + t) * pairs for j in range(pairs) for p in range(2) for t in range(2)]

    small = jnp.concatenate(
        [
            norm_gain_attn,
            norm_gain_ffn,
            shared_gate_weight,
            router_weight.T.reshape(-1),
            qkv_bias,
        ]
    )
    small_count = small.shape[0]
    small = jnp.pad(small, (0, 16 * HD - small_count)).reshape(16, HD)
    own_numbers = jnp.concatenate(
        [routes.reshape(tokens_dev, -1).T, segments.reshape(1, tokens_dev)], axis=0
    )
    number_count = own_numbers.shape[0]
    own_numbers = jnp.pad(own_numbers, ((0, 8 - number_count), (0, 0)))
    qkv_parts = (
        qkv_weight.reshape(shard, 3, head_count, HD)[:, :, jnp.array(head_order)]
        .reshape(shard, 3, ctx_count, 2 * HD)
        .transpose(2, 0, 1, 3)
        .reshape(ctx_count, shard, 6 * HD)
    )
    own_inputs = hidden_in.reshape(tokens_dev, width)
    row_inputs, qkv_c, out_pair, small_all, numbers = opening(
        ctx_count, 1, own_inputs, qkv_parts, out_weight, small, own_numbers
    )
    qkv_c = qkv_c.reshape(width, 6 * HD)
    out_c = lax.dynamic_index_in_dim(
        out_pair.reshape(2, 2 * HD, width), side, 0, keepdims=False
    )
    small_all = small_all.reshape(dev_count, 16 * HD)
    gain_attn = small_all[:, :shard].reshape(width).astype(full)
    gain_ffn = small_all[:, shard : 2 * shard].reshape(width).astype(full)
    gate_full = small_all[:, 2 * shard : 3 * shard].reshape(width)
    router_t = (
        small_all[:, 3 * shard : (3 + expert_count) * shard]
        .reshape(dev_count, expert_count, shard)
        .transpose(1, 0, 2)
        .reshape(expert_count, width)
    )
    bias_full = small_all[:, (3 + expert_count) * shard : small_count].reshape(3, head_count, HD)
    router_gate = jnp.concatenate([router_t, gate_full[None, :]], axis=0)
    row_seg = numbers[:, number_count - 1].reshape(row_len)
    routed_here = jnp.any(numbers[:, : number_count - 1] == ctx_rank, axis=1).reshape(row_len)

    shared_in_weight, numbers = lax.optimization_barrier((shared_in_weight, numbers))
    inner_parts = (
        shared_in_weight.reshape(shard, 2, fsdp_count, ctx_count, shared_shard)
        .transpose(3, 0, 1, 2, 4)
        .reshape(ctx_count, shard, 2 * shared_width)
    )
    expert_inner = over("fsdp", expert_in_weight[0])
    expert_outer = over("fsdp", expert_out_weight[0])
    outer_c = over("fsdp", shared_out_weight)
    inner_parts = exchange(inner_parts).reshape(ctx_count * shard, 2 * shared_width)
    inner_parts, late_grad = lax.optimization_barrier((inner_parts, out_grad))
    inner_c = over("fsdp", inner_parts)
    my_heads = [pair_rank + (side * 2 + t) * pairs for t in range(2)]
    bias_c = jnp.concatenate(
        [lax.dynamic_index_in_dim(bias_full, h, 1, keepdims=False) for h in my_heads], axis=1
    ).reshape(6 * HD)

    offsets = jnp.arange(block_len, dtype=jnp.int32)
    positions = (block_pairs[:, None] * block_len + offsets[None, :]).reshape(row_len)
    inputs = own_inputs.astype(full)
    row_inputs = row_inputs.reshape(row_len, width).astype(full)
    row_upstream = over("ctx", late_grad.reshape(tokens_dev, width))
    row_normed = rms_scale(row_inputs, gain_attn).astype(low)
    projected = matmul_low(row_normed, qkv_c) + bias_c.astype(full)
    query_pre = projected[:, : 2 * HD].reshape(row_len, 2, HD)
    key_pre = projected[:, 2 * HD : 4 * HD].reshape(row_len, 2, HD)

    def place_heads(query_in, key_in):
        return (rotate(query_in, positions) * HD ** (-0.5), rotate(key_in, positions))

    query_rot, key_rot = place_heads(query_pre, key_pre)
    queries = query_rot.astype(low)
    keys = key_rot.astype(low)
    values = projected[:, 4 * HD :].reshape(row_len, 2, HD).astype(low)
    seg_real = row_seg.astype(full)
    allowed = visible(positions, seg_real, positions, seg_real)

    def score_part():
        scores = jnp.einsum("qhd,khd->hqk", queries, keys, preferred_element_type=full)
        return jnp.where(allowed[None], scores, -1e30)

    scores = score_part()
    highest = jnp.max(scores, axis=-1, keepdims=True)
    log_total = highest + jnp.log(jnp.sum(jnp.exp(scores - highest), axis=-1, keepdims=True))
    probs = jnp.exp(scores - log_total)
    attended_row = (
        jnp.einsum("hqk,khd->qhd", probs.astype(low), values, preferred_element_type=full)
        .astype(low)
        .reshape(row_len, 2 * HD)
    )
    branch_part = matmul_low(attended_row, out_c).astype(low)
    (branch,) = line_scatter(ctx_count, 2, branch_part.reshape(ctx_count, tokens_dev, width))
    middle = inputs + branch
    normed_ffn = rms_scale(middle, gain_ffn).astype(low)

    (row_ffn,) = line_gather(ctx_count, 3, normed_ffn)
    row_ffn = row_ffn.reshape(row_len, width)
    row_logits = dot_transposed(row_ffn, router_gate)
    row_probs = jax.nn.softmax(row_logits[:, :expert_count], axis=-1)
    expert_ids = jnp.arange(expert_count, dtype=jnp.int32)
    here = jnp.where(
        routed_here, jnp.sum(jnp.where(expert_ids[None, :] == ctx_rank, row_probs, 0.0), axis=1), 0.0
    )
    row_gate = jax.nn.sigmoid(row_logits[:, expert_count])
    expert_gu = matmul_low(row_ffn, expert_inner)
    expert_hidden = swiglu_mix(expert_gu, expert_width).astype(low)
    expert_result = matmul_low(expert_hidden, expert_outer).astype(low).astype(full)
    row_shared, expert_result = lax.optimization_barrier((row_ffn, expert_result))
    shared_gu = matmul_low(row_shared, inner_c)
    shared_hidden = swiglu_mix(shared_gu, shared_width).astype(low)
    shared_out = matmul_low(shared_hidden, outer_c)
    row_upstream, shared_out = lax.optimization_barrier((row_upstream, shared_out))
    upstream_row = row_upstream.astype(full)
    out_part = (row_gate[:, None] * shared_out + here[:, None] * expert_result).astype(low)
    gate_dot = jnp.sum(upstream_row * shared_out, axis=1)
    expert_dot = jnp.where(routed_here, jnp.sum(upstream_row * expert_result, axis=1), 0.0)
    own_dots = exchange(
        jnp.stack([gate_dot, expert_dot]).reshape(2, ctx_count, tokens_dev).transpose(1, 0, 2)
    )

    grad_shared_out = (row_gate[:, None] * upstream_row).astype(low)
    grad_buffers = (here[:, None] * upstream_row).astype(low)
    grad_hidden = dot_transposed(grad_shared_out, outer_c)
    unused_mix, mix_pull = jax.vjp(functools.partial(swiglu_mix, hidden_width=shared_width), shared_gu)
    grad_shared_gu = mix_pull(grad_hidden)[0].astype(low)
    grad_expert_hidden = dot_transposed(grad_buffers, expert_outer)
    unused_mix, expert_pull = jax.vjp(functools.partial(swiglu_mix, hidden_width=expert_width), expert_gu)
    grad_expert_gu = expert_pull(grad_expert_hidden)[0].astype(low)
    grad_rows = dot_transposed(grad_expert_gu, expert_inner).astype(low).astype(full)
    grad_ffn_part = (dot_transposed(grad_shared_gu, inner_c) + grad_rows).astype(low)
    grad_expert_outer = transposed_dot(expert_hidden, grad_buffers).astype(low)
    grad_expert_inner = transposed_dot(row_ffn, grad_expert_gu).astype(low)
    grad_outer = transposed_dot(shared_hidden, grad_shared_out).astype(low)
    grad_inner = transposed_dot(row_ffn, grad_shared_gu).astype(low)
    (
        grad_ffn_part,
        out_part,
        grad_expert_outer,
        grad_expert_inner,
        grad_outer,
        grad_inner,
    ) = lax.optimization_barrier(
        (grad_ffn_part, out_part, grad_expert_outer, grad_expert_inner, grad_outer, grad_inner)
    )
    sum_expert_outer = reduce_over("fsdp", grad_expert_outer)
    sum_expert_inner = reduce_over("fsdp", grad_expert_inner)
    sum_outer = reduce_over("fsdp", grad_outer)
    sum_inner_c = reduce_over("fsdp", grad_inner)
    grad_normed, out_sum = line_scatter(
        ctx_count,
        4,
        grad_ffn_part.reshape(ctx_count, tokens_dev, width),
        out_part.reshape(ctx_count, tokens_dev, width),
    )
    hidden_out = (middle + out_sum).astype(low).reshape(1, tokens_dev, width)
    sum_inner = (
        exchange(sum_inner_c.reshape(ctx_count, shard, 2 * shared_width))
        .reshape(ctx_count, shard, 2, fsdp_count, shared_shard)
        .transpose(1, 2, 3, 0, 4)
        .reshape(shard, 2 * fsdp_count * ctx_count * shared_shard)
    )

    own_logits = dot_transposed(normed_ffn, router_gate)
    router_probs = jax.nn.softmax(own_logits[:, :expert_count], axis=-1)
    gate_value = jax.nn.sigmoid(own_logits[:, expert_count])
    grad_gate_logit = gate_value * (1.0 - gate_value) * jnp.sum(own_dots[:, 0], axis=0)
    grad_choice = own_dots[:, 1].T
    grad_logits = router_probs * (
        grad_choice - jnp.sum(router_probs * grad_choice, axis=1, keepdims=True)
    )
    grad_small = jnp.concatenate([grad_logits, grad_gate_logit[:, None]], axis=1).astype(low)
    grad_router_gate = transposed_dot(grad_small, normed_ffn)
    grad_normed = grad_normed + matmul_low(grad_small, router_gate)
    unused_norm, norm_pull = jax.vjp(rms_scale, middle, gain_ffn)
    grad_middle_norm, grad_gain_ffn = norm_pull(grad_normed)
    grad_middle = out_grad.reshape(tokens_dev, width).astype(full) + grad_middle_norm

    (row_branch,) = line_gather(ctx_count, 3, grad_middle.astype(low))
    row_branch = row_branch.reshape(row_len, width)
    grad_attended = dot_transposed(row_branch, out_c).astype(low).reshape(row_len, 2, HD)
    grad_out_c = transposed_dot(attended_row, row_branch).astype(low).reshape(2, HD, width)
    padded_out = jnp.concatenate(
        [jnp.where(side == p, grad_out_c, jnp.zeros_like(grad_out_c)) for p in range(2)], axis=0
    )

    grad_probs = jnp.einsum("qhd,khd->hqk", grad_attended, values, preferred_element_type=full)
    weights = jnp.exp(score_part() - log_total)
    offset_term = jnp.sum(weights * grad_probs, axis=-1, keepdims=True)
    grad_scores = (weights * (grad_probs - offset_term)).astype(low)
    grad_queries = jnp.einsum("hqk,khd->qhd", grad_scores, keys, preferred_element_type=full)
    grad_keys = jnp.einsum("hqk,qhd->khd", grad_scores, queries, preferred_element_type=full)
    grad_values = jnp.einsum(
        "hqk,qhd->khd", weights.astype(low), grad_attended, preferred_element_type=full
    )
    unused_rot, rotate_pull = jax.vjp(place_heads, query_pre, key_pre)
    grad_query_pre, grad_key_pre = rotate_pull((grad_queries, grad_keys))
    grad_projected = jnp.concatenate(
        [
            grad_query_pre.reshape(row_len, 2 * HD),
            grad_key_pre.reshape(row_len, 2 * HD),
            grad_values.reshape(row_len, 2 * HD),
        ],
        axis=1,
    ).astype(low)
    grad_attn_part = dot_transposed(grad_projected, qkv_c)
    row_scaled = row_inputs * lax.rsqrt(
        jnp.mean(row_inputs * row_inputs, axis=-1, keepdims=True) + EPSILON
    )
    grad_gain_attn = jnp.sum(grad_attn_part * row_scaled, axis=0)
    grad_bias_c = jnp.sum(grad_projected.astype(full), axis=0).reshape(3, 1, 2, HD)
    mine = (jnp.arange(ctx_count) == ctx_rank)[None, :, None, None]
    places_of = [head_order.index(h) for h in range(head_count)]
    grad_bias = (
        jnp.where(mine, grad_bias_c, 0.0)
        .reshape(3, head_count, HD)[:, jnp.array(places_of)]
        .reshape(dev_count, -1)
    )
    small_grads = jnp.concatenate(
        [
            grad_gain_attn.reshape(dev_count, shard),
            grad_gain_ffn.reshape(dev_count, shard),
            grad_router_gate.reshape(expert_count + 1, dev_count, shard)
            .transpose(1, 0, 2)
            .reshape(dev_count, (expert_count + 1) * shard),
            grad_bias,
        ],
        axis=1,
    )
    small_grads = jnp.pad(small_grads, ((0, 0), (0, 8 * HD - small_count)))
    grad_qkv_c = transposed_dot(row_normed, grad_projected).astype(low)
    grad_normed_attn, sum_qkv_c, sum_out, sums = closing(
        ctx_count,
        5,
        grad_attn_part.astype(low).reshape(ctx_count, tokens_dev, width),
        grad_qkv_c.reshape(fsdp_count, ctx_count * shard, 6 * HD),
        padded_out,
        small_grads.reshape(fsdp_count, ctx_count, 8, HD),
    )
    sums = sums.reshape(8 * HD)[:small_count]
    sum_qkv = (
        sum_qkv_c.reshape(ctx_count, shard, 3, 2, HD)
        .transpose(1, 2, 0, 3, 4)
        .reshape(shard, 3, head_count, HD)[:, :, jnp.array(places_of)]
        .reshape(shard, 3 * width)
    )
    unused_norm, first_pull = jax.vjp(lambda v: rms_scale(v, gain_attn), inputs)
    input_grad = grad_middle + first_pull(grad_normed_attn)[0]
    sum_router = sums[2 * shard : (2 + expert_count) * shard].reshape(expert_count, shard).T
    return (
        hidden_out,
        input_grad.reshape(1, tokens_dev, width),
        sums[:shard],
        sum_qkv.astype(full),
        sums[(3 + expert_count) * shard :],
        sum_out,
        sums[shard : 2 * shard],
        sum_router,
        sums[(2 + expert_count) * shard : (3 + expert_count) * shard],
        sum_inner.astype(full),
        sum_outer.astype(full),
        sum_expert_inner.astype(full)[None],
        sum_expert_outer.astype(full)[None],
    )


def local(*arrays):
    width = arrays[0].shape[2]
    ctx_count = lax.axis_size("ctx")
    shard = arrays[6].shape[0]
    fits = (
        width == 2 * ctx_count * HD
        and 2 * shard == HD
        and ctx_count % 2 == 0
        and lax.axis_size("fsdp") * ctx_count * shard == width
        and arrays[14].shape[0] == 1
    )
    return split_plan(*arrays) if fits else gathered_plan(*arrays)


def solution(mesh):
    in_specs = (
        P("fsdp", "ctx", None),
        P("fsdp", "ctx"),
        P(),
        P("fsdp", "ctx", None),
        P("fsdp", "ctx", None),
        P(("fsdp", "ctx")),
        P(("fsdp", "ctx"), None),
        P(("fsdp", "ctx")),
        P(("fsdp", "ctx"), None),
        P(("fsdp", "ctx")),
        P(("fsdp", "ctx"), None),
        P(("fsdp", "ctx")),
        P(("fsdp", "ctx"), None),
        P(("fsdp", "ctx"), None),
        P("ctx", "fsdp", None),
        P("ctx", "fsdp", None),
    )
    out_specs = (
        P("fsdp", "ctx", None),
        P("fsdp", "ctx", None),
        P(("fsdp", "ctx")),
        P(("fsdp", "ctx"), None),
        P(("fsdp", "ctx")),
        P(("fsdp", "ctx"), None),
        P(("fsdp", "ctx")),
        P(("fsdp", "ctx"), None),
        P(("fsdp", "ctx")),
        P(("fsdp", "ctx"), None),
        P(("fsdp", "ctx"), None),
        P("ctx", "fsdp", None),
        P("ctx", "fsdp", None),
    )
    return jax.shard_map(local, mesh=mesh, in_specs=in_specs, out_specs=out_specs, check_vma=False)
```

```python
import functools

import jax
import jax.numpy as jnp
from jax import lax
from jax.experimental import pallas as pl
from jax.experimental.pallas import tpu as pltpu
from jax.sharding import PartitionSpec as P

HD = 128


EPSILON = 1e-06
THETA = 1000000.0
heads_per_group = 4


def rms_scale(values, gain_vec):
    return (
        values * lax.rsqrt(jnp.mean(values * values, axis=-1, keepdims=True) + EPSILON) * gain_vec
    )


def rotate(values, positions):
    half_len = values.shape[-1] // 2
    frequency = THETA ** (-jnp.arange(half_len, dtype=jnp.float32) / half_len)
    angles = positions.astype(jnp.float32)[:, None] * frequency[None, :]
    cosine = jnp.cos(angles)[:, None, :]
    sine_part = jnp.sin(angles)[:, None, :]
    first_half = values[..., :half_len]
    second = values[..., half_len:]
    return jnp.concatenate(
        [first_half * cosine - second * sine_part, second * cosine + first_half * sine_part],
        axis=-1,
    )


def visible(query_pos, query_seg, key_pos, key_seg):
    same_doc = (key_seg[None, :] == query_seg[:, None]) & (query_seg[:, None] >= 0)
    causal = key_pos[None, :] <= query_pos[:, None]
    return same_doc & causal | (key_pos[None, :] == query_pos[:, None])


def swiglu_mix(gate_up, hidden_width):
    return jax.nn.silu(gate_up[..., :hidden_width]) * gate_up[..., hidden_width:]


def matmul_low(left, right):
    return jnp.dot(left, right, preferred_element_type=jnp.float32)


def gathered_plan(
    hidden_in,
    segments,
    block_pairs,
    routes,
    out_grad,
    norm_gain_attn,
    qkv_weight,
    qkv_bias,
    out_weight,
    norm_gain_ffn,
    router_weight,
    shared_gate_weight,
    shared_in_weight,
    shared_out_weight,
    expert_in_weight,
    expert_out_weight,
):
    tokens_dev = hidden_in.shape[1]
    model_width = hidden_in.shape[2]
    block_len = tokens_dev // 2
    inputs = hidden_in.reshape(tokens_dev, model_width).astype(jnp.float32)
    seg_local = segments.reshape(tokens_dev)
    token_routes = routes.reshape(tokens_dev, -1)
    top_count = token_routes.shape[1]
    ctx_count = lax.axis_size("ctx")
    ctx_rank = lax.axis_index("ctx")
    offsets = jnp.arange(block_len, dtype=jnp.int32)
    all_positions = (
        block_pairs.reshape(ctx_count, 2)[:, :, None] * block_len + offsets[None, None, :]
    ).reshape(ctx_count * tokens_dev)
    my_positions = lax.dynamic_slice_in_dim(all_positions, ctx_rank * tokens_dev, tokens_dev, 0)
    gathered = (
        lax.all_gather(norm_gain_attn, ("fsdp", "ctx"), axis=0, tiled=True),
        lax.all_gather(qkv_weight, ("fsdp", "ctx"), axis=0, tiled=True),
        lax.all_gather(qkv_bias, ("fsdp", "ctx"), axis=0, tiled=True),
        lax.all_gather(out_weight, ("fsdp", "ctx"), axis=0, tiled=True),
        lax.all_gather(norm_gain_ffn, ("fsdp", "ctx"), axis=0, tiled=True),
        lax.all_gather(router_weight, ("fsdp", "ctx"), axis=0, tiled=True),
        lax.all_gather(shared_gate_weight, ("fsdp", "ctx"), axis=0, tiled=True),
        lax.all_gather(shared_in_weight, ("fsdp", "ctx"), axis=0, tiled=True),
        lax.all_gather(shared_out_weight, ("fsdp", "ctx"), axis=0, tiled=True),
    )
    (
        gain_attn,
        qkv_full,
        shift_full,
        out_full,
        gain_ffn,
        router_full,
        gate_full,
        inner_full,
        outer_full,
    ) = gathered
    gain_attn = gain_attn.astype(jnp.float32)
    gain_ffn = gain_ffn.astype(jnp.float32)
    heads_width = out_full.shape[0]
    head_count = heads_width // HD
    group_width = heads_per_group * HD
    group_count = head_count // heads_per_group
    normed = rms_scale(inputs, gain_attn).astype(jnp.bfloat16)
    projected = matmul_low(normed, qkv_full) + shift_full.astype(jnp.float32)
    query_pre = projected[:, :heads_width].reshape(tokens_dev, head_count, HD)
    key_pre = projected[:, heads_width : 2 * heads_width].reshape(tokens_dev, head_count, HD)

    def place_heads(query_in, key_in):
        return (rotate(query_in, my_positions) * HD ** (-0.5), rotate(key_in, my_positions))

    query_rot, key_rot = place_heads(query_pre, key_pre)
    query_low = query_rot.reshape(tokens_dev, heads_width).astype(jnp.bfloat16)
    key_low = key_rot.reshape(tokens_dev, heads_width).astype(jnp.bfloat16)
    value_low = projected[:, 2 * heads_width :].astype(jnp.bfloat16)
    keys_all, values_all, segs_all = (
        lax.all_gather(key_low, "ctx", axis=0, tiled=True),
        lax.all_gather(value_low, "ctx", axis=0, tiled=True),
        lax.all_gather(seg_local.astype(jnp.bfloat16), "ctx", axis=0, tiled=True),
    )
    allowed = visible(
        my_positions, seg_local.astype(jnp.float32), all_positions, segs_all.astype(jnp.float32)
    )

    def head_slice(matrix, group_index):
        return lax.dynamic_slice_in_dim(matrix, group_index * group_width, group_width, 1).reshape(
            matrix.shape[0], heads_per_group, HD
        )

    def forward_group(group_index):
        query_part = head_slice(query_low, group_index)
        key_part = head_slice(keys_all, group_index)
        value_part = head_slice(values_all, group_index)
        scores = jnp.einsum(
            "qhd,khd->hqk", query_part, key_part, preferred_element_type=jnp.float32
        )
        scores = jnp.where(allowed[None], scores, -1e30)
        highest = jnp.max(scores, axis=-1, keepdims=True)
        log_total = highest + jnp.log(jnp.sum(jnp.exp(scores - highest), axis=-1, keepdims=True))
        weights = jnp.exp(scores - log_total).astype(jnp.bfloat16)
        mixed = jnp.einsum("hqk,khd->qhd", weights, value_part, preferred_element_type=jnp.float32)
        return (mixed, log_total[..., 0])

    mixed_groups, log_totals = lax.map(forward_group, jnp.arange(group_count, dtype=jnp.int32))
    attended = (
        jnp.moveaxis(mixed_groups, 0, 1).reshape(tokens_dev, heads_width).astype(jnp.bfloat16)
    )
    middle = inputs + matmul_low(attended, out_full)
    normed_ffn = rms_scale(middle, gain_ffn).astype(jnp.bfloat16)
    logits = matmul_low(normed_ffn, router_full)
    router_probs = jax.nn.softmax(logits, axis=-1)
    expert_count = logits.shape[1]
    expert_ids = jnp.arange(expert_count, dtype=jnp.int32)
    chosen = (token_routes[:, :, None] == expert_ids[None, None, :]).astype(jnp.float32)
    gate_weights = jnp.sum(chosen * router_probs[:, None, :], axis=-1)
    capacity = 2 * tokens_dev * top_count // expert_count
    local_experts = expert_in_weight.shape[0]
    assigned = tokens_dev * top_count
    flat_routes = token_routes.reshape(assigned)
    onehot = (flat_routes[:, None] == expert_ids[None, :]).astype(jnp.int32)
    earlier = jnp.cumsum(onehot, axis=0) - onehot
    places = flat_routes * capacity + jnp.sum(earlier * onehot, axis=1)
    slot_source = (
        jnp.full((expert_count * capacity,), assigned, jnp.int32)
        .at[places]
        .set(jnp.arange(assigned, dtype=jnp.int32))
    )
    slot_token = slot_source // top_count
    padded_rows = jnp.concatenate([normed_ffn, jnp.zeros((1, model_width), jnp.bfloat16)], axis=0)
    outgoing = padded_rows[slot_token].reshape(ctx_count, local_experts * capacity, model_width)
    expert_inner, expert_outer = (
        lax.all_gather(expert_in_weight, "fsdp", axis=1, tiled=True),
        lax.all_gather(expert_out_weight, "fsdp", axis=1, tiled=True),
    )
    landed_tokens = lax.all_to_all(outgoing, "ctx", split_axis=0, concat_axis=0, tiled=True)
    incoming = landed_tokens.reshape(ctx_count, local_experts, capacity, model_width)
    expert_gu = jnp.einsum(
        "necd,edf->necf", incoming, expert_inner, preferred_element_type=jnp.float32
    )
    expert_width = expert_outer.shape[1]
    expert_hidden = swiglu_mix(expert_gu, expert_width).astype(jnp.bfloat16)
    expert_result = jnp.einsum(
        "necf,efd->necd", expert_hidden, expert_outer, preferred_element_type=jnp.float32
    ).astype(jnp.bfloat16)
    returned = lax.all_to_all(
        expert_result.reshape(ctx_count, local_experts * capacity, model_width),
        "ctx",
        split_axis=0,
        concat_axis=0,
        tiled=True,
    )
    picked = (
        returned.reshape(expert_count * capacity, model_width)[places]
        .reshape(tokens_dev, top_count, model_width)
        .astype(jnp.float32)
    )
    routed = jnp.sum(gate_weights[:, :, None] * picked, axis=1)
    upstream = out_grad.reshape(tokens_dev, model_width).astype(jnp.float32)
    shared_gu = matmul_low(normed_ffn, inner_full)
    shared_width = outer_full.shape[0]
    shared_hidden = swiglu_mix(shared_gu, shared_width).astype(jnp.bfloat16)
    shared_out = matmul_low(shared_hidden, outer_full)
    gate_value = jax.nn.sigmoid(matmul_low(normed_ffn, gate_full))
    output = middle + gate_value[:, None] * shared_out + routed
    hidden_out = output.astype(jnp.bfloat16).reshape(1, tokens_dev, model_width)
    gain_ffn, router_full, gate_full, inner_full, outer_full = (
        lax.all_gather(norm_gain_ffn, ("fsdp", "ctx"), axis=0, tiled=True),
        lax.all_gather(router_weight, ("fsdp", "ctx"), axis=0, tiled=True),
        lax.all_gather(shared_gate_weight, ("fsdp", "ctx"), axis=0, tiled=True),
        lax.all_gather(shared_in_weight, ("fsdp", "ctx"), axis=0, tiled=True),
        lax.all_gather(shared_out_weight, ("fsdp", "ctx"), axis=0, tiled=True),
    )
    gain_ffn = gain_ffn.astype(jnp.float32)
    grad_shared_out = (gate_value[:, None] * upstream).astype(jnp.bfloat16)
    grad_outer = jnp.einsum(
        "tf,td->fd", shared_hidden, grad_shared_out, preferred_element_type=jnp.float32
    )
    grad_hidden = jnp.einsum(
        "td,fd->tf", grad_shared_out, outer_full, preferred_element_type=jnp.float32
    )
    unused_mix, mix_pull = jax.vjp(functools.partial(swiglu_mix, hidden_width=shared_width), shared_gu)
    grad_shared_gu = mix_pull(grad_hidden)[0].astype(jnp.bfloat16)
    grad_inner = jnp.einsum(
        "td,tf->df", normed_ffn, grad_shared_gu, preferred_element_type=jnp.float32
    )
    grad_normed = jnp.einsum(
        "tf,df->td", grad_shared_gu, inner_full, preferred_element_type=jnp.float32
    )
    grad_gate_logit = (
        gate_value * (1.0 - gate_value) * jnp.sum(upstream * shared_out, axis=1)
    ).astype(jnp.bfloat16)
    grad_gate_vec = jnp.einsum(
        "td,t->d", normed_ffn, grad_gate_logit, preferred_element_type=jnp.float32
    )
    grad_normed = (
        grad_normed
        + grad_gate_logit.astype(jnp.float32)[:, None] * gate_full.astype(jnp.float32)[None, :]
    )
    grad_gates = jnp.sum(upstream[:, None, :] * picked, axis=2)
    grad_choice_probs = jnp.sum(chosen * grad_gates[:, :, None], axis=1)
    grad_logits = (
        router_probs
        * (grad_choice_probs - jnp.sum(router_probs * grad_choice_probs, axis=1, keepdims=True))
    ).astype(jnp.bfloat16)
    grad_router = jnp.einsum(
        "td,te->de", normed_ffn, grad_logits, preferred_element_type=jnp.float32
    )
    grad_normed = grad_normed + jnp.einsum(
        "te,de->td", grad_logits, router_full, preferred_element_type=jnp.float32
    )
    grad_slots = (
        (gate_weights[:, :, None] * upstream[:, None, :])
        .astype(jnp.bfloat16)
        .reshape(assigned, model_width)
    )
    padded_grads = jnp.concatenate([grad_slots, jnp.zeros((1, model_width), jnp.bfloat16)], axis=0)
    grad_outgoing = padded_grads[slot_source].reshape(
        ctx_count, local_experts * capacity, model_width
    )
    grad_incoming = lax.all_to_all(
        grad_outgoing, "ctx", split_axis=0, concat_axis=0, tiled=True
    ).reshape(ctx_count, local_experts, capacity, model_width)
    grad_expert_hidden = jnp.einsum(
        "necd,efd->necf", grad_incoming, expert_outer, preferred_element_type=jnp.float32
    )
    grad_expert_outer = jnp.einsum(
        "necf,necd->efd", expert_hidden, grad_incoming, preferred_element_type=jnp.float32
    )
    unused_mix, expert_pull = jax.vjp(functools.partial(swiglu_mix, hidden_width=expert_width), expert_gu)
    grad_expert_gu = expert_pull(grad_expert_hidden)[0].astype(jnp.bfloat16)
    grad_expert_inner = jnp.einsum(
        "necd,necf->edf", incoming, grad_expert_gu, preferred_element_type=jnp.float32
    )
    grad_expert_rows = jnp.einsum(
        "necf,edf->necd", grad_expert_gu, expert_inner, preferred_element_type=jnp.float32
    ).astype(jnp.bfloat16)
    grad_returned = lax.all_to_all(
        grad_expert_rows.reshape(ctx_count, local_experts * capacity, model_width),
        "ctx",
        split_axis=0,
        concat_axis=0,
        tiled=True,
    )
    grad_picked = grad_returned.reshape(expert_count * capacity, model_width)[places].reshape(
        tokens_dev, top_count, model_width
    )
    grad_normed = grad_normed + jnp.sum(grad_picked.astype(jnp.float32), axis=1)
    sum_expert_inner, sum_expert_outer = (
        lax.psum_scatter(
            grad_expert_inner.astype(jnp.bfloat16), "fsdp", scatter_dimension=1, tiled=True
        ).astype(jnp.float32),
        lax.psum_scatter(
            grad_expert_outer.astype(jnp.bfloat16), "fsdp", scatter_dimension=1, tiled=True
        ).astype(jnp.float32),
    )
    unused_norm, norm_pull = jax.vjp(rms_scale, middle, gain_ffn)
    grad_middle_norm, grad_gain_ffn = norm_pull(grad_normed)
    grad_middle = upstream + grad_middle_norm
    sum_gain_ffn, sum_router, sum_gate_vec, sum_inner, sum_outer = (
        lax.psum_scatter(grad_gain_ffn, ("fsdp", "ctx"), scatter_dimension=0, tiled=True),
        lax.psum_scatter(grad_router, ("fsdp", "ctx"), scatter_dimension=0, tiled=True),
        lax.psum_scatter(grad_gate_vec, ("fsdp", "ctx"), scatter_dimension=0, tiled=True),
        lax.psum_scatter(grad_inner, ("fsdp", "ctx"), scatter_dimension=0, tiled=True),
        lax.psum_scatter(grad_outer, ("fsdp", "ctx"), scatter_dimension=0, tiled=True),
    )
    grad_branch = grad_middle.astype(jnp.bfloat16)
    grad_out_mat = jnp.einsum(
        "tc,td->cd", attended, grad_branch, preferred_element_type=jnp.float32
    )
    grad_attended = jnp.einsum(
        "td,cd->tc", grad_branch, out_full, preferred_element_type=jnp.float32
    ).astype(jnp.bfloat16)
    keys_again, values_again = (
        lax.all_gather(key_low, "ctx", axis=0, tiled=True),
        lax.all_gather(value_low, "ctx", axis=0, tiled=True),
    )

    def backward_group(group_index):
        query_part = head_slice(query_low, group_index)
        key_part = head_slice(keys_again, group_index)
        value_part = head_slice(values_again, group_index)
        grad_part = head_slice(grad_attended, group_index)
        log_total = lax.dynamic_index_in_dim(log_totals, group_index, 0, keepdims=False)
        scores = jnp.einsum(
            "qhd,khd->hqk", query_part, key_part, preferred_element_type=jnp.float32
        )
        scores = jnp.where(allowed[None], scores, -1e30)
        weights = jnp.exp(scores - log_total[..., None])
        grad_weights = jnp.einsum(
            "qhd,khd->hqk", grad_part, value_part, preferred_element_type=jnp.float32
        )
        offset_term = jnp.sum(weights * grad_weights, axis=-1, keepdims=True)
        grad_scores = (weights * (grad_weights - offset_term)).astype(jnp.bfloat16)
        grad_query = jnp.einsum(
            "hqk,khd->qhd", grad_scores, key_part, preferred_element_type=jnp.float32
        )
        grad_key = jnp.einsum(
            "hqk,qhd->khd", grad_scores, query_part, preferred_element_type=jnp.float32
        )
        grad_value = jnp.einsum(
            "hqk,qhd->khd",
            weights.astype(jnp.bfloat16),
            grad_part,
            preferred_element_type=jnp.float32,
        )
        return (grad_query, grad_key, grad_value)

    grad_queries, grad_keys, grad_values = lax.map(
        backward_group, jnp.arange(group_count, dtype=jnp.int32)
    )
    row_total = keys_again.shape[0]
    grad_key_rows = jnp.moveaxis(grad_keys, 0, 1).reshape(row_total, heads_width)
    grad_value_rows = jnp.moveaxis(grad_values, 0, 1).reshape(row_total, heads_width)
    key_share, value_share = (
        lax.psum_scatter(
            grad_key_rows.astype(jnp.bfloat16), "ctx", scatter_dimension=0, tiled=True
        ).astype(jnp.float32),
        lax.psum_scatter(
            grad_value_rows.astype(jnp.bfloat16), "ctx", scatter_dimension=0, tiled=True
        ).astype(jnp.float32),
    )
    grad_query_heads = jnp.moveaxis(grad_queries, 0, 1).reshape(tokens_dev, head_count, HD)
    unused_rot, rotate_pull = jax.vjp(place_heads, query_pre, key_pre)
    grad_query_pre, grad_key_pre = rotate_pull(
        (grad_query_heads, key_share.reshape(tokens_dev, head_count, HD))
    )
    grad_projected = jnp.concatenate(
        [
            grad_query_pre.reshape(tokens_dev, heads_width),
            grad_key_pre.reshape(tokens_dev, heads_width),
            value_share,
        ],
        axis=1,
    ).astype(jnp.bfloat16)
    grad_qkv = jnp.einsum("td,tc->dc", normed, grad_projected, preferred_element_type=jnp.float32)
    grad_shift = jnp.sum(grad_projected.astype(jnp.float32), axis=0)
    grad_normed_attn = jnp.einsum(
        "tc,dc->td", grad_projected, qkv_full, preferred_element_type=jnp.float32
    )
    unused_norm, first_pull = jax.vjp(rms_scale, inputs, gain_attn)
    grad_inputs_norm, grad_gain_attn = first_pull(grad_normed_attn)
    input_grad = grad_middle + grad_inputs_norm
    sum_gain_attn, sum_qkv, sum_shift, sum_out = (
        lax.psum_scatter(grad_gain_attn, ("fsdp", "ctx"), scatter_dimension=0, tiled=True),
        lax.psum_scatter(grad_qkv, ("fsdp", "ctx"), scatter_dimension=0, tiled=True),
        lax.psum_scatter(grad_shift, ("fsdp", "ctx"), scatter_dimension=0, tiled=True),
        lax.psum_scatter(grad_out_mat, ("fsdp", "ctx"), scatter_dimension=0, tiled=True),
    )
    return (
        hidden_out,
        input_grad.reshape(1, tokens_dev, model_width),
        sum_gain_attn,
        sum_qkv,
        sum_shift,
        sum_out,
        sum_gain_ffn,
        sum_router,
        sum_gate_vec,
        sum_inner,
        sum_outer,
        sum_expert_inner,
        sum_expert_outer,
    )


MESH = pl.DeviceIdType.MESH
ANY = pl.BlockSpec(memory_space=pl.ANY)
VMEM = pl.BlockSpec(memory_space=pltpu.VMEM)


def remote(source, target, send_sem, recv_sem, **place):
    return pltpu.make_async_remote_copy(
        src_ref=source,
        dst_ref=target,
        send_sem=send_sem,
        recv_sem=recv_sem,
        device_id=place,
        device_id_type=MESH,
    )


def line_place():
    here = lax.axis_index("ctx")
    line = here % 2
    return here, here // 2, line, here + 1 - 2 * line


def greet_line(last, here, level, side, others=0):
    barrier = pltpu.get_barrier_semaphore()
    pl.semaphore_signal(barrier, inc=1, device_id={"ctx": side}, device_id_type=MESH)

    @pl.when(level < last)
    def up():
        pl.semaphore_signal(barrier, inc=1, device_id={"ctx": here + 2}, device_id_type=MESH)

    @pl.when(level > 0)
    def down():
        pl.semaphore_signal(barrier, inc=1, device_id={"ctx": here - 2}, device_id_type=MESH)

    ends = jnp.where(level < last, 1, 0) + jnp.where(level > 0, 1, 0)
    pl.semaphore_wait(barrier, 1 + others + ends)


def line_copy(rows_ref, block, way, target, sems, source=None):
    send_sem, recv_sem = sems
    return remote(
        rows_ref.at[block] if source is None else source,
        rows_ref.at[block],
        send_sem.at[block, way],
        recv_sem.at[block],
        ctx=target,
    )


def line_start(rows_ref, own_ref, sems, place, last):
    here, level, line, side = place

    @pl.when(level < last)
    def up():
        line_copy(rows_ref, here, 0, here + 2, sems, own_ref).start()

    @pl.when(level > 0)
    def down():
        line_copy(rows_ref, here, 1, here - 2, sems, own_ref).start()

    line_copy(rows_ref, here, 2, side, sems, own_ref).start()


def line_step(rows_ref, sems, place, last, step):
    here, level, line, side = place

    @pl.when(level >= step)
    def from_below():
        block = here - 2 * step
        line_copy(rows_ref, block, 0, side, sems).wait_recv()

        @pl.when(level < last)
        def on():
            line_copy(rows_ref, block, 0, here + 2, sems).start()

        line_copy(rows_ref, block, 2, side, sems).start()

    @pl.when(level + step <= last)
    def from_above():
        block = here + 2 * step
        line_copy(rows_ref, block, 1, side, sems).wait_recv()

        @pl.when(level > 0)
        def on():
            line_copy(rows_ref, block, 1, here - 2, sems).start()

        line_copy(rows_ref, block, 2, side, sems).start()


def line_finish(rows_ref, sems, place, last):
    here, level, line, side = place
    for other in range(last + 1):
        block = 2 * other + line
        line_copy(rows_ref, 2 * other + 1 - line, 2, side, sems).wait_recv()
        line_copy(rows_ref, block, 2, side, sems).wait_send()

        @pl.when((other <= level) & (level < last))
        def up():
            line_copy(rows_ref, block, 0, side, sems).wait_send()

        @pl.when((other >= level) & (level > 0))
        def down():
            line_copy(rows_ref, block, 1, side, sems).wait_send()


ROWS_STEP = 16


def add_rows(target, pieces, row_count):
    def one(index, carry):
        rows = pl.ds(pl.multiple_of(index * ROWS_STEP, ROWS_STEP), ROWS_STEP)
        total = pieces[0][rows, :].astype(jnp.float32)
        for piece in pieces[1:]:
            total = total + piece[rows, :].astype(jnp.float32)
        target[rows, :] = total.astype(target.dtype)
        return carry

    lax.fori_loop(0, row_count // ROWS_STEP, one, 0)


def scatter_turns(last, part, total, crossed, rising, falling, sums, *sems):
    cross_send, cross_recv, move_send, rise_recv, fall_recv = sems
    here, level, line, side = line_place()
    row_count = total.shape[0]

    def turn(k):
        middle = (level > 0) & (level < last)
        swapped = k + jnp.where(middle, (0, 0, 1, -1)[k], 0)
        return jnp.where(level * 2 < last, last - swapped, swapped)

    def cross(goal):
        return remote(
            part.at[2 * goal + 1 - line],
            crossed.at[goal],
            cross_send.at[goal],
            cross_recv.at[goal],
            ctx=side,
        )

    def rise(goal):
        return remote(
            sums.at[goal], rising.at[goal], move_send.at[goal], rise_recv.at[goal], ctx=here + 2
        )

    def fall(goal):
        return remote(
            sums.at[goal], falling.at[goal], move_send.at[goal], fall_recv.at[goal], ctx=here - 2
        )

    for k in range(min(2, last + 1)):
        cross(turn(k)).start()
    for k in range(last + 1):
        yield k
        goal = turn(k)
        mine = part.at[2 * goal + line]
        cross(goal).wait_recv()
        if k + 2 <= last:
            cross(turn(k + 2)).start()

        @pl.when(goal > level)
        def upward():
            @pl.when(level > 0)
            def joined():
                rise(goal).wait_recv()
                add_rows(sums.at[goal], (mine, crossed.at[goal], rising.at[goal]), row_count)

            @pl.when(level == 0)
            def first():
                add_rows(sums.at[goal], (mine, crossed.at[goal]), row_count)

            rise(goal).start()

        @pl.when(goal < level)
        def downward():
            @pl.when(level < last)
            def joined():
                fall(goal).wait_recv()
                add_rows(sums.at[goal], (mine, crossed.at[goal], falling.at[goal]), row_count)

            @pl.when(level == last)
            def first():
                add_rows(sums.at[goal], (mine, crossed.at[goal]), row_count)

            fall(goal).start()

        @pl.when(goal == level)
        def here_at_last():
            @pl.when(level > 0)
            def from_below():
                rise(goal).wait_recv()

            @pl.when(level < last)
            def from_above():
                fall(goal).wait_recv()

            @pl.when(level == 0)
            def bottom():
                add_rows(total, (mine, crossed.at[goal], falling.at[goal]), row_count)

            @pl.when(level == last)
            def top():
                add_rows(total, (mine, crossed.at[goal], rising.at[goal]), row_count)

            @pl.when((level > 0) & (level < last))
            def between():
                add_rows(
                    total,
                    (mine, crossed.at[goal], rising.at[goal], falling.at[goal]),
                    row_count,
                )

    for goal in range(last + 1):
        cross(goal).wait_send()

        @pl.when(goal != level)
        def sent():
            rise(goal).wait_send()


def scatter_kernel(last, count, *refs):
    parts, totals = refs[:count], refs[count : 2 * count]
    slots, sems = refs[2 * count : 6 * count], refs[6 * count :]
    here, level, line, side = line_place()
    greet_line(last, here, level, side)
    turns = [
        scatter_turns(
            last, parts[i], totals[i], *slots[4 * i : 4 * i + 4], *sems[5 * i : 5 * i + 5]
        )
        for i in range(count)
    ]
    for each in turns:
        next(each)
    for each in turns:
        for step in each:
            pass


def line_scatter(ctx_count, call_id, *parts):
    rows, width = parts[0].shape[1:]
    count = len(parts)
    half = ctx_count // 2
    dma = pltpu.SemaphoreType.DMA((half,))
    slots = pltpu.VMEM((half, rows, width), parts[0].dtype)
    return pl.pallas_call(
        functools.partial(scatter_kernel, half - 1, count),
        out_shape=[jax.ShapeDtypeStruct((rows, width), jnp.float32)] * count,
        in_specs=[VMEM] * count,
        out_specs=[VMEM] * count,
        scratch_shapes=[slots] * (4 * count) + [dma] * (5 * count),
        compiler_params=pltpu.CompilerParams(
            collective_id=call_id, has_side_effects=True, vmem_limit_bytes=48 * 2**20
        ),
        name="line_scatter",
    )(*parts)


def fsdp_place():
    here = lax.axis_index("fsdp")
    beside = here + 1 - 2 * (here % 2)
    return here, beside, (here + 2) % 4, (beside + 2) % 4


def greet_all(ctx_count):
    barrier = pltpu.get_barrier_semaphore()
    here = lax.axis_index("ctx")
    group = lax.axis_index("fsdp")
    for k in range(1, ctx_count):
        pl.semaphore_signal(
            barrier, inc=1, device_id={"ctx": (here + k) % ctx_count}, device_id_type=MESH
        )
    for k in range(1, 4):
        pl.semaphore_signal(barrier, inc=1, device_id={"fsdp": (group + k) % 4}, device_id_type=MESH)
    pl.semaphore_wait(barrier, ctx_count + 2)


def share_start(blocks, sems, own=None):
    send_sem, recv_sem = sems
    here, beside, across, corner = fsdp_place()
    source = blocks.at[here] if own is None else own
    for way, target in ((0, across), (1, beside)):
        remote(source, blocks.at[here], send_sem.at[way], recv_sem.at[here], fsdp=target).start()


def share_step(blocks, sems):
    send_sem, recv_sem = sems
    here, beside, across, corner = fsdp_place()
    copy = remote(
        blocks.at[across], blocks.at[across], send_sem.at[2], recv_sem.at[across], fsdp=beside
    )
    copy.wait_recv()
    copy.start()


def share_finish(blocks, sems):
    send_sem, recv_sem = sems
    here, beside, across, corner = fsdp_place()
    for way, block in ((0, beside), (1, corner)):
        copy = remote(
            blocks.at[block], blocks.at[block], send_sem.at[way], recv_sem.at[block], fsdp=beside
        )
        copy.wait_recv()
        copy.wait_send()
    remote(
        blocks.at[here], blocks.at[here], send_sem.at[2], recv_sem.at[here], fsdp=beside
    ).wait_send()


def spread(pieces, landing, sems, ctx_count):
    send_sem, recv_sem = sems
    here = lax.axis_index("ctx")

    def copy(k, peer, source):
        return remote(pieces(peer), landing(source), send_sem.at[k], recv_sem.at[k], ctx=peer)

    starts = [copy(k, (here + k) % ctx_count, here) for k in range(1, ctx_count)]
    waits = [
        copy(k, (here + k) % ctx_count, (here + ctx_count - k) % ctx_count)
        for k in range(1, ctx_count)
    ]
    return starts, waits


def greet_near(last, here, level, side):
    barrier = pltpu.get_barrier_semaphore()
    group = lax.axis_index("fsdp")
    for k in range(1, 4):
        pl.semaphore_signal(barrier, inc=1, device_id={"fsdp": (group + k) % 4}, device_id_type=MESH)
    greet_line(last, here, level, side, 3)


def gather_kernel(last, shared_count, *refs):
    total = 1 + shared_count
    owns, rows, keep_sem = refs[:total], refs[total : 2 * total], refs[2 * total]
    refs = refs[2 * total + 1 :]
    place = line_place()
    here, level, line, side = place
    sems = [(refs[2 * i], refs[2 * i + 1]) for i in range(total)]
    group = lax.axis_index("fsdp")
    if shared_count:
        greet_near(last, here, level, side)
    else:
        greet_line(last, here, level, side)
    line_start(rows[0], owns[0], sems[0], place, last)
    for i in range(1, total):
        share_start(rows[i], sems[i], owns[i])
    keeps = [
        pltpu.make_async_copy(
            owns[i], rows[i].at[group if i else here], keep_sem.at[i]
        )
        for i in range(total)
    ]
    for copy in keeps:
        copy.start()
    for step in range(1, last + 1):
        line_step(rows[0], sems[0], place, last, step)
    for i in range(1, total):
        share_step(rows[i], sems[i])
    line_finish(rows[0], sems[0], place, last)
    for i in range(1, total):
        share_finish(rows[i], sems[i])
    for copy in keeps:
        copy.wait()


def line_gather(ctx_count, call_id, own, *shared):
    count = len(shared)
    dma = pltpu.SemaphoreType.DMA
    return pl.pallas_call(
        functools.partial(gather_kernel, ctx_count // 2 - 1, count),
        out_shape=[jax.ShapeDtypeStruct((ctx_count,) + own.shape, own.dtype)]
        + [jax.ShapeDtypeStruct((4,) + a.shape, a.dtype) for a in shared],
        in_specs=[VMEM] * (1 + count),
        out_specs=[ANY] * (1 + count),
        scratch_shapes=[dma((1 + count,)), dma((ctx_count, 3)), dma((ctx_count,))]
        + [dma((3,)), dma((4,))] * count,
        compiler_params=pltpu.CompilerParams(collective_id=call_id, has_side_effects=True),
        name="line_gather",
    )(own, *shared)


def opening_kernel(
    ctx_count,
    own,
    qkv_own,
    out_own,
    small_own,
    number_own,
    rows,
    qkv,
    out_pair,
    small,
    numbers,
    keep_sem,
    pair_send,
    pair_recv,
    row_send,
    row_recv,
    share_send,
    share_recv,
    *sems,
):
    last = ctx_count // 2 - 1
    place = line_place()
    here, level, line, side = place
    group, beside, across, corner = fsdp_place()
    sems = [(sems[2 * i], sems[2 * i + 1]) for i in range(5)]
    qkv_spread, small_spread, number_spread, out_share, small_share = sems
    row_sems = (row_send, row_recv)
    greet_all(ctx_count)
    qkv_start, qkv_wait = spread(
        lambda peer: qkv_own.at[peer], lambda source: qkv.at[group, source], qkv_spread, ctx_count
    )
    small_start, small_wait = spread(
        lambda peer: small_own, lambda source: small.at[group, source], small_spread, ctx_count
    )
    number_start, number_wait = spread(
        lambda peer: number_own, lambda source: numbers.at[source], number_spread, ctx_count
    )

    def piece_copy(way, owner, k, target, first=False):
        source = (here + ctx_count - k) % ctx_count
        return remote(
            qkv_own.at[here] if first else qkv.at[owner, source],
            qkv.at[owner, source],
            share_send.at[way, k],
            share_recv.at[owner, k],
            fsdp=target,
        )

    def piece_on(k):
        piece_copy(0, group, k, across, k == 0).start()
        piece_copy(1, group, k, beside, k == 0).start()

    for copy in small_start + number_start + qkv_start:
        copy.start()
    line_start(rows, own, row_sems, place, last)
    piece_on(0)
    pair = remote(
        out_own, out_pair.at[group, line], pair_send.at[0], pair_recv.at[0], ctx=side
    )
    pair.start()
    keeps = [
        pltpu.make_async_copy(source, target, keep_sem.at[i])
        for i, (source, target) in enumerate(
            (
                (qkv_own.at[here], qkv.at[group, here]),
                (out_own, out_pair.at[group, line]),
                (small_own, small.at[group, here]),
                (number_own, numbers.at[here]),
                (own, rows.at[here]),
            )
        )
    ]
    for copy in keeps:
        copy.start()
    for copy in small_wait:
        copy.wait_recv()
    keeps[2].wait()
    share_start(small, small_share)
    line_step(rows, row_sems, place, last, 1)
    for k in range(1, ctx_count):
        qkv_wait[k - 1].wait_recv()
        piece_on(k)
    remote(
        out_own, out_pair.at[group, 1 - line], pair_send.at[0], pair_recv.at[0], ctx=side
    ).wait_recv()
    keeps[1].wait()
    share_start(out_pair, out_share)
    line_step(rows, row_sems, place, last, 2)
    for k in range(ctx_count):
        piece_copy(0, across, k, across).wait_recv()
        piece_copy(2, across, k, beside).start()
    share_step(small, small_share)
    for step in range(3, last + 1):
        line_step(rows, row_sems, place, last, step)
    share_step(out_pair, out_share)
    line_finish(rows, row_sems, place, last)
    for copy in number_wait:
        copy.wait_recv()
    for copy in qkv_start + small_start + number_start:
        copy.wait_send()
    pair.wait_send()
    for k in range(ctx_count):
        piece_copy(1, beside, k, beside).wait_recv()
        piece_copy(2, corner, k, beside).wait_recv()
        for way in range(3):
            piece_copy(way, group, k, beside).wait_send()
    share_finish(small, small_share)
    share_finish(out_pair, out_share)
    for i in (0, 3, 4):
        keeps[i].wait()


def opening(ctx_count, call_id, own, qkv_own, out_own, small_own, number_own):
    def out(lead, array):
        return jax.ShapeDtypeStruct(lead + array.shape, array.dtype)

    dma = pltpu.SemaphoreType.DMA
    return pl.pallas_call(
        functools.partial(opening_kernel, ctx_count),
        out_shape=[
            out((ctx_count,), own),
            out((4,), qkv_own),
            out((4, 2), out_own),
            out((4, ctx_count), small_own),
            out((ctx_count,), number_own),
        ],
        in_specs=[VMEM] * 5,
        out_specs=[ANY] * 5,
        scratch_shapes=[
            dma((5,)),
            dma((1,)),
            dma((1,)),
            dma((ctx_count, 3)),
            dma((ctx_count,)),
            dma((3, ctx_count)),
            dma((4, ctx_count)),
        ]
        + [dma((ctx_count,))] * 6
        + [dma((3,)), dma((4,))] * 2,
        compiler_params=pltpu.CompilerParams(collective_id=call_id, has_side_effects=True),
        name="opening",
    )(own, qkv_own, out_own, small_own, number_own)


def group_reduce(blocks, beside_in, pair_sums, across_in, settled, sems):
    core_send, core_recv, far_send, far_recv = sems
    group, beside, across, corner = fsdp_place()
    rows = settled.shape[0]

    def core_copy(slot, block):
        return remote(
            blocks.at[block],
            beside_in.at[slot],
            core_send.at[slot],
            core_recv.at[slot],
            fsdp=beside,
        )

    far = remote(pair_sums.at[1], across_in, far_send.at[0], far_recv.at[0], fsdp=across)
    core_copy(1, corner).start()
    core_copy(0, beside).start()
    yield
    core_copy(1, corner).wait_recv()
    add_rows(pair_sums.at[1], (blocks.at[across], beside_in.at[1]), rows)
    far.start()
    core_copy(0, beside).wait_recv()
    add_rows(pair_sums.at[0], (blocks.at[group], beside_in.at[0]), rows)
    yield
    far.wait_recv()
    add_rows(settled, (pair_sums.at[0], across_in), rows)
    yield
    core_copy(1, corner).wait_send()
    core_copy(0, beside).wait_send()
    far.wait_send()
    yield


def closing_kernel(ctx_count, part, weight, pair, small, *refs):
    total, landed, pair_total, small_total = refs[:4]
    line_slots, weight_slots, pair_slots = refs[4:8], refs[8:12], refs[12:16]
    pair_in, small_in, small_sums, small_across = refs[16:20]
    line_sems, weight_sems, pair_sems = refs[20:25], refs[25:29], refs[29:33]
    keep_sem, half_send, half_recv = refs[33:36]
    weight_spread, small_spread, (group_send, group_recv) = refs[36:38], refs[38:40], refs[40:42]
    here, level, line, side = line_place()
    group = lax.axis_index("fsdp")
    greet_all(ctx_count)
    turns = scatter_turns(ctx_count // 2 - 1, part, total, *line_slots, *line_sems)
    settled, pair_settled = weight_slots[3], pair_slots[3]
    weight_steps = group_reduce(weight, *weight_slots, weight_sems)
    pair_steps = group_reduce(pair, *pair_slots, pair_sems)
    small_start, small_wait = spread(
        lambda peer: small.at[:, peer], lambda source: small_in.at[source], small_spread, ctx_count
    )
    for copy in small_start:
        copy.start()
    next(weight_steps)
    next(turns)
    next(weight_steps)
    next(pair_steps)
    next(turns)
    next(pair_steps)
    for copy in small_wait:
        copy.wait_recv()
    small_sum = small[:, here]
    for k in range(1, ctx_count):
        small_sum = small_sum + small_in[(here + k) % ctx_count]
    small_sums[...] = small_sum
    group_copies = [
        remote(
            small_sums.at[(group + k) % 4],
            small_across.at[k],
            group_send.at[k],
            group_recv.at[k],
            fsdp=(group + k) % 4,
        )
        for k in range(1, 4)
    ]
    for copy in group_copies:
        copy.start()
    next(weight_steps)
    piece = settled.shape[0] // ctx_count
    weight_start, weight_wait = spread(
        lambda peer: settled.at[pl.ds(pl.multiple_of(peer * piece, piece), piece)],
        lambda source: landed.at[source],
        weight_spread,
        ctx_count,
    )
    for copy in weight_start:
        copy.start()
    keep = pltpu.make_async_copy(
        settled.at[pl.ds(pl.multiple_of(here * piece, piece), piece)],
        landed.at[here],
        keep_sem.at[0],
    )
    keep.start()
    next(turns)
    next(pair_steps)
    half = pair_total.shape[0]
    half_copy = remote(
        pair_settled.at[pl.ds(pl.multiple_of((1 - line) * half, half), half)],
        pair_in,
        half_send.at[0],
        half_recv.at[0],
        ctx=side,
    )
    half_copy.start()
    for copy in group_copies:
        copy.wait_recv()
    small_total[...] = small_sums[group] + small_across[1] + small_across[2] + small_across[3]
    for step in turns:
        pass
    half_copy.wait_recv()
    kept = pair_settled.at[pl.ds(pl.multiple_of(line * half, half), half)]
    add_rows(pair_total, (kept, pair_in), half)
    for copy in weight_wait:
        copy.wait_recv()
    for copy in weight_start + small_start + group_copies:
        copy.wait_send()
    half_copy.wait_send()
    next(weight_steps)
    next(pair_steps)
    keep.wait()


def closing(ctx_count, call_id, part, weight, pair, small):
    rows, width = part.shape[1:]
    half = ctx_count // 2
    dma = pltpu.SemaphoreType.DMA
    slots = pltpu.VMEM((half, rows, width), part.dtype)

    def group_slots(array):
        one = pltpu.VMEM(array.shape[1:], array.dtype)
        two = pltpu.VMEM((2,) + array.shape[1:], array.dtype)
        return [two, two, one, one]

    block, columns = weight.shape[1:]
    pair_half = (pair.shape[1] // 2, pair.shape[2])
    return pl.pallas_call(
        functools.partial(closing_kernel, ctx_count),
        out_shape=[
            jax.ShapeDtypeStruct((rows, width), jnp.float32),
            jax.ShapeDtypeStruct((ctx_count, block // ctx_count, columns), weight.dtype),
            jax.ShapeDtypeStruct(pair_half, jnp.float32),
            jax.ShapeDtypeStruct(small.shape[2:], small.dtype),
        ],
        in_specs=[VMEM] * 4,
        out_specs=[VMEM] * 4,
        scratch_shapes=[slots] * 4
        + group_slots(weight)
        + group_slots(pair)
        + [
            pltpu.VMEM(pair_half, pair.dtype),
            pltpu.VMEM((ctx_count, 4) + small.shape[2:], small.dtype),
            pltpu.VMEM((4,) + small.shape[2:], small.dtype),
            pltpu.VMEM((4,) + small.shape[2:], small.dtype),
        ]
        + [dma((half,))] * 5
        + [dma((2,)), dma((2,)), dma((1,)), dma((1,))] * 2
        + [dma((1,))] * 3
        + [dma((ctx_count,))] * 4
        + [dma((4,))] * 2,
        compiler_params=pltpu.CompilerParams(
            collective_id=call_id, has_side_effects=True, vmem_limit_bytes=48 * 2**20
        ),
        name="closing",
    )(part, weight, pair, small)


def deal_kernel(pieces, weight, dealt):
    ctx_count = dealt.shape[0]
    width = dealt.shape[2] // pieces
    for c in range(ctx_count):
        dealt[c] = jnp.concatenate(
            [
                weight[:, (q * ctx_count + c) * width : (q * ctx_count + c + 1) * width]
                for q in range(pieces)
            ],
            axis=1,
        )


def deal_columns(weight, ctx_count, pieces):
    rows, columns = weight.shape
    return pl.pallas_call(
        functools.partial(deal_kernel, pieces),
        out_shape=jax.ShapeDtypeStruct((ctx_count, rows, columns // ctx_count), weight.dtype),
        name="deal_columns",
    )(weight)


def collect_kernel(pieces, dealt, whole):
    ctx_count = dealt.shape[0]
    width = dealt.shape[2] // pieces
    whole[...] = jnp.concatenate(
        [
            dealt[c, :, q * width : (q + 1) * width]
            for q in range(pieces)
            for c in range(ctx_count)
        ],
        axis=1,
    ).astype(whole.dtype)


def collect_columns(dealt, pieces):
    ctx_count, rows, columns = dealt.shape
    return pl.pallas_call(
        functools.partial(collect_kernel, pieces),
        out_shape=jax.ShapeDtypeStruct((rows, columns * ctx_count), jnp.float32),
        name="collect_columns",
    )(dealt)


def over(axis, array, dim=0):
    return lax.all_gather(array, axis, axis=dim, tiled=True)


def reduce_over(axis, array, dim=0):
    return lax.psum_scatter(array, axis, scatter_dimension=dim, tiled=True)


def exchange(array):
    return lax.all_to_all(array, "ctx", split_axis=0, concat_axis=0, tiled=True)


def transposed_dot(left, right):
    return lax.dot_general(
        left, right, (((0,), (0,)), ((), ())), preferred_element_type=jnp.float32
    )


def dot_transposed(left, right):
    return lax.dot_general(
        left, right, (((1,), (1,)), ((), ())), preferred_element_type=jnp.float32
    )


def split_plan(
    hidden_in,
    segments,
    block_pairs,
    routes,
    out_grad,
    norm_gain_attn,
    qkv_weight,
    qkv_bias,
    out_weight,
    norm_gain_ffn,
    router_weight,
    shared_gate_weight,
    shared_in_weight,
    shared_out_weight,
    expert_in_weight,
    expert_out_weight,
):
    low = jnp.bfloat16
    full = jnp.float32
    tokens_dev, width = hidden_in.shape[1:]
    block_len = tokens_dev // 2
    ctx_count = lax.axis_size("ctx")
    fsdp_count = lax.axis_size("fsdp")
    ctx_rank = lax.axis_index("ctx")
    dev_count = ctx_count * fsdp_count
    row_len = ctx_count * tokens_dev
    head_count = width // HD
    shard = qkv_weight.shape[0]
    expert_count = router_weight.shape[1]
    shared_shard = shared_out_weight.shape[0]
    shared_width = fsdp_count * shared_shard
    expert_width = expert_out_weight.shape[1] * fsdp_count
    pair_rank = ctx_rank // 2
    side = ctx_rank % 2
    pairs = ctx_count // 2
    head_order = [j + (p * 2 + t) * pairs for j in range(pairs) for p in range(2) for t in range(2)]

    small = jnp.concatenate(
        [
            norm_gain_attn,
            norm_gain_ffn,
            shared_gate_weight,
            router_weight.T.reshape(-1),
            qkv_bias,
        ]
    )
    small_count = small.shape[0]
    small = jnp.pad(small, (0, 16 * HD - small_count)).reshape(16, HD)
    own_numbers = jnp.concatenate(
        [routes.reshape(tokens_dev, -1).T, segments.reshape(1, tokens_dev)], axis=0
    )
    number_count = own_numbers.shape[0]
    own_numbers = jnp.pad(own_numbers, ((0, 8 - number_count), (0, 0)))
    qkv_parts = (
        qkv_weight.reshape(shard, 3, head_count, HD)[:, :, jnp.array(head_order)]
        .reshape(shard, 3, ctx_count, 2 * HD)
        .transpose(2, 0, 1, 3)
        .reshape(ctx_count, shard, 6 * HD)
    )
    own_inputs = hidden_in.reshape(tokens_dev, width)
    row_inputs, qkv_c, out_pair, small_all, numbers = opening(
        ctx_count, 1, own_inputs, qkv_parts, out_weight, small, own_numbers
    )
    qkv_c = qkv_c.reshape(width, 6 * HD)
    out_c = lax.dynamic_index_in_dim(
        out_pair.reshape(2, 2 * HD, width), side, 0, keepdims=False
    )
    small_all = small_all.reshape(dev_count, 16 * HD)
    gain_attn = small_all[:, :shard].reshape(width).astype(full)
    gain_ffn = small_all[:, shard : 2 * shard].reshape(width).astype(full)
    gate_full = small_all[:, 2 * shard : 3 * shard].reshape(width)
    router_t = (
        small_all[:, 3 * shard : (3 + expert_count) * shard]
        .reshape(dev_count, expert_count, shard)
        .transpose(1, 0, 2)
        .reshape(expert_count, width)
    )
    bias_full = small_all[:, (3 + expert_count) * shard : small_count].reshape(3, head_count, HD)
    router_gate = jnp.concatenate([router_t, gate_full[None, :]], axis=0)
    row_seg = numbers[:, number_count - 1].reshape(row_len)
    routed_here = jnp.any(numbers[:, : number_count - 1] == ctx_rank, axis=1).reshape(row_len)

    shared_in_weight, numbers = lax.optimization_barrier((shared_in_weight, numbers))
    inner_parts = deal_columns(shared_in_weight, ctx_count, 2 * fsdp_count)
    expert_inner = over("fsdp", expert_in_weight[0])
    expert_outer = over("fsdp", expert_out_weight[0])
    inner_parts = exchange(inner_parts)
    my_heads = [pair_rank + (side * 2 + t) * pairs for t in range(2)]
    bias_c = jnp.concatenate(
        [lax.dynamic_index_in_dim(bias_full, h, 1, keepdims=False) for h in my_heads], axis=1
    ).reshape(6 * HD)

    offsets = jnp.arange(block_len, dtype=jnp.int32)
    positions = (block_pairs[:, None] * block_len + offsets[None, :]).reshape(row_len)
    inputs = own_inputs.astype(full)
    row_inputs = row_inputs.reshape(row_len, width).astype(full)
    row_upstream = over("ctx", out_grad.reshape(tokens_dev, width))
    row_normed = rms_scale(row_inputs, gain_attn).astype(low)
    projected = matmul_low(row_normed, qkv_c) + bias_c.astype(full)
    query_pre = projected[:, : 2 * HD].reshape(row_len, 2, HD)
    key_pre = projected[:, 2 * HD : 4 * HD].reshape(row_len, 2, HD)

    def place_heads(query_in, key_in):
        return (rotate(query_in, positions) * HD ** (-0.5), rotate(key_in, positions))

    query_rot, key_rot = place_heads(query_pre, key_pre)
    queries = query_rot.astype(low)
    keys = key_rot.astype(low)
    values = projected[:, 4 * HD :].reshape(row_len, 2, HD).astype(low)
    seg_real = row_seg.astype(full)
    allowed = visible(positions, seg_real, positions, seg_real)

    def score_part():
        scores = jnp.einsum("qhd,khd->hqk", queries, keys, preferred_element_type=full)
        return jnp.where(allowed[None], scores, -1e30)

    scores = score_part()
    highest = jnp.max(scores, axis=-1, keepdims=True)
    log_total = highest + jnp.log(jnp.sum(jnp.exp(scores - highest), axis=-1, keepdims=True))
    probs = jnp.exp(scores - log_total)
    attended_row = (
        jnp.einsum("hqk,khd->qhd", probs.astype(low), values, preferred_element_type=full)
        .astype(low)
        .reshape(row_len, 2 * HD)
    )
    attended_row, inner_parts = lax.optimization_barrier((attended_row, inner_parts))
    branch_part = matmul_low(attended_row, out_c).astype(low)
    (branch,) = line_scatter(ctx_count, 2, branch_part.reshape(ctx_count, tokens_dev, width))
    middle = inputs + branch
    normed_ffn = rms_scale(middle, gain_ffn).astype(low)

    row_ffn, inner_c, outer_c = line_gather(
        ctx_count,
        4,
        normed_ffn,
        inner_parts.reshape(ctx_count * shard, 2 * shared_width),
        shared_out_weight,
    )
    row_ffn = row_ffn.reshape(row_len, width)
    inner_c = inner_c.reshape(width, 2 * shared_width)
    outer_c = outer_c.reshape(shared_width, width)
    row_logits = dot_transposed(row_ffn, router_gate)
    row_probs = jax.nn.softmax(row_logits[:, :expert_count], axis=-1)
    expert_ids = jnp.arange(expert_count, dtype=jnp.int32)
    here = jnp.where(
        routed_here, jnp.sum(jnp.where(expert_ids[None, :] == ctx_rank, row_probs, 0.0), axis=1), 0.0
    )
    row_gate = jax.nn.sigmoid(row_logits[:, expert_count])
    expert_gu = matmul_low(row_ffn, expert_inner)
    row_upstream, expert_gu = lax.optimization_barrier((row_upstream, expert_gu))
    expert_hidden = swiglu_mix(expert_gu, expert_width).astype(low)
    expert_result = matmul_low(expert_hidden, expert_outer).astype(low).astype(full)
    row_shared, expert_result = lax.optimization_barrier((row_ffn, expert_result))
    shared_gu = matmul_low(row_shared, inner_c)
    shared_hidden = swiglu_mix(shared_gu, shared_width).astype(low)
    shared_out = matmul_low(shared_hidden, outer_c)
    upstream_row = row_upstream.astype(full)
    out_part = (row_gate[:, None] * shared_out + here[:, None] * expert_result).astype(low)
    gate_dot = jnp.sum(upstream_row * shared_out, axis=1)
    expert_dot = jnp.where(routed_here, jnp.sum(upstream_row * expert_result, axis=1), 0.0)
    own_dots = exchange(
        jnp.stack([gate_dot, expert_dot]).reshape(2, ctx_count, tokens_dev).transpose(1, 0, 2)
    )

    grad_shared_out = (row_gate[:, None] * upstream_row).astype(low)
    grad_buffers = (here[:, None] * upstream_row).astype(low)
    grad_hidden = dot_transposed(grad_shared_out, outer_c)
    unused_mix, mix_pull = jax.vjp(functools.partial(swiglu_mix, hidden_width=shared_width), shared_gu)
    grad_shared_gu = mix_pull(grad_hidden)[0].astype(low)
    grad_expert_hidden = dot_transposed(grad_buffers, expert_outer)
    unused_mix, expert_pull = jax.vjp(functools.partial(swiglu_mix, hidden_width=expert_width), expert_gu)
    grad_expert_gu = expert_pull(grad_expert_hidden)[0].astype(low)
    grad_rows = dot_transposed(grad_expert_gu, expert_inner).astype(low).astype(full)
    grad_ffn_part = (dot_transposed(grad_shared_gu, inner_c) + grad_rows).astype(low)
    out_sum = reduce_over("ctx", out_part).astype(full)
    hidden_out = (middle + out_sum).astype(low)
    grad_expert_outer = transposed_dot(expert_hidden, grad_buffers).astype(low)
    grad_expert_inner = transposed_dot(row_ffn, grad_expert_gu).astype(low)
    grad_outer = transposed_dot(shared_hidden, grad_shared_out).astype(low)
    grad_inner = transposed_dot(row_ffn, grad_shared_gu).astype(low)
    (
        grad_ffn_part,
        hidden_out,
        grad_expert_outer,
        grad_expert_inner,
        grad_outer,
        grad_inner,
    ) = lax.optimization_barrier(
        (grad_ffn_part, hidden_out, grad_expert_outer, grad_expert_inner, grad_outer, grad_inner)
    )
    sum_expert_outer = reduce_over("fsdp", grad_expert_outer)
    sum_expert_inner = reduce_over("fsdp", grad_expert_inner)
    sum_outer = reduce_over("fsdp", grad_outer)
    sum_inner_c = reduce_over("fsdp", grad_inner)
    (grad_normed,) = line_scatter(
        ctx_count, 2, grad_ffn_part.reshape(ctx_count, tokens_dev, width)
    )
    hidden_out = hidden_out.reshape(1, tokens_dev, width)
    sum_inner = collect_columns(
        exchange(sum_inner_c.reshape(ctx_count, shard, 2 * shared_width)), 2 * fsdp_count
    )

    own_logits = dot_transposed(normed_ffn, router_gate)
    router_probs = jax.nn.softmax(own_logits[:, :expert_count], axis=-1)
    gate_value = jax.nn.sigmoid(own_logits[:, expert_count])
    grad_gate_logit = gate_value * (1.0 - gate_value) * jnp.sum(own_dots[:, 0], axis=0)
    grad_choice = own_dots[:, 1].T
    grad_logits = router_probs * (
        grad_choice - jnp.sum(router_probs * grad_choice, axis=1, keepdims=True)
    )
    grad_small = jnp.concatenate([grad_logits, grad_gate_logit[:, None]], axis=1).astype(low)
    grad_router_gate = transposed_dot(grad_small, normed_ffn)
    grad_normed = grad_normed + matmul_low(grad_small, router_gate)
    unused_norm, norm_pull = jax.vjp(rms_scale, middle, gain_ffn)
    grad_middle_norm, grad_gain_ffn = norm_pull(grad_normed)
    grad_middle = out_grad.reshape(tokens_dev, width).astype(full) + grad_middle_norm

    (row_branch,) = line_gather(ctx_count, 3, grad_middle.astype(low))
    row_branch = row_branch.reshape(row_len, width)
    grad_attended = dot_transposed(row_branch, out_c).astype(low).reshape(row_len, 2, HD)
    grad_out_c = transposed_dot(attended_row, row_branch).astype(low).reshape(2, HD, width)
    padded_out = jnp.concatenate(
        [jnp.where(side == p, grad_out_c, jnp.zeros_like(grad_out_c)) for p in range(2)], axis=0
    )

    grad_probs = jnp.einsum("qhd,khd->hqk", grad_attended, values, preferred_element_type=full)
    weights = jnp.exp(score_part() - log_total)
    offset_term = jnp.sum(weights * grad_probs, axis=-1, keepdims=True)
    grad_scores = (weights * (grad_probs - offset_term)).astype(low)
    grad_queries = jnp.einsum("hqk,khd->qhd", grad_scores, keys, preferred_element_type=full)
    grad_keys = jnp.einsum("hqk,qhd->khd", grad_scores, queries, preferred_element_type=full)
    grad_values = jnp.einsum(
        "hqk,qhd->khd", weights.astype(low), grad_attended, preferred_element_type=full
    )
    unused_rot, rotate_pull = jax.vjp(place_heads, query_pre, key_pre)
    grad_query_pre, grad_key_pre = rotate_pull((grad_queries, grad_keys))
    grad_projected = jnp.concatenate(
        [
            grad_query_pre.reshape(row_len, 2 * HD),
            grad_key_pre.reshape(row_len, 2 * HD),
            grad_values.reshape(row_len, 2 * HD),
        ],
        axis=1,
    ).astype(low)
    grad_attn_part = dot_transposed(grad_projected, qkv_c)
    row_scaled = row_inputs * lax.rsqrt(
        jnp.mean(row_inputs * row_inputs, axis=-1, keepdims=True) + EPSILON
    )
    grad_gain_attn = jnp.sum(grad_attn_part * row_scaled, axis=0)
    grad_bias_c = jnp.sum(grad_projected.astype(full), axis=0).reshape(3, 1, 2, HD)
    mine = (jnp.arange(ctx_count) == ctx_rank)[None, :, None, None]
    places_of = [head_order.index(h) for h in range(head_count)]
    grad_bias = (
        jnp.where(mine, grad_bias_c, 0.0)
        .reshape(3, head_count, HD)[:, jnp.array(places_of)]
        .reshape(dev_count, -1)
    )
    small_grads = jnp.concatenate(
        [
            grad_gain_attn.reshape(dev_count, shard),
            grad_gain_ffn.reshape(dev_count, shard),
            grad_router_gate.reshape(expert_count + 1, dev_count, shard)
            .transpose(1, 0, 2)
            .reshape(dev_count, (expert_count + 1) * shard),
            grad_bias,
        ],
        axis=1,
    )
    small_grads = jnp.pad(small_grads, ((0, 0), (0, 8 * HD - small_count)))
    grad_qkv_c = transposed_dot(row_normed, grad_projected).astype(low)
    grad_normed_attn, sum_qkv_c, sum_out, sums = closing(
        ctx_count,
        5,
        grad_attn_part.astype(low).reshape(ctx_count, tokens_dev, width),
        grad_qkv_c.reshape(fsdp_count, ctx_count * shard, 6 * HD),
        padded_out,
        small_grads.reshape(fsdp_count, ctx_count, 8, HD),
    )
    sums = sums.reshape(8 * HD)[:small_count]
    sum_qkv = (
        sum_qkv_c.reshape(ctx_count, shard, 3, 2, HD)
        .transpose(1, 2, 0, 3, 4)
        .reshape(shard, 3, head_count, HD)[:, :, jnp.array(places_of)]
        .reshape(shard, 3 * width)
    )
    unused_norm, first_pull = jax.vjp(lambda v: rms_scale(v, gain_attn), inputs)
    input_grad = grad_middle + first_pull(grad_normed_attn)[0]
    sum_router = sums[2 * shard : (2 + expert_count) * shard].reshape(expert_count, shard).T
    return (
        hidden_out,
        input_grad.reshape(1, tokens_dev, width),
        sums[:shard],
        sum_qkv.astype(full),
        sums[(3 + expert_count) * shard :],
        sum_out,
        sums[shard : 2 * shard],
        sum_router,
        sums[(2 + expert_count) * shard : (3 + expert_count) * shard],
        sum_inner,
        sum_outer.astype(full),
        sum_expert_inner.astype(full)[None],
        sum_expert_outer.astype(full)[None],
    )


def local(*arrays):
    width = arrays[0].shape[2]
    ctx_count = lax.axis_size("ctx")
    shard = arrays[6].shape[0]
    fits = (
        width == 2 * ctx_count * HD
        and 2 * shard == HD
        and ctx_count % 2 == 0
        and lax.axis_size("fsdp") * ctx_count * shard == width
        and arrays[14].shape[0] == 1
    )
    return split_plan(*arrays) if fits else gathered_plan(*arrays)


def solution(mesh):
    in_specs = (
        P("fsdp", "ctx", None),
        P("fsdp", "ctx"),
        P(),
        P("fsdp", "ctx", None),
        P("fsdp", "ctx", None),
        P(("fsdp", "ctx")),
        P(("fsdp", "ctx"), None),
        P(("fsdp", "ctx")),
        P(("fsdp", "ctx"), None),
        P(("fsdp", "ctx")),
        P(("fsdp", "ctx"), None),
        P(("fsdp", "ctx")),
        P(("fsdp", "ctx"), None),
        P(("fsdp", "ctx"), None),
        P("ctx", "fsdp", None),
        P("ctx", "fsdp", None),
    )
    out_specs = (
        P("fsdp", "ctx", None),
        P("fsdp", "ctx", None),
        P(("fsdp", "ctx")),
        P(("fsdp", "ctx"), None),
        P(("fsdp", "ctx")),
        P(("fsdp", "ctx"), None),
        P(("fsdp", "ctx")),
        P(("fsdp", "ctx"), None),
        P(("fsdp", "ctx")),
        P(("fsdp", "ctx"), None),
        P(("fsdp", "ctx"), None),
        P("ctx", "fsdp", None),
        P("ctx", "fsdp", None),
    )
    return jax.shard_map(local, mesh=mesh, in_specs=in_specs, out_specs=out_specs, check_vma=False)
```

```python
import functools

import jax
import jax.numpy as jnp
from jax import lax
from jax.experimental import pallas as pl
from jax.experimental.pallas import tpu as pltpu
from jax.sharding import PartitionSpec as P

HD = 128


EPSILON = 1e-06
THETA = 1000000.0
heads_per_group = 4


def rms_scale(values, gain_vec):
    return (
        values * lax.rsqrt(jnp.mean(values * values, axis=-1, keepdims=True) + EPSILON) * gain_vec
    )


def rotate(values, positions):
    half_len = values.shape[-1] // 2
    frequency = THETA ** (-jnp.arange(half_len, dtype=jnp.float32) / half_len)
    angles = positions.astype(jnp.float32)[:, None] * frequency[None, :]
    cosine = jnp.cos(angles)[:, None, :]
    sine_part = jnp.sin(angles)[:, None, :]
    first_half = values[..., :half_len]
    second = values[..., half_len:]
    return jnp.concatenate(
        [first_half * cosine - second * sine_part, second * cosine + first_half * sine_part],
        axis=-1,
    )


def visible(query_pos, query_seg, key_pos, key_seg):
    same_doc = (key_seg[None, :] == query_seg[:, None]) & (query_seg[:, None] >= 0)
    causal = key_pos[None, :] <= query_pos[:, None]
    return same_doc & causal | (key_pos[None, :] == query_pos[:, None])


def swiglu_mix(gate_up, hidden_width):
    return jax.nn.silu(gate_up[..., :hidden_width]) * gate_up[..., hidden_width:]


def matmul_low(left, right):
    return jnp.dot(left, right, preferred_element_type=jnp.float32)


def gathered_plan(
    hidden_in,
    segments,
    block_pairs,
    routes,
    out_grad,
    norm_gain_attn,
    qkv_weight,
    qkv_bias,
    out_weight,
    norm_gain_ffn,
    router_weight,
    shared_gate_weight,
    shared_in_weight,
    shared_out_weight,
    expert_in_weight,
    expert_out_weight,
):
    tokens_dev = hidden_in.shape[1]
    model_width = hidden_in.shape[2]
    block_len = tokens_dev // 2
    inputs = hidden_in.reshape(tokens_dev, model_width).astype(jnp.float32)
    seg_local = segments.reshape(tokens_dev)
    token_routes = routes.reshape(tokens_dev, -1)
    top_count = token_routes.shape[1]
    ctx_count = lax.axis_size("ctx")
    ctx_rank = lax.axis_index("ctx")
    offsets = jnp.arange(block_len, dtype=jnp.int32)
    all_positions = (
        block_pairs.reshape(ctx_count, 2)[:, :, None] * block_len + offsets[None, None, :]
    ).reshape(ctx_count * tokens_dev)
    my_positions = lax.dynamic_slice_in_dim(all_positions, ctx_rank * tokens_dev, tokens_dev, 0)
    gathered = (
        lax.all_gather(norm_gain_attn, ("fsdp", "ctx"), axis=0, tiled=True),
        lax.all_gather(qkv_weight, ("fsdp", "ctx"), axis=0, tiled=True),
        lax.all_gather(qkv_bias, ("fsdp", "ctx"), axis=0, tiled=True),
        lax.all_gather(out_weight, ("fsdp", "ctx"), axis=0, tiled=True),
        lax.all_gather(norm_gain_ffn, ("fsdp", "ctx"), axis=0, tiled=True),
        lax.all_gather(router_weight, ("fsdp", "ctx"), axis=0, tiled=True),
        lax.all_gather(shared_gate_weight, ("fsdp", "ctx"), axis=0, tiled=True),
        lax.all_gather(shared_in_weight, ("fsdp", "ctx"), axis=0, tiled=True),
        lax.all_gather(shared_out_weight, ("fsdp", "ctx"), axis=0, tiled=True),
    )
    (
        gain_attn,
        qkv_full,
        shift_full,
        out_full,
        gain_ffn,
        router_full,
        gate_full,
        inner_full,
        outer_full,
    ) = gathered
    gain_attn = gain_attn.astype(jnp.float32)
    gain_ffn = gain_ffn.astype(jnp.float32)
    heads_width = out_full.shape[0]
    head_count = heads_width // HD
    group_width = heads_per_group * HD
    group_count = head_count // heads_per_group
    normed = rms_scale(inputs, gain_attn).astype(jnp.bfloat16)
    projected = matmul_low(normed, qkv_full) + shift_full.astype(jnp.float32)
    query_pre = projected[:, :heads_width].reshape(tokens_dev, head_count, HD)
    key_pre = projected[:, heads_width : 2 * heads_width].reshape(tokens_dev, head_count, HD)

    def place_heads(query_in, key_in):
        return (rotate(query_in, my_positions) * HD ** (-0.5), rotate(key_in, my_positions))

    query_rot, key_rot = place_heads(query_pre, key_pre)
    query_low = query_rot.reshape(tokens_dev, heads_width).astype(jnp.bfloat16)
    key_low = key_rot.reshape(tokens_dev, heads_width).astype(jnp.bfloat16)
    value_low = projected[:, 2 * heads_width :].astype(jnp.bfloat16)
    keys_all, values_all, segs_all = (
        lax.all_gather(key_low, "ctx", axis=0, tiled=True),
        lax.all_gather(value_low, "ctx", axis=0, tiled=True),
        lax.all_gather(seg_local.astype(jnp.bfloat16), "ctx", axis=0, tiled=True),
    )
    allowed = visible(
        my_positions, seg_local.astype(jnp.float32), all_positions, segs_all.astype(jnp.float32)
    )

    def head_slice(matrix, group_index):
        return lax.dynamic_slice_in_dim(matrix, group_index * group_width, group_width, 1).reshape(
            matrix.shape[0], heads_per_group, HD
        )

    def forward_group(group_index):
        query_part = head_slice(query_low, group_index)
        key_part = head_slice(keys_all, group_index)
        value_part = head_slice(values_all, group_index)
        scores = jnp.einsum(
            "qhd,khd->hqk", query_part, key_part, preferred_element_type=jnp.float32
        )
        scores = jnp.where(allowed[None], scores, -1e30)
        highest = jnp.max(scores, axis=-1, keepdims=True)
        log_total = highest + jnp.log(jnp.sum(jnp.exp(scores - highest), axis=-1, keepdims=True))
        weights = jnp.exp(scores - log_total).astype(jnp.bfloat16)
        mixed = jnp.einsum("hqk,khd->qhd", weights, value_part, preferred_element_type=jnp.float32)
        return (mixed, log_total[..., 0])

    mixed_groups, log_totals = lax.map(forward_group, jnp.arange(group_count, dtype=jnp.int32))
    attended = (
        jnp.moveaxis(mixed_groups, 0, 1).reshape(tokens_dev, heads_width).astype(jnp.bfloat16)
    )
    middle = inputs + matmul_low(attended, out_full)
    normed_ffn = rms_scale(middle, gain_ffn).astype(jnp.bfloat16)
    logits = matmul_low(normed_ffn, router_full)
    router_probs = jax.nn.softmax(logits, axis=-1)
    expert_count = logits.shape[1]
    expert_ids = jnp.arange(expert_count, dtype=jnp.int32)
    chosen = (token_routes[:, :, None] == expert_ids[None, None, :]).astype(jnp.float32)
    gate_weights = jnp.sum(chosen * router_probs[:, None, :], axis=-1)
    capacity = 2 * tokens_dev * top_count // expert_count
    local_experts = expert_in_weight.shape[0]
    assigned = tokens_dev * top_count
    flat_routes = token_routes.reshape(assigned)
    onehot = (flat_routes[:, None] == expert_ids[None, :]).astype(jnp.int32)
    earlier = jnp.cumsum(onehot, axis=0) - onehot
    places = flat_routes * capacity + jnp.sum(earlier * onehot, axis=1)
    slot_source = (
        jnp.full((expert_count * capacity,), assigned, jnp.int32)
        .at[places]
        .set(jnp.arange(assigned, dtype=jnp.int32))
    )
    slot_token = slot_source // top_count
    padded_rows = jnp.concatenate([normed_ffn, jnp.zeros((1, model_width), jnp.bfloat16)], axis=0)
    outgoing = padded_rows[slot_token].reshape(ctx_count, local_experts * capacity, model_width)
    expert_inner, expert_outer = (
        lax.all_gather(expert_in_weight, "fsdp", axis=1, tiled=True),
        lax.all_gather(expert_out_weight, "fsdp", axis=1, tiled=True),
    )
    landed_tokens = lax.all_to_all(outgoing, "ctx", split_axis=0, concat_axis=0, tiled=True)
    incoming = landed_tokens.reshape(ctx_count, local_experts, capacity, model_width)
    expert_gu = jnp.einsum(
        "necd,edf->necf", incoming, expert_inner, preferred_element_type=jnp.float32
    )
    expert_width = expert_outer.shape[1]
    expert_hidden = swiglu_mix(expert_gu, expert_width).astype(jnp.bfloat16)
    expert_result = jnp.einsum(
        "necf,efd->necd", expert_hidden, expert_outer, preferred_element_type=jnp.float32
    ).astype(jnp.bfloat16)
    returned = lax.all_to_all(
        expert_result.reshape(ctx_count, local_experts * capacity, model_width),
        "ctx",
        split_axis=0,
        concat_axis=0,
        tiled=True,
    )
    picked = (
        returned.reshape(expert_count * capacity, model_width)[places]
        .reshape(tokens_dev, top_count, model_width)
        .astype(jnp.float32)
    )
    routed = jnp.sum(gate_weights[:, :, None] * picked, axis=1)
    upstream = out_grad.reshape(tokens_dev, model_width).astype(jnp.float32)
    shared_gu = matmul_low(normed_ffn, inner_full)
    shared_width = outer_full.shape[0]
    shared_hidden = swiglu_mix(shared_gu, shared_width).astype(jnp.bfloat16)
    shared_out = matmul_low(shared_hidden, outer_full)
    gate_value = jax.nn.sigmoid(matmul_low(normed_ffn, gate_full))
    output = middle + gate_value[:, None] * shared_out + routed
    hidden_out = output.astype(jnp.bfloat16).reshape(1, tokens_dev, model_width)
    gain_ffn, router_full, gate_full, inner_full, outer_full = (
        lax.all_gather(norm_gain_ffn, ("fsdp", "ctx"), axis=0, tiled=True),
        lax.all_gather(router_weight, ("fsdp", "ctx"), axis=0, tiled=True),
        lax.all_gather(shared_gate_weight, ("fsdp", "ctx"), axis=0, tiled=True),
        lax.all_gather(shared_in_weight, ("fsdp", "ctx"), axis=0, tiled=True),
        lax.all_gather(shared_out_weight, ("fsdp", "ctx"), axis=0, tiled=True),
    )
    gain_ffn = gain_ffn.astype(jnp.float32)
    grad_shared_out = (gate_value[:, None] * upstream).astype(jnp.bfloat16)
    grad_outer = jnp.einsum(
        "tf,td->fd", shared_hidden, grad_shared_out, preferred_element_type=jnp.float32
    )
    grad_hidden = jnp.einsum(
        "td,fd->tf", grad_shared_out, outer_full, preferred_element_type=jnp.float32
    )
    unused_mix, mix_pull = jax.vjp(functools.partial(swiglu_mix, hidden_width=shared_width), shared_gu)
    grad_shared_gu = mix_pull(grad_hidden)[0].astype(jnp.bfloat16)
    grad_inner = jnp.einsum(
        "td,tf->df", normed_ffn, grad_shared_gu, preferred_element_type=jnp.float32
    )
    grad_normed = jnp.einsum(
        "tf,df->td", grad_shared_gu, inner_full, preferred_element_type=jnp.float32
    )
    grad_gate_logit = (
        gate_value * (1.0 - gate_value) * jnp.sum(upstream * shared_out, axis=1)
    ).astype(jnp.bfloat16)
    grad_gate_vec = jnp.einsum(
        "td,t->d", normed_ffn, grad_gate_logit, preferred_element_type=jnp.float32
    )
    grad_normed = (
        grad_normed
        + grad_gate_logit.astype(jnp.float32)[:, None] * gate_full.astype(jnp.float32)[None, :]
    )
    grad_gates = jnp.sum(upstream[:, None, :] * picked, axis=2)
    grad_choice_probs = jnp.sum(chosen * grad_gates[:, :, None], axis=1)
    grad_logits = (
        router_probs
        * (grad_choice_probs - jnp.sum(router_probs * grad_choice_probs, axis=1, keepdims=True))
    ).astype(jnp.bfloat16)
    grad_router = jnp.einsum(
        "td,te->de", normed_ffn, grad_logits, preferred_element_type=jnp.float32
    )
    grad_normed = grad_normed + jnp.einsum(
        "te,de->td", grad_logits, router_full, preferred_element_type=jnp.float32
    )
    grad_slots = (
        (gate_weights[:, :, None] * upstream[:, None, :])
        .astype(jnp.bfloat16)
        .reshape(assigned, model_width)
    )
    padded_grads = jnp.concatenate([grad_slots, jnp.zeros((1, model_width), jnp.bfloat16)], axis=0)
    grad_outgoing = padded_grads[slot_source].reshape(
        ctx_count, local_experts * capacity, model_width
    )
    grad_incoming = lax.all_to_all(
        grad_outgoing, "ctx", split_axis=0, concat_axis=0, tiled=True
    ).reshape(ctx_count, local_experts, capacity, model_width)
    grad_expert_hidden = jnp.einsum(
        "necd,efd->necf", grad_incoming, expert_outer, preferred_element_type=jnp.float32
    )
    grad_expert_outer = jnp.einsum(
        "necf,necd->efd", expert_hidden, grad_incoming, preferred_element_type=jnp.float32
    )
    unused_mix, expert_pull = jax.vjp(functools.partial(swiglu_mix, hidden_width=expert_width), expert_gu)
    grad_expert_gu = expert_pull(grad_expert_hidden)[0].astype(jnp.bfloat16)
    grad_expert_inner = jnp.einsum(
        "necd,necf->edf", incoming, grad_expert_gu, preferred_element_type=jnp.float32
    )
    grad_expert_rows = jnp.einsum(
        "necf,edf->necd", grad_expert_gu, expert_inner, preferred_element_type=jnp.float32
    ).astype(jnp.bfloat16)
    grad_returned = lax.all_to_all(
        grad_expert_rows.reshape(ctx_count, local_experts * capacity, model_width),
        "ctx",
        split_axis=0,
        concat_axis=0,
        tiled=True,
    )
    grad_picked = grad_returned.reshape(expert_count * capacity, model_width)[places].reshape(
        tokens_dev, top_count, model_width
    )
    grad_normed = grad_normed + jnp.sum(grad_picked.astype(jnp.float32), axis=1)
    sum_expert_inner, sum_expert_outer = (
        lax.psum_scatter(
            grad_expert_inner.astype(jnp.bfloat16), "fsdp", scatter_dimension=1, tiled=True
        ).astype(jnp.float32),
        lax.psum_scatter(
            grad_expert_outer.astype(jnp.bfloat16), "fsdp", scatter_dimension=1, tiled=True
        ).astype(jnp.float32),
    )
    unused_norm, norm_pull = jax.vjp(rms_scale, middle, gain_ffn)
    grad_middle_norm, grad_gain_ffn = norm_pull(grad_normed)
    grad_middle = upstream + grad_middle_norm
    sum_gain_ffn, sum_router, sum_gate_vec, sum_inner, sum_outer = (
        lax.psum_scatter(grad_gain_ffn, ("fsdp", "ctx"), scatter_dimension=0, tiled=True),
        lax.psum_scatter(grad_router, ("fsdp", "ctx"), scatter_dimension=0, tiled=True),
        lax.psum_scatter(grad_gate_vec, ("fsdp", "ctx"), scatter_dimension=0, tiled=True),
        lax.psum_scatter(grad_inner, ("fsdp", "ctx"), scatter_dimension=0, tiled=True),
        lax.psum_scatter(grad_outer, ("fsdp", "ctx"), scatter_dimension=0, tiled=True),
    )
    grad_branch = grad_middle.astype(jnp.bfloat16)
    grad_out_mat = jnp.einsum(
        "tc,td->cd", attended, grad_branch, preferred_element_type=jnp.float32
    )
    grad_attended = jnp.einsum(
        "td,cd->tc", grad_branch, out_full, preferred_element_type=jnp.float32
    ).astype(jnp.bfloat16)
    keys_again, values_again = (
        lax.all_gather(key_low, "ctx", axis=0, tiled=True),
        lax.all_gather(value_low, "ctx", axis=0, tiled=True),
    )

    def backward_group(group_index):
        query_part = head_slice(query_low, group_index)
        key_part = head_slice(keys_again, group_index)
        value_part = head_slice(values_again, group_index)
        grad_part = head_slice(grad_attended, group_index)
        log_total = lax.dynamic_index_in_dim(log_totals, group_index, 0, keepdims=False)
        scores = jnp.einsum(
            "qhd,khd->hqk", query_part, key_part, preferred_element_type=jnp.float32
        )
        scores = jnp.where(allowed[None], scores, -1e30)
        weights = jnp.exp(scores - log_total[..., None])
        grad_weights = jnp.einsum(
            "qhd,khd->hqk", grad_part, value_part, preferred_element_type=jnp.float32
        )
        offset_term = jnp.sum(weights * grad_weights, axis=-1, keepdims=True)
        grad_scores = (weights * (grad_weights - offset_term)).astype(jnp.bfloat16)
        grad_query = jnp.einsum(
            "hqk,khd->qhd", grad_scores, key_part, preferred_element_type=jnp.float32
        )
        grad_key = jnp.einsum(
            "hqk,qhd->khd", grad_scores, query_part, preferred_element_type=jnp.float32
        )
        grad_value = jnp.einsum(
            "hqk,qhd->khd",
            weights.astype(jnp.bfloat16),
            grad_part,
            preferred_element_type=jnp.float32,
        )
        return (grad_query, grad_key, grad_value)

    grad_queries, grad_keys, grad_values = lax.map(
        backward_group, jnp.arange(group_count, dtype=jnp.int32)
    )
    row_total = keys_again.shape[0]
    grad_key_rows = jnp.moveaxis(grad_keys, 0, 1).reshape(row_total, heads_width)
    grad_value_rows = jnp.moveaxis(grad_values, 0, 1).reshape(row_total, heads_width)
    key_share, value_share = (
        lax.psum_scatter(
            grad_key_rows.astype(jnp.bfloat16), "ctx", scatter_dimension=0, tiled=True
        ).astype(jnp.float32),
        lax.psum_scatter(
            grad_value_rows.astype(jnp.bfloat16), "ctx", scatter_dimension=0, tiled=True
        ).astype(jnp.float32),
    )
    grad_query_heads = jnp.moveaxis(grad_queries, 0, 1).reshape(tokens_dev, head_count, HD)
    unused_rot, rotate_pull = jax.vjp(place_heads, query_pre, key_pre)
    grad_query_pre, grad_key_pre = rotate_pull(
        (grad_query_heads, key_share.reshape(tokens_dev, head_count, HD))
    )
    grad_projected = jnp.concatenate(
        [
            grad_query_pre.reshape(tokens_dev, heads_width),
            grad_key_pre.reshape(tokens_dev, heads_width),
            value_share,
        ],
        axis=1,
    ).astype(jnp.bfloat16)
    grad_qkv = jnp.einsum("td,tc->dc", normed, grad_projected, preferred_element_type=jnp.float32)
    grad_shift = jnp.sum(grad_projected.astype(jnp.float32), axis=0)
    grad_normed_attn = jnp.einsum(
        "tc,dc->td", grad_projected, qkv_full, preferred_element_type=jnp.float32
    )
    unused_norm, first_pull = jax.vjp(rms_scale, inputs, gain_attn)
    grad_inputs_norm, grad_gain_attn = first_pull(grad_normed_attn)
    input_grad = grad_middle + grad_inputs_norm
    sum_gain_attn, sum_qkv, sum_shift, sum_out = (
        lax.psum_scatter(grad_gain_attn, ("fsdp", "ctx"), scatter_dimension=0, tiled=True),
        lax.psum_scatter(grad_qkv, ("fsdp", "ctx"), scatter_dimension=0, tiled=True),
        lax.psum_scatter(grad_shift, ("fsdp", "ctx"), scatter_dimension=0, tiled=True),
        lax.psum_scatter(grad_out_mat, ("fsdp", "ctx"), scatter_dimension=0, tiled=True),
    )
    return (
        hidden_out,
        input_grad.reshape(1, tokens_dev, model_width),
        sum_gain_attn,
        sum_qkv,
        sum_shift,
        sum_out,
        sum_gain_ffn,
        sum_router,
        sum_gate_vec,
        sum_inner,
        sum_outer,
        sum_expert_inner,
        sum_expert_outer,
    )


MESH = pl.DeviceIdType.MESH
ANY = pl.BlockSpec(memory_space=pl.ANY)
VMEM = pl.BlockSpec(memory_space=pltpu.VMEM)


def remote(source, target, send_sem, recv_sem, **place):
    return pltpu.make_async_remote_copy(
        src_ref=source,
        dst_ref=target,
        send_sem=send_sem,
        recv_sem=recv_sem,
        device_id=place,
        device_id_type=MESH,
    )


def line_place():
    here = lax.axis_index("ctx")
    line = here % 2
    return here, here // 2, line, here + 1 - 2 * line


def greet_line(last, here, level, side, others=0):
    barrier = pltpu.get_barrier_semaphore()
    pl.semaphore_signal(barrier, inc=1, device_id={"ctx": side}, device_id_type=MESH)

    @pl.when(level < last)
    def up():
        pl.semaphore_signal(barrier, inc=1, device_id={"ctx": here + 2}, device_id_type=MESH)

    @pl.when(level > 0)
    def down():
        pl.semaphore_signal(barrier, inc=1, device_id={"ctx": here - 2}, device_id_type=MESH)

    ends = jnp.where(level < last, 1, 0) + jnp.where(level > 0, 1, 0)
    pl.semaphore_wait(barrier, 1 + others + ends)


def line_copy(rows_ref, block, way, target, sems, source=None):
    send_sem, recv_sem = sems
    return remote(
        rows_ref.at[block] if source is None else source,
        rows_ref.at[block],
        send_sem.at[block, way],
        recv_sem.at[block],
        ctx=target,
    )


def line_start(rows_ref, own_ref, sems, place, last):
    here, level, line, side = place

    @pl.when(level < last)
    def up():
        line_copy(rows_ref, here, 0, here + 2, sems, own_ref).start()

    @pl.when(level > 0)
    def down():
        line_copy(rows_ref, here, 1, here - 2, sems, own_ref).start()

    line_copy(rows_ref, here, 2, side, sems, own_ref).start()


def line_step(rows_ref, sems, place, last, step):
    here, level, line, side = place

    @pl.when(level >= step)
    def from_below():
        block = here - 2 * step
        line_copy(rows_ref, block, 0, side, sems).wait_recv()

        @pl.when(level < last)
        def on():
            line_copy(rows_ref, block, 0, here + 2, sems).start()

        line_copy(rows_ref, block, 2, side, sems).start()

    @pl.when(level + step <= last)
    def from_above():
        block = here + 2 * step
        line_copy(rows_ref, block, 1, side, sems).wait_recv()

        @pl.when(level > 0)
        def on():
            line_copy(rows_ref, block, 1, here - 2, sems).start()

        line_copy(rows_ref, block, 2, side, sems).start()


def line_finish(rows_ref, sems, place, last):
    here, level, line, side = place
    for other in range(last + 1):
        block = 2 * other + line
        line_copy(rows_ref, 2 * other + 1 - line, 2, side, sems).wait_recv()
        line_copy(rows_ref, block, 2, side, sems).wait_send()

        @pl.when((other <= level) & (level < last))
        def up():
            line_copy(rows_ref, block, 0, side, sems).wait_send()

        @pl.when((other >= level) & (level > 0))
        def down():
            line_copy(rows_ref, block, 1, side, sems).wait_send()


ROWS_STEP = 16


def add_rows(target, pieces, row_count):
    def one(index, carry):
        rows = pl.ds(pl.multiple_of(index * ROWS_STEP, ROWS_STEP), ROWS_STEP)
        total = pieces[0][rows, :].astype(jnp.float32)
        for piece in pieces[1:]:
            total = total + piece[rows, :].astype(jnp.float32)
        target[rows, :] = total.astype(target.dtype)
        return carry

    lax.fori_loop(0, row_count // ROWS_STEP, one, 0)


def scatter_turns(last, part, total, crossed, rising, falling, sums, *sems):
    cross_send, cross_recv, move_send, rise_recv, fall_recv = sems
    here, level, line, side = line_place()
    row_count = total.shape[0]

    def turn(k):
        middle = (level > 0) & (level < last)
        swapped = k + jnp.where(middle, (0, 0, 1, -1)[k], 0)
        return jnp.where(level * 2 < last, last - swapped, swapped)

    def cross(goal):
        return remote(
            part.at[2 * goal + 1 - line],
            crossed.at[goal],
            cross_send.at[goal],
            cross_recv.at[goal],
            ctx=side,
        )

    def rise(goal):
        return remote(
            sums.at[goal], rising.at[goal], move_send.at[goal], rise_recv.at[goal], ctx=here + 2
        )

    def fall(goal):
        return remote(
            sums.at[goal], falling.at[goal], move_send.at[goal], fall_recv.at[goal], ctx=here - 2
        )

    for k in range(min(2, last + 1)):
        cross(turn(k)).start()
    for k in range(last + 1):
        yield k
        goal = turn(k)
        mine = part.at[2 * goal + line]
        cross(goal).wait_recv()
        if k + 2 <= last:
            cross(turn(k + 2)).start()

        @pl.when(goal > level)
        def upward():
            @pl.when(level > 0)
            def joined():
                rise(goal).wait_recv()
                add_rows(sums.at[goal], (mine, crossed.at[goal], rising.at[goal]), row_count)

            @pl.when(level == 0)
            def first():
                add_rows(sums.at[goal], (mine, crossed.at[goal]), row_count)

            rise(goal).start()

        @pl.when(goal < level)
        def downward():
            @pl.when(level < last)
            def joined():
                fall(goal).wait_recv()
                add_rows(sums.at[goal], (mine, crossed.at[goal], falling.at[goal]), row_count)

            @pl.when(level == last)
            def first():
                add_rows(sums.at[goal], (mine, crossed.at[goal]), row_count)

            fall(goal).start()

        @pl.when(goal == level)
        def here_at_last():
            @pl.when(level > 0)
            def from_below():
                rise(goal).wait_recv()

            @pl.when(level < last)
            def from_above():
                fall(goal).wait_recv()

            @pl.when(level == 0)
            def bottom():
                add_rows(total, (mine, crossed.at[goal], falling.at[goal]), row_count)

            @pl.when(level == last)
            def top():
                add_rows(total, (mine, crossed.at[goal], rising.at[goal]), row_count)

            @pl.when((level > 0) & (level < last))
            def between():
                add_rows(
                    total,
                    (mine, crossed.at[goal], rising.at[goal], falling.at[goal]),
                    row_count,
                )

    for goal in range(last + 1):
        cross(goal).wait_send()

        @pl.when(goal != level)
        def sent():
            rise(goal).wait_send()


def scatter_kernel(ctx_count, part, small, total, small_in, *refs):
    greet_all(ctx_count)
    here = lax.axis_index("ctx")
    starts, waits = spread(
        lambda peer: small.at[peer], lambda source: small_in.at[source], refs[9:11], ctx_count
    )
    for copy in starts:
        copy.start()
    small_in[here] = small[here]
    for step in scatter_turns(ctx_count // 2 - 1, part, total, *refs[:9]):
        pass
    for copy in waits:
        copy.wait_recv()
    for copy in starts:
        copy.wait_send()


def line_scatter_kernel(last, part, total, *refs):
    here, level, line, side = line_place()
    greet_line(last, here, level, side)
    for step in scatter_turns(last, part, total, *refs):
        pass


def line_scatter(ctx_count, call_id, part, small=None):
    rows, width = part.shape[1:]
    half = ctx_count // 2
    dma = pltpu.SemaphoreType.DMA((half,))
    spread_dma = pltpu.SemaphoreType.DMA((ctx_count,))
    slots = pltpu.VMEM((half, rows, width), part.dtype)
    total = jax.ShapeDtypeStruct((rows, width), jnp.float32)
    params = pltpu.CompilerParams(
        collective_id=call_id, has_side_effects=True, vmem_limit_bytes=40 * 2**20
    )
    if small is None:
        return pl.pallas_call(
            functools.partial(line_scatter_kernel, half - 1),
            out_shape=total,
            in_specs=[VMEM],
            out_specs=VMEM,
            scratch_shapes=[slots] * 4 + [dma] * 5,
            compiler_params=params,
            name="line_scatter",
        )(part)
    return pl.pallas_call(
        functools.partial(scatter_kernel, ctx_count),
        out_shape=[total, jax.ShapeDtypeStruct(small.shape, small.dtype)],
        in_specs=[VMEM] * 2,
        out_specs=[VMEM] * 2,
        scratch_shapes=[slots] * 4 + [dma] * 5 + [spread_dma] * 2,
        compiler_params=params,
        name="line_scatter",
    )(part, small)


def fsdp_place():
    here = lax.axis_index("fsdp")
    beside = here + 1 - 2 * (here % 2)
    return here, beside, (here + 2) % 4, (beside + 2) % 4


def greet_all(ctx_count):
    barrier = pltpu.get_barrier_semaphore()
    here = lax.axis_index("ctx")
    group = lax.axis_index("fsdp")
    for k in range(1, ctx_count):
        pl.semaphore_signal(
            barrier, inc=1, device_id={"ctx": (here + k) % ctx_count}, device_id_type=MESH
        )
    for k in range(1, 4):
        pl.semaphore_signal(barrier, inc=1, device_id={"fsdp": (group + k) % 4}, device_id_type=MESH)
    pl.semaphore_wait(barrier, ctx_count + 2)


def share_start(blocks, sems, own=None):
    send_sem, recv_sem = sems
    here, beside, across, corner = fsdp_place()
    source = blocks.at[here] if own is None else own
    for way, target in ((0, across), (1, beside)):
        remote(source, blocks.at[here], send_sem.at[way], recv_sem.at[here], fsdp=target).start()


def share_step(blocks, sems):
    send_sem, recv_sem = sems
    here, beside, across, corner = fsdp_place()
    copy = remote(
        blocks.at[across], blocks.at[across], send_sem.at[2], recv_sem.at[across], fsdp=beside
    )
    copy.wait_recv()
    copy.start()


def share_finish(blocks, sems):
    send_sem, recv_sem = sems
    here, beside, across, corner = fsdp_place()
    for way, block in ((0, beside), (1, corner)):
        copy = remote(
            blocks.at[block], blocks.at[block], send_sem.at[way], recv_sem.at[block], fsdp=beside
        )
        copy.wait_recv()
        copy.wait_send()
    remote(
        blocks.at[here], blocks.at[here], send_sem.at[2], recv_sem.at[here], fsdp=beside
    ).wait_send()


def spread(pieces, landing, sems, ctx_count):
    send_sem, recv_sem = sems
    here = lax.axis_index("ctx")

    def copy(k, peer, source):
        return remote(pieces(peer), landing(source), send_sem.at[k], recv_sem.at[k], ctx=peer)

    starts = [copy(k, (here + k) % ctx_count, here) for k in range(1, ctx_count)]
    waits = [
        copy(k, (here + k) % ctx_count, (here + ctx_count - k) % ctx_count)
        for k in range(1, ctx_count)
    ]
    return starts, waits


def greet_near(last, here, level, side):
    barrier = pltpu.get_barrier_semaphore()
    group = lax.axis_index("fsdp")
    for k in range(1, 4):
        pl.semaphore_signal(barrier, inc=1, device_id={"fsdp": (group + k) % 4}, device_id_type=MESH)
    greet_line(last, here, level, side, 3)


def gather_kernel(last, shared_count, *refs):
    total = 1 + shared_count
    owns, rows, keep_sem = refs[:total], refs[total : 2 * total], refs[2 * total]
    refs = refs[2 * total + 1 :]
    place = line_place()
    here, level, line, side = place
    sems = [(refs[2 * i], refs[2 * i + 1]) for i in range(total)]
    group = lax.axis_index("fsdp")
    if shared_count:
        greet_near(last, here, level, side)
    else:
        greet_line(last, here, level, side)
    line_start(rows[0], owns[0], sems[0], place, last)
    for i in range(1, total):
        share_start(rows[i], sems[i], owns[i])
    keeps = [
        pltpu.make_async_copy(
            owns[i], rows[i].at[group if i else here], keep_sem.at[i]
        )
        for i in range(total)
    ]
    for copy in keeps:
        copy.start()
    for step in range(1, last + 1):
        line_step(rows[0], sems[0], place, last, step)
    for i in range(1, total):
        share_step(rows[i], sems[i])
    line_finish(rows[0], sems[0], place, last)
    for i in range(1, total):
        share_finish(rows[i], sems[i])
    for copy in keeps:
        copy.wait()


def line_gather(ctx_count, call_id, own, *shared):
    count = len(shared)
    dma = pltpu.SemaphoreType.DMA
    return pl.pallas_call(
        functools.partial(gather_kernel, ctx_count // 2 - 1, count),
        out_shape=[jax.ShapeDtypeStruct((ctx_count,) + own.shape, own.dtype)]
        + [jax.ShapeDtypeStruct((4,) + a.shape, a.dtype) for a in shared],
        in_specs=[VMEM] * (1 + count),
        out_specs=[ANY] * (1 + count),
        scratch_shapes=[dma((1 + count,)), dma((ctx_count, 3)), dma((ctx_count,))]
        + [dma((3,)), dma((4,))] * count,
        compiler_params=pltpu.CompilerParams(collective_id=call_id, has_side_effects=True),
        name="line_gather",
    )(own, *shared)


def opening_kernel(
    ctx_count,
    own,
    qkv_own,
    out_own,
    small_own,
    number_own,
    rows,
    qkv,
    out_pair,
    small,
    numbers,
    keep_sem,
    pair_send,
    pair_recv,
    row_send,
    row_recv,
    share_send,
    share_recv,
    *sems,
):
    last = ctx_count // 2 - 1
    place = line_place()
    here, level, line, side = place
    group, beside, across, corner = fsdp_place()
    sems = [(sems[2 * i], sems[2 * i + 1]) for i in range(5)]
    qkv_spread, small_spread, number_spread, out_share, small_share = sems
    row_sems = (row_send, row_recv)
    greet_all(ctx_count)
    qkv_start, qkv_wait = spread(
        lambda peer: qkv_own.at[peer], lambda source: qkv.at[group, source], qkv_spread, ctx_count
    )
    small_start, small_wait = spread(
        lambda peer: small_own, lambda source: small.at[group, source], small_spread, ctx_count
    )
    number_start, number_wait = spread(
        lambda peer: number_own, lambda source: numbers.at[source], number_spread, ctx_count
    )

    def piece_copy(way, owner, k, target, first=False):
        source = (here + ctx_count - k) % ctx_count
        return remote(
            qkv_own.at[here] if first else qkv.at[owner, source],
            qkv.at[owner, source],
            share_send.at[way, k],
            share_recv.at[owner, k],
            fsdp=target,
        )

    def piece_on(k):
        piece_copy(0, group, k, across, k == 0).start()
        piece_copy(1, group, k, beside, k == 0).start()

    for copy in small_start + number_start + qkv_start:
        copy.start()
    line_start(rows, own, row_sems, place, last)
    piece_on(0)
    pair = remote(
        out_own, out_pair.at[group, line], pair_send.at[0], pair_recv.at[0], ctx=side
    )
    pair.start()
    keeps = [
        pltpu.make_async_copy(source, target, keep_sem.at[i])
        for i, (source, target) in enumerate(
            (
                (qkv_own.at[here], qkv.at[group, here]),
                (out_own, out_pair.at[group, line]),
                (small_own, small.at[group, here]),
                (number_own, numbers.at[here]),
                (own, rows.at[here]),
            )
        )
    ]
    for copy in keeps:
        copy.start()
    for copy in small_wait:
        copy.wait_recv()
    keeps[2].wait()
    share_start(small, small_share)
    line_step(rows, row_sems, place, last, 1)
    for k in range(1, ctx_count):
        qkv_wait[k - 1].wait_recv()
        piece_on(k)
    remote(
        out_own, out_pair.at[group, 1 - line], pair_send.at[0], pair_recv.at[0], ctx=side
    ).wait_recv()
    keeps[1].wait()
    share_start(out_pair, out_share)
    line_step(rows, row_sems, place, last, 2)
    for k in range(ctx_count):
        piece_copy(0, across, k, across).wait_recv()
        piece_copy(2, across, k, beside).start()
    share_step(small, small_share)
    for step in range(3, last + 1):
        line_step(rows, row_sems, place, last, step)
    share_step(out_pair, out_share)
    line_finish(rows, row_sems, place, last)
    for copy in number_wait:
        copy.wait_recv()
    for copy in qkv_start + small_start + number_start:
        copy.wait_send()
    pair.wait_send()
    for k in range(ctx_count):
        piece_copy(1, beside, k, beside).wait_recv()
        piece_copy(2, corner, k, beside).wait_recv()
        for way in range(3):
            piece_copy(way, group, k, beside).wait_send()
    share_finish(small, small_share)
    share_finish(out_pair, out_share)
    for i in (0, 3, 4):
        keeps[i].wait()


def opening(ctx_count, call_id, own, qkv_own, out_own, small_own, number_own):
    def out(lead, array):
        return jax.ShapeDtypeStruct(lead + array.shape, array.dtype)

    dma = pltpu.SemaphoreType.DMA
    return pl.pallas_call(
        functools.partial(opening_kernel, ctx_count),
        out_shape=[
            out((ctx_count,), own),
            out((4,), qkv_own),
            out((4, 2), out_own),
            out((4, ctx_count), small_own),
            out((ctx_count,), number_own),
        ],
        in_specs=[VMEM] * 5,
        out_specs=[ANY] * 5,
        scratch_shapes=[
            dma((5,)),
            dma((1,)),
            dma((1,)),
            dma((ctx_count, 3)),
            dma((ctx_count,)),
            dma((3, ctx_count)),
            dma((4, ctx_count)),
        ]
        + [dma((ctx_count,))] * 6
        + [dma((3,)), dma((4,))] * 2,
        compiler_params=pltpu.CompilerParams(collective_id=call_id, has_side_effects=True),
        name="opening",
    )(own, qkv_own, out_own, small_own, number_own)


def group_reduce(blocks, beside_in, pair_sums, across_in, settled, sems):
    core_send, core_recv, far_send, far_recv = sems
    group, beside, across, corner = fsdp_place()
    rows = settled.shape[0]

    def core_copy(slot, block):
        return remote(
            blocks.at[block],
            beside_in.at[slot],
            core_send.at[slot],
            core_recv.at[slot],
            fsdp=beside,
        )

    far = remote(pair_sums.at[1], across_in, far_send.at[0], far_recv.at[0], fsdp=across)
    core_copy(1, corner).start()
    core_copy(0, beside).start()
    yield
    core_copy(1, corner).wait_recv()
    add_rows(pair_sums.at[1], (blocks.at[across], beside_in.at[1]), rows)
    far.start()
    core_copy(0, beside).wait_recv()
    add_rows(pair_sums.at[0], (blocks.at[group], beside_in.at[0]), rows)
    yield
    far.wait_recv()
    add_rows(settled, (pair_sums.at[0], across_in), rows)
    yield
    core_copy(1, corner).wait_send()
    core_copy(0, beside).wait_send()
    far.wait_send()
    yield


def closing_kernel(ctx_count, part, weight, pair, plain, small, *refs):
    total, landed, pair_total, plain_total, small_total = refs[:5]
    line_slots, weight_slots, pair_slots, plain_slots = (
        refs[5:9],
        refs[9:13],
        refs[13:17],
        refs[17:20],
    )
    pair_in, small_in, small_sums, small_across = refs[20:24]
    sems = refs[24:]
    line_sems, weight_sems, pair_sems, plain_sems = sems[:5], sems[5:9], sems[9:13], sems[13:17]
    keep_sem, half_send, half_recv = sems[17:20]
    weight_spread, small_spread, (group_send, group_recv) = sems[20:22], sems[22:24], sems[24:26]
    here, level, line, side = line_place()
    group = lax.axis_index("fsdp")
    greet_all(ctx_count)
    turns = scatter_turns(ctx_count // 2 - 1, part, total, *line_slots, *line_sems)
    settled, pair_settled = weight_slots[3], pair_slots[3]
    weight_steps = group_reduce(weight, *weight_slots, weight_sems)
    pair_steps = group_reduce(pair, *pair_slots, pair_sems)
    plain_steps = group_reduce(plain, *plain_slots, plain_total, plain_sems)
    small_start, small_wait = spread(
        lambda peer: small.at[:, peer], lambda source: small_in.at[source], small_spread, ctx_count
    )
    for copy in small_start:
        copy.start()
    next(weight_steps)
    next(turns)
    next(weight_steps)
    next(pair_steps)
    next(turns)
    next(pair_steps)
    next(plain_steps)
    for copy in small_wait:
        copy.wait_recv()
    small_sum = small[:, here]
    for k in range(1, ctx_count):
        small_sum = small_sum + small_in[(here + k) % ctx_count]
    small_sums[...] = small_sum
    group_copies = [
        remote(
            small_sums.at[(group + k) % 4],
            small_across.at[k],
            group_send.at[k],
            group_recv.at[k],
            fsdp=(group + k) % 4,
        )
        for k in range(1, 4)
    ]
    for copy in group_copies:
        copy.start()
    next(weight_steps)
    piece = settled.shape[0] // ctx_count
    weight_start, weight_wait = spread(
        lambda peer: settled.at[pl.ds(pl.multiple_of(peer * piece, piece), piece)],
        lambda source: landed.at[source],
        weight_spread,
        ctx_count,
    )
    for copy in weight_start:
        copy.start()
    keep = pltpu.make_async_copy(
        settled.at[pl.ds(pl.multiple_of(here * piece, piece), piece)],
        landed.at[here],
        keep_sem.at[0],
    )
    keep.start()
    next(plain_steps)
    next(turns)
    next(pair_steps)
    half = pair_total.shape[0]
    half_copy = remote(
        pair_settled.at[pl.ds(pl.multiple_of((1 - line) * half, half), half)],
        pair_in,
        half_send.at[0],
        half_recv.at[0],
        ctx=side,
    )
    half_copy.start()
    for copy in group_copies:
        copy.wait_recv()
    small_total[...] = small_sums[group] + small_across[1] + small_across[2] + small_across[3]
    for step in turns:
        pass
    next(plain_steps)
    half_copy.wait_recv()
    kept = pair_settled.at[pl.ds(pl.multiple_of(line * half, half), half)]
    add_rows(pair_total, (kept, pair_in), half)
    for copy in weight_wait:
        copy.wait_recv()
    for copy in weight_start + small_start + group_copies:
        copy.wait_send()
    half_copy.wait_send()
    next(weight_steps)
    next(pair_steps)
    next(plain_steps)
    keep.wait()


def closing(ctx_count, call_id, part, weight, pair, plain, small):
    rows, width = part.shape[1:]
    half = ctx_count // 2
    dma = pltpu.SemaphoreType.DMA
    slots = pltpu.VMEM((half, rows, width), part.dtype)

    def group_slots(array):
        one = pltpu.VMEM(array.shape[1:], array.dtype)
        two = pltpu.VMEM((2,) + array.shape[1:], array.dtype)
        return [two, two, one, one]

    block, columns = weight.shape[1:]
    pair_half = (pair.shape[1] // 2, pair.shape[2])
    return pl.pallas_call(
        functools.partial(closing_kernel, ctx_count),
        out_shape=[
            jax.ShapeDtypeStruct((rows, width), jnp.float32),
            jax.ShapeDtypeStruct((ctx_count, block // ctx_count, columns), weight.dtype),
            jax.ShapeDtypeStruct(pair_half, jnp.float32),
            jax.ShapeDtypeStruct(plain.shape[1:], jnp.float32),
            jax.ShapeDtypeStruct(small.shape[2:], small.dtype),
        ],
        in_specs=[VMEM] * 5,
        out_specs=[VMEM] * 5,
        scratch_shapes=[slots] * 4
        + group_slots(weight)
        + group_slots(pair)
        + group_slots(plain)[:3]
        + [
            pltpu.VMEM(pair_half, pair.dtype),
            pltpu.VMEM((ctx_count, 4) + small.shape[2:], small.dtype),
            pltpu.VMEM((4,) + small.shape[2:], small.dtype),
            pltpu.VMEM((4,) + small.shape[2:], small.dtype),
        ]
        + [dma((half,))] * 5
        + [dma((2,)), dma((2,)), dma((1,)), dma((1,))] * 3
        + [dma((1,))] * 3
        + [dma((ctx_count,))] * 4
        + [dma((4,))] * 2,
        compiler_params=pltpu.CompilerParams(
            collective_id=call_id, has_side_effects=True, vmem_limit_bytes=56 * 2**20
        ),
        name="closing",
    )(part, weight, pair, plain, small)


def deal_kernel(pieces, weight, dealt):
    ctx_count = dealt.shape[0]
    width = dealt.shape[2] // pieces
    for c in range(ctx_count):
        dealt[c] = jnp.concatenate(
            [
                weight[:, (q * ctx_count + c) * width : (q * ctx_count + c + 1) * width]
                for q in range(pieces)
            ],
            axis=1,
        )


def deal_columns(weight, ctx_count, pieces):
    rows, columns = weight.shape
    return pl.pallas_call(
        functools.partial(deal_kernel, pieces),
        out_shape=jax.ShapeDtypeStruct((ctx_count, rows, columns // ctx_count), weight.dtype),
        name="deal_columns",
    )(weight)


def collect_kernel(pieces, dealt, whole):
    ctx_count = dealt.shape[0]
    width = dealt.shape[2] // pieces
    whole[...] = jnp.concatenate(
        [
            dealt[c, :, q * width : (q + 1) * width]
            for q in range(pieces)
            for c in range(ctx_count)
        ],
        axis=1,
    ).astype(whole.dtype)


def collect_columns(dealt, pieces):
    ctx_count, rows, columns = dealt.shape
    return pl.pallas_call(
        functools.partial(collect_kernel, pieces),
        out_shape=jax.ShapeDtypeStruct((rows, columns * ctx_count), jnp.float32),
        name="collect_columns",
    )(dealt)


def heads_kernel(order, dealt, whole):
    pairs = dealt.shape[0] * 2
    for place, head in enumerate(order):
        for which in range(3):
            column = (which * 2 + place % 2) * HD
            target = (which * pairs + head) * HD
            whole[:, target : target + HD] = dealt[
                place // 2, :, column : column + HD
            ].astype(whole.dtype)


def collect_heads(dealt, order):
    ctx_count, rows, columns = dealt.shape
    return pl.pallas_call(
        functools.partial(heads_kernel, order),
        out_shape=jax.ShapeDtypeStruct((rows, columns * ctx_count), jnp.float32),
        name="collect_heads",
    )(dealt)


def over(axis, array, dim=0):
    return lax.all_gather(array, axis, axis=dim, tiled=True)


def reduce_over(axis, array, dim=0):
    return lax.psum_scatter(array, axis, scatter_dimension=dim, tiled=True)


def exchange(array):
    return lax.all_to_all(array, "ctx", split_axis=0, concat_axis=0, tiled=True)


def transposed_dot(left, right):
    return lax.dot_general(
        left, right, (((0,), (0,)), ((), ())), preferred_element_type=jnp.float32
    )


def dot_transposed(left, right):
    return lax.dot_general(
        left, right, (((1,), (1,)), ((), ())), preferred_element_type=jnp.float32
    )


def split_plan(
    hidden_in,
    segments,
    block_pairs,
    routes,
    out_grad,
    norm_gain_attn,
    qkv_weight,
    qkv_bias,
    out_weight,
    norm_gain_ffn,
    router_weight,
    shared_gate_weight,
    shared_in_weight,
    shared_out_weight,
    expert_in_weight,
    expert_out_weight,
):
    low = jnp.bfloat16
    full = jnp.float32
    tokens_dev, width = hidden_in.shape[1:]
    block_len = tokens_dev // 2
    ctx_count = lax.axis_size("ctx")
    fsdp_count = lax.axis_size("fsdp")
    ctx_rank = lax.axis_index("ctx")
    dev_count = ctx_count * fsdp_count
    row_len = ctx_count * tokens_dev
    head_count = width // HD
    shard = qkv_weight.shape[0]
    expert_count = router_weight.shape[1]
    shared_shard = shared_out_weight.shape[0]
    shared_width = fsdp_count * shared_shard
    expert_width = expert_out_weight.shape[1] * fsdp_count
    pair_rank = ctx_rank // 2
    side = ctx_rank % 2
    pairs = ctx_count // 2
    head_order = [j + (p * 2 + t) * pairs for j in range(pairs) for p in range(2) for t in range(2)]

    small = jnp.concatenate(
        [
            norm_gain_attn,
            norm_gain_ffn,
            shared_gate_weight,
            router_weight.T.reshape(-1),
            qkv_bias,
        ]
    )
    small_count = small.shape[0]
    small = jnp.pad(small, (0, 16 * HD - small_count)).reshape(16, HD)
    own_numbers = jnp.concatenate(
        [routes.reshape(tokens_dev, -1).T, segments.reshape(1, tokens_dev)], axis=0
    )
    number_count = own_numbers.shape[0]
    own_numbers = jnp.pad(own_numbers, ((0, 8 - number_count), (0, 0)))
    qkv_parts = (
        qkv_weight.reshape(shard, 3, head_count, HD)[:, :, jnp.array(head_order)]
        .reshape(shard, 3, ctx_count, 2 * HD)
        .transpose(2, 0, 1, 3)
        .reshape(ctx_count, shard, 6 * HD)
    )
    own_inputs = hidden_in.reshape(tokens_dev, width)
    row_inputs, qkv_c, out_pair, small_all, numbers = opening(
        ctx_count, 1, own_inputs, qkv_parts, out_weight, small, own_numbers
    )
    qkv_c = qkv_c.reshape(width, 6 * HD)
    out_c = lax.dynamic_index_in_dim(
        out_pair.reshape(2, 2 * HD, width), side, 0, keepdims=False
    )
    small_all = small_all.reshape(dev_count, 16 * HD)
    gain_attn = small_all[:, :shard].reshape(width).astype(full)
    gain_ffn = small_all[:, shard : 2 * shard].reshape(width).astype(full)
    gate_full = small_all[:, 2 * shard : 3 * shard].reshape(width)
    router_t = (
        small_all[:, 3 * shard : (3 + expert_count) * shard]
        .reshape(dev_count, expert_count, shard)
        .transpose(1, 0, 2)
        .reshape(expert_count, width)
    )
    bias_full = small_all[:, (3 + expert_count) * shard : small_count].reshape(3, head_count, HD)
    router_gate = jnp.concatenate([router_t, gate_full[None, :]], axis=0)
    row_seg = numbers[:, number_count - 1].reshape(row_len)
    routed_here = jnp.any(numbers[:, : number_count - 1] == ctx_rank, axis=1).reshape(row_len)

    shared_in_weight, numbers = lax.optimization_barrier((shared_in_weight, numbers))
    inner_parts = deal_columns(shared_in_weight, ctx_count, 2 * fsdp_count)
    expert_inner = over("fsdp", expert_in_weight[0])
    expert_outer = over("fsdp", expert_out_weight[0])
    inner_parts = exchange(inner_parts)
    my_heads = [pair_rank + (side * 2 + t) * pairs for t in range(2)]
    bias_c = jnp.concatenate(
        [lax.dynamic_index_in_dim(bias_full, h, 1, keepdims=False) for h in my_heads], axis=1
    ).reshape(6 * HD)

    offsets = jnp.arange(block_len, dtype=jnp.int32)
    positions = (block_pairs[:, None] * block_len + offsets[None, :]).reshape(row_len)
    inputs = own_inputs.astype(full)
    row_inputs = row_inputs.reshape(row_len, width).astype(full)
    row_upstream = over("ctx", out_grad.reshape(tokens_dev, width))
    row_normed = rms_scale(row_inputs, gain_attn).astype(low)
    projected = matmul_low(row_normed, qkv_c) + bias_c.astype(full)
    query_pre = projected[:, : 2 * HD].reshape(row_len, 2, HD)
    key_pre = projected[:, 2 * HD : 4 * HD].reshape(row_len, 2, HD)

    def place_heads(query_in, key_in):
        return (rotate(query_in, positions) * HD ** (-0.5), rotate(key_in, positions))

    query_rot, key_rot = place_heads(query_pre, key_pre)
    queries = query_rot.astype(low)
    keys = key_rot.astype(low)
    values = projected[:, 4 * HD :].reshape(row_len, 2, HD).astype(low)
    seg_real = row_seg.astype(full)
    allowed = visible(positions, seg_real, positions, seg_real)

    def score_part():
        scores = jnp.einsum("qhd,khd->hqk", queries, keys, preferred_element_type=full)
        return jnp.where(allowed[None], scores, -1e30)

    scores = score_part()
    highest = jnp.max(scores, axis=-1, keepdims=True)
    log_total = highest + jnp.log(jnp.sum(jnp.exp(scores - highest), axis=-1, keepdims=True))
    probs = jnp.exp(scores - log_total)
    attended_row = (
        jnp.einsum("hqk,khd->qhd", probs.astype(low), values, preferred_element_type=full)
        .astype(low)
        .reshape(row_len, 2 * HD)
    )
    attended_row, inner_parts = lax.optimization_barrier((attended_row, inner_parts))
    branch_part = matmul_low(attended_row, out_c).astype(low)
    branch = line_scatter(ctx_count, 2, branch_part.reshape(ctx_count, tokens_dev, width))
    middle = inputs + branch
    normed_ffn = rms_scale(middle, gain_ffn).astype(low)

    row_ffn, inner_c, outer_c = line_gather(
        ctx_count,
        4,
        normed_ffn,
        inner_parts.reshape(ctx_count * shard, 2 * shared_width),
        shared_out_weight,
    )
    row_ffn = row_ffn.reshape(row_len, width)
    inner_c = inner_c.reshape(width, 2 * shared_width)
    outer_c = outer_c.reshape(shared_width, width)
    row_logits = dot_transposed(row_ffn, router_gate)
    row_probs = jax.nn.softmax(row_logits[:, :expert_count], axis=-1)
    expert_ids = jnp.arange(expert_count, dtype=jnp.int32)
    here = jnp.where(
        routed_here, jnp.sum(jnp.where(expert_ids[None, :] == ctx_rank, row_probs, 0.0), axis=1), 0.0
    )
    row_gate = jax.nn.sigmoid(row_logits[:, expert_count])
    expert_gu = matmul_low(row_ffn, expert_inner)
    row_upstream, expert_gu = lax.optimization_barrier((row_upstream, expert_gu))
    expert_hidden = swiglu_mix(expert_gu, expert_width).astype(low)
    expert_result = matmul_low(expert_hidden, expert_outer).astype(low).astype(full)
    row_shared, expert_result = lax.optimization_barrier((row_ffn, expert_result))
    shared_gu = matmul_low(row_shared, inner_c)
    shared_hidden = swiglu_mix(shared_gu, shared_width).astype(low)
    shared_out = matmul_low(shared_hidden, outer_c)
    upstream_row = row_upstream.astype(full)
    out_part = (row_gate[:, None] * shared_out + here[:, None] * expert_result).astype(low)
    gate_dot = jnp.sum(upstream_row * shared_out, axis=1)
    expert_dot = jnp.where(routed_here, jnp.sum(upstream_row * expert_result, axis=1), 0.0)
    out_landed = reduce_over("ctx", out_part)

    upstream_row, out_part = lax.optimization_barrier((upstream_row, out_part))
    grad_buffers = (here[:, None] * upstream_row).astype(low)
    sum_expert_outer = reduce_over("fsdp", transposed_dot(expert_hidden, grad_buffers).astype(low))
    grad_expert_hidden = dot_transposed(grad_buffers, expert_outer)
    unused_mix, expert_pull = jax.vjp(
        functools.partial(swiglu_mix, hidden_width=expert_width), expert_gu
    )
    grad_expert_gu = expert_pull(grad_expert_hidden)[0].astype(low)
    grad_rows = dot_transposed(grad_expert_gu, expert_inner).astype(low)
    upstream_row, grad_rows = lax.optimization_barrier((upstream_row, grad_rows))
    grad_shared_out = (row_gate[:, None] * upstream_row).astype(low)
    grad_hidden = dot_transposed(grad_shared_out, outer_c)
    unused_mix, mix_pull = jax.vjp(
        functools.partial(swiglu_mix, hidden_width=shared_width), shared_gu
    )
    grad_shared_gu = mix_pull(grad_hidden)[0].astype(low)
    grad_inner = transposed_dot(row_ffn, grad_shared_gu).astype(low)
    sum_inner_c = reduce_over("fsdp", grad_inner)
    grad_outer = transposed_dot(shared_hidden, grad_shared_out).astype(low)
    grad_ffn_part = (
        dot_transposed(grad_shared_gu, inner_c) + grad_rows.astype(full)
    ).astype(low)
    grad_expert_gu, grad_ffn_part, grad_inner = lax.optimization_barrier(
        (grad_expert_gu, grad_ffn_part, grad_inner)
    )
    grad_expert_inner = transposed_dot(row_ffn, grad_expert_gu).astype(low)
    dots = jnp.stack([gate_dot, expert_dot]).reshape(2, ctx_count, tokens_dev).transpose(1, 0, 2)
    grad_ffn_part, grad_expert_inner, grad_outer = lax.optimization_barrier(
        (grad_ffn_part, grad_expert_inner, grad_outer)
    )
    sum_expert_inner = reduce_over("fsdp", grad_expert_inner)
    grad_normed, own_dots = line_scatter(
        ctx_count,
        6,
        grad_ffn_part.reshape(ctx_count, tokens_dev, width),
        jnp.pad(dots, ((0, 0), (0, 6), (0, 0))),
    )
    hidden_out = (middle + out_landed.astype(full)).astype(low).reshape(1, tokens_dev, width)

    own_logits = dot_transposed(normed_ffn, router_gate)
    router_probs = jax.nn.softmax(own_logits[:, :expert_count], axis=-1)
    gate_value = jax.nn.sigmoid(own_logits[:, expert_count])
    grad_gate_logit = gate_value * (1.0 - gate_value) * jnp.sum(own_dots[:, 0], axis=0)
    grad_choice = own_dots[:, 1].T
    grad_logits = router_probs * (
        grad_choice - jnp.sum(router_probs * grad_choice, axis=1, keepdims=True)
    )
    grad_small = jnp.concatenate([grad_logits, grad_gate_logit[:, None]], axis=1).astype(low)
    grad_router_gate = transposed_dot(grad_small, normed_ffn)
    grad_normed = grad_normed + matmul_low(grad_small, router_gate)
    unused_norm, norm_pull = jax.vjp(rms_scale, middle, gain_ffn)
    grad_middle_norm, grad_gain_ffn = norm_pull(grad_normed)
    grad_middle = out_grad.reshape(tokens_dev, width).astype(full) + grad_middle_norm

    grad_branch, sum_expert_outer, hidden_out = lax.optimization_barrier(
        (grad_middle.astype(low), sum_expert_outer, hidden_out)
    )
    (row_branch,) = line_gather(ctx_count, 3, grad_branch)
    row_branch, sum_inner_c = lax.optimization_barrier(
        (row_branch.reshape(row_len, width), sum_inner_c)
    )
    sum_inner = collect_columns(
        exchange(sum_inner_c.reshape(ctx_count, shard, 2 * shared_width)), 2 * fsdp_count
    )
    grad_attended = dot_transposed(row_branch, out_c).astype(low).reshape(row_len, 2, HD)
    grad_out_c = transposed_dot(attended_row, row_branch).astype(low).reshape(2, HD, width)
    padded_out = jnp.concatenate(
        [jnp.where(side == p, grad_out_c, jnp.zeros_like(grad_out_c)) for p in range(2)], axis=0
    )

    grad_probs = jnp.einsum("qhd,khd->hqk", grad_attended, values, preferred_element_type=full)
    weights = jnp.exp(score_part() - log_total)
    offset_term = jnp.sum(weights * grad_probs, axis=-1, keepdims=True)
    grad_scores = (weights * (grad_probs - offset_term)).astype(low)
    grad_queries = jnp.einsum("hqk,khd->qhd", grad_scores, keys, preferred_element_type=full)
    grad_keys = jnp.einsum("hqk,qhd->khd", grad_scores, queries, preferred_element_type=full)
    grad_values = jnp.einsum(
        "hqk,qhd->khd", weights.astype(low), grad_attended, preferred_element_type=full
    )
    unused_rot, rotate_pull = jax.vjp(place_heads, query_pre, key_pre)
    grad_query_pre, grad_key_pre = rotate_pull((grad_queries, grad_keys))
    grad_projected = jnp.concatenate(
        [
            grad_query_pre.reshape(row_len, 2 * HD),
            grad_key_pre.reshape(row_len, 2 * HD),
            grad_values.reshape(row_len, 2 * HD),
        ],
        axis=1,
    ).astype(low)
    grad_projected, sum_inner = lax.optimization_barrier((grad_projected, sum_inner))
    grad_attn_part = dot_transposed(grad_projected, qkv_c)
    row_scaled = row_inputs * lax.rsqrt(
        jnp.mean(row_inputs * row_inputs, axis=-1, keepdims=True) + EPSILON
    )
    grad_gain_attn = jnp.sum(grad_attn_part * row_scaled, axis=0)
    grad_bias_c = jnp.sum(grad_projected.astype(full), axis=0).reshape(3, 1, 2, HD)
    mine = (jnp.arange(ctx_count) == ctx_rank)[None, :, None, None]
    places_of = [head_order.index(h) for h in range(head_count)]
    grad_bias = (
        jnp.where(mine, grad_bias_c, 0.0)
        .reshape(3, head_count, HD)[:, jnp.array(places_of)]
        .reshape(dev_count, -1)
    )
    small_grads = jnp.concatenate(
        [
            grad_gain_attn.reshape(dev_count, shard),
            grad_gain_ffn.reshape(dev_count, shard),
            grad_router_gate.reshape(expert_count + 1, dev_count, shard)
            .transpose(1, 0, 2)
            .reshape(dev_count, (expert_count + 1) * shard),
            grad_bias,
        ],
        axis=1,
    )
    small_grads = jnp.pad(small_grads, ((0, 0), (0, 8 * HD - small_count)))
    grad_qkv_c = transposed_dot(row_normed, grad_projected).astype(low)
    grad_normed_attn, sum_qkv_c, sum_out, sum_outer, sums = closing(
        ctx_count,
        5,
        grad_attn_part.astype(low).reshape(ctx_count, tokens_dev, width),
        grad_qkv_c.reshape(fsdp_count, ctx_count * shard, 6 * HD),
        padded_out,
        grad_outer.reshape(fsdp_count, shared_shard, width),
        small_grads.reshape(fsdp_count, ctx_count, 8, HD),
    )
    sums = sums.reshape(8 * HD)[:small_count]
    sum_qkv = collect_heads(sum_qkv_c, head_order)
    unused_norm, first_pull = jax.vjp(lambda v: rms_scale(v, gain_attn), inputs)
    input_grad = grad_middle + first_pull(grad_normed_attn)[0]
    sum_router = sums[2 * shard : (2 + expert_count) * shard].reshape(expert_count, shard).T
    return (
        hidden_out,
        input_grad.reshape(1, tokens_dev, width),
        sums[:shard],
        sum_qkv,
        sums[(3 + expert_count) * shard :],
        sum_out,
        sums[shard : 2 * shard],
        sum_router,
        sums[(2 + expert_count) * shard : (3 + expert_count) * shard],
        sum_inner,
        sum_outer,
        sum_expert_inner.astype(full)[None],
        sum_expert_outer.astype(full)[None],
    )


def local(*arrays):
    width = arrays[0].shape[2]
    ctx_count = lax.axis_size("ctx")
    shard = arrays[6].shape[0]
    fits = (
        width == 2 * ctx_count * HD
        and 2 * shard == HD
        and ctx_count % 2 == 0
        and lax.axis_size("fsdp") * ctx_count * shard == width
        and arrays[14].shape[0] == 1
    )
    return split_plan(*arrays) if fits else gathered_plan(*arrays)


def solution(mesh):
    in_specs = (
        P("fsdp", "ctx", None),
        P("fsdp", "ctx"),
        P(),
        P("fsdp", "ctx", None),
        P("fsdp", "ctx", None),
        P(("fsdp", "ctx")),
        P(("fsdp", "ctx"), None),
        P(("fsdp", "ctx")),
        P(("fsdp", "ctx"), None),
        P(("fsdp", "ctx")),
        P(("fsdp", "ctx"), None),
        P(("fsdp", "ctx")),
        P(("fsdp", "ctx"), None),
        P(("fsdp", "ctx"), None),
        P("ctx", "fsdp", None),
        P("ctx", "fsdp", None),
    )
    out_specs = (
        P("fsdp", "ctx", None),
        P("fsdp", "ctx", None),
        P(("fsdp", "ctx")),
        P(("fsdp", "ctx"), None),
        P(("fsdp", "ctx")),
        P(("fsdp", "ctx"), None),
        P(("fsdp", "ctx")),
        P(("fsdp", "ctx"), None),
        P(("fsdp", "ctx")),
        P(("fsdp", "ctx"), None),
        P(("fsdp", "ctx"), None),
        P("ctx", "fsdp", None),
        P("ctx", "fsdp", None),
    )
    return jax.shard_map(local, mesh=mesh, in_specs=in_specs, out_specs=out_specs, check_vma=False)
```

```python
import functools

import jax
import jax.numpy as jnp
from jax import lax
from jax.experimental import pallas as pl
from jax.experimental.pallas import tpu as pltpu
from jax.sharding import PartitionSpec as P

HD = 128


EPSILON = 1e-06
THETA = 1000000.0
heads_per_group = 4


def rms_scale(values, gain_vec):
    return (
        values * lax.rsqrt(jnp.mean(values * values, axis=-1, keepdims=True) + EPSILON) * gain_vec
    )


def rotate(values, positions):
    half_len = values.shape[-1] // 2
    frequency = THETA ** (-jnp.arange(half_len, dtype=jnp.float32) / half_len)
    angles = positions.astype(jnp.float32)[:, None] * frequency[None, :]
    cosine = jnp.cos(angles)[:, None, :]
    sine_part = jnp.sin(angles)[:, None, :]
    first_half = values[..., :half_len]
    second = values[..., half_len:]
    return jnp.concatenate(
        [first_half * cosine - second * sine_part, second * cosine + first_half * sine_part],
        axis=-1,
    )


def visible(query_pos, query_seg, key_pos, key_seg):
    same_doc = (key_seg[None, :] == query_seg[:, None]) & (query_seg[:, None] >= 0)
    causal = key_pos[None, :] <= query_pos[:, None]
    return same_doc & causal | (key_pos[None, :] == query_pos[:, None])


def swiglu_mix(gate_up, hidden_width):
    return jax.nn.silu(gate_up[..., :hidden_width]) * gate_up[..., hidden_width:]


def matmul_low(left, right):
    return jnp.dot(left, right, preferred_element_type=jnp.float32)


def gathered_plan(
    hidden_in,
    segments,
    block_pairs,
    routes,
    out_grad,
    norm_gain_attn,
    qkv_weight,
    qkv_bias,
    out_weight,
    norm_gain_ffn,
    router_weight,
    shared_gate_weight,
    shared_in_weight,
    shared_out_weight,
    expert_in_weight,
    expert_out_weight,
):
    tokens_dev = hidden_in.shape[1]
    model_width = hidden_in.shape[2]
    block_len = tokens_dev // 2
    inputs = hidden_in.reshape(tokens_dev, model_width).astype(jnp.float32)
    seg_local = segments.reshape(tokens_dev)
    token_routes = routes.reshape(tokens_dev, -1)
    top_count = token_routes.shape[1]
    ctx_count = lax.axis_size("ctx")
    ctx_rank = lax.axis_index("ctx")
    offsets = jnp.arange(block_len, dtype=jnp.int32)
    all_positions = (
        block_pairs.reshape(ctx_count, 2)[:, :, None] * block_len + offsets[None, None, :]
    ).reshape(ctx_count * tokens_dev)
    my_positions = lax.dynamic_slice_in_dim(all_positions, ctx_rank * tokens_dev, tokens_dev, 0)
    gathered = (
        lax.all_gather(norm_gain_attn, ("fsdp", "ctx"), axis=0, tiled=True),
        lax.all_gather(qkv_weight, ("fsdp", "ctx"), axis=0, tiled=True),
        lax.all_gather(qkv_bias, ("fsdp", "ctx"), axis=0, tiled=True),
        lax.all_gather(out_weight, ("fsdp", "ctx"), axis=0, tiled=True),
        lax.all_gather(norm_gain_ffn, ("fsdp", "ctx"), axis=0, tiled=True),
        lax.all_gather(router_weight, ("fsdp", "ctx"), axis=0, tiled=True),
        lax.all_gather(shared_gate_weight, ("fsdp", "ctx"), axis=0, tiled=True),
        lax.all_gather(shared_in_weight, ("fsdp", "ctx"), axis=0, tiled=True),
        lax.all_gather(shared_out_weight, ("fsdp", "ctx"), axis=0, tiled=True),
    )
    (
        gain_attn,
        qkv_full,
        shift_full,
        out_full,
        gain_ffn,
        router_full,
        gate_full,
        inner_full,
        outer_full,
    ) = gathered
    gain_attn = gain_attn.astype(jnp.float32)
    gain_ffn = gain_ffn.astype(jnp.float32)
    heads_width = out_full.shape[0]
    head_count = heads_width // HD
    group_width = heads_per_group * HD
    group_count = head_count // heads_per_group
    normed = rms_scale(inputs, gain_attn).astype(jnp.bfloat16)
    projected = matmul_low(normed, qkv_full) + shift_full.astype(jnp.float32)
    query_pre = projected[:, :heads_width].reshape(tokens_dev, head_count, HD)
    key_pre = projected[:, heads_width : 2 * heads_width].reshape(tokens_dev, head_count, HD)

    def place_heads(query_in, key_in):
        return (rotate(query_in, my_positions) * HD ** (-0.5), rotate(key_in, my_positions))

    query_rot, key_rot = place_heads(query_pre, key_pre)
    query_low = query_rot.reshape(tokens_dev, heads_width).astype(jnp.bfloat16)
    key_low = key_rot.reshape(tokens_dev, heads_width).astype(jnp.bfloat16)
    value_low = projected[:, 2 * heads_width :].astype(jnp.bfloat16)
    keys_all, values_all, segs_all = (
        lax.all_gather(key_low, "ctx", axis=0, tiled=True),
        lax.all_gather(value_low, "ctx", axis=0, tiled=True),
        lax.all_gather(seg_local.astype(jnp.bfloat16), "ctx", axis=0, tiled=True),
    )
    allowed = visible(
        my_positions, seg_local.astype(jnp.float32), all_positions, segs_all.astype(jnp.float32)
    )

    def head_slice(matrix, group_index):
        return lax.dynamic_slice_in_dim(matrix, group_index * group_width, group_width, 1).reshape(
            matrix.shape[0], heads_per_group, HD
        )

    def forward_group(group_index):
        query_part = head_slice(query_low, group_index)
        key_part = head_slice(keys_all, group_index)
        value_part = head_slice(values_all, group_index)
        scores = jnp.einsum(
            "qhd,khd->hqk", query_part, key_part, preferred_element_type=jnp.float32
        )
        scores = jnp.where(allowed[None], scores, -1e30)
        highest = jnp.max(scores, axis=-1, keepdims=True)
        log_total = highest + jnp.log(jnp.sum(jnp.exp(scores - highest), axis=-1, keepdims=True))
        weights = jnp.exp(scores - log_total).astype(jnp.bfloat16)
        mixed = jnp.einsum("hqk,khd->qhd", weights, value_part, preferred_element_type=jnp.float32)
        return (mixed, log_total[..., 0])

    mixed_groups, log_totals = lax.map(forward_group, jnp.arange(group_count, dtype=jnp.int32))
    attended = (
        jnp.moveaxis(mixed_groups, 0, 1).reshape(tokens_dev, heads_width).astype(jnp.bfloat16)
    )
    middle = inputs + matmul_low(attended, out_full)
    normed_ffn = rms_scale(middle, gain_ffn).astype(jnp.bfloat16)
    logits = matmul_low(normed_ffn, router_full)
    router_probs = jax.nn.softmax(logits, axis=-1)
    expert_count = logits.shape[1]
    expert_ids = jnp.arange(expert_count, dtype=jnp.int32)
    chosen = (token_routes[:, :, None] == expert_ids[None, None, :]).astype(jnp.float32)
    gate_weights = jnp.sum(chosen * router_probs[:, None, :], axis=-1)
    capacity = 2 * tokens_dev * top_count // expert_count
    local_experts = expert_in_weight.shape[0]
    assigned = tokens_dev * top_count
    flat_routes = token_routes.reshape(assigned)
    onehot = (flat_routes[:, None] == expert_ids[None, :]).astype(jnp.int32)
    earlier = jnp.cumsum(onehot, axis=0) - onehot
    places = flat_routes * capacity + jnp.sum(earlier * onehot, axis=1)
    slot_source = (
        jnp.full((expert_count * capacity,), assigned, jnp.int32)
        .at[places]
        .set(jnp.arange(assigned, dtype=jnp.int32))
    )
    slot_token = slot_source // top_count
    padded_rows = jnp.concatenate([normed_ffn, jnp.zeros((1, model_width), jnp.bfloat16)], axis=0)
    outgoing = padded_rows[slot_token].reshape(ctx_count, local_experts * capacity, model_width)
    expert_inner, expert_outer = (
        lax.all_gather(expert_in_weight, "fsdp", axis=1, tiled=True),
        lax.all_gather(expert_out_weight, "fsdp", axis=1, tiled=True),
    )
    landed_tokens = lax.all_to_all(outgoing, "ctx", split_axis=0, concat_axis=0, tiled=True)
    incoming = landed_tokens.reshape(ctx_count, local_experts, capacity, model_width)
    expert_gu = jnp.einsum(
        "necd,edf->necf", incoming, expert_inner, preferred_element_type=jnp.float32
    )
    expert_width = expert_outer.shape[1]
    expert_hidden = swiglu_mix(expert_gu, expert_width).astype(jnp.bfloat16)
    expert_result = jnp.einsum(
        "necf,efd->necd", expert_hidden, expert_outer, preferred_element_type=jnp.float32
    ).astype(jnp.bfloat16)
    returned = lax.all_to_all(
        expert_result.reshape(ctx_count, local_experts * capacity, model_width),
        "ctx",
        split_axis=0,
        concat_axis=0,
        tiled=True,
    )
    picked = (
        returned.reshape(expert_count * capacity, model_width)[places]
        .reshape(tokens_dev, top_count, model_width)
        .astype(jnp.float32)
    )
    routed = jnp.sum(gate_weights[:, :, None] * picked, axis=1)
    upstream = out_grad.reshape(tokens_dev, model_width).astype(jnp.float32)
    shared_gu = matmul_low(normed_ffn, inner_full)
    shared_width = outer_full.shape[0]
    shared_hidden = swiglu_mix(shared_gu, shared_width).astype(jnp.bfloat16)
    shared_out = matmul_low(shared_hidden, outer_full)
    gate_value = jax.nn.sigmoid(matmul_low(normed_ffn, gate_full))
    output = middle + gate_value[:, None] * shared_out + routed
    hidden_out = output.astype(jnp.bfloat16).reshape(1, tokens_dev, model_width)
    gain_ffn, router_full, gate_full, inner_full, outer_full = (
        lax.all_gather(norm_gain_ffn, ("fsdp", "ctx"), axis=0, tiled=True),
        lax.all_gather(router_weight, ("fsdp", "ctx"), axis=0, tiled=True),
        lax.all_gather(shared_gate_weight, ("fsdp", "ctx"), axis=0, tiled=True),
        lax.all_gather(shared_in_weight, ("fsdp", "ctx"), axis=0, tiled=True),
        lax.all_gather(shared_out_weight, ("fsdp", "ctx"), axis=0, tiled=True),
    )
    gain_ffn = gain_ffn.astype(jnp.float32)
    grad_shared_out = (gate_value[:, None] * upstream).astype(jnp.bfloat16)
    grad_outer = jnp.einsum(
        "tf,td->fd", shared_hidden, grad_shared_out, preferred_element_type=jnp.float32
    )
    grad_hidden = jnp.einsum(
        "td,fd->tf", grad_shared_out, outer_full, preferred_element_type=jnp.float32
    )
    unused_mix, mix_pull = jax.vjp(functools.partial(swiglu_mix, hidden_width=shared_width), shared_gu)
    grad_shared_gu = mix_pull(grad_hidden)[0].astype(jnp.bfloat16)
    grad_inner = jnp.einsum(
        "td,tf->df", normed_ffn, grad_shared_gu, preferred_element_type=jnp.float32
    )
    grad_normed = jnp.einsum(
        "tf,df->td", grad_shared_gu, inner_full, preferred_element_type=jnp.float32
    )
    grad_gate_logit = (
        gate_value * (1.0 - gate_value) * jnp.sum(upstream * shared_out, axis=1)
    ).astype(jnp.bfloat16)
    grad_gate_vec = jnp.einsum(
        "td,t->d", normed_ffn, grad_gate_logit, preferred_element_type=jnp.float32
    )
    grad_normed = (
        grad_normed
        + grad_gate_logit.astype(jnp.float32)[:, None] * gate_full.astype(jnp.float32)[None, :]
    )
    grad_gates = jnp.sum(upstream[:, None, :] * picked, axis=2)
    grad_choice_probs = jnp.sum(chosen * grad_gates[:, :, None], axis=1)
    grad_logits = (
        router_probs
        * (grad_choice_probs - jnp.sum(router_probs * grad_choice_probs, axis=1, keepdims=True))
    ).astype(jnp.bfloat16)
    grad_router = jnp.einsum(
        "td,te->de", normed_ffn, grad_logits, preferred_element_type=jnp.float32
    )
    grad_normed = grad_normed + jnp.einsum(
        "te,de->td", grad_logits, router_full, preferred_element_type=jnp.float32
    )
    grad_slots = (
        (gate_weights[:, :, None] * upstream[:, None, :])
        .astype(jnp.bfloat16)
        .reshape(assigned, model_width)
    )
    padded_grads = jnp.concatenate([grad_slots, jnp.zeros((1, model_width), jnp.bfloat16)], axis=0)
    grad_outgoing = padded_grads[slot_source].reshape(
        ctx_count, local_experts * capacity, model_width
    )
    grad_incoming = lax.all_to_all(
        grad_outgoing, "ctx", split_axis=0, concat_axis=0, tiled=True
    ).reshape(ctx_count, local_experts, capacity, model_width)
    grad_expert_hidden = jnp.einsum(
        "necd,efd->necf", grad_incoming, expert_outer, preferred_element_type=jnp.float32
    )
    grad_expert_outer = jnp.einsum(
        "necf,necd->efd", expert_hidden, grad_incoming, preferred_element_type=jnp.float32
    )
    unused_mix, expert_pull = jax.vjp(functools.partial(swiglu_mix, hidden_width=expert_width), expert_gu)
    grad_expert_gu = expert_pull(grad_expert_hidden)[0].astype(jnp.bfloat16)
    grad_expert_inner = jnp.einsum(
        "necd,necf->edf", incoming, grad_expert_gu, preferred_element_type=jnp.float32
    )
    grad_expert_rows = jnp.einsum(
        "necf,edf->necd", grad_expert_gu, expert_inner, preferred_element_type=jnp.float32
    ).astype(jnp.bfloat16)
    grad_returned = lax.all_to_all(
        grad_expert_rows.reshape(ctx_count, local_experts * capacity, model_width),
        "ctx",
        split_axis=0,
        concat_axis=0,
        tiled=True,
    )
    grad_picked = grad_returned.reshape(expert_count * capacity, model_width)[places].reshape(
        tokens_dev, top_count, model_width
    )
    grad_normed = grad_normed + jnp.sum(grad_picked.astype(jnp.float32), axis=1)
    sum_expert_inner, sum_expert_outer = (
        lax.psum_scatter(
            grad_expert_inner.astype(jnp.bfloat16), "fsdp", scatter_dimension=1, tiled=True
        ).astype(jnp.float32),
        lax.psum_scatter(
            grad_expert_outer.astype(jnp.bfloat16), "fsdp", scatter_dimension=1, tiled=True
        ).astype(jnp.float32),
    )
    unused_norm, norm_pull = jax.vjp(rms_scale, middle, gain_ffn)
    grad_middle_norm, grad_gain_ffn = norm_pull(grad_normed)
    grad_middle = upstream + grad_middle_norm
    sum_gain_ffn, sum_router, sum_gate_vec, sum_inner, sum_outer = (
        lax.psum_scatter(grad_gain_ffn, ("fsdp", "ctx"), scatter_dimension=0, tiled=True),
        lax.psum_scatter(grad_router, ("fsdp", "ctx"), scatter_dimension=0, tiled=True),
        lax.psum_scatter(grad_gate_vec, ("fsdp", "ctx"), scatter_dimension=0, tiled=True),
        lax.psum_scatter(grad_inner, ("fsdp", "ctx"), scatter_dimension=0, tiled=True),
        lax.psum_scatter(grad_outer, ("fsdp", "ctx"), scatter_dimension=0, tiled=True),
    )
    grad_branch = grad_middle.astype(jnp.bfloat16)
    grad_out_mat = jnp.einsum(
        "tc,td->cd", attended, grad_branch, preferred_element_type=jnp.float32
    )
    grad_attended = jnp.einsum(
        "td,cd->tc", grad_branch, out_full, preferred_element_type=jnp.float32
    ).astype(jnp.bfloat16)
    keys_again, values_again = (
        lax.all_gather(key_low, "ctx", axis=0, tiled=True),
        lax.all_gather(value_low, "ctx", axis=0, tiled=True),
    )

    def backward_group(group_index):
        query_part = head_slice(query_low, group_index)
        key_part = head_slice(keys_again, group_index)
        value_part = head_slice(values_again, group_index)
        grad_part = head_slice(grad_attended, group_index)
        log_total = lax.dynamic_index_in_dim(log_totals, group_index, 0, keepdims=False)
        scores = jnp.einsum(
            "qhd,khd->hqk", query_part, key_part, preferred_element_type=jnp.float32
        )
        scores = jnp.where(allowed[None], scores, -1e30)
        weights = jnp.exp(scores - log_total[..., None])
        grad_weights = jnp.einsum(
            "qhd,khd->hqk", grad_part, value_part, preferred_element_type=jnp.float32
        )
        offset_term = jnp.sum(weights * grad_weights, axis=-1, keepdims=True)
        grad_scores = (weights * (grad_weights - offset_term)).astype(jnp.bfloat16)
        grad_query = jnp.einsum(
            "hqk,khd->qhd", grad_scores, key_part, preferred_element_type=jnp.float32
        )
        grad_key = jnp.einsum(
            "hqk,qhd->khd", grad_scores, query_part, preferred_element_type=jnp.float32
        )
        grad_value = jnp.einsum(
            "hqk,qhd->khd",
            weights.astype(jnp.bfloat16),
            grad_part,
            preferred_element_type=jnp.float32,
        )
        return (grad_query, grad_key, grad_value)

    grad_queries, grad_keys, grad_values = lax.map(
        backward_group, jnp.arange(group_count, dtype=jnp.int32)
    )
    row_total = keys_again.shape[0]
    grad_key_rows = jnp.moveaxis(grad_keys, 0, 1).reshape(row_total, heads_width)
    grad_value_rows = jnp.moveaxis(grad_values, 0, 1).reshape(row_total, heads_width)
    key_share, value_share = (
        lax.psum_scatter(
            grad_key_rows.astype(jnp.bfloat16), "ctx", scatter_dimension=0, tiled=True
        ).astype(jnp.float32),
        lax.psum_scatter(
            grad_value_rows.astype(jnp.bfloat16), "ctx", scatter_dimension=0, tiled=True
        ).astype(jnp.float32),
    )
    grad_query_heads = jnp.moveaxis(grad_queries, 0, 1).reshape(tokens_dev, head_count, HD)
    unused_rot, rotate_pull = jax.vjp(place_heads, query_pre, key_pre)
    grad_query_pre, grad_key_pre = rotate_pull(
        (grad_query_heads, key_share.reshape(tokens_dev, head_count, HD))
    )
    grad_projected = jnp.concatenate(
        [
            grad_query_pre.reshape(tokens_dev, heads_width),
            grad_key_pre.reshape(tokens_dev, heads_width),
            value_share,
        ],
        axis=1,
    ).astype(jnp.bfloat16)
    grad_qkv = jnp.einsum("td,tc->dc", normed, grad_projected, preferred_element_type=jnp.float32)
    grad_shift = jnp.sum(grad_projected.astype(jnp.float32), axis=0)
    grad_normed_attn = jnp.einsum(
        "tc,dc->td", grad_projected, qkv_full, preferred_element_type=jnp.float32
    )
    unused_norm, first_pull = jax.vjp(rms_scale, inputs, gain_attn)
    grad_inputs_norm, grad_gain_attn = first_pull(grad_normed_attn)
    input_grad = grad_middle + grad_inputs_norm
    sum_gain_attn, sum_qkv, sum_shift, sum_out = (
        lax.psum_scatter(grad_gain_attn, ("fsdp", "ctx"), scatter_dimension=0, tiled=True),
        lax.psum_scatter(grad_qkv, ("fsdp", "ctx"), scatter_dimension=0, tiled=True),
        lax.psum_scatter(grad_shift, ("fsdp", "ctx"), scatter_dimension=0, tiled=True),
        lax.psum_scatter(grad_out_mat, ("fsdp", "ctx"), scatter_dimension=0, tiled=True),
    )
    return (
        hidden_out,
        input_grad.reshape(1, tokens_dev, model_width),
        sum_gain_attn,
        sum_qkv,
        sum_shift,
        sum_out,
        sum_gain_ffn,
        sum_router,
        sum_gate_vec,
        sum_inner,
        sum_outer,
        sum_expert_inner,
        sum_expert_outer,
    )


MESH = pl.DeviceIdType.MESH
ANY = pl.BlockSpec(memory_space=pl.ANY)
VMEM = pl.BlockSpec(memory_space=pltpu.VMEM)


def remote(source, target, send_sem, recv_sem, **place):
    return pltpu.make_async_remote_copy(
        src_ref=source,
        dst_ref=target,
        send_sem=send_sem,
        recv_sem=recv_sem,
        device_id=place,
        device_id_type=MESH,
    )


def line_place():
    here = lax.axis_index("ctx")
    line = here % 2
    return here, here // 2, line, here + 1 - 2 * line


def greet_line(last, here, level, side, others=0):
    barrier = pltpu.get_barrier_semaphore()
    pl.semaphore_signal(barrier, inc=1, device_id={"ctx": side}, device_id_type=MESH)

    @pl.when(level < last)
    def up():
        pl.semaphore_signal(barrier, inc=1, device_id={"ctx": here + 2}, device_id_type=MESH)

    @pl.when(level > 0)
    def down():
        pl.semaphore_signal(barrier, inc=1, device_id={"ctx": here - 2}, device_id_type=MESH)

    ends = jnp.where(level < last, 1, 0) + jnp.where(level > 0, 1, 0)
    pl.semaphore_wait(barrier, 1 + others + ends)


def line_copy(rows_ref, block, way, target, sems, source=None):
    send_sem, recv_sem = sems
    return remote(
        rows_ref.at[block] if source is None else source,
        rows_ref.at[block],
        send_sem.at[block, way],
        recv_sem.at[block],
        ctx=target,
    )


def line_start(rows_ref, own_ref, sems, place, last):
    here, level, line, side = place

    @pl.when(level < last)
    def up():
        line_copy(rows_ref, here, 0, here + 2, sems, own_ref).start()

    @pl.when(level > 0)
    def down():
        line_copy(rows_ref, here, 1, here - 2, sems, own_ref).start()

    line_copy(rows_ref, here, 2, side, sems, own_ref).start()


def line_step(rows_ref, sems, place, last, step):
    here, level, line, side = place

    @pl.when(level >= step)
    def from_below():
        block = here - 2 * step
        line_copy(rows_ref, block, 0, side, sems).wait_recv()

        @pl.when(level < last)
        def on():
            line_copy(rows_ref, block, 0, here + 2, sems).start()

        line_copy(rows_ref, block, 2, side, sems).start()

    @pl.when(level + step <= last)
    def from_above():
        block = here + 2 * step
        line_copy(rows_ref, block, 1, side, sems).wait_recv()

        @pl.when(level > 0)
        def on():
            line_copy(rows_ref, block, 1, here - 2, sems).start()

        line_copy(rows_ref, block, 2, side, sems).start()


def line_finish(rows_ref, sems, place, last):
    here, level, line, side = place
    for other in range(last + 1):
        block = 2 * other + line
        line_copy(rows_ref, 2 * other + 1 - line, 2, side, sems).wait_recv()
        line_copy(rows_ref, block, 2, side, sems).wait_send()

        @pl.when((other <= level) & (level < last))
        def up():
            line_copy(rows_ref, block, 0, side, sems).wait_send()

        @pl.when((other >= level) & (level > 0))
        def down():
            line_copy(rows_ref, block, 1, side, sems).wait_send()


ROWS_STEP = 16


def add_rows(target, pieces, row_count):
    def one(index, carry):
        rows = pl.ds(pl.multiple_of(index * ROWS_STEP, ROWS_STEP), ROWS_STEP)
        total = pieces[0][rows, :].astype(jnp.float32)
        for piece in pieces[1:]:
            total = total + piece[rows, :].astype(jnp.float32)
        target[rows, :] = total.astype(target.dtype)
        return carry

    lax.fori_loop(0, row_count // ROWS_STEP, one, 0)


def scatter_turns(last, part, total, crossed, rising, falling, sums, *sems):
    cross_send, cross_recv, move_send, rise_recv, fall_recv = sems
    here, level, line, side = line_place()
    row_count = total.shape[0]

    def turn(k):
        middle = (level > 0) & (level < last)
        swapped = k + jnp.where(middle, (0, 0, 1, -1)[k], 0)
        return jnp.where(level * 2 < last, last - swapped, swapped)

    def cross(goal):
        return remote(
            part.at[2 * goal + 1 - line],
            crossed.at[goal],
            cross_send.at[goal],
            cross_recv.at[goal],
            ctx=side,
        )

    def rise(goal):
        return remote(
            sums.at[goal], rising.at[goal], move_send.at[goal], rise_recv.at[goal], ctx=here + 2
        )

    def fall(goal):
        return remote(
            sums.at[goal], falling.at[goal], move_send.at[goal], fall_recv.at[goal], ctx=here - 2
        )

    for k in range(min(2, last + 1)):
        cross(turn(k)).start()
    for k in range(last + 1):
        yield k
        goal = turn(k)
        mine = part.at[2 * goal + line]
        cross(goal).wait_recv()
        if k + 2 <= last:
            cross(turn(k + 2)).start()

        @pl.when(goal > level)
        def upward():
            @pl.when(level > 0)
            def joined():
                rise(goal).wait_recv()
                add_rows(sums.at[goal], (mine, crossed.at[goal], rising.at[goal]), row_count)

            @pl.when(level == 0)
            def first():
                add_rows(sums.at[goal], (mine, crossed.at[goal]), row_count)

            rise(goal).start()

        @pl.when(goal < level)
        def downward():
            @pl.when(level < last)
            def joined():
                fall(goal).wait_recv()
                add_rows(sums.at[goal], (mine, crossed.at[goal], falling.at[goal]), row_count)

            @pl.when(level == last)
            def first():
                add_rows(sums.at[goal], (mine, crossed.at[goal]), row_count)

            fall(goal).start()

        @pl.when(goal == level)
        def here_at_last():
            @pl.when(level > 0)
            def from_below():
                rise(goal).wait_recv()

            @pl.when(level < last)
            def from_above():
                fall(goal).wait_recv()

            @pl.when(level == 0)
            def bottom():
                add_rows(total, (mine, crossed.at[goal], falling.at[goal]), row_count)

            @pl.when(level == last)
            def top():
                add_rows(total, (mine, crossed.at[goal], rising.at[goal]), row_count)

            @pl.when((level > 0) & (level < last))
            def between():
                add_rows(
                    total,
                    (mine, crossed.at[goal], rising.at[goal], falling.at[goal]),
                    row_count,
                )

    for goal in range(last + 1):
        cross(goal).wait_send()

        @pl.when(goal != level)
        def sent():
            rise(goal).wait_send()


def scatter_kernel(ctx_count, part, small, total, small_in, *refs):
    greet_all(ctx_count)
    here = lax.axis_index("ctx")
    starts, waits = spread(
        lambda peer: small.at[peer], lambda source: small_in.at[source], refs[9:11], ctx_count
    )
    for copy in starts:
        copy.start()
    small_in[here] = small[here]
    for step in scatter_turns(ctx_count // 2 - 1, part, total, *refs[:9]):
        pass
    for copy in waits:
        copy.wait_recv()
    for copy in starts:
        copy.wait_send()


def line_scatter_kernel(last, part, total, *refs):
    here, level, line, side = line_place()
    greet_line(last, here, level, side)
    for step in scatter_turns(last, part, total, *refs):
        pass


def line_scatter(ctx_count, call_id, part, small=None):
    rows, width = part.shape[1:]
    half = ctx_count // 2
    dma = pltpu.SemaphoreType.DMA((half,))
    spread_dma = pltpu.SemaphoreType.DMA((ctx_count,))
    slots = pltpu.VMEM((half, rows, width), part.dtype)
    total = jax.ShapeDtypeStruct((rows, width), jnp.float32)
    params = pltpu.CompilerParams(
        collective_id=call_id, has_side_effects=True, vmem_limit_bytes=40 * 2**20
    )
    if small is None:
        return pl.pallas_call(
            functools.partial(line_scatter_kernel, half - 1),
            out_shape=total,
            in_specs=[VMEM],
            out_specs=VMEM,
            scratch_shapes=[slots] * 4 + [dma] * 5,
            compiler_params=params,
            name="line_scatter",
        )(part)
    return pl.pallas_call(
        functools.partial(scatter_kernel, ctx_count),
        out_shape=[total, jax.ShapeDtypeStruct(small.shape, small.dtype)],
        in_specs=[VMEM] * 2,
        out_specs=[VMEM] * 2,
        scratch_shapes=[slots] * 4 + [dma] * 5 + [spread_dma] * 2,
        compiler_params=params,
        name="line_scatter",
    )(part, small)


def fsdp_place():
    here = lax.axis_index("fsdp")
    beside = here + 1 - 2 * (here % 2)
    return here, beside, (here + 2) % 4, (beside + 2) % 4


def greet_all(ctx_count):
    barrier = pltpu.get_barrier_semaphore()
    here = lax.axis_index("ctx")
    group = lax.axis_index("fsdp")
    for k in range(1, ctx_count):
        pl.semaphore_signal(
            barrier, inc=1, device_id={"ctx": (here + k) % ctx_count}, device_id_type=MESH
        )
    for k in range(1, 4):
        pl.semaphore_signal(barrier, inc=1, device_id={"fsdp": (group + k) % 4}, device_id_type=MESH)
    pl.semaphore_wait(barrier, ctx_count + 2)


def share_start(blocks, sems, own=None):
    send_sem, recv_sem = sems
    here, beside, across, corner = fsdp_place()
    source = blocks.at[here] if own is None else own
    for way, target in ((0, across), (1, beside)):
        remote(source, blocks.at[here], send_sem.at[way], recv_sem.at[here], fsdp=target).start()


def share_step(blocks, sems):
    send_sem, recv_sem = sems
    here, beside, across, corner = fsdp_place()
    copy = remote(
        blocks.at[across], blocks.at[across], send_sem.at[2], recv_sem.at[across], fsdp=beside
    )
    copy.wait_recv()
    copy.start()


def share_finish(blocks, sems):
    send_sem, recv_sem = sems
    here, beside, across, corner = fsdp_place()
    for way, block in ((0, beside), (1, corner)):
        copy = remote(
            blocks.at[block], blocks.at[block], send_sem.at[way], recv_sem.at[block], fsdp=beside
        )
        copy.wait_recv()
        copy.wait_send()
    remote(
        blocks.at[here], blocks.at[here], send_sem.at[2], recv_sem.at[here], fsdp=beside
    ).wait_send()


def spread(pieces, landing, sems, ctx_count):
    send_sem, recv_sem = sems
    here = lax.axis_index("ctx")

    def copy(k, peer, source):
        return remote(pieces(peer), landing(source), send_sem.at[k], recv_sem.at[k], ctx=peer)

    starts = [copy(k, (here + k) % ctx_count, here) for k in range(1, ctx_count)]
    waits = [
        copy(k, (here + k) % ctx_count, (here + ctx_count - k) % ctx_count)
        for k in range(1, ctx_count)
    ]
    return starts, waits


def greet_near(last, here, level, side):
    barrier = pltpu.get_barrier_semaphore()
    group = lax.axis_index("fsdp")
    for k in range(1, 4):
        pl.semaphore_signal(barrier, inc=1, device_id={"fsdp": (group + k) % 4}, device_id_type=MESH)
    greet_line(last, here, level, side, 3)


def gather_kernel(last, shared_count, *refs):
    total = 1 + shared_count
    owns, rows, keep_sem = refs[:total], refs[total : 2 * total], refs[2 * total]
    refs = refs[2 * total + 1 :]
    place = line_place()
    here, level, line, side = place
    sems = [(refs[2 * i], refs[2 * i + 1]) for i in range(total)]
    group = lax.axis_index("fsdp")
    if shared_count:
        greet_near(last, here, level, side)
    else:
        greet_line(last, here, level, side)
    line_start(rows[0], owns[0], sems[0], place, last)
    for i in range(1, total):
        share_start(rows[i], sems[i], owns[i])
    keeps = [
        pltpu.make_async_copy(
            owns[i], rows[i].at[group if i else here], keep_sem.at[i]
        )
        for i in range(total)
    ]
    for copy in keeps:
        copy.start()
    for step in range(1, last + 1):
        line_step(rows[0], sems[0], place, last, step)
    for i in range(1, total):
        share_step(rows[i], sems[i])
    line_finish(rows[0], sems[0], place, last)
    for i in range(1, total):
        share_finish(rows[i], sems[i])
    for copy in keeps:
        copy.wait()


def line_gather(ctx_count, call_id, own, *shared):
    count = len(shared)
    dma = pltpu.SemaphoreType.DMA
    return pl.pallas_call(
        functools.partial(gather_kernel, ctx_count // 2 - 1, count),
        out_shape=[jax.ShapeDtypeStruct((ctx_count,) + own.shape, own.dtype)]
        + [jax.ShapeDtypeStruct((4,) + a.shape, a.dtype) for a in shared],
        in_specs=[VMEM] * (1 + count),
        out_specs=[ANY] * (1 + count),
        scratch_shapes=[dma((1 + count,)), dma((ctx_count, 3)), dma((ctx_count,))]
        + [dma((3,)), dma((4,))] * count,
        compiler_params=pltpu.CompilerParams(collective_id=call_id, has_side_effects=True),
        name="line_gather",
    )(own, *shared)


def opening_kernel(
    ctx_count,
    own,
    qkv_own,
    out_own,
    small_own,
    number_own,
    rows,
    qkv,
    out_pair,
    small,
    numbers,
    keep_sem,
    pair_send,
    pair_recv,
    row_send,
    row_recv,
    share_send,
    share_recv,
    *sems,
):
    last = ctx_count // 2 - 1
    place = line_place()
    here, level, line, side = place
    group, beside, across, corner = fsdp_place()
    sems = [(sems[2 * i], sems[2 * i + 1]) for i in range(5)]
    qkv_spread, small_spread, number_spread, out_share, small_share = sems
    row_sems = (row_send, row_recv)
    greet_all(ctx_count)
    qkv_start, qkv_wait = spread(
        lambda peer: qkv_own.at[peer], lambda source: qkv.at[group, source], qkv_spread, ctx_count
    )
    small_start, small_wait = spread(
        lambda peer: small_own, lambda source: small.at[group, source], small_spread, ctx_count
    )
    number_start, number_wait = spread(
        lambda peer: number_own, lambda source: numbers.at[source], number_spread, ctx_count
    )

    def piece_copy(way, owner, k, target, first=False):
        source = (here + ctx_count - k) % ctx_count
        return remote(
            qkv_own.at[here] if first else qkv.at[owner, source],
            qkv.at[owner, source],
            share_send.at[way, k],
            share_recv.at[owner, k],
            fsdp=target,
        )

    def piece_on(k):
        piece_copy(0, group, k, across, k == 0).start()
        piece_copy(1, group, k, beside, k == 0).start()

    for copy in small_start + number_start + qkv_start:
        copy.start()
    line_start(rows, own, row_sems, place, last)
    piece_on(0)
    pair = remote(
        out_own, out_pair.at[group, line], pair_send.at[0], pair_recv.at[0], ctx=side
    )
    pair.start()
    keeps = [
        pltpu.make_async_copy(source, target, keep_sem.at[i])
        for i, (source, target) in enumerate(
            (
                (qkv_own.at[here], qkv.at[group, here]),
                (out_own, out_pair.at[group, line]),
                (small_own, small.at[group, here]),
                (number_own, numbers.at[here]),
                (own, rows.at[here]),
            )
        )
    ]
    for copy in keeps:
        copy.start()
    for copy in small_wait:
        copy.wait_recv()
    keeps[2].wait()
    share_start(small, small_share)
    line_step(rows, row_sems, place, last, 1)
    for k in range(1, ctx_count):
        qkv_wait[k - 1].wait_recv()
        piece_on(k)
    remote(
        out_own, out_pair.at[group, 1 - line], pair_send.at[0], pair_recv.at[0], ctx=side
    ).wait_recv()
    keeps[1].wait()
    share_start(out_pair, out_share)
    line_step(rows, row_sems, place, last, 2)
    for k in range(ctx_count):
        piece_copy(0, across, k, across).wait_recv()
        piece_copy(2, across, k, beside).start()
    share_step(small, small_share)
    for step in range(3, last + 1):
        line_step(rows, row_sems, place, last, step)
    share_step(out_pair, out_share)
    line_finish(rows, row_sems, place, last)
    for copy in number_wait:
        copy.wait_recv()
    for copy in qkv_start + small_start + number_start:
        copy.wait_send()
    pair.wait_send()
    for k in range(ctx_count):
        piece_copy(1, beside, k, beside).wait_recv()
        piece_copy(2, corner, k, beside).wait_recv()
        for way in range(3):
            piece_copy(way, group, k, beside).wait_send()
    share_finish(small, small_share)
    share_finish(out_pair, out_share)
    for i in (0, 3, 4):
        keeps[i].wait()


def opening(ctx_count, call_id, own, qkv_own, out_own, small_own, number_own):
    def out(lead, array):
        return jax.ShapeDtypeStruct(lead + array.shape, array.dtype)

    dma = pltpu.SemaphoreType.DMA
    return pl.pallas_call(
        functools.partial(opening_kernel, ctx_count),
        out_shape=[
            out((ctx_count,), own),
            out((4,), qkv_own),
            out((4, 2), out_own),
            out((4, ctx_count), small_own),
            out((ctx_count,), number_own),
        ],
        in_specs=[VMEM] * 5,
        out_specs=[ANY] * 5,
        scratch_shapes=[
            dma((5,)),
            dma((1,)),
            dma((1,)),
            dma((ctx_count, 3)),
            dma((ctx_count,)),
            dma((3, ctx_count)),
            dma((4, ctx_count)),
        ]
        + [dma((ctx_count,))] * 6
        + [dma((3,)), dma((4,))] * 2,
        compiler_params=pltpu.CompilerParams(collective_id=call_id, has_side_effects=True),
        name="opening",
    )(own, qkv_own, out_own, small_own, number_own)


def group_reduce(blocks, beside_in, pair_sums, across_in, settled, sems):
    core_send, core_recv, far_send, far_recv = sems
    group, beside, across, corner = fsdp_place()
    rows = settled.shape[0]

    def core_copy(slot, block):
        return remote(
            blocks.at[block],
            beside_in.at[slot],
            core_send.at[slot],
            core_recv.at[slot],
            fsdp=beside,
        )

    far = remote(pair_sums.at[1], across_in, far_send.at[0], far_recv.at[0], fsdp=across)
    core_copy(1, corner).start()
    core_copy(0, beside).start()
    yield
    core_copy(1, corner).wait_recv()
    add_rows(pair_sums.at[1], (blocks.at[across], beside_in.at[1]), rows)
    far.start()
    core_copy(0, beside).wait_recv()
    add_rows(pair_sums.at[0], (blocks.at[group], beside_in.at[0]), rows)
    yield
    far.wait_recv()
    add_rows(settled, (pair_sums.at[0], across_in), rows)
    yield
    core_copy(1, corner).wait_send()
    core_copy(0, beside).wait_send()
    far.wait_send()
    yield


def closing_kernel(ctx_count, part, weight, pair, plain, small, *refs):
    total, landed, pair_total, plain_total, small_total = refs[:5]
    line_slots, weight_slots, pair_slots, plain_slots = (
        refs[5:9],
        refs[9:13],
        refs[13:17],
        refs[17:20],
    )
    pair_in, small_in, small_sums, small_across = refs[20:24]
    sems = refs[24:]
    line_sems, weight_sems, pair_sems, plain_sems = sems[:5], sems[5:9], sems[9:13], sems[13:17]
    keep_sem, half_send, half_recv = sems[17:20]
    weight_spread, small_spread, (group_send, group_recv) = sems[20:22], sems[22:24], sems[24:26]
    here, level, line, side = line_place()
    group = lax.axis_index("fsdp")
    greet_all(ctx_count)
    turns = scatter_turns(ctx_count // 2 - 1, part, total, *line_slots, *line_sems)
    settled, pair_settled = weight_slots[3], pair_slots[3]
    weight_steps = group_reduce(weight, *weight_slots, weight_sems)
    pair_steps = group_reduce(pair, *pair_slots, pair_sems)
    plain_steps = group_reduce(plain, *plain_slots, plain_total, plain_sems)
    small_start, small_wait = spread(
        lambda peer: small.at[:, peer], lambda source: small_in.at[source], small_spread, ctx_count
    )
    for copy in small_start:
        copy.start()
    next(weight_steps)
    next(turns)
    next(weight_steps)
    next(pair_steps)
    next(turns)
    next(pair_steps)
    next(plain_steps)
    for copy in small_wait:
        copy.wait_recv()
    small_sum = small[:, here]
    for k in range(1, ctx_count):
        small_sum = small_sum + small_in[(here + k) % ctx_count]
    small_sums[...] = small_sum
    group_copies = [
        remote(
            small_sums.at[(group + k) % 4],
            small_across.at[k],
            group_send.at[k],
            group_recv.at[k],
            fsdp=(group + k) % 4,
        )
        for k in range(1, 4)
    ]
    for copy in group_copies:
        copy.start()
    next(weight_steps)
    piece = settled.shape[0] // ctx_count
    weight_start, weight_wait = spread(
        lambda peer: settled.at[pl.ds(pl.multiple_of(peer * piece, piece), piece)],
        lambda source: landed.at[source],
        weight_spread,
        ctx_count,
    )
    for copy in weight_start:
        copy.start()
    keep = pltpu.make_async_copy(
        settled.at[pl.ds(pl.multiple_of(here * piece, piece), piece)],
        landed.at[here],
        keep_sem.at[0],
    )
    keep.start()
    next(plain_steps)
    next(turns)
    next(pair_steps)
    half = pair_total.shape[0]
    half_copy = remote(
        pair_settled.at[pl.ds(pl.multiple_of((1 - line) * half, half), half)],
        pair_in,
        half_send.at[0],
        half_recv.at[0],
        ctx=side,
    )
    half_copy.start()
    for copy in group_copies:
        copy.wait_recv()
    small_total[...] = small_sums[group] + small_across[1] + small_across[2] + small_across[3]
    for step in turns:
        pass
    next(plain_steps)
    half_copy.wait_recv()
    kept = pair_settled.at[pl.ds(pl.multiple_of(line * half, half), half)]
    add_rows(pair_total, (kept, pair_in), half)
    for copy in weight_wait:
        copy.wait_recv()
    for copy in weight_start + small_start + group_copies:
        copy.wait_send()
    half_copy.wait_send()
    next(weight_steps)
    next(pair_steps)
    next(plain_steps)
    keep.wait()


def closing(ctx_count, call_id, part, weight, pair, plain, small):
    rows, width = part.shape[1:]
    half = ctx_count // 2
    dma = pltpu.SemaphoreType.DMA
    slots = pltpu.VMEM((half, rows, width), part.dtype)

    def group_slots(array):
        one = pltpu.VMEM(array.shape[1:], array.dtype)
        two = pltpu.VMEM((2,) + array.shape[1:], array.dtype)
        return [two, two, one, one]

    block, columns = weight.shape[1:]
    pair_half = (pair.shape[1] // 2, pair.shape[2])
    return pl.pallas_call(
        functools.partial(closing_kernel, ctx_count),
        out_shape=[
            jax.ShapeDtypeStruct((rows, width), jnp.float32),
            jax.ShapeDtypeStruct((ctx_count, block // ctx_count, columns), weight.dtype),
            jax.ShapeDtypeStruct(pair_half, jnp.float32),
            jax.ShapeDtypeStruct(plain.shape[1:], jnp.float32),
            jax.ShapeDtypeStruct(small.shape[2:], small.dtype),
        ],
        in_specs=[VMEM] * 5,
        out_specs=[VMEM] * 5,
        scratch_shapes=[slots] * 4
        + group_slots(weight)
        + group_slots(pair)
        + group_slots(plain)[:3]
        + [
            pltpu.VMEM(pair_half, pair.dtype),
            pltpu.VMEM((ctx_count, 4) + small.shape[2:], small.dtype),
            pltpu.VMEM((4,) + small.shape[2:], small.dtype),
            pltpu.VMEM((4,) + small.shape[2:], small.dtype),
        ]
        + [dma((half,))] * 5
        + [dma((2,)), dma((2,)), dma((1,)), dma((1,))] * 3
        + [dma((1,))] * 3
        + [dma((ctx_count,))] * 4
        + [dma((4,))] * 2,
        compiler_params=pltpu.CompilerParams(
            collective_id=call_id, has_side_effects=True, vmem_limit_bytes=56 * 2**20
        ),
        name="closing",
    )(part, weight, pair, plain, small)


SPAN = 256


def flat_dot(left, right):
    return lax.dot_general(left, right, (((1,), (0,)), ((), ())), preferred_element_type=jnp.float32)


def turned_dot(left, right):
    return lax.dot_general(left, right, (((1,), (1,)), ((), ())), preferred_element_type=jnp.float32)


def span_of(index, size=SPAN):
    return pl.ds(pl.multiple_of(index * size, size), size)


def scaled_rows(values):
    return values * lax.rsqrt(jnp.mean(values * values, axis=-1, keepdims=True) + EPSILON)


def attend_kernel(
    inputs,
    gain,
    weight,
    bias,
    cosine,
    sine,
    columns,
    lines,
    out_weight,
    normed,
    queries,
    keys,
    values,
    attended,
    log_totals,
    part,
):
    rows = inputs.shape[0]
    low = jnp.bfloat16
    heads = queries.shape[1] // HD

    @pl.loop(0, rows // SPAN)
    def project(index):
        here = span_of(index)
        unit = scaled_rows(inputs[here, :].astype(jnp.float32)) * gain[...]
        normed[here, :] = unit.astype(low)
        projected = flat_dot(normed[here, :], weight[...]) + bias[...]
        turn, tilt = cosine[here, :], sine[here, :]
        for head in range(heads):
            own = slice(head * HD, (head + 1) * HD)
            query = projected[:, own]
            query = query * turn + pltpu.roll(query, HD // 2, 1) * tilt
            queries[here, own] = (query * HD ** (-0.5)).astype(low)
            key = projected[:, (heads + head) * HD : (heads + head + 1) * HD]
            keys[here, own] = (key * turn + pltpu.roll(key, HD // 2, 1) * tilt).astype(low)
            values[here, own] = projected[
                :, (2 * heads + head) * HD : (2 * heads + head + 1) * HD
            ].astype(low)

    @pl.loop(0, rows // SPAN)
    def attend(index):
        here = span_of(index)
        position, segment = columns[here, 0:1], columns[here, 1:2]
        allowed = (lines[1:2, :] == segment) & (lines[0:1, :] <= position)
        allowed = allowed | (lines[0:1, :] == position)
        for head in range(heads):
            own = slice(head * HD, (head + 1) * HD)
            scores = turned_dot(queries[here, own], keys[:, own])
            scores = jnp.where(allowed, scores, -1e30)
            highest = jnp.max(scores, axis=1, keepdims=True)
            weights = jnp.exp(scores - highest)
            sums = jnp.sum(weights, axis=1, keepdims=True)
            log_totals[here, head : head + 1] = highest + jnp.log(sums)
            probs = (weights * (1.0 / sums)).astype(low)
            attended[here, own] = flat_dot(probs, values[:, own]).astype(low)
        part[here, :] = flat_dot(attended[here, :], out_weight[...]).astype(low)


def attend(inputs, gain, weight, bias, cosine, sine, columns, lines, out_weight):
    rows, width = inputs.shape
    wide = out_weight.shape[0]
    low = jnp.bfloat16
    shape = jax.ShapeDtypeStruct
    return pl.pallas_call(
        attend_kernel,
        out_shape=[shape((rows, width), low)]
        + [shape((rows, wide), low)] * 4
        + [shape((rows, wide // HD), jnp.float32), shape((rows, width), low)],
        in_specs=[VMEM] * 9,
        out_specs=[VMEM] * 7,
        compiler_params=pltpu.CompilerParams(vmem_limit_bytes=40 * 2**20),
        cost_estimate=pl.CostEstimate(
            flops=2 * rows * width * 4 * wide + 4 * rows * rows * wide,
            bytes_accessed=20 * 2**20,
            transcendentals=rows * rows * wide // HD,
        ),
        name="attend",
    )(inputs, gain, weight, bias, cosine, sine, columns, lines, out_weight)


def attend_back_kernel(
    branch,
    out_weight,
    queries,
    keys,
    values,
    attended,
    totals,
    cosine,
    sine,
    columns,
    lines,
    inputs,
    normed,
    weight,
    part,
    grad_weight,
    grad_out,
    grad_bias,
    grad_gain,
    grads,
    grad_attended,
    grad_keys,
    grad_values,
    gain_sum,
):
    rows, width = branch.shape
    low = jnp.bfloat16
    full = jnp.float32
    wide = queries.shape[1]
    heads = wide // HD

    @pl.loop(0, rows // SPAN)
    def into_heads(index):
        here = span_of(index)
        grad_attended[here, :] = turned_dot(branch[here, :], out_weight[...]).astype(low)

    for head in range(heads):
        own = slice(head * HD, (head + 1) * HD)
        grad_keys[...] = jnp.zeros_like(grad_keys)
        grad_values[...] = jnp.zeros_like(grad_values)

        @pl.loop(0, rows // SPAN)
        def scores_back(index):
            here = span_of(index)
            position, segment = lines[0:1, here], lines[1:2, here]
            allowed = (columns[:, 1:2] == segment) & (columns[:, 0:1] <= position)
            allowed = allowed | (columns[:, 0:1] == position)
            query, grad = queries[here, own], grad_attended[here, own]
            scores = jnp.where(allowed, turned_dot(keys[:, own], query), -1e30)
            probs = jnp.exp(scores - totals[head : head + 1, here])
            grad_probs = turned_dot(values[:, own], grad)
            delta = jnp.sum(probs * grad_probs, axis=0, keepdims=True)
            grad_scores = (probs * (grad_probs - delta)).astype(low)
            grad_keys[...] += flat_dot(grad_scores, query)
            grad_values[...] += flat_dot(probs.astype(low), grad)
            grad_query = flat_dot(grad_scores.T, keys[:, own]) * HD ** (-0.5)
            grads[here, own] = (
                grad_query * cosine[here, :] + pltpu.roll(grad_query * sine[here, :], HD // 2, 1)
            ).astype(low)

        @pl.loop(0, rows // SPAN)
        def keys_back(index):
            here = span_of(index)
            grad_key = grad_keys[here, :]
            grads[here, (heads + head) * HD : (heads + head + 1) * HD] = (
                grad_key * cosine[here, :] + pltpu.roll(grad_key * sine[here, :], HD // 2, 1)
            ).astype(low)
            grads[here, (2 * heads + head) * HD : (2 * heads + head + 1) * HD] = grad_values[
                here, :
            ].astype(low)

    gain_sum[...] = jnp.zeros_like(gain_sum)
    grad_bias[...] = jnp.zeros_like(grad_bias)

    @pl.loop(0, rows // SPAN)
    def project_back(index):
        here = span_of(index)
        grad_rows = turned_dot(grads[here, :], weight[...])
        part[here, :] = grad_rows.astype(low)
        unit = scaled_rows(inputs[here, :].astype(full))
        gain_sum[...] += jnp.sum(grad_rows * unit, axis=0, keepdims=True)
        grad_bias[...] += jnp.sum(grads[here, :].astype(full), axis=0, keepdims=True)

    grad_gain[...] = gain_sum[...]

    @pl.loop(0, width // SPAN)
    def weight_back(index):
        here = span_of(index)
        grad_weight[here, :] = flat_dot(normed[:, here].T, grads[...]).astype(low)

    attended_turned = attended[...].T

    @pl.loop(0, width // (2 * SPAN))
    def out_back(index):
        here = span_of(index, 2 * SPAN)
        grad_out[:, here] = flat_dot(attended_turned, branch[:, here]).astype(low)


def attend_back(
    branch,
    out_weight,
    queries,
    keys,
    values,
    attended,
    totals,
    cosine,
    sine,
    columns,
    lines,
    inputs,
    normed,
    weight,
):
    rows, width = branch.shape
    wide = out_weight.shape[0]
    low = jnp.bfloat16
    full = jnp.float32
    shape = jax.ShapeDtypeStruct
    return pl.pallas_call(
        attend_back_kernel,
        out_shape=[
            shape((rows, width), low),
            shape(weight.shape, low),
            shape((wide, width), low),
            shape((1, 3 * wide), full),
            shape((1, width), full),
        ],
        in_specs=[VMEM] * 14,
        out_specs=[VMEM] * 5,
        scratch_shapes=[
            pltpu.VMEM((rows, 3 * wide), low),
            pltpu.VMEM((rows, wide), low),
            pltpu.VMEM((rows, HD), full),
            pltpu.VMEM((rows, HD), full),
            pltpu.VMEM((1, width), full),
        ],
        compiler_params=pltpu.CompilerParams(vmem_limit_bytes=56 * 2**20),
        cost_estimate=pl.CostEstimate(
            flops=2 * rows * width * 8 * wide + 10 * rows * rows * wide,
            bytes_accessed=35 * 2**20,
            transcendentals=rows * rows * wide // HD,
        ),
        name="attend_back",
    )(
        branch,
        out_weight,
        queries,
        keys,
        values,
        attended,
        totals,
        cosine,
        sine,
        columns,
        lines,
        inputs,
        normed,
        weight,
    )


def deal_kernel(pieces, weight, dealt):
    ctx_count = dealt.shape[0]
    width = dealt.shape[2] // pieces
    for c in range(ctx_count):
        dealt[c] = jnp.concatenate(
            [
                weight[:, (q * ctx_count + c) * width : (q * ctx_count + c + 1) * width]
                for q in range(pieces)
            ],
            axis=1,
        )


def deal_columns(weight, ctx_count, pieces):
    rows, columns = weight.shape
    return pl.pallas_call(
        functools.partial(deal_kernel, pieces),
        out_shape=jax.ShapeDtypeStruct((ctx_count, rows, columns // ctx_count), weight.dtype),
        name="deal_columns",
    )(weight)


def collect_kernel(pieces, dealt, whole):
    ctx_count = dealt.shape[0]
    width = dealt.shape[2] // pieces
    whole[...] = jnp.concatenate(
        [
            dealt[c, :, q * width : (q + 1) * width]
            for q in range(pieces)
            for c in range(ctx_count)
        ],
        axis=1,
    ).astype(whole.dtype)


def collect_columns(dealt, pieces):
    ctx_count, rows, columns = dealt.shape
    return pl.pallas_call(
        functools.partial(collect_kernel, pieces),
        out_shape=jax.ShapeDtypeStruct((rows, columns * ctx_count), jnp.float32),
        name="collect_columns",
    )(dealt)


def heads_kernel(order, dealt, whole):
    pairs = dealt.shape[0] * 2
    for place, head in enumerate(order):
        for which in range(3):
            column = (which * 2 + place % 2) * HD
            target = (which * pairs + head) * HD
            whole[:, target : target + HD] = dealt[
                place // 2, :, column : column + HD
            ].astype(whole.dtype)


def collect_heads(dealt, order):
    ctx_count, rows, columns = dealt.shape
    return pl.pallas_call(
        functools.partial(heads_kernel, order),
        out_shape=jax.ShapeDtypeStruct((rows, columns * ctx_count), jnp.float32),
        name="collect_heads",
    )(dealt)


def over(axis, array, dim=0):
    return lax.all_gather(array, axis, axis=dim, tiled=True)


def reduce_over(axis, array, dim=0):
    return lax.psum_scatter(array, axis, scatter_dimension=dim, tiled=True)


def exchange(array):
    return lax.all_to_all(array, "ctx", split_axis=0, concat_axis=0, tiled=True)


def transposed_dot(left, right):
    return lax.dot_general(
        left, right, (((0,), (0,)), ((), ())), preferred_element_type=jnp.float32
    )


def dot_transposed(left, right):
    return lax.dot_general(
        left, right, (((1,), (1,)), ((), ())), preferred_element_type=jnp.float32
    )


def split_plan(
    hidden_in,
    segments,
    block_pairs,
    routes,
    out_grad,
    norm_gain_attn,
    qkv_weight,
    qkv_bias,
    out_weight,
    norm_gain_ffn,
    router_weight,
    shared_gate_weight,
    shared_in_weight,
    shared_out_weight,
    expert_in_weight,
    expert_out_weight,
):
    low = jnp.bfloat16
    full = jnp.float32
    tokens_dev, width = hidden_in.shape[1:]
    block_len = tokens_dev // 2
    ctx_count = lax.axis_size("ctx")
    fsdp_count = lax.axis_size("fsdp")
    ctx_rank = lax.axis_index("ctx")
    dev_count = ctx_count * fsdp_count
    row_len = ctx_count * tokens_dev
    early = width * 3 // 8
    head_count = width // HD
    shard = qkv_weight.shape[0]
    expert_count = router_weight.shape[1]
    shared_shard = shared_out_weight.shape[0]
    shared_width = fsdp_count * shared_shard
    expert_width = expert_out_weight.shape[1] * fsdp_count
    pair_rank = ctx_rank // 2
    side = ctx_rank % 2
    pairs = ctx_count // 2
    head_order = [j + (p * 2 + t) * pairs for j in range(pairs) for p in range(2) for t in range(2)]

    small = jnp.concatenate(
        [
            norm_gain_attn,
            norm_gain_ffn,
            shared_gate_weight,
            router_weight.T.reshape(-1),
            qkv_bias,
        ]
    )
    small_count = small.shape[0]
    small = jnp.pad(small, (0, 16 * HD - small_count)).reshape(16, HD)
    own_numbers = jnp.concatenate(
        [routes.reshape(tokens_dev, -1).T, segments.reshape(1, tokens_dev)], axis=0
    )
    number_count = own_numbers.shape[0]
    own_numbers = jnp.pad(own_numbers, ((0, 8 - number_count), (0, 0)))
    qkv_parts = (
        qkv_weight.reshape(shard, 3, head_count, HD)[:, :, jnp.array(head_order)]
        .reshape(shard, 3, ctx_count, 2 * HD)
        .transpose(2, 0, 1, 3)
        .reshape(ctx_count, shard, 6 * HD)
    )
    own_inputs = hidden_in.reshape(tokens_dev, width)
    row_inputs, qkv_c, out_pair, small_all, numbers = opening(
        ctx_count, 1, own_inputs, qkv_parts, out_weight, small, own_numbers
    )
    qkv_c = qkv_c.reshape(width, 6 * HD)
    out_c = lax.dynamic_index_in_dim(
        out_pair.reshape(2, 2 * HD, width), side, 0, keepdims=False
    )
    small_all = small_all.reshape(dev_count, 16 * HD)
    gain_attn = small_all[:, :shard].reshape(width).astype(full)
    gain_ffn = small_all[:, shard : 2 * shard].reshape(width).astype(full)
    gate_full = small_all[:, 2 * shard : 3 * shard].reshape(width)
    router_t = (
        small_all[:, 3 * shard : (3 + expert_count) * shard]
        .reshape(dev_count, expert_count, shard)
        .transpose(1, 0, 2)
        .reshape(expert_count, width)
    )
    bias_full = small_all[:, (3 + expert_count) * shard : small_count].reshape(3, head_count, HD)
    router_gate = jnp.concatenate([router_t, gate_full[None, :]], axis=0)
    row_seg = numbers[:, number_count - 1].reshape(row_len)
    routed_here = jnp.any(numbers[:, : number_count - 1] == ctx_rank, axis=1).reshape(row_len)

    shared_in_weight, numbers = lax.optimization_barrier((shared_in_weight, numbers))
    early_upstream = over("ctx", out_grad.reshape(tokens_dev, width)[:, :early])
    inner_parts = deal_columns(shared_in_weight, ctx_count, 2 * fsdp_count)
    expert_inner = over("fsdp", expert_in_weight[0])
    expert_outer = over("fsdp", expert_out_weight[0])
    inner_parts = exchange(inner_parts)
    my_heads = [pair_rank + (side * 2 + t) * pairs for t in range(2)]
    bias_c = jnp.concatenate(
        [lax.dynamic_index_in_dim(bias_full, h, 1, keepdims=False) for h in my_heads], axis=1
    ).reshape(6 * HD)

    offsets = jnp.arange(block_len, dtype=jnp.int32)
    positions = (block_pairs[:, None] * block_len + offsets[None, :]).reshape(row_len)
    inputs = own_inputs.astype(full)
    row_inputs = row_inputs.reshape(row_len, width)
    half_len = HD // 2
    frequency = THETA ** (-jnp.arange(half_len, dtype=full) / half_len)
    places = positions.astype(full)
    angles = places[:, None] * frequency[None, :]
    cosine, sine = jnp.cos(angles), jnp.sin(angles)
    cosine = jnp.concatenate([cosine, cosine], axis=1)
    sine = jnp.concatenate([-sine, sine], axis=1)
    key_seg = row_seg.astype(full)
    query_seg = jnp.where(row_seg >= 0, key_seg, -2.0)
    query_marks = jnp.stack([places, query_seg])
    key_marks = jnp.stack([places, key_seg])
    row_normed, queries, keys, values, attended_row, log_totals, branch_part = attend(
        row_inputs,
        gain_attn[None, :],
        qkv_c,
        bias_c.astype(full)[None, :],
        cosine,
        sine,
        query_marks.T,
        key_marks,
        out_c,
    )
    branch_part, inner_parts, early_upstream = lax.optimization_barrier(
        (branch_part, inner_parts, early_upstream)
    )
    branch = line_scatter(ctx_count, 2, branch_part.reshape(ctx_count, tokens_dev, width))
    middle = inputs + branch
    normed_ffn = rms_scale(middle, gain_ffn).astype(low)

    row_ffn, inner_c, outer_c = line_gather(
        ctx_count,
        4,
        normed_ffn,
        inner_parts.reshape(ctx_count * shard, 2 * shared_width),
        shared_out_weight,
    )
    row_ffn = row_ffn.reshape(row_len, width)
    row_ffn, late_grad = lax.optimization_barrier((row_ffn, out_grad))
    late_upstream = over("ctx", late_grad.reshape(tokens_dev, width)[:, early:])
    inner_c = inner_c.reshape(width, 2 * shared_width)
    outer_c = outer_c.reshape(shared_width, width)
    row_logits = dot_transposed(row_ffn, router_gate)
    row_probs = jax.nn.softmax(row_logits[:, :expert_count], axis=-1)
    expert_ids = jnp.arange(expert_count, dtype=jnp.int32)
    here = jnp.where(
        routed_here, jnp.sum(jnp.where(expert_ids[None, :] == ctx_rank, row_probs, 0.0), axis=1), 0.0
    )
    row_gate = jax.nn.sigmoid(row_logits[:, expert_count])
    expert_gu = matmul_low(row_ffn, expert_inner)
    expert_hidden = swiglu_mix(expert_gu, expert_width).astype(low)
    expert_result = matmul_low(expert_hidden, expert_outer).astype(low).astype(full)
    row_shared, expert_result = lax.optimization_barrier((row_ffn, expert_result))
    shared_gu = matmul_low(row_shared, inner_c)
    shared_hidden = swiglu_mix(shared_gu, shared_width).astype(low)
    shared_out = matmul_low(shared_hidden, outer_c)
    shared_out, late_upstream = lax.optimization_barrier((shared_out, late_upstream))
    upstream_row = jnp.concatenate([early_upstream, late_upstream], axis=1).astype(full)
    out_part = (row_gate[:, None] * shared_out + here[:, None] * expert_result).astype(low)
    gate_dot = jnp.sum(upstream_row * shared_out, axis=1)
    expert_dot = jnp.where(routed_here, jnp.sum(upstream_row * expert_result, axis=1), 0.0)
    out_landed = reduce_over("ctx", out_part)

    upstream_row, out_part = lax.optimization_barrier((upstream_row, out_part))
    grad_buffers = (here[:, None] * upstream_row).astype(low)
    sum_expert_outer = reduce_over("fsdp", transposed_dot(expert_hidden, grad_buffers).astype(low))
    grad_expert_hidden = dot_transposed(grad_buffers, expert_outer)
    unused_mix, expert_pull = jax.vjp(
        functools.partial(swiglu_mix, hidden_width=expert_width), expert_gu
    )
    grad_expert_gu = expert_pull(grad_expert_hidden)[0].astype(low)
    grad_rows = dot_transposed(grad_expert_gu, expert_inner).astype(low)
    upstream_row, grad_rows = lax.optimization_barrier((upstream_row, grad_rows))
    grad_shared_out = (row_gate[:, None] * upstream_row).astype(low)
    grad_hidden = dot_transposed(grad_shared_out, outer_c)
    unused_mix, mix_pull = jax.vjp(
        functools.partial(swiglu_mix, hidden_width=shared_width), shared_gu
    )
    grad_shared_gu = mix_pull(grad_hidden)[0].astype(low)
    grad_inner = transposed_dot(row_ffn, grad_shared_gu).astype(low)
    sum_inner_c = reduce_over("fsdp", grad_inner)
    grad_outer = transposed_dot(shared_hidden, grad_shared_out).astype(low)
    grad_ffn_part = (
        dot_transposed(grad_shared_gu, inner_c) + grad_rows.astype(full)
    ).astype(low)
    grad_expert_gu, grad_ffn_part, grad_inner = lax.optimization_barrier(
        (grad_expert_gu, grad_ffn_part, grad_inner)
    )
    grad_expert_inner = transposed_dot(row_ffn, grad_expert_gu).astype(low)
    dots = jnp.stack([gate_dot, expert_dot]).reshape(2, ctx_count, tokens_dev).transpose(1, 0, 2)
    grad_ffn_part, grad_expert_inner, grad_outer = lax.optimization_barrier(
        (grad_ffn_part, grad_expert_inner, grad_outer)
    )
    sum_expert_inner = reduce_over("fsdp", grad_expert_inner)
    grad_normed, own_dots = line_scatter(
        ctx_count,
        6,
        grad_ffn_part.reshape(ctx_count, tokens_dev, width),
        jnp.pad(dots, ((0, 0), (0, 6), (0, 0))),
    )
    hidden_out = (middle + out_landed.astype(full)).astype(low).reshape(1, tokens_dev, width)

    own_logits = dot_transposed(normed_ffn, router_gate)
    router_probs = jax.nn.softmax(own_logits[:, :expert_count], axis=-1)
    gate_value = jax.nn.sigmoid(own_logits[:, expert_count])
    grad_gate_logit = gate_value * (1.0 - gate_value) * jnp.sum(own_dots[:, 0], axis=0)
    grad_choice = own_dots[:, 1].T
    grad_logits = router_probs * (
        grad_choice - jnp.sum(router_probs * grad_choice, axis=1, keepdims=True)
    )
    grad_small = jnp.concatenate([grad_logits, grad_gate_logit[:, None]], axis=1).astype(low)
    grad_router_gate = transposed_dot(grad_small, normed_ffn)
    grad_normed = grad_normed + matmul_low(grad_small, router_gate)
    unused_norm, norm_pull = jax.vjp(rms_scale, middle, gain_ffn)
    grad_middle_norm, grad_gain_ffn = norm_pull(grad_normed)
    grad_middle = out_grad.reshape(tokens_dev, width).astype(full) + grad_middle_norm

    grad_branch, sum_expert_outer, hidden_out = lax.optimization_barrier(
        (grad_middle.astype(low), sum_expert_outer, hidden_out)
    )
    (row_branch,) = line_gather(ctx_count, 3, grad_branch)
    row_branch, sum_inner_c = lax.optimization_barrier(
        (row_branch.reshape(row_len, width), sum_inner_c)
    )
    sum_inner = collect_columns(
        exchange(sum_inner_c.reshape(ctx_count, shard, 2 * shared_width)), 2 * fsdp_count
    )
    grad_attn_part, grad_qkv_c, grad_out_c, grad_bias_c, grad_gain_attn = attend_back(
        row_branch,
        out_c,
        queries,
        keys,
        values,
        attended_row,
        log_totals.T,
        cosine,
        sine,
        key_marks.T,
        query_marks,
        row_inputs,
        row_normed,
        qkv_c,
    )
    grad_out_c = grad_out_c.reshape(2, HD, width)
    padded_out = jnp.concatenate(
        [jnp.where(side == p, grad_out_c, jnp.zeros_like(grad_out_c)) for p in range(2)], axis=0
    )
    grad_attn_part, sum_inner = lax.optimization_barrier((grad_attn_part, sum_inner))
    grad_bias_c = grad_bias_c.reshape(3, 1, 2, HD)
    mine = (jnp.arange(ctx_count) == ctx_rank)[None, :, None, None]
    places_of = [head_order.index(h) for h in range(head_count)]
    grad_bias = (
        jnp.where(mine, grad_bias_c, 0.0)
        .reshape(3, head_count, HD)[:, jnp.array(places_of)]
        .reshape(dev_count, -1)
    )
    small_grads = jnp.concatenate(
        [
            grad_gain_attn.reshape(dev_count, shard),
            grad_gain_ffn.reshape(dev_count, shard),
            grad_router_gate.reshape(expert_count + 1, dev_count, shard)
            .transpose(1, 0, 2)
            .reshape(dev_count, (expert_count + 1) * shard),
            grad_bias,
        ],
        axis=1,
    )
    small_grads = jnp.pad(small_grads, ((0, 0), (0, 8 * HD - small_count)))
    grad_normed_attn, sum_qkv_c, sum_out, sum_outer, sums = closing(
        ctx_count,
        5,
        grad_attn_part.reshape(ctx_count, tokens_dev, width),
        grad_qkv_c.reshape(fsdp_count, ctx_count * shard, 6 * HD),
        padded_out,
        grad_outer.reshape(fsdp_count, shared_shard, width),
        small_grads.reshape(fsdp_count, ctx_count, 8, HD),
    )
    sums = sums.reshape(8 * HD)[:small_count]
    sum_qkv = collect_heads(sum_qkv_c, head_order)
    unused_norm, first_pull = jax.vjp(lambda v: rms_scale(v, gain_attn), inputs)
    input_grad = grad_middle + first_pull(grad_normed_attn)[0]
    sum_router = sums[2 * shard : (2 + expert_count) * shard].reshape(expert_count, shard).T
    return (
        hidden_out,
        input_grad.reshape(1, tokens_dev, width),
        sums[:shard],
        sum_qkv,
        sums[(3 + expert_count) * shard :],
        sum_out,
        sums[shard : 2 * shard],
        sum_router,
        sums[(2 + expert_count) * shard : (3 + expert_count) * shard],
        sum_inner,
        sum_outer,
        sum_expert_inner.astype(full)[None],
        sum_expert_outer.astype(full)[None],
    )


def local(*arrays):
    width = arrays[0].shape[2]
    ctx_count = lax.axis_size("ctx")
    shard = arrays[6].shape[0]
    fits = (
        width == 2 * ctx_count * HD
        and 2 * shard == HD
        and ctx_count % 2 == 0
        and lax.axis_size("fsdp") * ctx_count * shard == width
        and arrays[14].shape[0] == 1
    )
    return split_plan(*arrays) if fits else gathered_plan(*arrays)


def solution(mesh):
    in_specs = (
        P("fsdp", "ctx", None),
        P("fsdp", "ctx"),
        P(),
        P("fsdp", "ctx", None),
        P("fsdp", "ctx", None),
        P(("fsdp", "ctx")),
        P(("fsdp", "ctx"), None),
        P(("fsdp", "ctx")),
        P(("fsdp", "ctx"), None),
        P(("fsdp", "ctx")),
        P(("fsdp", "ctx"), None),
        P(("fsdp", "ctx")),
        P(("fsdp", "ctx"), None),
        P(("fsdp", "ctx"), None),
        P("ctx", "fsdp", None),
        P("ctx", "fsdp", None),
    )
    out_specs = (
        P("fsdp", "ctx", None),
        P("fsdp", "ctx", None),
        P(("fsdp", "ctx")),
        P(("fsdp", "ctx"), None),
        P(("fsdp", "ctx")),
        P(("fsdp", "ctx"), None),
        P(("fsdp", "ctx")),
        P(("fsdp", "ctx"), None),
        P(("fsdp", "ctx")),
        P(("fsdp", "ctx"), None),
        P(("fsdp", "ctx"), None),
        P("ctx", "fsdp", None),
        P("ctx", "fsdp", None),
    )
    return jax.shard_map(local, mesh=mesh, in_specs=in_specs, out_specs=out_specs, check_vma=False)
```

```python
import functools

import jax
import jax.numpy as jnp
from jax import lax
from jax.experimental import pallas as pl
from jax.experimental.pallas import tpu as pltpu
from jax.sharding import PartitionSpec as P

HD = 128


EPSILON = 1e-06
THETA = 1000000.0
heads_per_group = 4


def rms_scale(values, gain_vec):
    return (
        values * lax.rsqrt(jnp.mean(values * values, axis=-1, keepdims=True) + EPSILON) * gain_vec
    )


def rotate(values, positions):
    half_len = values.shape[-1] // 2
    frequency = THETA ** (-jnp.arange(half_len, dtype=jnp.float32) / half_len)
    angles = positions.astype(jnp.float32)[:, None] * frequency[None, :]
    cosine = jnp.cos(angles)[:, None, :]
    sine_part = jnp.sin(angles)[:, None, :]
    first_half = values[..., :half_len]
    second = values[..., half_len:]
    return jnp.concatenate(
        [first_half * cosine - second * sine_part, second * cosine + first_half * sine_part],
        axis=-1,
    )


def visible(query_pos, query_seg, key_pos, key_seg):
    same_doc = (key_seg[None, :] == query_seg[:, None]) & (query_seg[:, None] >= 0)
    causal = key_pos[None, :] <= query_pos[:, None]
    return same_doc & causal | (key_pos[None, :] == query_pos[:, None])


def swiglu_mix(gate_up, hidden_width):
    return jax.nn.silu(gate_up[..., :hidden_width]) * gate_up[..., hidden_width:]


def matmul_low(left, right):
    return jnp.dot(left, right, preferred_element_type=jnp.float32)


def gathered_plan(
    hidden_in,
    segments,
    block_pairs,
    routes,
    out_grad,
    norm_gain_attn,
    qkv_weight,
    qkv_bias,
    out_weight,
    norm_gain_ffn,
    router_weight,
    shared_gate_weight,
    shared_in_weight,
    shared_out_weight,
    expert_in_weight,
    expert_out_weight,
):
    tokens_dev = hidden_in.shape[1]
    model_width = hidden_in.shape[2]
    block_len = tokens_dev // 2
    inputs = hidden_in.reshape(tokens_dev, model_width).astype(jnp.float32)
    seg_local = segments.reshape(tokens_dev)
    token_routes = routes.reshape(tokens_dev, -1)
    top_count = token_routes.shape[1]
    ctx_count = lax.axis_size("ctx")
    ctx_rank = lax.axis_index("ctx")
    offsets = jnp.arange(block_len, dtype=jnp.int32)
    all_positions = (
        block_pairs.reshape(ctx_count, 2)[:, :, None] * block_len + offsets[None, None, :]
    ).reshape(ctx_count * tokens_dev)
    my_positions = lax.dynamic_slice_in_dim(all_positions, ctx_rank * tokens_dev, tokens_dev, 0)
    gathered = (
        lax.all_gather(norm_gain_attn, ("fsdp", "ctx"), axis=0, tiled=True),
        lax.all_gather(qkv_weight, ("fsdp", "ctx"), axis=0, tiled=True),
        lax.all_gather(qkv_bias, ("fsdp", "ctx"), axis=0, tiled=True),
        lax.all_gather(out_weight, ("fsdp", "ctx"), axis=0, tiled=True),
        lax.all_gather(norm_gain_ffn, ("fsdp", "ctx"), axis=0, tiled=True),
        lax.all_gather(router_weight, ("fsdp", "ctx"), axis=0, tiled=True),
        lax.all_gather(shared_gate_weight, ("fsdp", "ctx"), axis=0, tiled=True),
        lax.all_gather(shared_in_weight, ("fsdp", "ctx"), axis=0, tiled=True),
        lax.all_gather(shared_out_weight, ("fsdp", "ctx"), axis=0, tiled=True),
    )
    (
        gain_attn,
        qkv_full,
        shift_full,
        out_full,
        gain_ffn,
        router_full,
        gate_full,
        inner_full,
        outer_full,
    ) = gathered
    gain_attn = gain_attn.astype(jnp.float32)
    gain_ffn = gain_ffn.astype(jnp.float32)
    heads_width = out_full.shape[0]
    head_count = heads_width // HD
    group_width = heads_per_group * HD
    group_count = head_count // heads_per_group
    normed = rms_scale(inputs, gain_attn).astype(jnp.bfloat16)
    projected = matmul_low(normed, qkv_full) + shift_full.astype(jnp.float32)
    query_pre = projected[:, :heads_width].reshape(tokens_dev, head_count, HD)
    key_pre = projected[:, heads_width : 2 * heads_width].reshape(tokens_dev, head_count, HD)

    def place_heads(query_in, key_in):
        return (rotate(query_in, my_positions) * HD ** (-0.5), rotate(key_in, my_positions))

    query_rot, key_rot = place_heads(query_pre, key_pre)
    query_low = query_rot.reshape(tokens_dev, heads_width).astype(jnp.bfloat16)
    key_low = key_rot.reshape(tokens_dev, heads_width).astype(jnp.bfloat16)
    value_low = projected[:, 2 * heads_width :].astype(jnp.bfloat16)
    keys_all, values_all, segs_all = (
        lax.all_gather(key_low, "ctx", axis=0, tiled=True),
        lax.all_gather(value_low, "ctx", axis=0, tiled=True),
        lax.all_gather(seg_local.astype(jnp.bfloat16), "ctx", axis=0, tiled=True),
    )
    allowed = visible(
        my_positions, seg_local.astype(jnp.float32), all_positions, segs_all.astype(jnp.float32)
    )

    def head_slice(matrix, group_index):
        return lax.dynamic_slice_in_dim(matrix, group_index * group_width, group_width, 1).reshape(
            matrix.shape[0], heads_per_group, HD
        )

    def forward_group(group_index):
        query_part = head_slice(query_low, group_index)
        key_part = head_slice(keys_all, group_index)
        value_part = head_slice(values_all, group_index)
        scores = jnp.einsum(
            "qhd,khd->hqk", query_part, key_part, preferred_element_type=jnp.float32
        )
        scores = jnp.where(allowed[None], scores, -1e30)
        highest = jnp.max(scores, axis=-1, keepdims=True)
        log_total = highest + jnp.log(jnp.sum(jnp.exp(scores - highest), axis=-1, keepdims=True))
        weights = jnp.exp(scores - log_total).astype(jnp.bfloat16)
        mixed = jnp.einsum("hqk,khd->qhd", weights, value_part, preferred_element_type=jnp.float32)
        return (mixed, log_total[..., 0])

    mixed_groups, log_totals = lax.map(forward_group, jnp.arange(group_count, dtype=jnp.int32))
    attended = (
        jnp.moveaxis(mixed_groups, 0, 1).reshape(tokens_dev, heads_width).astype(jnp.bfloat16)
    )
    middle = inputs + matmul_low(attended, out_full)
    normed_ffn = rms_scale(middle, gain_ffn).astype(jnp.bfloat16)
    logits = matmul_low(normed_ffn, router_full)
    router_probs = jax.nn.softmax(logits, axis=-1)
    expert_count = logits.shape[1]
    expert_ids = jnp.arange(expert_count, dtype=jnp.int32)
    chosen = (token_routes[:, :, None] == expert_ids[None, None, :]).astype(jnp.float32)
    gate_weights = jnp.sum(chosen * router_probs[:, None, :], axis=-1)
    capacity = 2 * tokens_dev * top_count // expert_count
    local_experts = expert_in_weight.shape[0]
    assigned = tokens_dev * top_count
    flat_routes = token_routes.reshape(assigned)
    onehot = (flat_routes[:, None] == expert_ids[None, :]).astype(jnp.int32)
    earlier = jnp.cumsum(onehot, axis=0) - onehot
    places = flat_routes * capacity + jnp.sum(earlier * onehot, axis=1)
    slot_source = (
        jnp.full((expert_count * capacity,), assigned, jnp.int32)
        .at[places]
        .set(jnp.arange(assigned, dtype=jnp.int32))
    )
    slot_token = slot_source // top_count
    padded_rows = jnp.concatenate([normed_ffn, jnp.zeros((1, model_width), jnp.bfloat16)], axis=0)
    outgoing = padded_rows[slot_token].reshape(ctx_count, local_experts * capacity, model_width)
    expert_inner, expert_outer = (
        lax.all_gather(expert_in_weight, "fsdp", axis=1, tiled=True),
        lax.all_gather(expert_out_weight, "fsdp", axis=1, tiled=True),
    )
    landed_tokens = lax.all_to_all(outgoing, "ctx", split_axis=0, concat_axis=0, tiled=True)
    incoming = landed_tokens.reshape(ctx_count, local_experts, capacity, model_width)
    expert_gu = jnp.einsum(
        "necd,edf->necf", incoming, expert_inner, preferred_element_type=jnp.float32
    )
    expert_width = expert_outer.shape[1]
    expert_hidden = swiglu_mix(expert_gu, expert_width).astype(jnp.bfloat16)
    expert_result = jnp.einsum(
        "necf,efd->necd", expert_hidden, expert_outer, preferred_element_type=jnp.float32
    ).astype(jnp.bfloat16)
    returned = lax.all_to_all(
        expert_result.reshape(ctx_count, local_experts * capacity, model_width),
        "ctx",
        split_axis=0,
        concat_axis=0,
        tiled=True,
    )
    picked = (
        returned.reshape(expert_count * capacity, model_width)[places]
        .reshape(tokens_dev, top_count, model_width)
        .astype(jnp.float32)
    )
    routed = jnp.sum(gate_weights[:, :, None] * picked, axis=1)
    upstream = out_grad.reshape(tokens_dev, model_width).astype(jnp.float32)
    shared_gu = matmul_low(normed_ffn, inner_full)
    shared_width = outer_full.shape[0]
    shared_hidden = swiglu_mix(shared_gu, shared_width).astype(jnp.bfloat16)
    shared_out = matmul_low(shared_hidden, outer_full)
    gate_value = jax.nn.sigmoid(matmul_low(normed_ffn, gate_full))
    output = middle + gate_value[:, None] * shared_out + routed
    hidden_out = output.astype(jnp.bfloat16).reshape(1, tokens_dev, model_width)
    gain_ffn, router_full, gate_full, inner_full, outer_full = (
        lax.all_gather(norm_gain_ffn, ("fsdp", "ctx"), axis=0, tiled=True),
        lax.all_gather(router_weight, ("fsdp", "ctx"), axis=0, tiled=True),
        lax.all_gather(shared_gate_weight, ("fsdp", "ctx"), axis=0, tiled=True),
        lax.all_gather(shared_in_weight, ("fsdp", "ctx"), axis=0, tiled=True),
        lax.all_gather(shared_out_weight, ("fsdp", "ctx"), axis=0, tiled=True),
    )
    gain_ffn = gain_ffn.astype(jnp.float32)
    grad_shared_out = (gate_value[:, None] * upstream).astype(jnp.bfloat16)
    grad_outer = jnp.einsum(
        "tf,td->fd", shared_hidden, grad_shared_out, preferred_element_type=jnp.float32
    )
    grad_hidden = jnp.einsum(
        "td,fd->tf", grad_shared_out, outer_full, preferred_element_type=jnp.float32
    )
    unused_mix, mix_pull = jax.vjp(functools.partial(swiglu_mix, hidden_width=shared_width), shared_gu)
    grad_shared_gu = mix_pull(grad_hidden)[0].astype(jnp.bfloat16)
    grad_inner = jnp.einsum(
        "td,tf->df", normed_ffn, grad_shared_gu, preferred_element_type=jnp.float32
    )
    grad_normed = jnp.einsum(
        "tf,df->td", grad_shared_gu, inner_full, preferred_element_type=jnp.float32
    )
    grad_gate_logit = (
        gate_value * (1.0 - gate_value) * jnp.sum(upstream * shared_out, axis=1)
    ).astype(jnp.bfloat16)
    grad_gate_vec = jnp.einsum(
        "td,t->d", normed_ffn, grad_gate_logit, preferred_element_type=jnp.float32
    )
    grad_normed = (
        grad_normed
        + grad_gate_logit.astype(jnp.float32)[:, None] * gate_full.astype(jnp.float32)[None, :]
    )
    grad_gates = jnp.sum(upstream[:, None, :] * picked, axis=2)
    grad_choice_probs = jnp.sum(chosen * grad_gates[:, :, None], axis=1)
    grad_logits = (
        router_probs
        * (grad_choice_probs - jnp.sum(router_probs * grad_choice_probs, axis=1, keepdims=True))
    ).astype(jnp.bfloat16)
    grad_router = jnp.einsum(
        "td,te->de", normed_ffn, grad_logits, preferred_element_type=jnp.float32
    )
    grad_normed = grad_normed + jnp.einsum(
        "te,de->td", grad_logits, router_full, preferred_element_type=jnp.float32
    )
    grad_slots = (
        (gate_weights[:, :, None] * upstream[:, None, :])
        .astype(jnp.bfloat16)
        .reshape(assigned, model_width)
    )
    padded_grads = jnp.concatenate([grad_slots, jnp.zeros((1, model_width), jnp.bfloat16)], axis=0)
    grad_outgoing = padded_grads[slot_source].reshape(
        ctx_count, local_experts * capacity, model_width
    )
    grad_incoming = lax.all_to_all(
        grad_outgoing, "ctx", split_axis=0, concat_axis=0, tiled=True
    ).reshape(ctx_count, local_experts, capacity, model_width)
    grad_expert_hidden = jnp.einsum(
        "necd,efd->necf", grad_incoming, expert_outer, preferred_element_type=jnp.float32
    )
    grad_expert_outer = jnp.einsum(
        "necf,necd->efd", expert_hidden, grad_incoming, preferred_element_type=jnp.float32
    )
    unused_mix, expert_pull = jax.vjp(functools.partial(swiglu_mix, hidden_width=expert_width), expert_gu)
    grad_expert_gu = expert_pull(grad_expert_hidden)[0].astype(jnp.bfloat16)
    grad_expert_inner = jnp.einsum(
        "necd,necf->edf", incoming, grad_expert_gu, preferred_element_type=jnp.float32
    )
    grad_expert_rows = jnp.einsum(
        "necf,edf->necd", grad_expert_gu, expert_inner, preferred_element_type=jnp.float32
    ).astype(jnp.bfloat16)
    grad_returned = lax.all_to_all(
        grad_expert_rows.reshape(ctx_count, local_experts * capacity, model_width),
        "ctx",
        split_axis=0,
        concat_axis=0,
        tiled=True,
    )
    grad_picked = grad_returned.reshape(expert_count * capacity, model_width)[places].reshape(
        tokens_dev, top_count, model_width
    )
    grad_normed = grad_normed + jnp.sum(grad_picked.astype(jnp.float32), axis=1)
    sum_expert_inner, sum_expert_outer = (
        lax.psum_scatter(
            grad_expert_inner.astype(jnp.bfloat16), "fsdp", scatter_dimension=1, tiled=True
        ).astype(jnp.float32),
        lax.psum_scatter(
            grad_expert_outer.astype(jnp.bfloat16), "fsdp", scatter_dimension=1, tiled=True
        ).astype(jnp.float32),
    )
    unused_norm, norm_pull = jax.vjp(rms_scale, middle, gain_ffn)
    grad_middle_norm, grad_gain_ffn = norm_pull(grad_normed)
    grad_middle = upstream + grad_middle_norm
    sum_gain_ffn, sum_router, sum_gate_vec, sum_inner, sum_outer = (
        lax.psum_scatter(grad_gain_ffn, ("fsdp", "ctx"), scatter_dimension=0, tiled=True),
        lax.psum_scatter(grad_router, ("fsdp", "ctx"), scatter_dimension=0, tiled=True),
        lax.psum_scatter(grad_gate_vec, ("fsdp", "ctx"), scatter_dimension=0, tiled=True),
        lax.psum_scatter(grad_inner, ("fsdp", "ctx"), scatter_dimension=0, tiled=True),
        lax.psum_scatter(grad_outer, ("fsdp", "ctx"), scatter_dimension=0, tiled=True),
    )
    grad_branch = grad_middle.astype(jnp.bfloat16)
    grad_out_mat = jnp.einsum(
        "tc,td->cd", attended, grad_branch, preferred_element_type=jnp.float32
    )
    grad_attended = jnp.einsum(
        "td,cd->tc", grad_branch, out_full, preferred_element_type=jnp.float32
    ).astype(jnp.bfloat16)
    keys_again, values_again = (
        lax.all_gather(key_low, "ctx", axis=0, tiled=True),
        lax.all_gather(value_low, "ctx", axis=0, tiled=True),
    )

    def backward_group(group_index):
        query_part = head_slice(query_low, group_index)
        key_part = head_slice(keys_again, group_index)
        value_part = head_slice(values_again, group_index)
        grad_part = head_slice(grad_attended, group_index)
        log_total = lax.dynamic_index_in_dim(log_totals, group_index, 0, keepdims=False)
        scores = jnp.einsum(
            "qhd,khd->hqk", query_part, key_part, preferred_element_type=jnp.float32
        )
        scores = jnp.where(allowed[None], scores, -1e30)
        weights = jnp.exp(scores - log_total[..., None])
        grad_weights = jnp.einsum(
            "qhd,khd->hqk", grad_part, value_part, preferred_element_type=jnp.float32
        )
        offset_term = jnp.sum(weights * grad_weights, axis=-1, keepdims=True)
        grad_scores = (weights * (grad_weights - offset_term)).astype(jnp.bfloat16)
        grad_query = jnp.einsum(
            "hqk,khd->qhd", grad_scores, key_part, preferred_element_type=jnp.float32
        )
        grad_key = jnp.einsum(
            "hqk,qhd->khd", grad_scores, query_part, preferred_element_type=jnp.float32
        )
        grad_value = jnp.einsum(
            "hqk,qhd->khd",
            weights.astype(jnp.bfloat16),
            grad_part,
            preferred_element_type=jnp.float32,
        )
        return (grad_query, grad_key, grad_value)

    grad_queries, grad_keys, grad_values = lax.map(
        backward_group, jnp.arange(group_count, dtype=jnp.int32)
    )
    row_total = keys_again.shape[0]
    grad_key_rows = jnp.moveaxis(grad_keys, 0, 1).reshape(row_total, heads_width)
    grad_value_rows = jnp.moveaxis(grad_values, 0, 1).reshape(row_total, heads_width)
    key_share, value_share = (
        lax.psum_scatter(
            grad_key_rows.astype(jnp.bfloat16), "ctx", scatter_dimension=0, tiled=True
        ).astype(jnp.float32),
        lax.psum_scatter(
            grad_value_rows.astype(jnp.bfloat16), "ctx", scatter_dimension=0, tiled=True
        ).astype(jnp.float32),
    )
    grad_query_heads = jnp.moveaxis(grad_queries, 0, 1).reshape(tokens_dev, head_count, HD)
    unused_rot, rotate_pull = jax.vjp(place_heads, query_pre, key_pre)
    grad_query_pre, grad_key_pre = rotate_pull(
        (grad_query_heads, key_share.reshape(tokens_dev, head_count, HD))
    )
    grad_projected = jnp.concatenate(
        [
            grad_query_pre.reshape(tokens_dev, heads_width),
            grad_key_pre.reshape(tokens_dev, heads_width),
            value_share,
        ],
        axis=1,
    ).astype(jnp.bfloat16)
    grad_qkv = jnp.einsum("td,tc->dc", normed, grad_projected, preferred_element_type=jnp.float32)
    grad_shift = jnp.sum(grad_projected.astype(jnp.float32), axis=0)
    grad_normed_attn = jnp.einsum(
        "tc,dc->td", grad_projected, qkv_full, preferred_element_type=jnp.float32
    )
    unused_norm, first_pull = jax.vjp(rms_scale, inputs, gain_attn)
    grad_inputs_norm, grad_gain_attn = first_pull(grad_normed_attn)
    input_grad = grad_middle + grad_inputs_norm
    sum_gain_attn, sum_qkv, sum_shift, sum_out = (
        lax.psum_scatter(grad_gain_attn, ("fsdp", "ctx"), scatter_dimension=0, tiled=True),
        lax.psum_scatter(grad_qkv, ("fsdp", "ctx"), scatter_dimension=0, tiled=True),
        lax.psum_scatter(grad_shift, ("fsdp", "ctx"), scatter_dimension=0, tiled=True),
        lax.psum_scatter(grad_out_mat, ("fsdp", "ctx"), scatter_dimension=0, tiled=True),
    )
    return (
        hidden_out,
        input_grad.reshape(1, tokens_dev, model_width),
        sum_gain_attn,
        sum_qkv,
        sum_shift,
        sum_out,
        sum_gain_ffn,
        sum_router,
        sum_gate_vec,
        sum_inner,
        sum_outer,
        sum_expert_inner,
        sum_expert_outer,
    )


SPAN = 256


def flat_dot(left, right):
    return lax.dot_general(left, right, (((1,), (0,)), ((), ())), preferred_element_type=jnp.float32)


def turned_dot(left, right):
    return lax.dot_general(left, right, (((1,), (1,)), ((), ())), preferred_element_type=jnp.float32)


def span_of(index, size=SPAN):
    return pl.ds(pl.multiple_of(index * size, size), size)


MESH = pl.DeviceIdType.MESH
ANY = pl.BlockSpec(memory_space=pl.ANY)
VMEM = pl.BlockSpec(memory_space=pltpu.VMEM)


def remote(source, target, send_sem, recv_sem, **place):
    return pltpu.make_async_remote_copy(
        src_ref=source,
        dst_ref=target,
        send_sem=send_sem,
        recv_sem=recv_sem,
        device_id=place,
        device_id_type=MESH,
    )


def line_place():
    here = lax.axis_index("ctx")
    line = here % 2
    return here, here // 2, line, here + 1 - 2 * line


def greet_line(last, here, level, side, others=0):
    barrier = pltpu.get_barrier_semaphore()
    pl.semaphore_signal(barrier, inc=1, device_id={"ctx": side}, device_id_type=MESH)

    @pl.when(level < last)
    def up():
        pl.semaphore_signal(barrier, inc=1, device_id={"ctx": here + 2}, device_id_type=MESH)

    @pl.when(level > 0)
    def down():
        pl.semaphore_signal(barrier, inc=1, device_id={"ctx": here - 2}, device_id_type=MESH)

    ends = jnp.where(level < last, 1, 0) + jnp.where(level > 0, 1, 0)
    pl.semaphore_wait(barrier, 1 + others + ends)


def line_copy(rows_ref, block, way, target, sems, source=None):
    send_sem, recv_sem = sems
    return remote(
        rows_ref.at[block] if source is None else source,
        rows_ref.at[block],
        send_sem.at[block, way],
        recv_sem.at[block],
        ctx=target,
    )


def line_start(rows_ref, own_ref, sems, place, last):
    here, level, line, side = place

    @pl.when(level < last)
    def up():
        line_copy(rows_ref, here, 0, here + 2, sems, own_ref).start()

    @pl.when(level > 0)
    def down():
        line_copy(rows_ref, here, 1, here - 2, sems, own_ref).start()

    line_copy(rows_ref, here, 2, side, sems, own_ref).start()


def line_step(rows_ref, sems, place, last, step):
    here, level, line, side = place

    @pl.when(level >= step)
    def from_below():
        block = here - 2 * step
        line_copy(rows_ref, block, 0, side, sems).wait_recv()

        @pl.when(level < last)
        def on():
            line_copy(rows_ref, block, 0, here + 2, sems).start()

        line_copy(rows_ref, block, 2, side, sems).start()

    @pl.when(level + step <= last)
    def from_above():
        block = here + 2 * step
        line_copy(rows_ref, block, 1, side, sems).wait_recv()

        @pl.when(level > 0)
        def on():
            line_copy(rows_ref, block, 1, here - 2, sems).start()

        line_copy(rows_ref, block, 2, side, sems).start()


def line_finish(rows_ref, sems, place, last):
    here, level, line, side = place
    for other in range(last + 1):
        block = 2 * other + line
        line_copy(rows_ref, 2 * other + 1 - line, 2, side, sems).wait_recv()
        line_copy(rows_ref, block, 2, side, sems).wait_send()

        @pl.when((other <= level) & (level < last))
        def up():
            line_copy(rows_ref, block, 0, side, sems).wait_send()

        @pl.when((other >= level) & (level > 0))
        def down():
            line_copy(rows_ref, block, 1, side, sems).wait_send()


ROWS_STEP = 16


def add_rows(target, pieces, row_count):
    def one(index, carry):
        rows = pl.ds(pl.multiple_of(index * ROWS_STEP, ROWS_STEP), ROWS_STEP)
        total = pieces[0][rows, :].astype(jnp.float32)
        for piece in pieces[1:]:
            total = total + piece[rows, :].astype(jnp.float32)
        target[rows, :] = total.astype(target.dtype)
        return carry

    lax.fori_loop(0, row_count // ROWS_STEP, one, 0)


def scatter_turns(last, part, total, crossed, rising, falling, sums, *sems):
    cross_send, cross_recv, move_send, rise_recv, fall_recv = sems
    here, level, line, side = line_place()
    row_count = total.shape[0]

    def turn(k):
        middle = (level > 0) & (level < last)
        swapped = k + jnp.where(middle, (0, 0, 1, -1)[k], 0)
        return jnp.where(level * 2 < last, last - swapped, swapped)

    def cross(goal):
        return remote(
            part.at[2 * goal + 1 - line],
            crossed.at[goal],
            cross_send.at[goal],
            cross_recv.at[goal],
            ctx=side,
        )

    def rise(goal):
        return remote(
            sums.at[goal], rising.at[goal], move_send.at[goal], rise_recv.at[goal], ctx=here + 2
        )

    def fall(goal):
        return remote(
            sums.at[goal], falling.at[goal], move_send.at[goal], fall_recv.at[goal], ctx=here - 2
        )

    for k in range(min(2, last + 1)):
        cross(turn(k)).start()
    for k in range(last + 1):
        yield k
        goal = turn(k)
        mine = part.at[2 * goal + line]
        cross(goal).wait_recv()
        if k + 2 <= last:
            cross(turn(k + 2)).start()

        @pl.when(goal > level)
        def upward():
            @pl.when(level > 0)
            def joined():
                rise(goal).wait_recv()
                add_rows(sums.at[goal], (mine, crossed.at[goal], rising.at[goal]), row_count)

            @pl.when(level == 0)
            def first():
                add_rows(sums.at[goal], (mine, crossed.at[goal]), row_count)

            rise(goal).start()

        @pl.when(goal < level)
        def downward():
            @pl.when(level < last)
            def joined():
                fall(goal).wait_recv()
                add_rows(sums.at[goal], (mine, crossed.at[goal], falling.at[goal]), row_count)

            @pl.when(level == last)
            def first():
                add_rows(sums.at[goal], (mine, crossed.at[goal]), row_count)

            fall(goal).start()

        @pl.when(goal == level)
        def here_at_last():
            @pl.when(level > 0)
            def from_below():
                rise(goal).wait_recv()

            @pl.when(level < last)
            def from_above():
                fall(goal).wait_recv()

            @pl.when(level == 0)
            def bottom():
                add_rows(total, (mine, crossed.at[goal], falling.at[goal]), row_count)

            @pl.when(level == last)
            def top():
                add_rows(total, (mine, crossed.at[goal], rising.at[goal]), row_count)

            @pl.when((level > 0) & (level < last))
            def between():
                add_rows(
                    total,
                    (mine, crossed.at[goal], rising.at[goal], falling.at[goal]),
                    row_count,
                )

    for goal in range(last + 1):
        cross(goal).wait_send()

        @pl.when(goal != level)
        def sent():
            rise(goal).wait_send()


def scatter_kernel(
    ctx_count, part, small, tokens, grads, total, small_in, weight_grad, *refs
):
    *refs, product, store_sem = refs
    greet_all(ctx_count)
    here = lax.axis_index("ctx")
    starts, waits = spread(
        lambda peer: small.at[peer], lambda source: small_in.at[source], refs[9:11], ctx_count
    )
    for copy in starts:
        copy.start()
    small_in[here] = small[here]
    turns = scatter_turns(ctx_count // 2 - 1, part, total, *refs[:9])
    next(turns)
    pieces = ctx_count // 2
    depth = tokens.shape[1] // pieces
    stores = []
    for piece in range(pieces):

        @pl.loop(0, depth // SPAN)
        def multiply(index):
            here = pl.ds(pl.multiple_of(piece * depth + index * SPAN, SPAN), SPAN)
            product[here, :] = flat_dot(tokens[:, here].T, grads[...]).astype(product.dtype)

        rows = pl.ds(piece * depth, depth)
        stores.append(
            pltpu.make_async_copy(product.at[rows], weight_grad.at[rows], store_sem.at[piece])
        )
        stores[-1].start()
        next(turns, None)
    for copy in waits:
        copy.wait_recv()
    for copy in starts:
        copy.wait_send()
    for copy in stores:
        copy.wait()


def line_scatter_kernel(last, part, total, *refs):
    here, level, line, side = line_place()
    greet_line(last, here, level, side)
    for step in scatter_turns(last, part, total, *refs):
        pass


def line_scatter(ctx_count, call_id, part, small=None, tokens=None, grads=None):
    rows, width = part.shape[1:]
    half = ctx_count // 2
    dma = pltpu.SemaphoreType.DMA((half,))
    spread_dma = pltpu.SemaphoreType.DMA((ctx_count,))
    slots = pltpu.VMEM((half, rows, width), part.dtype)
    total = jax.ShapeDtypeStruct((rows, width), jnp.float32)
    params = pltpu.CompilerParams(
        collective_id=call_id, has_side_effects=True, vmem_limit_bytes=40 * 2**20
    )
    if small is None:
        return pl.pallas_call(
            functools.partial(line_scatter_kernel, half - 1),
            out_shape=total,
            in_specs=[VMEM],
            out_specs=VMEM,
            scratch_shapes=[slots] * 4 + [dma] * 5,
            compiler_params=params,
            name="line_scatter",
        )(part)
    product = (tokens.shape[1], grads.shape[1])
    params = pltpu.CompilerParams(
        collective_id=call_id, has_side_effects=True, vmem_limit_bytes=56 * 2**20
    )
    return pl.pallas_call(
        functools.partial(scatter_kernel, ctx_count),
        out_shape=[
            total,
            jax.ShapeDtypeStruct(small.shape, small.dtype),
            jax.ShapeDtypeStruct(product, part.dtype),
        ],
        in_specs=[VMEM] * 4,
        out_specs=[VMEM] * 2 + [ANY],
        scratch_shapes=[slots] * 4
        + [dma] * 5
        + [spread_dma] * 2
        + [pltpu.VMEM(product, part.dtype), pltpu.SemaphoreType.DMA((half,))],
        compiler_params=params,
        name="line_scatter",
    )(part, small, tokens, grads)


def fsdp_place():
    here = lax.axis_index("fsdp")
    beside = here + 1 - 2 * (here % 2)
    return here, beside, (here + 2) % 4, (beside + 2) % 4


def greet_all(ctx_count):
    barrier = pltpu.get_barrier_semaphore()
    here = lax.axis_index("ctx")
    group = lax.axis_index("fsdp")
    for k in range(1, ctx_count):
        pl.semaphore_signal(
            barrier, inc=1, device_id={"ctx": (here + k) % ctx_count}, device_id_type=MESH
        )
    for k in range(1, 4):
        pl.semaphore_signal(barrier, inc=1, device_id={"fsdp": (group + k) % 4}, device_id_type=MESH)
    pl.semaphore_wait(barrier, ctx_count + 2)


def share_start(blocks, sems, own=None):
    send_sem, recv_sem = sems
    here, beside, across, corner = fsdp_place()
    source = blocks.at[here] if own is None else own
    for way, target in ((0, across), (1, beside)):
        remote(source, blocks.at[here], send_sem.at[way], recv_sem.at[here], fsdp=target).start()


def share_step(blocks, sems):
    send_sem, recv_sem = sems
    here, beside, across, corner = fsdp_place()
    copy = remote(
        blocks.at[across], blocks.at[across], send_sem.at[2], recv_sem.at[across], fsdp=beside
    )
    copy.wait_recv()
    copy.start()


def share_finish(blocks, sems):
    send_sem, recv_sem = sems
    here, beside, across, corner = fsdp_place()
    for way, block in ((0, beside), (1, corner)):
        copy = remote(
            blocks.at[block], blocks.at[block], send_sem.at[way], recv_sem.at[block], fsdp=beside
        )
        copy.wait_recv()
        copy.wait_send()
    remote(
        blocks.at[here], blocks.at[here], send_sem.at[2], recv_sem.at[here], fsdp=beside
    ).wait_send()


def spread(pieces, landing, sems, ctx_count):
    send_sem, recv_sem = sems
    here = lax.axis_index("ctx")

    def copy(k, peer, source):
        return remote(pieces(peer), landing(source), send_sem.at[k], recv_sem.at[k], ctx=peer)

    starts = [copy(k, (here + k) % ctx_count, here) for k in range(1, ctx_count)]
    waits = [
        copy(k, (here + k) % ctx_count, (here + ctx_count - k) % ctx_count)
        for k in range(1, ctx_count)
    ]
    return starts, waits


def greet_near(last, here, level, side):
    barrier = pltpu.get_barrier_semaphore()
    group = lax.axis_index("fsdp")
    for k in range(1, 4):
        pl.semaphore_signal(barrier, inc=1, device_id={"fsdp": (group + k) % 4}, device_id_type=MESH)
    greet_line(last, here, level, side, 3)


def gather_kernel(last, shared_count, *refs):
    total = 1 + shared_count
    owns, rows, keep_sem = refs[:total], refs[total : 2 * total], refs[2 * total]
    refs = refs[2 * total + 1 :]
    place = line_place()
    here, level, line, side = place
    sems = [(refs[2 * i], refs[2 * i + 1]) for i in range(total)]
    group = lax.axis_index("fsdp")
    if shared_count:
        greet_near(last, here, level, side)
    else:
        greet_line(last, here, level, side)
    line_start(rows[0], owns[0], sems[0], place, last)
    for i in range(1, total):
        share_start(rows[i], sems[i], owns[i])
    keeps = [
        pltpu.make_async_copy(
            owns[i], rows[i].at[group if i else here], keep_sem.at[i]
        )
        for i in range(total)
    ]
    for copy in keeps:
        copy.start()
    for step in range(1, last + 1):
        line_step(rows[0], sems[0], place, last, step)
    for i in range(1, total):
        share_step(rows[i], sems[i])
    line_finish(rows[0], sems[0], place, last)
    for i in range(1, total):
        share_finish(rows[i], sems[i])
    for copy in keeps:
        copy.wait()


def product_kernel(last, own, units, grads, rows, product, keep_sem, send_sem, recv_sem):
    place = line_place()
    here, level, line, side = place
    sems = (send_sem, recv_sem)
    greet_line(last, here, level, side)
    line_start(rows, own, sems, place, last)
    keep = pltpu.make_async_copy(own, rows.at[here], keep_sem.at[0])
    keep.start()
    turned = units[...].T
    piece = grads.shape[1] // (last + 1)
    for step in range(last + 1):
        columns = pl.ds(step * piece, piece)
        product[:, columns] = flat_dot(turned, grads[:, columns]).astype(product.dtype)
        if step < last:
            line_step(rows, sems, place, last, step + 1)
    line_finish(rows, sems, place, last)
    keep.wait()


def product_gather(ctx_count, call_id, own, units, grads):
    dma = pltpu.SemaphoreType.DMA
    return pl.pallas_call(
        functools.partial(product_kernel, ctx_count // 2 - 1),
        out_shape=[
            jax.ShapeDtypeStruct((ctx_count,) + own.shape, own.dtype),
            jax.ShapeDtypeStruct((units.shape[1], grads.shape[1]), own.dtype),
        ],
        in_specs=[VMEM] * 3,
        out_specs=[ANY, VMEM],
        scratch_shapes=[dma((1,)), dma((ctx_count, 3)), dma((ctx_count,))],
        compiler_params=pltpu.CompilerParams(
            collective_id=call_id, has_side_effects=True, vmem_limit_bytes=32 * 2**20
        ),
        name="product_gather",
    )(own, units, grads)


def line_gather(ctx_count, call_id, own, *shared):
    count = len(shared)
    dma = pltpu.SemaphoreType.DMA
    return pl.pallas_call(
        functools.partial(gather_kernel, ctx_count // 2 - 1, count),
        out_shape=[jax.ShapeDtypeStruct((ctx_count,) + own.shape, own.dtype)]
        + [jax.ShapeDtypeStruct((4,) + a.shape, a.dtype) for a in shared],
        in_specs=[VMEM] * (1 + count),
        out_specs=[ANY] * (1 + count),
        scratch_shapes=[dma((1 + count,)), dma((ctx_count, 3)), dma((ctx_count,))]
        + [dma((3,)), dma((4,))] * count,
        compiler_params=pltpu.CompilerParams(collective_id=call_id, has_side_effects=True),
        name="line_gather",
    )(own, *shared)


def opening_kernel(
    ctx_count,
    own,
    qkv_own,
    out_own,
    small_own,
    number_own,
    rows,
    qkv,
    out_pair,
    small,
    numbers,
    keep_sem,
    pair_send,
    pair_recv,
    row_send,
    row_recv,
    share_send,
    share_recv,
    *sems,
):
    last = ctx_count // 2 - 1
    place = line_place()
    here, level, line, side = place
    group, beside, across, corner = fsdp_place()
    sems = [(sems[2 * i], sems[2 * i + 1]) for i in range(5)]
    qkv_spread, small_spread, number_spread, out_share, small_share = sems
    row_sems = (row_send, row_recv)
    greet_all(ctx_count)
    qkv_start, qkv_wait = spread(
        lambda peer: qkv_own.at[peer], lambda source: qkv.at[group, source], qkv_spread, ctx_count
    )
    small_start, small_wait = spread(
        lambda peer: small_own, lambda source: small.at[group, source], small_spread, ctx_count
    )
    number_start, number_wait = spread(
        lambda peer: number_own, lambda source: numbers.at[source], number_spread, ctx_count
    )

    def piece_copy(way, owner, k, target, first=False):
        source = (here + ctx_count - k) % ctx_count
        return remote(
            qkv_own.at[here] if first else qkv.at[owner, source],
            qkv.at[owner, source],
            share_send.at[way, k],
            share_recv.at[owner, k],
            fsdp=target,
        )

    def piece_on(k):
        piece_copy(0, group, k, across, k == 0).start()
        piece_copy(1, group, k, beside, k == 0).start()

    for copy in small_start + number_start + qkv_start:
        copy.start()
    line_start(rows, own, row_sems, place, last)
    piece_on(0)
    pair = remote(
        out_own, out_pair.at[group, line], pair_send.at[0], pair_recv.at[0], ctx=side
    )
    pair.start()
    keeps = [
        pltpu.make_async_copy(source, target, keep_sem.at[i])
        for i, (source, target) in enumerate(
            (
                (qkv_own.at[here], qkv.at[group, here]),
                (out_own, out_pair.at[group, line]),
                (small_own, small.at[group, here]),
                (number_own, numbers.at[here]),
                (own, rows.at[here]),
            )
        )
    ]
    for copy in keeps:
        copy.start()
    for copy in small_wait:
        copy.wait_recv()
    keeps[2].wait()
    share_start(small, small_share)
    line_step(rows, row_sems, place, last, 1)
    for k in range(1, ctx_count):
        qkv_wait[k - 1].wait_recv()
        piece_on(k)
    remote(
        out_own, out_pair.at[group, 1 - line], pair_send.at[0], pair_recv.at[0], ctx=side
    ).wait_recv()
    keeps[1].wait()
    share_start(out_pair, out_share)
    line_step(rows, row_sems, place, last, 2)
    for k in range(ctx_count):
        piece_copy(0, across, k, across).wait_recv()
        piece_copy(2, across, k, beside).start()
    share_step(small, small_share)
    for step in range(3, last + 1):
        line_step(rows, row_sems, place, last, step)
    share_step(out_pair, out_share)
    line_finish(rows, row_sems, place, last)
    for copy in number_wait:
        copy.wait_recv()
    for copy in qkv_start + small_start + number_start:
        copy.wait_send()
    pair.wait_send()
    for k in range(ctx_count):
        piece_copy(1, beside, k, beside).wait_recv()
        piece_copy(2, corner, k, beside).wait_recv()
        for way in range(3):
            piece_copy(way, group, k, beside).wait_send()
    share_finish(small, small_share)
    share_finish(out_pair, out_share)
    for i in (0, 3, 4):
        keeps[i].wait()


def opening(ctx_count, call_id, own, qkv_own, out_own, small_own, number_own):
    def out(lead, array):
        return jax.ShapeDtypeStruct(lead + array.shape, array.dtype)

    dma = pltpu.SemaphoreType.DMA
    return pl.pallas_call(
        functools.partial(opening_kernel, ctx_count),
        out_shape=[
            out((ctx_count,), own),
            out((4,), qkv_own),
            out((4, 2), out_own),
            out((4, ctx_count), small_own),
            out((ctx_count,), number_own),
        ],
        in_specs=[VMEM] * 5,
        out_specs=[ANY] * 5,
        scratch_shapes=[
            dma((5,)),
            dma((1,)),
            dma((1,)),
            dma((ctx_count, 3)),
            dma((ctx_count,)),
            dma((3, ctx_count)),
            dma((4, ctx_count)),
        ]
        + [dma((ctx_count,))] * 6
        + [dma((3,)), dma((4,))] * 2,
        compiler_params=pltpu.CompilerParams(collective_id=call_id, has_side_effects=True),
        name="opening",
    )(own, qkv_own, out_own, small_own, number_own)


def group_reduce(blocks, beside_in, pair_sums, across_in, settled, sems):
    core_send, core_recv, far_send, far_recv = sems
    group, beside, across, corner = fsdp_place()
    rows = settled.shape[0]

    def core_copy(slot, block):
        return remote(
            blocks.at[block],
            beside_in.at[slot],
            core_send.at[slot],
            core_recv.at[slot],
            fsdp=beside,
        )

    far = remote(pair_sums.at[1], across_in, far_send.at[0], far_recv.at[0], fsdp=across)
    core_copy(1, corner).start()
    core_copy(0, beside).start()
    yield
    core_copy(1, corner).wait_recv()
    add_rows(pair_sums.at[1], (blocks.at[across], beside_in.at[1]), rows)
    far.start()
    core_copy(0, beside).wait_recv()
    add_rows(pair_sums.at[0], (blocks.at[group], beside_in.at[0]), rows)
    yield
    far.wait_recv()
    add_rows(settled, (pair_sums.at[0], across_in), rows)
    yield
    core_copy(1, corner).wait_send()
    core_copy(0, beside).wait_send()
    far.wait_send()
    yield


def closing_kernel(ctx_count, part, weight, pair, plain, small, *refs):
    total, landed, pair_total, plain_total, small_total = refs[:5]
    line_slots, weight_slots, pair_slots, plain_slots = (
        refs[5:9],
        refs[9:13],
        refs[13:17],
        refs[17:20],
    )
    pair_in, small_in, small_sums, small_across = refs[20:24]
    sems = refs[24:]
    line_sems, weight_sems, pair_sems, plain_sems = sems[:5], sems[5:9], sems[9:13], sems[13:17]
    keep_sem, half_send, half_recv = sems[17:20]
    weight_spread, small_spread, (group_send, group_recv) = sems[20:22], sems[22:24], sems[24:26]
    here, level, line, side = line_place()
    group = lax.axis_index("fsdp")
    greet_all(ctx_count)
    turns = scatter_turns(ctx_count // 2 - 1, part, total, *line_slots, *line_sems)
    settled, pair_settled = weight_slots[3], pair_slots[3]
    weight_steps = group_reduce(weight, *weight_slots, weight_sems)
    pair_steps = group_reduce(pair, *pair_slots, pair_sems)
    plain_steps = group_reduce(plain, *plain_slots, plain_total, plain_sems)
    small_start, small_wait = spread(
        lambda peer: small.at[:, peer], lambda source: small_in.at[source], small_spread, ctx_count
    )
    for copy in small_start:
        copy.start()
    next(weight_steps)
    next(turns)
    next(weight_steps)
    next(pair_steps)
    next(turns)
    next(pair_steps)
    next(plain_steps)
    for copy in small_wait:
        copy.wait_recv()
    small_sum = small[:, here]
    for k in range(1, ctx_count):
        small_sum = small_sum + small_in[(here + k) % ctx_count]
    small_sums[...] = small_sum
    group_copies = [
        remote(
            small_sums.at[(group + k) % 4],
            small_across.at[k],
            group_send.at[k],
            group_recv.at[k],
            fsdp=(group + k) % 4,
        )
        for k in range(1, 4)
    ]
    for copy in group_copies:
        copy.start()
    next(weight_steps)
    piece = settled.shape[0] // ctx_count
    weight_start, weight_wait = spread(
        lambda peer: settled.at[pl.ds(pl.multiple_of(peer * piece, piece), piece)],
        lambda source: landed.at[source],
        weight_spread,
        ctx_count,
    )
    for copy in weight_start:
        copy.start()
    keep = pltpu.make_async_copy(
        settled.at[pl.ds(pl.multiple_of(here * piece, piece), piece)],
        landed.at[here],
        keep_sem.at[0],
    )
    keep.start()
    next(plain_steps)
    next(turns)
    next(pair_steps)
    half = pair_total.shape[0]
    half_copy = remote(
        pair_settled.at[pl.ds(pl.multiple_of((1 - line) * half, half), half)],
        pair_in,
        half_send.at[0],
        half_recv.at[0],
        ctx=side,
    )
    half_copy.start()
    for copy in group_copies:
        copy.wait_recv()
    small_total[...] = small_sums[group] + small_across[1] + small_across[2] + small_across[3]
    for step in turns:
        pass
    next(plain_steps)
    half_copy.wait_recv()
    kept = pair_settled.at[pl.ds(pl.multiple_of(line * half, half), half)]
    add_rows(pair_total, (kept, pair_in), half)
    for copy in weight_wait:
        copy.wait_recv()
    for copy in weight_start + small_start + group_copies:
        copy.wait_send()
    half_copy.wait_send()
    next(weight_steps)
    next(pair_steps)
    next(plain_steps)
    keep.wait()


def closing(ctx_count, call_id, part, weight, pair, plain, small):
    rows, width = part.shape[1:]
    half = ctx_count // 2
    dma = pltpu.SemaphoreType.DMA
    slots = pltpu.VMEM((half, rows, width), part.dtype)

    def group_slots(array):
        one = pltpu.VMEM(array.shape[1:], array.dtype)
        two = pltpu.VMEM((2,) + array.shape[1:], array.dtype)
        return [two, two, one, one]

    block, columns = weight.shape[1:]
    pair_half = (pair.shape[1] // 2, pair.shape[2])
    return pl.pallas_call(
        functools.partial(closing_kernel, ctx_count),
        out_shape=[
            jax.ShapeDtypeStruct((rows, width), jnp.float32),
            jax.ShapeDtypeStruct((ctx_count, block // ctx_count, columns), weight.dtype),
            jax.ShapeDtypeStruct(pair_half, jnp.float32),
            jax.ShapeDtypeStruct(plain.shape[1:], jnp.float32),
            jax.ShapeDtypeStruct(small.shape[2:], small.dtype),
        ],
        in_specs=[VMEM] * 5,
        out_specs=[VMEM] * 5,
        scratch_shapes=[slots] * 4
        + group_slots(weight)
        + group_slots(pair)
        + group_slots(plain)[:3]
        + [
            pltpu.VMEM(pair_half, pair.dtype),
            pltpu.VMEM((ctx_count, 4) + small.shape[2:], small.dtype),
            pltpu.VMEM((4,) + small.shape[2:], small.dtype),
            pltpu.VMEM((4,) + small.shape[2:], small.dtype),
        ]
        + [dma((half,))] * 5
        + [dma((2,)), dma((2,)), dma((1,)), dma((1,))] * 3
        + [dma((1,))] * 3
        + [dma((ctx_count,))] * 4
        + [dma((4,))] * 2,
        compiler_params=pltpu.CompilerParams(
            collective_id=call_id, has_side_effects=True, vmem_limit_bytes=56 * 2**20
        ),
        name="closing",
    )(part, weight, pair, plain, small)


def scaled_rows(values):
    return values * lax.rsqrt(jnp.mean(values * values, axis=-1, keepdims=True) + EPSILON)


def attend_kernel(
    inputs,
    gain,
    weight,
    bias,
    cosine,
    sine,
    columns,
    lines,
    out_weight,
    normed,
    queries,
    keys,
    values,
    attended,
    log_totals,
    part,
):
    rows = inputs.shape[0]
    low = jnp.bfloat16
    heads = queries.shape[1] // HD

    @pl.loop(0, rows // SPAN)
    def project(index):
        here = span_of(index)
        unit = scaled_rows(inputs[here, :].astype(jnp.float32)) * gain[...]
        normed[here, :] = unit.astype(low)
        projected = flat_dot(normed[here, :], weight[...]) + bias[...]
        turn, tilt = cosine[here, :], sine[here, :]
        for head in range(heads):
            own = slice(head * HD, (head + 1) * HD)
            query = projected[:, own]
            query = query * turn + pltpu.roll(query, HD // 2, 1) * tilt
            queries[here, own] = (query * HD ** (-0.5)).astype(low)
            key = projected[:, (heads + head) * HD : (heads + head + 1) * HD]
            keys[here, own] = (key * turn + pltpu.roll(key, HD // 2, 1) * tilt).astype(low)
            values[here, own] = projected[
                :, (2 * heads + head) * HD : (2 * heads + head + 1) * HD
            ].astype(low)

    @pl.loop(0, rows // SPAN)
    def attend(index):
        here = span_of(index)
        position, segment = columns[here, 0:1], columns[here, 1:2]
        allowed = (lines[1:2, :] == segment) & (lines[0:1, :] <= position)
        allowed = allowed | (lines[0:1, :] == position)
        for head in range(heads):
            own = slice(head * HD, (head + 1) * HD)
            scores = turned_dot(queries[here, own], keys[:, own])
            scores = jnp.where(allowed, scores, -1e30)
            highest = jnp.max(scores, axis=1, keepdims=True)
            weights = jnp.exp(scores - highest)
            sums = jnp.sum(weights, axis=1, keepdims=True)
            log_totals[here, head : head + 1] = highest + jnp.log(sums)
            probs = (weights * (1.0 / sums)).astype(low)
            attended[here, own] = flat_dot(probs, values[:, own]).astype(low)
        part[here, :] = flat_dot(attended[here, :], out_weight[...]).astype(low)


def attend(inputs, gain, weight, bias, cosine, sine, columns, lines, out_weight):
    rows, width = inputs.shape
    wide = out_weight.shape[0]
    low = jnp.bfloat16
    shape = jax.ShapeDtypeStruct
    return pl.pallas_call(
        attend_kernel,
        out_shape=[shape((rows, width), low)]
        + [shape((rows, wide), low)] * 4
        + [shape((rows, wide // HD), jnp.float32), shape((rows, width), low)],
        in_specs=[VMEM] * 9,
        out_specs=[VMEM] * 7,
        compiler_params=pltpu.CompilerParams(vmem_limit_bytes=40 * 2**20),
        cost_estimate=pl.CostEstimate(
            flops=2 * rows * width * 4 * wide + 4 * rows * rows * wide,
            bytes_accessed=20 * 2**20,
            transcendentals=rows * rows * wide // HD,
        ),
        name="attend",
    )(inputs, gain, weight, bias, cosine, sine, columns, lines, out_weight)


def attend_back_kernel(
    branch,
    out_weight,
    queries,
    keys,
    values,
    attended,
    totals,
    cosine,
    sine,
    columns,
    lines,
    inputs,
    normed,
    weight,
    part,
    grad_weight,
    grad_out,
    grad_bias,
    grad_gain,
    grads,
    grad_attended,
    grad_keys,
    grad_values,
    gain_sum,
):
    rows, width = branch.shape
    low = jnp.bfloat16
    full = jnp.float32
    wide = queries.shape[1]
    heads = wide // HD

    @pl.loop(0, rows // SPAN)
    def into_heads(index):
        here = span_of(index)
        grad_attended[here, :] = turned_dot(branch[here, :], out_weight[...]).astype(low)

    for head in range(heads):
        own = slice(head * HD, (head + 1) * HD)
        grad_keys[...] = jnp.zeros_like(grad_keys)
        grad_values[...] = jnp.zeros_like(grad_values)

        @pl.loop(0, rows // SPAN)
        def scores_back(index):
            here = span_of(index)
            position, segment = lines[0:1, here], lines[1:2, here]
            allowed = (columns[:, 1:2] == segment) & (columns[:, 0:1] <= position)
            allowed = allowed | (columns[:, 0:1] == position)
            query, grad = queries[here, own], grad_attended[here, own]
            scores = jnp.where(allowed, turned_dot(keys[:, own], query), -1e30)
            probs = jnp.exp(scores - totals[head : head + 1, here])
            grad_probs = turned_dot(values[:, own], grad)
            delta = jnp.sum(probs * grad_probs, axis=0, keepdims=True)
            grad_scores = (probs * (grad_probs - delta)).astype(low)
            grad_keys[...] += flat_dot(grad_scores, query)
            grad_values[...] += flat_dot(probs.astype(low), grad)
            grad_query = flat_dot(grad_scores.T, keys[:, own]) * HD ** (-0.5)
            grads[here, own] = (
                grad_query * cosine[here, :] + pltpu.roll(grad_query * sine[here, :], HD // 2, 1)
            ).astype(low)

        @pl.loop(0, rows // SPAN)
        def keys_back(index):
            here = span_of(index)
            grad_key = grad_keys[here, :]
            grads[here, (heads + head) * HD : (heads + head + 1) * HD] = (
                grad_key * cosine[here, :] + pltpu.roll(grad_key * sine[here, :], HD // 2, 1)
            ).astype(low)
            grads[here, (2 * heads + head) * HD : (2 * heads + head + 1) * HD] = grad_values[
                here, :
            ].astype(low)

    gain_sum[...] = jnp.zeros_like(gain_sum)
    grad_bias[...] = jnp.zeros_like(grad_bias)

    @pl.loop(0, rows // SPAN)
    def project_back(index):
        here = span_of(index)
        grad_rows = turned_dot(grads[here, :], weight[...])
        part[here, :] = grad_rows.astype(low)
        unit = scaled_rows(inputs[here, :].astype(full))
        gain_sum[...] += jnp.sum(grad_rows * unit, axis=0, keepdims=True)
        grad_bias[...] += jnp.sum(grads[here, :].astype(full), axis=0, keepdims=True)

    grad_gain[...] = gain_sum[...]

    @pl.loop(0, width // SPAN)
    def weight_back(index):
        here = span_of(index)
        grad_weight[here, :] = flat_dot(normed[:, here].T, grads[...]).astype(low)

    attended_turned = attended[...].T

    @pl.loop(0, width // (2 * SPAN))
    def out_back(index):
        here = span_of(index, 2 * SPAN)
        grad_out[:, here] = flat_dot(attended_turned, branch[:, here]).astype(low)


def attend_back(
    branch,
    out_weight,
    queries,
    keys,
    values,
    attended,
    totals,
    cosine,
    sine,
    columns,
    lines,
    inputs,
    normed,
    weight,
):
    rows, width = branch.shape
    wide = out_weight.shape[0]
    low = jnp.bfloat16
    full = jnp.float32
    shape = jax.ShapeDtypeStruct
    return pl.pallas_call(
        attend_back_kernel,
        out_shape=[
            shape((rows, width), low),
            shape(weight.shape, low),
            shape((wide, width), low),
            shape((1, 3 * wide), full),
            shape((1, width), full),
        ],
        in_specs=[VMEM] * 14,
        out_specs=[VMEM] * 5,
        scratch_shapes=[
            pltpu.VMEM((rows, 3 * wide), low),
            pltpu.VMEM((rows, wide), low),
            pltpu.VMEM((rows, HD), full),
            pltpu.VMEM((rows, HD), full),
            pltpu.VMEM((1, width), full),
        ],
        compiler_params=pltpu.CompilerParams(vmem_limit_bytes=56 * 2**20),
        cost_estimate=pl.CostEstimate(
            flops=2 * rows * width * 8 * wide + 10 * rows * rows * wide,
            bytes_accessed=35 * 2**20,
            transcendentals=rows * rows * wide // HD,
        ),
        name="attend_back",
    )(
        branch,
        out_weight,
        queries,
        keys,
        values,
        attended,
        totals,
        cosine,
        sine,
        columns,
        lines,
        inputs,
        normed,
        weight,
    )


def deal_kernel(pieces, weight, dealt):
    ctx_count = dealt.shape[0]
    width = dealt.shape[2] // pieces
    for c in range(ctx_count):
        dealt[c] = jnp.concatenate(
            [
                weight[:, (q * ctx_count + c) * width : (q * ctx_count + c + 1) * width]
                for q in range(pieces)
            ],
            axis=1,
        )


def deal_columns(weight, ctx_count, pieces):
    rows, columns = weight.shape
    return pl.pallas_call(
        functools.partial(deal_kernel, pieces),
        out_shape=jax.ShapeDtypeStruct((ctx_count, rows, columns // ctx_count), weight.dtype),
        name="deal_columns",
    )(weight)


def collect_kernel(pieces, dealt, whole):
    ctx_count = dealt.shape[0]
    width = dealt.shape[2] // pieces
    whole[...] = jnp.concatenate(
        [
            dealt[c, :, q * width : (q + 1) * width]
            for q in range(pieces)
            for c in range(ctx_count)
        ],
        axis=1,
    ).astype(whole.dtype)


def collect_columns(dealt, pieces):
    ctx_count, rows, columns = dealt.shape
    return pl.pallas_call(
        functools.partial(collect_kernel, pieces),
        out_shape=jax.ShapeDtypeStruct((rows, columns * ctx_count), jnp.float32),
        name="collect_columns",
    )(dealt)


def heads_kernel(order, dealt, whole):
    pairs = dealt.shape[0] * 2
    for place, head in enumerate(order):
        for which in range(3):
            column = (which * 2 + place % 2) * HD
            target = (which * pairs + head) * HD
            whole[:, target : target + HD] = dealt[
                place // 2, :, column : column + HD
            ].astype(whole.dtype)


def collect_heads(dealt, order):
    ctx_count, rows, columns = dealt.shape
    return pl.pallas_call(
        functools.partial(heads_kernel, order),
        out_shape=jax.ShapeDtypeStruct((rows, columns * ctx_count), jnp.float32),
        name="collect_heads",
    )(dealt)


def over(axis, array, dim=0):
    return lax.all_gather(array, axis, axis=dim, tiled=True)


def reduce_over(axis, array, dim=0):
    return lax.psum_scatter(array, axis, scatter_dimension=dim, tiled=True)


def exchange(array):
    return lax.all_to_all(array, "ctx", split_axis=0, concat_axis=0, tiled=True)


def transposed_dot(left, right):
    return lax.dot_general(
        left, right, (((0,), (0,)), ((), ())), preferred_element_type=jnp.float32
    )


def dot_transposed(left, right):
    return lax.dot_general(
        left, right, (((1,), (1,)), ((), ())), preferred_element_type=jnp.float32
    )


def split_plan(
    hidden_in,
    segments,
    block_pairs,
    routes,
    out_grad,
    norm_gain_attn,
    qkv_weight,
    qkv_bias,
    out_weight,
    norm_gain_ffn,
    router_weight,
    shared_gate_weight,
    shared_in_weight,
    shared_out_weight,
    expert_in_weight,
    expert_out_weight,
):
    low = jnp.bfloat16
    full = jnp.float32
    tokens_dev, width = hidden_in.shape[1:]
    block_len = tokens_dev // 2
    ctx_count = lax.axis_size("ctx")
    fsdp_count = lax.axis_size("fsdp")
    ctx_rank = lax.axis_index("ctx")
    dev_count = ctx_count * fsdp_count
    row_len = ctx_count * tokens_dev
    early = width * 3 // 8
    head_count = width // HD
    shard = qkv_weight.shape[0]
    expert_count = router_weight.shape[1]
    shared_shard = shared_out_weight.shape[0]
    shared_width = fsdp_count * shared_shard
    expert_width = expert_out_weight.shape[1] * fsdp_count
    pair_rank = ctx_rank // 2
    side = ctx_rank % 2
    pairs = ctx_count // 2
    head_order = [j + (p * 2 + t) * pairs for j in range(pairs) for p in range(2) for t in range(2)]

    small = jnp.concatenate(
        [
            norm_gain_attn,
            norm_gain_ffn,
            shared_gate_weight,
            router_weight.T.reshape(-1),
            qkv_bias,
        ]
    )
    small_count = small.shape[0]
    small = jnp.pad(small, (0, 16 * HD - small_count)).reshape(16, HD)
    own_numbers = jnp.concatenate(
        [routes.reshape(tokens_dev, -1).T, segments.reshape(1, tokens_dev)], axis=0
    )
    number_count = own_numbers.shape[0]
    own_numbers = jnp.pad(own_numbers, ((0, 8 - number_count), (0, 0)))
    qkv_parts = (
        qkv_weight.reshape(shard, 3, head_count, HD)[:, :, jnp.array(head_order)]
        .reshape(shard, 3, ctx_count, 2 * HD)
        .transpose(2, 0, 1, 3)
        .reshape(ctx_count, shard, 6 * HD)
    )
    own_inputs = hidden_in.reshape(tokens_dev, width)
    row_inputs, qkv_c, out_pair, small_all, numbers = opening(
        ctx_count, 1, own_inputs, qkv_parts, out_weight, small, own_numbers
    )
    qkv_c = qkv_c.reshape(width, 6 * HD)
    out_c = lax.dynamic_index_in_dim(
        out_pair.reshape(2, 2 * HD, width), side, 0, keepdims=False
    )
    small_all = small_all.reshape(dev_count, 16 * HD)
    gain_attn = small_all[:, :shard].reshape(width).astype(full)
    gain_ffn = small_all[:, shard : 2 * shard].reshape(width).astype(full)
    gate_full = small_all[:, 2 * shard : 3 * shard].reshape(width)
    router_t = (
        small_all[:, 3 * shard : (3 + expert_count) * shard]
        .reshape(dev_count, expert_count, shard)
        .transpose(1, 0, 2)
        .reshape(expert_count, width)
    )
    bias_full = small_all[:, (3 + expert_count) * shard : small_count].reshape(3, head_count, HD)
    router_gate = jnp.concatenate([router_t, gate_full[None, :]], axis=0)
    row_seg = numbers[:, number_count - 1].reshape(row_len)
    routed_here = jnp.any(numbers[:, : number_count - 1] == ctx_rank, axis=1).reshape(row_len)

    expert_outer = over("fsdp", expert_out_weight[0])
    shared_in_weight, early_grad, numbers, expert_outer = lax.optimization_barrier(
        (shared_in_weight, out_grad, numbers, expert_outer)
    )
    early_upstream = over("ctx", early_grad.reshape(tokens_dev, width)[:, :early])
    inner_parts = deal_columns(shared_in_weight, ctx_count, 2 * fsdp_count)
    expert_inner = over("fsdp", expert_in_weight[0])
    inner_parts = exchange(inner_parts)
    my_heads = [pair_rank + (side * 2 + t) * pairs for t in range(2)]
    bias_c = jnp.concatenate(
        [lax.dynamic_index_in_dim(bias_full, h, 1, keepdims=False) for h in my_heads], axis=1
    ).reshape(6 * HD)

    offsets = jnp.arange(block_len, dtype=jnp.int32)
    positions = (block_pairs[:, None] * block_len + offsets[None, :]).reshape(row_len)
    inputs = own_inputs.astype(full)
    row_inputs = row_inputs.reshape(row_len, width)
    half_len = HD // 2
    frequency = THETA ** (-jnp.arange(half_len, dtype=full) / half_len)
    places = positions.astype(full)
    angles = places[:, None] * frequency[None, :]
    cosine, sine = jnp.cos(angles), jnp.sin(angles)
    cosine = jnp.concatenate([cosine, cosine], axis=1)
    sine = jnp.concatenate([-sine, sine], axis=1)
    key_seg = row_seg.astype(full)
    query_seg = jnp.where(row_seg >= 0, key_seg, -2.0)
    query_marks = jnp.stack([places, query_seg])
    key_marks = jnp.stack([places, key_seg])
    row_normed, queries, keys, values, attended_row, log_totals, branch_part = attend(
        row_inputs,
        gain_attn[None, :],
        qkv_c,
        bias_c.astype(full)[None, :],
        cosine,
        sine,
        query_marks.T,
        key_marks,
        out_c,
    )
    branch_part, inner_parts, early_upstream = lax.optimization_barrier(
        (branch_part, inner_parts, early_upstream)
    )
    branch = line_scatter(ctx_count, 2, branch_part.reshape(ctx_count, tokens_dev, width))
    middle = inputs + branch
    normed_ffn = rms_scale(middle, gain_ffn).astype(low)

    row_ffn, inner_c, outer_c = line_gather(
        ctx_count,
        4,
        normed_ffn,
        inner_parts.reshape(ctx_count * shard, 2 * shared_width),
        shared_out_weight,
    )
    row_ffn = row_ffn.reshape(row_len, width)
    row_ffn, late_grad = lax.optimization_barrier((row_ffn, out_grad))
    late_upstream = over("ctx", late_grad.reshape(tokens_dev, width)[:, early:])
    inner_c = inner_c.reshape(width, 2 * shared_width)
    outer_c = outer_c.reshape(shared_width, width)
    row_logits = dot_transposed(row_ffn, router_gate)
    row_probs = jax.nn.softmax(row_logits[:, :expert_count], axis=-1)
    expert_ids = jnp.arange(expert_count, dtype=jnp.int32)
    here = jnp.where(
        routed_here, jnp.sum(jnp.where(expert_ids[None, :] == ctx_rank, row_probs, 0.0), axis=1), 0.0
    )
    row_gate = jax.nn.sigmoid(row_logits[:, expert_count])
    expert_gu = matmul_low(row_ffn, expert_inner)
    expert_hidden = swiglu_mix(expert_gu, expert_width).astype(low)
    expert_result = matmul_low(expert_hidden, expert_outer).astype(low).astype(full)
    row_shared, expert_result = lax.optimization_barrier((row_ffn, expert_result))
    shared_gu = matmul_low(row_shared, inner_c)
    shared_hidden = swiglu_mix(shared_gu, shared_width).astype(low)
    shared_out = matmul_low(shared_hidden, outer_c)
    shared_out, late_upstream = lax.optimization_barrier((shared_out, late_upstream))
    upstream_row = jnp.concatenate([early_upstream, late_upstream], axis=1).astype(full)
    out_part = (row_gate[:, None] * shared_out + here[:, None] * expert_result).astype(low)
    gate_dot = jnp.sum(upstream_row * shared_out, axis=1)
    expert_dot = jnp.where(routed_here, jnp.sum(upstream_row * expert_result, axis=1), 0.0)
    out_landed = reduce_over("ctx", out_part)

    upstream_row, out_part = lax.optimization_barrier((upstream_row, out_part))
    grad_buffers = (here[:, None] * upstream_row).astype(low)
    sum_expert_outer = reduce_over("fsdp", transposed_dot(expert_hidden, grad_buffers).astype(low))
    grad_expert_hidden = dot_transposed(grad_buffers, expert_outer)
    unused_mix, expert_pull = jax.vjp(
        functools.partial(swiglu_mix, hidden_width=expert_width), expert_gu
    )
    grad_expert_gu = expert_pull(grad_expert_hidden)[0].astype(low)
    grad_rows = dot_transposed(grad_expert_gu, expert_inner).astype(low)
    upstream_row, grad_rows = lax.optimization_barrier((upstream_row, grad_rows))
    grad_shared_out = (row_gate[:, None] * upstream_row).astype(low)
    grad_hidden = dot_transposed(grad_shared_out, outer_c)
    unused_mix, mix_pull = jax.vjp(
        functools.partial(swiglu_mix, hidden_width=shared_width), shared_gu
    )
    grad_shared_gu = mix_pull(grad_hidden)[0].astype(low)
    grad_inner = transposed_dot(row_ffn, grad_shared_gu).astype(low)
    sum_inner_c = reduce_over("fsdp", grad_inner)
    grad_ffn_part = (
        dot_transposed(grad_shared_gu, inner_c) + grad_rows.astype(full)
    ).astype(low)
    dots = jnp.stack([gate_dot, expert_dot]).reshape(2, ctx_count, tokens_dev).transpose(1, 0, 2)
    grad_ffn_part, grad_inner = lax.optimization_barrier((grad_ffn_part, grad_inner))
    grad_normed, own_dots, grad_expert_inner = line_scatter(
        ctx_count,
        6,
        grad_ffn_part.reshape(ctx_count, tokens_dev, width),
        jnp.pad(dots, ((0, 0), (0, 6), (0, 0))),
        row_ffn,
        grad_expert_gu,
    )
    sum_expert_inner = reduce_over("fsdp", grad_expert_inner)
    hidden_out = (middle + out_landed.astype(full)).astype(low).reshape(1, tokens_dev, width)

    own_logits = dot_transposed(normed_ffn, router_gate)
    router_probs = jax.nn.softmax(own_logits[:, :expert_count], axis=-1)
    gate_value = jax.nn.sigmoid(own_logits[:, expert_count])
    grad_gate_logit = gate_value * (1.0 - gate_value) * jnp.sum(own_dots[:, 0], axis=0)
    grad_choice = own_dots[:, 1].T
    grad_logits = router_probs * (
        grad_choice - jnp.sum(router_probs * grad_choice, axis=1, keepdims=True)
    )
    grad_small = jnp.concatenate([grad_logits, grad_gate_logit[:, None]], axis=1).astype(low)
    grad_router_gate = transposed_dot(grad_small, normed_ffn)
    grad_normed = grad_normed + matmul_low(grad_small, router_gate)
    unused_norm, norm_pull = jax.vjp(rms_scale, middle, gain_ffn)
    grad_middle_norm, grad_gain_ffn = norm_pull(grad_normed)
    grad_middle = out_grad.reshape(tokens_dev, width).astype(full) + grad_middle_norm

    grad_branch, sum_expert_outer, hidden_out = lax.optimization_barrier(
        (grad_middle.astype(low), sum_expert_outer, hidden_out)
    )
    row_branch, grad_outer = product_gather(
        ctx_count, 3, grad_branch, shared_hidden, grad_shared_out
    )
    row_branch, sum_inner_c = lax.optimization_barrier(
        (row_branch.reshape(row_len, width), sum_inner_c)
    )
    sum_inner = collect_columns(
        exchange(sum_inner_c.reshape(ctx_count, shard, 2 * shared_width)), 2 * fsdp_count
    )
    grad_attn_part, grad_qkv_c, grad_out_c, grad_bias_c, grad_gain_attn = attend_back(
        row_branch,
        out_c,
        queries,
        keys,
        values,
        attended_row,
        log_totals.T,
        cosine,
        sine,
        key_marks.T,
        query_marks,
        row_inputs,
        row_normed,
        qkv_c,
    )
    grad_out_c = grad_out_c.reshape(2, HD, width)
    padded_out = jnp.concatenate(
        [jnp.where(side == p, grad_out_c, jnp.zeros_like(grad_out_c)) for p in range(2)], axis=0
    )
    grad_attn_part, sum_inner = lax.optimization_barrier((grad_attn_part, sum_inner))
    grad_bias_c = grad_bias_c.reshape(3, 1, 2, HD)
    mine = (jnp.arange(ctx_count) == ctx_rank)[None, :, None, None]
    places_of = [head_order.index(h) for h in range(head_count)]
    grad_bias = (
        jnp.where(mine, grad_bias_c, 0.0)
        .reshape(3, pairs, 2, 2, HD)
        .transpose(0, 2, 3, 1, 4)
        .reshape(dev_count, -1)
    )
    small_grads = jnp.concatenate(
        [
            grad_gain_attn.reshape(dev_count, shard),
            grad_gain_ffn.reshape(dev_count, shard),
            grad_router_gate.reshape(expert_count + 1, dev_count, shard)
            .transpose(1, 0, 2)
            .reshape(dev_count, (expert_count + 1) * shard),
            grad_bias,
        ],
        axis=1,
    )
    small_grads = jnp.pad(small_grads, ((0, 0), (0, 8 * HD - small_count)))
    grad_normed_attn, sum_qkv_c, sum_out, sum_outer, sums = closing(
        ctx_count,
        5,
        grad_attn_part.reshape(ctx_count, tokens_dev, width),
        grad_qkv_c.reshape(fsdp_count, ctx_count * shard, 6 * HD),
        padded_out,
        grad_outer.reshape(fsdp_count, shared_shard, width),
        small_grads.reshape(fsdp_count, ctx_count, 8, HD),
    )
    sums = sums.reshape(8 * HD)[:small_count]
    sum_qkv = collect_heads(sum_qkv_c, head_order)
    unused_norm, first_pull = jax.vjp(lambda v: rms_scale(v, gain_attn), inputs)
    input_grad = grad_middle + first_pull(grad_normed_attn)[0]
    sum_router = sums[2 * shard : (2 + expert_count) * shard].reshape(expert_count, shard).T
    return (
        hidden_out,
        input_grad.reshape(1, tokens_dev, width),
        sums[:shard],
        sum_qkv,
        sums[(3 + expert_count) * shard :],
        sum_out,
        sums[shard : 2 * shard],
        sum_router,
        sums[(2 + expert_count) * shard : (3 + expert_count) * shard],
        sum_inner,
        sum_outer,
        sum_expert_inner.astype(full)[None],
        sum_expert_outer.astype(full)[None],
    )


def local(*arrays):
    width = arrays[0].shape[2]
    ctx_count = lax.axis_size("ctx")
    shard = arrays[6].shape[0]
    fits = (
        width == 2 * ctx_count * HD
        and 2 * shard == HD
        and ctx_count % 2 == 0
        and lax.axis_size("fsdp") * ctx_count * shard == width
        and arrays[14].shape[0] == 1
    )
    return split_plan(*arrays) if fits else gathered_plan(*arrays)


def solution(mesh):
    in_specs = (
        P("fsdp", "ctx", None),
        P("fsdp", "ctx"),
        P(),
        P("fsdp", "ctx", None),
        P("fsdp", "ctx", None),
        P(("fsdp", "ctx")),
        P(("fsdp", "ctx"), None),
        P(("fsdp", "ctx")),
        P(("fsdp", "ctx"), None),
        P(("fsdp", "ctx")),
        P(("fsdp", "ctx"), None),
        P(("fsdp", "ctx")),
        P(("fsdp", "ctx"), None),
        P(("fsdp", "ctx"), None),
        P("ctx", "fsdp", None),
        P("ctx", "fsdp", None),
    )
    out_specs = (
        P("fsdp", "ctx", None),
        P("fsdp", "ctx", None),
        P(("fsdp", "ctx")),
        P(("fsdp", "ctx"), None),
        P(("fsdp", "ctx")),
        P(("fsdp", "ctx"), None),
        P(("fsdp", "ctx")),
        P(("fsdp", "ctx"), None),
        P(("fsdp", "ctx")),
        P(("fsdp", "ctx"), None),
        P(("fsdp", "ctx"), None),
        P("ctx", "fsdp", None),
        P("ctx", "fsdp", None),
    )
    return jax.shard_map(local, mesh=mesh, in_specs=in_specs, out_specs=out_specs, check_vma=False)
```

```python
import functools

import jax
import jax.numpy as jnp
from jax import lax
from jax.experimental import pallas as pl
from jax.experimental.pallas import tpu as pltpu
from jax.sharding import PartitionSpec as P

HD = 128


EPSILON = 1e-06
THETA = 1000000.0
heads_per_group = 4


def rms_scale(values, gain_vec):
    return (
        values * lax.rsqrt(jnp.mean(values * values, axis=-1, keepdims=True) + EPSILON) * gain_vec
    )


def rotate(values, positions):
    half_len = values.shape[-1] // 2
    frequency = THETA ** (-jnp.arange(half_len, dtype=jnp.float32) / half_len)
    angles = positions.astype(jnp.float32)[:, None] * frequency[None, :]
    cosine = jnp.cos(angles)[:, None, :]
    sine_part = jnp.sin(angles)[:, None, :]
    first_half = values[..., :half_len]
    second = values[..., half_len:]
    return jnp.concatenate(
        [first_half * cosine - second * sine_part, second * cosine + first_half * sine_part],
        axis=-1,
    )


def visible(query_pos, query_seg, key_pos, key_seg):
    same_doc = (key_seg[None, :] == query_seg[:, None]) & (query_seg[:, None] >= 0)
    causal = key_pos[None, :] <= query_pos[:, None]
    return same_doc & causal | (key_pos[None, :] == query_pos[:, None])


def swiglu_mix(gate_up, hidden_width):
    return jax.nn.silu(gate_up[..., :hidden_width]) * gate_up[..., hidden_width:]


def matmul_low(left, right):
    return jnp.dot(left, right, preferred_element_type=jnp.float32)


def gathered_plan(
    hidden_in,
    segments,
    block_pairs,
    routes,
    out_grad,
    norm_gain_attn,
    qkv_weight,
    qkv_bias,
    out_weight,
    norm_gain_ffn,
    router_weight,
    shared_gate_weight,
    shared_in_weight,
    shared_out_weight,
    expert_in_weight,
    expert_out_weight,
):
    tokens_dev = hidden_in.shape[1]
    model_width = hidden_in.shape[2]
    block_len = tokens_dev // 2
    inputs = hidden_in.reshape(tokens_dev, model_width).astype(jnp.float32)
    seg_local = segments.reshape(tokens_dev)
    token_routes = routes.reshape(tokens_dev, -1)
    top_count = token_routes.shape[1]
    ctx_count = lax.axis_size("ctx")
    ctx_rank = lax.axis_index("ctx")
    offsets = jnp.arange(block_len, dtype=jnp.int32)
    all_positions = (
        block_pairs.reshape(ctx_count, 2)[:, :, None] * block_len + offsets[None, None, :]
    ).reshape(ctx_count * tokens_dev)
    my_positions = lax.dynamic_slice_in_dim(all_positions, ctx_rank * tokens_dev, tokens_dev, 0)
    gathered = (
        lax.all_gather(norm_gain_attn, ("fsdp", "ctx"), axis=0, tiled=True),
        lax.all_gather(qkv_weight, ("fsdp", "ctx"), axis=0, tiled=True),
        lax.all_gather(qkv_bias, ("fsdp", "ctx"), axis=0, tiled=True),
        lax.all_gather(out_weight, ("fsdp", "ctx"), axis=0, tiled=True),
        lax.all_gather(norm_gain_ffn, ("fsdp", "ctx"), axis=0, tiled=True),
        lax.all_gather(router_weight, ("fsdp", "ctx"), axis=0, tiled=True),
        lax.all_gather(shared_gate_weight, ("fsdp", "ctx"), axis=0, tiled=True),
        lax.all_gather(shared_in_weight, ("fsdp", "ctx"), axis=0, tiled=True),
        lax.all_gather(shared_out_weight, ("fsdp", "ctx"), axis=0, tiled=True),
    )
    (
        gain_attn,
        qkv_full,
        shift_full,
        out_full,
        gain_ffn,
        router_full,
        gate_full,
        inner_full,
        outer_full,
    ) = gathered
    gain_attn = gain_attn.astype(jnp.float32)
    gain_ffn = gain_ffn.astype(jnp.float32)
    heads_width = out_full.shape[0]
    head_count = heads_width // HD
    group_width = heads_per_group * HD
    group_count = head_count // heads_per_group
    normed = rms_scale(inputs, gain_attn).astype(jnp.bfloat16)
    projected = matmul_low(normed, qkv_full) + shift_full.astype(jnp.float32)
    query_pre = projected[:, :heads_width].reshape(tokens_dev, head_count, HD)
    key_pre = projected[:, heads_width : 2 * heads_width].reshape(tokens_dev, head_count, HD)

    def place_heads(query_in, key_in):
        return (rotate(query_in, my_positions) * HD ** (-0.5), rotate(key_in, my_positions))

    query_rot, key_rot = place_heads(query_pre, key_pre)
    query_low = query_rot.reshape(tokens_dev, heads_width).astype(jnp.bfloat16)
    key_low = key_rot.reshape(tokens_dev, heads_width).astype(jnp.bfloat16)
    value_low = projected[:, 2 * heads_width :].astype(jnp.bfloat16)
    keys_all, values_all, segs_all = (
        lax.all_gather(key_low, "ctx", axis=0, tiled=True),
        lax.all_gather(value_low, "ctx", axis=0, tiled=True),
        lax.all_gather(seg_local.astype(jnp.bfloat16), "ctx", axis=0, tiled=True),
    )
    allowed = visible(
        my_positions, seg_local.astype(jnp.float32), all_positions, segs_all.astype(jnp.float32)
    )

    def head_slice(matrix, group_index):
        return lax.dynamic_slice_in_dim(matrix, group_index * group_width, group_width, 1).reshape(
            matrix.shape[0], heads_per_group, HD
        )

    def forward_group(group_index):
        query_part = head_slice(query_low, group_index)
        key_part = head_slice(keys_all, group_index)
        value_part = head_slice(values_all, group_index)
        scores = jnp.einsum(
            "qhd,khd->hqk", query_part, key_part, preferred_element_type=jnp.float32
        )
        scores = jnp.where(allowed[None], scores, -1e30)
        highest = jnp.max(scores, axis=-1, keepdims=True)
        log_total = highest + jnp.log(jnp.sum(jnp.exp(scores - highest), axis=-1, keepdims=True))
        weights = jnp.exp(scores - log_total).astype(jnp.bfloat16)
        mixed = jnp.einsum("hqk,khd->qhd", weights, value_part, preferred_element_type=jnp.float32)
        return (mixed, log_total[..., 0])

    mixed_groups, log_totals = lax.map(forward_group, jnp.arange(group_count, dtype=jnp.int32))
    attended = (
        jnp.moveaxis(mixed_groups, 0, 1).reshape(tokens_dev, heads_width).astype(jnp.bfloat16)
    )
    middle = inputs + matmul_low(attended, out_full)
    normed_ffn = rms_scale(middle, gain_ffn).astype(jnp.bfloat16)
    logits = matmul_low(normed_ffn, router_full)
    router_probs = jax.nn.softmax(logits, axis=-1)
    expert_count = logits.shape[1]
    expert_ids = jnp.arange(expert_count, dtype=jnp.int32)
    chosen = (token_routes[:, :, None] == expert_ids[None, None, :]).astype(jnp.float32)
    gate_weights = jnp.sum(chosen * router_probs[:, None, :], axis=-1)
    capacity = 2 * tokens_dev * top_count // expert_count
    local_experts = expert_in_weight.shape[0]
    assigned = tokens_dev * top_count
    flat_routes = token_routes.reshape(assigned)
    onehot = (flat_routes[:, None] == expert_ids[None, :]).astype(jnp.int32)
    earlier = jnp.cumsum(onehot, axis=0) - onehot
    places = flat_routes * capacity + jnp.sum(earlier * onehot, axis=1)
    slot_source = (
        jnp.full((expert_count * capacity,), assigned, jnp.int32)
        .at[places]
        .set(jnp.arange(assigned, dtype=jnp.int32))
    )
    slot_token = slot_source // top_count
    padded_rows = jnp.concatenate([normed_ffn, jnp.zeros((1, model_width), jnp.bfloat16)], axis=0)
    outgoing = padded_rows[slot_token].reshape(ctx_count, local_experts * capacity, model_width)
    expert_inner, expert_outer = (
        lax.all_gather(expert_in_weight, "fsdp", axis=1, tiled=True),
        lax.all_gather(expert_out_weight, "fsdp", axis=1, tiled=True),
    )
    landed_tokens = lax.all_to_all(outgoing, "ctx", split_axis=0, concat_axis=0, tiled=True)
    incoming = landed_tokens.reshape(ctx_count, local_experts, capacity, model_width)
    expert_gu = jnp.einsum(
        "necd,edf->necf", incoming, expert_inner, preferred_element_type=jnp.float32
    )
    expert_width = expert_outer.shape[1]
    expert_hidden = swiglu_mix(expert_gu, expert_width).astype(jnp.bfloat16)
    expert_result = jnp.einsum(
        "necf,efd->necd", expert_hidden, expert_outer, preferred_element_type=jnp.float32
    ).astype(jnp.bfloat16)
    returned = lax.all_to_all(
        expert_result.reshape(ctx_count, local_experts * capacity, model_width),
        "ctx",
        split_axis=0,
        concat_axis=0,
        tiled=True,
    )
    picked = (
        returned.reshape(expert_count * capacity, model_width)[places]
        .reshape(tokens_dev, top_count, model_width)
        .astype(jnp.float32)
    )
    routed = jnp.sum(gate_weights[:, :, None] * picked, axis=1)
    upstream = out_grad.reshape(tokens_dev, model_width).astype(jnp.float32)
    shared_gu = matmul_low(normed_ffn, inner_full)
    shared_width = outer_full.shape[0]
    shared_hidden = swiglu_mix(shared_gu, shared_width).astype(jnp.bfloat16)
    shared_out = matmul_low(shared_hidden, outer_full)
    gate_value = jax.nn.sigmoid(matmul_low(normed_ffn, gate_full))
    output = middle + gate_value[:, None] * shared_out + routed
    hidden_out = output.astype(jnp.bfloat16).reshape(1, tokens_dev, model_width)
    gain_ffn, router_full, gate_full, inner_full, outer_full = (
        lax.all_gather(norm_gain_ffn, ("fsdp", "ctx"), axis=0, tiled=True),
        lax.all_gather(router_weight, ("fsdp", "ctx"), axis=0, tiled=True),
        lax.all_gather(shared_gate_weight, ("fsdp", "ctx"), axis=0, tiled=True),
        lax.all_gather(shared_in_weight, ("fsdp", "ctx"), axis=0, tiled=True),
        lax.all_gather(shared_out_weight, ("fsdp", "ctx"), axis=0, tiled=True),
    )
    gain_ffn = gain_ffn.astype(jnp.float32)
    grad_shared_out = (gate_value[:, None] * upstream).astype(jnp.bfloat16)
    grad_outer = jnp.einsum(
        "tf,td->fd", shared_hidden, grad_shared_out, preferred_element_type=jnp.float32
    )
    grad_hidden = jnp.einsum(
        "td,fd->tf", grad_shared_out, outer_full, preferred_element_type=jnp.float32
    )
    unused_mix, mix_pull = jax.vjp(functools.partial(swiglu_mix, hidden_width=shared_width), shared_gu)
    grad_shared_gu = mix_pull(grad_hidden)[0].astype(jnp.bfloat16)
    grad_inner = jnp.einsum(
        "td,tf->df", normed_ffn, grad_shared_gu, preferred_element_type=jnp.float32
    )
    grad_normed = jnp.einsum(
        "tf,df->td", grad_shared_gu, inner_full, preferred_element_type=jnp.float32
    )
    grad_gate_logit = (
        gate_value * (1.0 - gate_value) * jnp.sum(upstream * shared_out, axis=1)
    ).astype(jnp.bfloat16)
    grad_gate_vec = jnp.einsum(
        "td,t->d", normed_ffn, grad_gate_logit, preferred_element_type=jnp.float32
    )
    grad_normed = (
        grad_normed
        + grad_gate_logit.astype(jnp.float32)[:, None] * gate_full.astype(jnp.float32)[None, :]
    )
    grad_gates = jnp.sum(upstream[:, None, :] * picked, axis=2)
    grad_choice_probs = jnp.sum(chosen * grad_gates[:, :, None], axis=1)
    grad_logits = (
        router_probs
        * (grad_choice_probs - jnp.sum(router_probs * grad_choice_probs, axis=1, keepdims=True))
    ).astype(jnp.bfloat16)
    grad_router = jnp.einsum(
        "td,te->de", normed_ffn, grad_logits, preferred_element_type=jnp.float32
    )
    grad_normed = grad_normed + jnp.einsum(
        "te,de->td", grad_logits, router_full, preferred_element_type=jnp.float32
    )
    grad_slots = (
        (gate_weights[:, :, None] * upstream[:, None, :])
        .astype(jnp.bfloat16)
        .reshape(assigned, model_width)
    )
    padded_grads = jnp.concatenate([grad_slots, jnp.zeros((1, model_width), jnp.bfloat16)], axis=0)
    grad_outgoing = padded_grads[slot_source].reshape(
        ctx_count, local_experts * capacity, model_width
    )
    grad_incoming = lax.all_to_all(
        grad_outgoing, "ctx", split_axis=0, concat_axis=0, tiled=True
    ).reshape(ctx_count, local_experts, capacity, model_width)
    grad_expert_hidden = jnp.einsum(
        "necd,efd->necf", grad_incoming, expert_outer, preferred_element_type=jnp.float32
    )
    grad_expert_outer = jnp.einsum(
        "necf,necd->efd", expert_hidden, grad_incoming, preferred_element_type=jnp.float32
    )
    unused_mix, expert_pull = jax.vjp(functools.partial(swiglu_mix, hidden_width=expert_width), expert_gu)
    grad_expert_gu = expert_pull(grad_expert_hidden)[0].astype(jnp.bfloat16)
    grad_expert_inner = jnp.einsum(
        "necd,necf->edf", incoming, grad_expert_gu, preferred_element_type=jnp.float32
    )
    grad_expert_rows = jnp.einsum(
        "necf,edf->necd", grad_expert_gu, expert_inner, preferred_element_type=jnp.float32
    ).astype(jnp.bfloat16)
    grad_returned = lax.all_to_all(
        grad_expert_rows.reshape(ctx_count, local_experts * capacity, model_width),
        "ctx",
        split_axis=0,
        concat_axis=0,
        tiled=True,
    )
    grad_picked = grad_returned.reshape(expert_count * capacity, model_width)[places].reshape(
        tokens_dev, top_count, model_width
    )
    grad_normed = grad_normed + jnp.sum(grad_picked.astype(jnp.float32), axis=1)
    sum_expert_inner, sum_expert_outer = (
        lax.psum_scatter(
            grad_expert_inner.astype(jnp.bfloat16), "fsdp", scatter_dimension=1, tiled=True
        ).astype(jnp.float32),
        lax.psum_scatter(
            grad_expert_outer.astype(jnp.bfloat16), "fsdp", scatter_dimension=1, tiled=True
        ).astype(jnp.float32),
    )
    unused_norm, norm_pull = jax.vjp(rms_scale, middle, gain_ffn)
    grad_middle_norm, grad_gain_ffn = norm_pull(grad_normed)
    grad_middle = upstream + grad_middle_norm
    sum_gain_ffn, sum_router, sum_gate_vec, sum_inner, sum_outer = (
        lax.psum_scatter(grad_gain_ffn, ("fsdp", "ctx"), scatter_dimension=0, tiled=True),
        lax.psum_scatter(grad_router, ("fsdp", "ctx"), scatter_dimension=0, tiled=True),
        lax.psum_scatter(grad_gate_vec, ("fsdp", "ctx"), scatter_dimension=0, tiled=True),
        lax.psum_scatter(grad_inner, ("fsdp", "ctx"), scatter_dimension=0, tiled=True),
        lax.psum_scatter(grad_outer, ("fsdp", "ctx"), scatter_dimension=0, tiled=True),
    )
    grad_branch = grad_middle.astype(jnp.bfloat16)
    grad_out_mat = jnp.einsum(
        "tc,td->cd", attended, grad_branch, preferred_element_type=jnp.float32
    )
    grad_attended = jnp.einsum(
        "td,cd->tc", grad_branch, out_full, preferred_element_type=jnp.float32
    ).astype(jnp.bfloat16)
    keys_again, values_again = (
        lax.all_gather(key_low, "ctx", axis=0, tiled=True),
        lax.all_gather(value_low, "ctx", axis=0, tiled=True),
    )

    def backward_group(group_index):
        query_part = head_slice(query_low, group_index)
        key_part = head_slice(keys_again, group_index)
        value_part = head_slice(values_again, group_index)
        grad_part = head_slice(grad_attended, group_index)
        log_total = lax.dynamic_index_in_dim(log_totals, group_index, 0, keepdims=False)
        scores = jnp.einsum(
            "qhd,khd->hqk", query_part, key_part, preferred_element_type=jnp.float32
        )
        scores = jnp.where(allowed[None], scores, -1e30)
        weights = jnp.exp(scores - log_total[..., None])
        grad_weights = jnp.einsum(
            "qhd,khd->hqk", grad_part, value_part, preferred_element_type=jnp.float32
        )
        offset_term = jnp.sum(weights * grad_weights, axis=-1, keepdims=True)
        grad_scores = (weights * (grad_weights - offset_term)).astype(jnp.bfloat16)
        grad_query = jnp.einsum(
            "hqk,khd->qhd", grad_scores, key_part, preferred_element_type=jnp.float32
        )
        grad_key = jnp.einsum(
            "hqk,qhd->khd", grad_scores, query_part, preferred_element_type=jnp.float32
        )
        grad_value = jnp.einsum(
            "hqk,qhd->khd",
            weights.astype(jnp.bfloat16),
            grad_part,
            preferred_element_type=jnp.float32,
        )
        return (grad_query, grad_key, grad_value)

    grad_queries, grad_keys, grad_values = lax.map(
        backward_group, jnp.arange(group_count, dtype=jnp.int32)
    )
    row_total = keys_again.shape[0]
    grad_key_rows = jnp.moveaxis(grad_keys, 0, 1).reshape(row_total, heads_width)
    grad_value_rows = jnp.moveaxis(grad_values, 0, 1).reshape(row_total, heads_width)
    key_share, value_share = (
        lax.psum_scatter(
            grad_key_rows.astype(jnp.bfloat16), "ctx", scatter_dimension=0, tiled=True
        ).astype(jnp.float32),
        lax.psum_scatter(
            grad_value_rows.astype(jnp.bfloat16), "ctx", scatter_dimension=0, tiled=True
        ).astype(jnp.float32),
    )
    grad_query_heads = jnp.moveaxis(grad_queries, 0, 1).reshape(tokens_dev, head_count, HD)
    unused_rot, rotate_pull = jax.vjp(place_heads, query_pre, key_pre)
    grad_query_pre, grad_key_pre = rotate_pull(
        (grad_query_heads, key_share.reshape(tokens_dev, head_count, HD))
    )
    grad_projected = jnp.concatenate(
        [
            grad_query_pre.reshape(tokens_dev, heads_width),
            grad_key_pre.reshape(tokens_dev, heads_width),
            value_share,
        ],
        axis=1,
    ).astype(jnp.bfloat16)
    grad_qkv = jnp.einsum("td,tc->dc", normed, grad_projected, preferred_element_type=jnp.float32)
    grad_shift = jnp.sum(grad_projected.astype(jnp.float32), axis=0)
    grad_normed_attn = jnp.einsum(
        "tc,dc->td", grad_projected, qkv_full, preferred_element_type=jnp.float32
    )
    unused_norm, first_pull = jax.vjp(rms_scale, inputs, gain_attn)
    grad_inputs_norm, grad_gain_attn = first_pull(grad_normed_attn)
    input_grad = grad_middle + grad_inputs_norm
    sum_gain_attn, sum_qkv, sum_shift, sum_out = (
        lax.psum_scatter(grad_gain_attn, ("fsdp", "ctx"), scatter_dimension=0, tiled=True),
        lax.psum_scatter(grad_qkv, ("fsdp", "ctx"), scatter_dimension=0, tiled=True),
        lax.psum_scatter(grad_shift, ("fsdp", "ctx"), scatter_dimension=0, tiled=True),
        lax.psum_scatter(grad_out_mat, ("fsdp", "ctx"), scatter_dimension=0, tiled=True),
    )
    return (
        hidden_out,
        input_grad.reshape(1, tokens_dev, model_width),
        sum_gain_attn,
        sum_qkv,
        sum_shift,
        sum_out,
        sum_gain_ffn,
        sum_router,
        sum_gate_vec,
        sum_inner,
        sum_outer,
        sum_expert_inner,
        sum_expert_outer,
    )


SPAN = 256


def flat_dot(left, right):
    return lax.dot_general(left, right, (((1,), (0,)), ((), ())), preferred_element_type=jnp.float32)


def turned_dot(left, right):
    return lax.dot_general(left, right, (((1,), (1,)), ((), ())), preferred_element_type=jnp.float32)


def span_of(index, size=SPAN):
    return pl.ds(pl.multiple_of(index * size, size), size)


MESH = pl.DeviceIdType.MESH
ANY = pl.BlockSpec(memory_space=pl.ANY)
VMEM = pl.BlockSpec(memory_space=pltpu.VMEM)


def remote(source, target, send_sem, recv_sem, **place):
    return pltpu.make_async_remote_copy(
        src_ref=source,
        dst_ref=target,
        send_sem=send_sem,
        recv_sem=recv_sem,
        device_id=place,
        device_id_type=MESH,
    )


def line_place():
    here = lax.axis_index("ctx")
    line = here % 2
    return here, here // 2, line, here + 1 - 2 * line


def greet_line(last, here, level, side, others=0):
    barrier = pltpu.get_barrier_semaphore()
    pl.semaphore_signal(barrier, inc=1, device_id={"ctx": side}, device_id_type=MESH)

    @pl.when(level < last)
    def up():
        pl.semaphore_signal(barrier, inc=1, device_id={"ctx": here + 2}, device_id_type=MESH)

    @pl.when(level > 0)
    def down():
        pl.semaphore_signal(barrier, inc=1, device_id={"ctx": here - 2}, device_id_type=MESH)

    ends = jnp.where(level < last, 1, 0) + jnp.where(level > 0, 1, 0)
    pl.semaphore_wait(barrier, 1 + others + ends)


def line_copy(rows_ref, block, way, target, sems, source=None):
    send_sem, recv_sem = sems
    return remote(
        rows_ref.at[block] if source is None else source,
        rows_ref.at[block],
        send_sem.at[block, way],
        recv_sem.at[block],
        ctx=target,
    )


def line_start(rows_ref, own_ref, sems, place, last):
    here, level, line, side = place

    @pl.when(level < last)
    def up():
        line_copy(rows_ref, here, 0, here + 2, sems, own_ref).start()

    @pl.when(level > 0)
    def down():
        line_copy(rows_ref, here, 1, here - 2, sems, own_ref).start()

    line_copy(rows_ref, here, 2, side, sems, own_ref).start()


def line_step(rows_ref, sems, place, last, step):
    here, level, line, side = place

    @pl.when(level >= step)
    def from_below():
        block = here - 2 * step
        line_copy(rows_ref, block, 0, side, sems).wait_recv()

        @pl.when(level < last)
        def on():
            line_copy(rows_ref, block, 0, here + 2, sems).start()

        line_copy(rows_ref, block, 2, side, sems).start()

    @pl.when(level + step <= last)
    def from_above():
        block = here + 2 * step
        line_copy(rows_ref, block, 1, side, sems).wait_recv()

        @pl.when(level > 0)
        def on():
            line_copy(rows_ref, block, 1, here - 2, sems).start()

        line_copy(rows_ref, block, 2, side, sems).start()


def line_finish(rows_ref, sems, place, last):
    here, level, line, side = place
    for other in range(last + 1):
        block = 2 * other + line
        line_copy(rows_ref, 2 * other + 1 - line, 2, side, sems).wait_recv()
        line_copy(rows_ref, block, 2, side, sems).wait_send()

        @pl.when((other <= level) & (level < last))
        def up():
            line_copy(rows_ref, block, 0, side, sems).wait_send()

        @pl.when((other >= level) & (level > 0))
        def down():
            line_copy(rows_ref, block, 1, side, sems).wait_send()


ROWS_STEP = 16


def add_rows(target, pieces, row_count):
    def one(index, carry):
        rows = pl.ds(pl.multiple_of(index * ROWS_STEP, ROWS_STEP), ROWS_STEP)
        total = pieces[0][rows, :].astype(jnp.float32)
        for piece in pieces[1:]:
            total = total + piece[rows, :].astype(jnp.float32)
        target[rows, :] = total.astype(target.dtype)
        return carry

    lax.fori_loop(0, row_count // ROWS_STEP, one, 0)


def scatter_turns(last, part, total, crossed, rising, falling, sums, *sems):
    cross_send, cross_recv, move_send, rise_recv, fall_recv = sems
    here, level, line, side = line_place()
    row_count = total.shape[0]

    def turn(k):
        middle = (level > 0) & (level < last)
        swapped = k + jnp.where(middle, (0, 0, 1, -1)[k], 0)
        return jnp.where(level * 2 < last, last - swapped, swapped)

    def cross(goal):
        return remote(
            part.at[2 * goal + 1 - line],
            crossed.at[goal],
            cross_send.at[goal],
            cross_recv.at[goal],
            ctx=side,
        )

    def rise(goal):
        return remote(
            sums.at[goal], rising.at[goal], move_send.at[goal], rise_recv.at[goal], ctx=here + 2
        )

    def fall(goal):
        return remote(
            sums.at[goal], falling.at[goal], move_send.at[goal], fall_recv.at[goal], ctx=here - 2
        )

    for k in range(min(2, last + 1)):
        cross(turn(k)).start()
    for k in range(last + 1):
        yield k
        goal = turn(k)
        mine = part.at[2 * goal + line]
        cross(goal).wait_recv()
        if k + 2 <= last:
            cross(turn(k + 2)).start()

        @pl.when(goal > level)
        def upward():
            @pl.when(level > 0)
            def joined():
                rise(goal).wait_recv()
                add_rows(sums.at[goal], (mine, crossed.at[goal], rising.at[goal]), row_count)

            @pl.when(level == 0)
            def first():
                add_rows(sums.at[goal], (mine, crossed.at[goal]), row_count)

            rise(goal).start()

        @pl.when(goal < level)
        def downward():
            @pl.when(level < last)
            def joined():
                fall(goal).wait_recv()
                add_rows(sums.at[goal], (mine, crossed.at[goal], falling.at[goal]), row_count)

            @pl.when(level == last)
            def first():
                add_rows(sums.at[goal], (mine, crossed.at[goal]), row_count)

            fall(goal).start()

        @pl.when(goal == level)
        def here_at_last():
            @pl.when(level > 0)
            def from_below():
                rise(goal).wait_recv()

            @pl.when(level < last)
            def from_above():
                fall(goal).wait_recv()

            @pl.when(level == 0)
            def bottom():
                add_rows(total, (mine, crossed.at[goal], falling.at[goal]), row_count)

            @pl.when(level == last)
            def top():
                add_rows(total, (mine, crossed.at[goal], rising.at[goal]), row_count)

            @pl.when((level > 0) & (level < last))
            def between():
                add_rows(
                    total,
                    (mine, crossed.at[goal], rising.at[goal], falling.at[goal]),
                    row_count,
                )

    for goal in range(last + 1):
        cross(goal).wait_send()

        @pl.when(goal != level)
        def sent():
            rise(goal).wait_send()


def scatter_kernel(
    ctx_count, part, small, tokens, grads, total, small_in, weight_grad, *refs
):
    *refs, product, store_sem = refs
    greet_all(ctx_count)
    here = lax.axis_index("ctx")
    starts, waits = spread(
        lambda peer: small.at[peer], lambda source: small_in.at[source], refs[9:11], ctx_count
    )
    for copy in starts:
        copy.start()
    small_in[here] = small[here]
    turns = scatter_turns(ctx_count // 2 - 1, part, total, *refs[:9])
    next(turns)
    pieces = ctx_count // 2
    depth = tokens.shape[1] // pieces
    stores = []
    for piece in range(pieces):

        @pl.loop(0, depth // SPAN)
        def multiply(index):
            here = pl.ds(pl.multiple_of(piece * depth + index * SPAN, SPAN), SPAN)
            product[here, :] = flat_dot(tokens[:, here].T, grads[...]).astype(product.dtype)

        rows = pl.ds(piece * depth, depth)
        stores.append(
            pltpu.make_async_copy(product.at[rows], weight_grad.at[rows], store_sem.at[piece])
        )
        stores[-1].start()
        next(turns, None)
    for copy in waits:
        copy.wait_recv()
    for copy in starts:
        copy.wait_send()
    for copy in stores:
        copy.wait()


def line_scatter_kernel(last, part, total, *refs):
    here, level, line, side = line_place()
    greet_line(last, here, level, side)
    for step in scatter_turns(last, part, total, *refs):
        pass


def line_scatter(ctx_count, call_id, part, small=None, tokens=None, grads=None):
    rows, width = part.shape[1:]
    half = ctx_count // 2
    dma = pltpu.SemaphoreType.DMA((half,))
    spread_dma = pltpu.SemaphoreType.DMA((ctx_count,))
    slots = pltpu.VMEM((half, rows, width), part.dtype)
    total = jax.ShapeDtypeStruct((rows, width), jnp.float32)
    params = pltpu.CompilerParams(
        collective_id=call_id, has_side_effects=True, vmem_limit_bytes=40 * 2**20
    )
    if small is None:
        return pl.pallas_call(
            functools.partial(line_scatter_kernel, half - 1),
            out_shape=total,
            in_specs=[VMEM],
            out_specs=VMEM,
            scratch_shapes=[slots] * 4 + [dma] * 5,
            compiler_params=params,
            name="line_scatter",
        )(part)
    product = (tokens.shape[1], grads.shape[1])
    params = pltpu.CompilerParams(
        collective_id=call_id, has_side_effects=True, vmem_limit_bytes=56 * 2**20
    )
    return pl.pallas_call(
        functools.partial(scatter_kernel, ctx_count),
        out_shape=[
            total,
            jax.ShapeDtypeStruct(small.shape, small.dtype),
            jax.ShapeDtypeStruct(product, part.dtype),
        ],
        in_specs=[VMEM] * 4,
        out_specs=[VMEM] * 2 + [ANY],
        scratch_shapes=[slots] * 4
        + [dma] * 5
        + [spread_dma] * 2
        + [pltpu.VMEM(product, part.dtype), pltpu.SemaphoreType.DMA((half,))],
        compiler_params=params,
        name="line_scatter",
    )(part, small, tokens, grads)


def fsdp_place():
    here = lax.axis_index("fsdp")
    beside = here + 1 - 2 * (here % 2)
    return here, beside, (here + 2) % 4, (beside + 2) % 4


def greet_all(ctx_count):
    barrier = pltpu.get_barrier_semaphore()
    here = lax.axis_index("ctx")
    group = lax.axis_index("fsdp")
    for k in range(1, ctx_count):
        pl.semaphore_signal(
            barrier, inc=1, device_id={"ctx": (here + k) % ctx_count}, device_id_type=MESH
        )
    for k in range(1, 4):
        pl.semaphore_signal(barrier, inc=1, device_id={"fsdp": (group + k) % 4}, device_id_type=MESH)
    pl.semaphore_wait(barrier, ctx_count + 2)


def share_start(blocks, sems, own=None):
    send_sem, recv_sem = sems
    here, beside, across, corner = fsdp_place()
    source = blocks.at[here] if own is None else own
    for way, target in ((0, across), (1, beside)):
        remote(source, blocks.at[here], send_sem.at[way], recv_sem.at[here], fsdp=target).start()


def share_step(blocks, sems):
    send_sem, recv_sem = sems
    here, beside, across, corner = fsdp_place()
    copy = remote(
        blocks.at[across], blocks.at[across], send_sem.at[2], recv_sem.at[across], fsdp=beside
    )
    copy.wait_recv()
    copy.start()


def share_finish(blocks, sems):
    send_sem, recv_sem = sems
    here, beside, across, corner = fsdp_place()
    for way, block in ((0, beside), (1, corner)):
        copy = remote(
            blocks.at[block], blocks.at[block], send_sem.at[way], recv_sem.at[block], fsdp=beside
        )
        copy.wait_recv()
        copy.wait_send()
    remote(
        blocks.at[here], blocks.at[here], send_sem.at[2], recv_sem.at[here], fsdp=beside
    ).wait_send()


def spread(pieces, landing, sems, ctx_count):
    send_sem, recv_sem = sems
    here = lax.axis_index("ctx")

    def copy(k, peer, source):
        return remote(pieces(peer), landing(source), send_sem.at[k], recv_sem.at[k], ctx=peer)

    starts = [copy(k, (here + k) % ctx_count, here) for k in range(1, ctx_count)]
    waits = [
        copy(k, (here + k) % ctx_count, (here + ctx_count - k) % ctx_count)
        for k in range(1, ctx_count)
    ]
    return starts, waits


def greet_near(last, here, level, side):
    barrier = pltpu.get_barrier_semaphore()
    group = lax.axis_index("fsdp")
    for k in range(1, 4):
        pl.semaphore_signal(barrier, inc=1, device_id={"fsdp": (group + k) % 4}, device_id_type=MESH)
    greet_line(last, here, level, side, 3)


def gather_kernel(last, shared_count, *refs):
    total = 1 + shared_count
    owns, rows, keep_sem = refs[:total], refs[total : 2 * total], refs[2 * total]
    refs = refs[2 * total + 1 :]
    place = line_place()
    here, level, line, side = place
    sems = [(refs[2 * i], refs[2 * i + 1]) for i in range(total)]
    group = lax.axis_index("fsdp")
    if shared_count:
        greet_near(last, here, level, side)
    else:
        greet_line(last, here, level, side)
    line_start(rows[0], owns[0], sems[0], place, last)
    for i in range(1, total):
        share_start(rows[i], sems[i], owns[i])
    keeps = [
        pltpu.make_async_copy(
            owns[i], rows[i].at[group if i else here], keep_sem.at[i]
        )
        for i in range(total)
    ]
    for copy in keeps:
        copy.start()
    for step in range(1, last + 1):
        line_step(rows[0], sems[0], place, last, step)
    for i in range(1, total):
        share_step(rows[i], sems[i])
    line_finish(rows[0], sems[0], place, last)
    for i in range(1, total):
        share_finish(rows[i], sems[i])
    for copy in keeps:
        copy.wait()


def product_kernel(last, own, units, grads, rows, product, keep_sem, send_sem, recv_sem):
    place = line_place()
    here, level, line, side = place
    sems = (send_sem, recv_sem)
    greet_line(last, here, level, side)
    line_start(rows, own, sems, place, last)
    keep = pltpu.make_async_copy(own, rows.at[here], keep_sem.at[0])
    keep.start()
    turned = units[...].T
    piece = grads.shape[1] // (last + 1)
    for step in range(last + 1):
        columns = pl.ds(step * piece, piece)
        product[:, columns] = flat_dot(turned, grads[:, columns]).astype(product.dtype)
        if step < last:
            line_step(rows, sems, place, last, step + 1)
    line_finish(rows, sems, place, last)
    keep.wait()


def product_gather(ctx_count, call_id, own, units, grads):
    dma = pltpu.SemaphoreType.DMA
    return pl.pallas_call(
        functools.partial(product_kernel, ctx_count // 2 - 1),
        out_shape=[
            jax.ShapeDtypeStruct((ctx_count,) + own.shape, own.dtype),
            jax.ShapeDtypeStruct((units.shape[1], grads.shape[1]), own.dtype),
        ],
        in_specs=[VMEM] * 3,
        out_specs=[ANY, VMEM],
        scratch_shapes=[dma((1,)), dma((ctx_count, 3)), dma((ctx_count,))],
        compiler_params=pltpu.CompilerParams(
            collective_id=call_id, has_side_effects=True, vmem_limit_bytes=32 * 2**20
        ),
        name="product_gather",
    )(own, units, grads)


def line_gather(ctx_count, call_id, own, *shared):
    count = len(shared)
    dma = pltpu.SemaphoreType.DMA
    return pl.pallas_call(
        functools.partial(gather_kernel, ctx_count // 2 - 1, count),
        out_shape=[jax.ShapeDtypeStruct((ctx_count,) + own.shape, own.dtype)]
        + [jax.ShapeDtypeStruct((4,) + a.shape, a.dtype) for a in shared],
        in_specs=[VMEM] * (1 + count),
        out_specs=[ANY] * (1 + count),
        scratch_shapes=[dma((1 + count,)), dma((ctx_count, 3)), dma((ctx_count,))]
        + [dma((3,)), dma((4,))] * count,
        compiler_params=pltpu.CompilerParams(collective_id=call_id, has_side_effects=True),
        name="line_gather",
    )(own, *shared)


def opening_kernel(
    ctx_count,
    own,
    qkv_own,
    out_own,
    small_own,
    number_own,
    rows,
    qkv,
    out_pair,
    small,
    numbers,
    keep_sem,
    pair_send,
    pair_recv,
    row_send,
    row_recv,
    share_send,
    share_recv,
    *sems,
):
    last = ctx_count // 2 - 1
    place = line_place()
    here, level, line, side = place
    group, beside, across, corner = fsdp_place()
    sems = [(sems[2 * i], sems[2 * i + 1]) for i in range(5)]
    qkv_spread, small_spread, number_spread, out_share, small_share = sems
    row_sems = (row_send, row_recv)
    greet_all(ctx_count)
    qkv_start, qkv_wait = spread(
        lambda peer: qkv_own.at[peer], lambda source: qkv.at[group, source], qkv_spread, ctx_count
    )
    small_start, small_wait = spread(
        lambda peer: small_own, lambda source: small.at[group, source], small_spread, ctx_count
    )
    number_start, number_wait = spread(
        lambda peer: number_own, lambda source: numbers.at[source], number_spread, ctx_count
    )

    def piece_copy(way, owner, k, target, first=False):
        source = (here + ctx_count - k) % ctx_count
        return remote(
            qkv_own.at[here] if first else qkv.at[owner, source],
            qkv.at[owner, source],
            share_send.at[way, k],
            share_recv.at[owner, k],
            fsdp=target,
        )

    def piece_on(k):
        piece_copy(0, group, k, across, k == 0).start()
        piece_copy(1, group, k, beside, k == 0).start()

    for copy in small_start + number_start + qkv_start:
        copy.start()
    line_start(rows, own, row_sems, place, last)
    piece_on(0)
    pair = remote(
        out_own, out_pair.at[group, line], pair_send.at[0], pair_recv.at[0], ctx=side
    )
    pair.start()
    keeps = [
        pltpu.make_async_copy(source, target, keep_sem.at[i])
        for i, (source, target) in enumerate(
            (
                (qkv_own.at[here], qkv.at[group, here]),
                (out_own, out_pair.at[group, line]),
                (small_own, small.at[group, here]),
                (number_own, numbers.at[here]),
                (own, rows.at[here]),
            )
        )
    ]
    for copy in keeps:
        copy.start()
    for copy in small_wait:
        copy.wait_recv()
    keeps[2].wait()
    share_start(small, small_share)
    line_step(rows, row_sems, place, last, 1)
    for k in range(1, ctx_count):
        qkv_wait[k - 1].wait_recv()
        piece_on(k)
    remote(
        out_own, out_pair.at[group, 1 - line], pair_send.at[0], pair_recv.at[0], ctx=side
    ).wait_recv()
    keeps[1].wait()
    share_start(out_pair, out_share)
    line_step(rows, row_sems, place, last, 2)
    for k in range(ctx_count):
        piece_copy(0, across, k, across).wait_recv()
        piece_copy(2, across, k, beside).start()
    share_step(small, small_share)
    for step in range(3, last + 1):
        line_step(rows, row_sems, place, last, step)
    share_step(out_pair, out_share)
    line_finish(rows, row_sems, place, last)
    for copy in number_wait:
        copy.wait_recv()
    for copy in qkv_start + small_start + number_start:
        copy.wait_send()
    pair.wait_send()
    for k in range(ctx_count):
        piece_copy(1, beside, k, beside).wait_recv()
        piece_copy(2, corner, k, beside).wait_recv()
        for way in range(3):
            piece_copy(way, group, k, beside).wait_send()
    share_finish(small, small_share)
    share_finish(out_pair, out_share)
    for i in (0, 3, 4):
        keeps[i].wait()


def opening(ctx_count, call_id, own, qkv_own, out_own, small_own, number_own):
    def out(lead, array):
        return jax.ShapeDtypeStruct(lead + array.shape, array.dtype)

    dma = pltpu.SemaphoreType.DMA
    return pl.pallas_call(
        functools.partial(opening_kernel, ctx_count),
        out_shape=[
            out((ctx_count,), own),
            out((4,), qkv_own),
            out((4, 2), out_own),
            out((4, ctx_count), small_own),
            out((ctx_count,), number_own),
        ],
        in_specs=[VMEM] * 5,
        out_specs=[ANY] * 5,
        scratch_shapes=[
            dma((5,)),
            dma((1,)),
            dma((1,)),
            dma((ctx_count, 3)),
            dma((ctx_count,)),
            dma((3, ctx_count)),
            dma((4, ctx_count)),
        ]
        + [dma((ctx_count,))] * 6
        + [dma((3,)), dma((4,))] * 2,
        compiler_params=pltpu.CompilerParams(collective_id=call_id, has_side_effects=True),
        name="opening",
    )(own, qkv_own, out_own, small_own, number_own)


def group_reduce(blocks, beside_in, pair_sums, across_in, settled, sems):
    core_send, core_recv, far_send, far_recv = sems
    group, beside, across, corner = fsdp_place()
    rows = settled.shape[0]

    def core_copy(slot, block):
        return remote(
            blocks.at[block],
            beside_in.at[slot],
            core_send.at[slot],
            core_recv.at[slot],
            fsdp=beside,
        )

    far = remote(pair_sums.at[1], across_in, far_send.at[0], far_recv.at[0], fsdp=across)
    core_copy(1, corner).start()
    core_copy(0, beside).start()
    yield
    core_copy(1, corner).wait_recv()
    add_rows(pair_sums.at[1], (blocks.at[across], beside_in.at[1]), rows)
    far.start()
    core_copy(0, beside).wait_recv()
    add_rows(pair_sums.at[0], (blocks.at[group], beside_in.at[0]), rows)
    yield
    far.wait_recv()
    add_rows(settled, (pair_sums.at[0], across_in), rows)
    yield
    core_copy(1, corner).wait_send()
    core_copy(0, beside).wait_send()
    far.wait_send()
    yield


def closing_kernel(ctx_count, part, weight, pair, plain, small, *refs):
    total, landed, pair_total, plain_total, small_total = refs[:5]
    line_slots, weight_slots, pair_slots, plain_slots = (
        refs[5:9],
        refs[9:13],
        refs[13:17],
        refs[17:20],
    )
    pair_in, small_in, small_sums, small_across = refs[20:24]
    sems = refs[24:]
    line_sems, weight_sems, pair_sems, plain_sems = sems[:5], sems[5:9], sems[9:13], sems[13:17]
    keep_sem, half_send, half_recv = sems[17:20]
    weight_spread, small_spread, (group_send, group_recv) = sems[20:22], sems[22:24], sems[24:26]
    here, level, line, side = line_place()
    group = lax.axis_index("fsdp")
    greet_all(ctx_count)
    turns = scatter_turns(ctx_count // 2 - 1, part, total, *line_slots, *line_sems)
    settled, pair_settled = weight_slots[3], pair_slots[3]
    weight_steps = group_reduce(weight, *weight_slots, weight_sems)
    pair_steps = group_reduce(pair, *pair_slots, pair_sems)
    plain_steps = group_reduce(plain, *plain_slots, plain_total, plain_sems)
    small_start, small_wait = spread(
        lambda peer: small.at[:, peer], lambda source: small_in.at[source], small_spread, ctx_count
    )
    for copy in small_start:
        copy.start()
    next(weight_steps)
    next(turns)
    next(weight_steps)
    next(pair_steps)
    next(turns)
    next(pair_steps)
    next(plain_steps)
    for copy in small_wait:
        copy.wait_recv()
    small_sum = small[:, here]
    for k in range(1, ctx_count):
        small_sum = small_sum + small_in[(here + k) % ctx_count]
    small_sums[...] = small_sum
    group_copies = [
        remote(
            small_sums.at[(group + k) % 4],
            small_across.at[k],
            group_send.at[k],
            group_recv.at[k],
            fsdp=(group + k) % 4,
        )
        for k in range(1, 4)
    ]
    for copy in group_copies:
        copy.start()
    next(weight_steps)
    piece = settled.shape[0] // ctx_count
    weight_start, weight_wait = spread(
        lambda peer: settled.at[pl.ds(pl.multiple_of(peer * piece, piece), piece)],
        lambda source: landed.at[source],
        weight_spread,
        ctx_count,
    )
    for copy in weight_start:
        copy.start()
    keep = pltpu.make_async_copy(
        settled.at[pl.ds(pl.multiple_of(here * piece, piece), piece)],
        landed.at[here],
        keep_sem.at[0],
    )
    keep.start()
    next(plain_steps)
    next(turns)
    next(pair_steps)
    half = pair_total.shape[0]
    half_copy = remote(
        pair_settled.at[pl.ds(pl.multiple_of((1 - line) * half, half), half)],
        pair_in,
        half_send.at[0],
        half_recv.at[0],
        ctx=side,
    )
    half_copy.start()
    for copy in group_copies:
        copy.wait_recv()
    small_total[...] = small_sums[group] + small_across[1] + small_across[2] + small_across[3]
    for step in turns:
        pass
    next(plain_steps)
    half_copy.wait_recv()
    kept = pair_settled.at[pl.ds(pl.multiple_of(line * half, half), half)]
    add_rows(pair_total, (kept, pair_in), half)
    for copy in weight_wait:
        copy.wait_recv()
    for copy in weight_start + small_start + group_copies:
        copy.wait_send()
    half_copy.wait_send()
    next(weight_steps)
    next(pair_steps)
    next(plain_steps)
    keep.wait()


def closing(ctx_count, call_id, part, weight, pair, plain, small):
    rows, width = part.shape[1:]
    half = ctx_count // 2
    dma = pltpu.SemaphoreType.DMA
    slots = pltpu.VMEM((half, rows, width), part.dtype)

    def group_slots(array):
        one = pltpu.VMEM(array.shape[1:], array.dtype)
        two = pltpu.VMEM((2,) + array.shape[1:], array.dtype)
        return [two, two, one, one]

    block, columns = weight.shape[1:]
    pair_half = (pair.shape[1] // 2, pair.shape[2])
    return pl.pallas_call(
        functools.partial(closing_kernel, ctx_count),
        out_shape=[
            jax.ShapeDtypeStruct((rows, width), jnp.float32),
            jax.ShapeDtypeStruct((ctx_count, block // ctx_count, columns), weight.dtype),
            jax.ShapeDtypeStruct(pair_half, jnp.float32),
            jax.ShapeDtypeStruct(plain.shape[1:], jnp.float32),
            jax.ShapeDtypeStruct(small.shape[2:], small.dtype),
        ],
        in_specs=[VMEM] * 5,
        out_specs=[VMEM] * 5,
        scratch_shapes=[slots] * 4
        + group_slots(weight)
        + group_slots(pair)
        + group_slots(plain)[:3]
        + [
            pltpu.VMEM(pair_half, pair.dtype),
            pltpu.VMEM((ctx_count, 4) + small.shape[2:], small.dtype),
            pltpu.VMEM((4,) + small.shape[2:], small.dtype),
            pltpu.VMEM((4,) + small.shape[2:], small.dtype),
        ]
        + [dma((half,))] * 5
        + [dma((2,)), dma((2,)), dma((1,)), dma((1,))] * 3
        + [dma((1,))] * 3
        + [dma((ctx_count,))] * 4
        + [dma((4,))] * 2,
        compiler_params=pltpu.CompilerParams(
            collective_id=call_id, has_side_effects=True, vmem_limit_bytes=56 * 2**20
        ),
        name="closing",
    )(part, weight, pair, plain, small)


def scaled_rows(values):
    return values * lax.rsqrt(jnp.mean(values * values, axis=-1, keepdims=True) + EPSILON)


def attend_kernel(
    inputs,
    gain,
    weight,
    bias,
    cosine,
    sine,
    columns,
    lines,
    out_weight,
    normed,
    queries,
    keys,
    values,
    attended,
    log_totals,
    part,
):
    rows = inputs.shape[0]
    low = jnp.bfloat16
    heads = queries.shape[1] // HD

    @pl.loop(0, rows // SPAN)
    def project(index):
        here = span_of(index)
        unit = scaled_rows(inputs[here, :].astype(jnp.float32)) * gain[...]
        normed[here, :] = unit.astype(low)
        projected = flat_dot(normed[here, :], weight[...]) + bias[...]
        turn, tilt = cosine[here, :], sine[here, :]
        for head in range(heads):
            own = slice(head * HD, (head + 1) * HD)
            query = projected[:, own]
            query = query * turn + pltpu.roll(query, HD // 2, 1) * tilt
            queries[here, own] = (query * HD ** (-0.5)).astype(low)
            key = projected[:, (heads + head) * HD : (heads + head + 1) * HD]
            keys[here, own] = (key * turn + pltpu.roll(key, HD // 2, 1) * tilt).astype(low)
            values[here, own] = projected[
                :, (2 * heads + head) * HD : (2 * heads + head + 1) * HD
            ].astype(low)

    @pl.loop(0, rows // SPAN)
    def attend(index):
        here = span_of(index)
        position, segment = columns[here, 0:1], columns[here, 1:2]
        allowed = (lines[1:2, :] == segment) & (lines[0:1, :] <= position)
        allowed = allowed | (lines[0:1, :] == position)
        for head in range(heads):
            own = slice(head * HD, (head + 1) * HD)
            scores = turned_dot(queries[here, own], keys[:, own])
            scores = jnp.where(allowed, scores, -1e30)
            highest = jnp.max(scores, axis=1, keepdims=True)
            weights = jnp.exp(scores - highest)
            sums = jnp.sum(weights, axis=1, keepdims=True)
            log_totals[here, head : head + 1] = highest + jnp.log(sums)
            probs = (weights * (1.0 / sums)).astype(low)
            attended[here, own] = flat_dot(probs, values[:, own]).astype(low)
        part[here, :] = flat_dot(attended[here, :], out_weight[...]).astype(low)


def attend(inputs, gain, weight, bias, cosine, sine, columns, lines, out_weight):
    rows, width = inputs.shape
    wide = out_weight.shape[0]
    low = jnp.bfloat16
    shape = jax.ShapeDtypeStruct
    return pl.pallas_call(
        attend_kernel,
        out_shape=[shape((rows, width), low)]
        + [shape((rows, wide), low)] * 4
        + [shape((rows, wide // HD), jnp.float32), shape((rows, width), low)],
        in_specs=[VMEM] * 9,
        out_specs=[VMEM] * 7,
        compiler_params=pltpu.CompilerParams(vmem_limit_bytes=40 * 2**20),
        cost_estimate=pl.CostEstimate(
            flops=2 * rows * width * 4 * wide + 4 * rows * rows * wide,
            bytes_accessed=20 * 2**20,
            transcendentals=rows * rows * wide // HD,
        ),
        name="attend",
    )(inputs, gain, weight, bias, cosine, sine, columns, lines, out_weight)


def attend_back_kernel(
    branch,
    out_weight,
    queries,
    keys,
    values,
    attended,
    totals,
    cosine,
    sine,
    columns,
    lines,
    inputs,
    normed,
    weight,
    part,
    grad_weight,
    grad_out,
    grad_bias,
    grad_gain,
    grads,
    grad_attended,
    grad_keys,
    grad_values,
    gain_sum,
):
    rows, width = branch.shape
    low = jnp.bfloat16
    full = jnp.float32
    wide = queries.shape[1]
    heads = wide // HD

    @pl.loop(0, rows // SPAN)
    def into_heads(index):
        here = span_of(index)
        grad_attended[here, :] = turned_dot(branch[here, :], out_weight[...]).astype(low)

    for head in range(heads):
        own = slice(head * HD, (head + 1) * HD)
        grad_keys[...] = jnp.zeros_like(grad_keys)
        grad_values[...] = jnp.zeros_like(grad_values)

        @pl.loop(0, rows // SPAN)
        def scores_back(index):
            here = span_of(index)
            position, segment = lines[0:1, here], lines[1:2, here]
            allowed = (columns[:, 1:2] == segment) & (columns[:, 0:1] <= position)
            allowed = allowed | (columns[:, 0:1] == position)
            query, grad = queries[here, own], grad_attended[here, own]
            scores = jnp.where(allowed, turned_dot(keys[:, own], query), -1e30)
            probs = jnp.exp(scores - totals[head : head + 1, here])
            grad_probs = turned_dot(values[:, own], grad)
            delta = jnp.sum(probs * grad_probs, axis=0, keepdims=True)
            grad_scores = (probs * (grad_probs - delta)).astype(low)
            grad_keys[...] += flat_dot(grad_scores, query)
            grad_values[...] += flat_dot(probs.astype(low), grad)
            grad_query = flat_dot(grad_scores.T, keys[:, own]) * HD ** (-0.5)
            grads[here, own] = (
                grad_query * cosine[here, :] + pltpu.roll(grad_query * sine[here, :], HD // 2, 1)
            ).astype(low)

        @pl.loop(0, rows // SPAN)
        def keys_back(index):
            here = span_of(index)
            grad_key = grad_keys[here, :]
            grads[here, (heads + head) * HD : (heads + head + 1) * HD] = (
                grad_key * cosine[here, :] + pltpu.roll(grad_key * sine[here, :], HD // 2, 1)
            ).astype(low)
            grads[here, (2 * heads + head) * HD : (2 * heads + head + 1) * HD] = grad_values[
                here, :
            ].astype(low)

    gain_sum[...] = jnp.zeros_like(gain_sum)
    grad_bias[...] = jnp.zeros_like(grad_bias)

    @pl.loop(0, rows // SPAN)
    def project_back(index):
        here = span_of(index)
        grad_rows = turned_dot(grads[here, :], weight[...])
        part[here, :] = grad_rows.astype(low)
        unit = scaled_rows(inputs[here, :].astype(full))
        gain_sum[...] += jnp.sum(grad_rows * unit, axis=0, keepdims=True)
        grad_bias[...] += jnp.sum(grads[here, :].astype(full), axis=0, keepdims=True)

    grad_gain[...] = gain_sum[...]

    @pl.loop(0, width // SPAN)
    def weight_back(index):
        here = span_of(index)
        grad_weight[here, :] = flat_dot(normed[:, here].T, grads[...]).astype(low)

    attended_turned = attended[...].T

    @pl.loop(0, width // (2 * SPAN))
    def out_back(index):
        here = span_of(index, 2 * SPAN)
        grad_out[:, here] = flat_dot(attended_turned, branch[:, here]).astype(low)


def attend_back(
    branch,
    out_weight,
    queries,
    keys,
    values,
    attended,
    totals,
    cosine,
    sine,
    columns,
    lines,
    inputs,
    normed,
    weight,
):
    rows, width = branch.shape
    wide = out_weight.shape[0]
    low = jnp.bfloat16
    full = jnp.float32
    shape = jax.ShapeDtypeStruct
    return pl.pallas_call(
        attend_back_kernel,
        out_shape=[
            shape((rows, width), low),
            shape(weight.shape, low),
            shape((wide, width), low),
            shape((1, 3 * wide), full),
            shape((1, width), full),
        ],
        in_specs=[VMEM] * 14,
        out_specs=[VMEM] * 5,
        scratch_shapes=[
            pltpu.VMEM((rows, 3 * wide), low),
            pltpu.VMEM((rows, wide), low),
            pltpu.VMEM((rows, HD), full),
            pltpu.VMEM((rows, HD), full),
            pltpu.VMEM((1, width), full),
        ],
        compiler_params=pltpu.CompilerParams(vmem_limit_bytes=56 * 2**20),
        cost_estimate=pl.CostEstimate(
            flops=2 * rows * width * 8 * wide + 10 * rows * rows * wide,
            bytes_accessed=35 * 2**20,
            transcendentals=rows * rows * wide // HD,
        ),
        name="attend_back",
    )(
        branch,
        out_weight,
        queries,
        keys,
        values,
        attended,
        totals,
        cosine,
        sine,
        columns,
        lines,
        inputs,
        normed,
        weight,
    )


def gate_back_kernel(upstream, scale, gate_up, weight_out, grads, scaled):
    low = jnp.bfloat16
    half = gate_up.shape[1] // 2
    scaled[...] = (scale[...] * upstream[...].astype(jnp.float32)).astype(low)
    grad_unit = turned_dot(scaled[...], weight_out[...])
    gate, up = gate_up[:, :half], gate_up[:, half:]
    sigmoid = 1.0 / (1.0 + jnp.exp(-gate))
    grad_gate = grad_unit * up * (sigmoid * (1.0 + gate * (1.0 - sigmoid)))
    grad_up = grad_unit * (gate * sigmoid)
    grads[...] = jnp.concatenate([grad_gate.astype(low), grad_up.astype(low)], axis=1)


def gate_back(upstream, scale, gate_up, weight_out):
    rows, width = upstream.shape
    hidden = weight_out.shape[0]
    low = jnp.bfloat16

    def block(columns):
        return pl.BlockSpec((SPAN, columns), lambda i: (i, 0))

    return pl.pallas_call(
        gate_back_kernel,
        grid=(rows // SPAN,),
        out_shape=[
            jax.ShapeDtypeStruct((rows, 2 * hidden), low),
            jax.ShapeDtypeStruct((rows, width), low),
        ],
        in_specs=[
            block(width),
            block(1),
            block(2 * hidden),
            pl.BlockSpec((hidden, width), lambda i: (0, 0)),
        ],
        out_specs=[block(2 * hidden), block(width)],
        compiler_params=pltpu.CompilerParams(vmem_limit_bytes=48 * 2**20),
        cost_estimate=pl.CostEstimate(
            flops=2 * rows * width * hidden,
            bytes_accessed=rows * (12 * hidden + 4 * width) + 2 * hidden * width,
            transcendentals=rows * hidden,
        ),
        name="gate_back",
    )(upstream, scale, gate_up, weight_out)


def deal_kernel(pieces, weight, dealt):
    ctx_count = dealt.shape[0]
    width = dealt.shape[2] // pieces
    for c in range(ctx_count):
        dealt[c] = jnp.concatenate(
            [
                weight[:, (q * ctx_count + c) * width : (q * ctx_count + c + 1) * width]
                for q in range(pieces)
            ],
            axis=1,
        )


def deal_columns(weight, ctx_count, pieces):
    rows, columns = weight.shape
    return pl.pallas_call(
        functools.partial(deal_kernel, pieces),
        out_shape=jax.ShapeDtypeStruct((ctx_count, rows, columns // ctx_count), weight.dtype),
        name="deal_columns",
    )(weight)


def collect_kernel(pieces, dealt, whole):
    ctx_count = dealt.shape[0]
    width = dealt.shape[2] // pieces
    whole[...] = jnp.concatenate(
        [
            dealt[c, :, q * width : (q + 1) * width]
            for q in range(pieces)
            for c in range(ctx_count)
        ],
        axis=1,
    ).astype(whole.dtype)


def collect_columns(dealt, pieces):
    ctx_count, rows, columns = dealt.shape
    return pl.pallas_call(
        functools.partial(collect_kernel, pieces),
        out_shape=jax.ShapeDtypeStruct((rows, columns * ctx_count), jnp.float32),
        name="collect_columns",
    )(dealt)


def heads_kernel(order, dealt, whole):
    pairs = dealt.shape[0] * 2
    for place, head in enumerate(order):
        for which in range(3):
            column = (which * 2 + place % 2) * HD
            target = (which * pairs + head) * HD
            whole[:, target : target + HD] = dealt[
                place // 2, :, column : column + HD
            ].astype(whole.dtype)


def collect_heads(dealt, order):
    ctx_count, rows, columns = dealt.shape
    return pl.pallas_call(
        functools.partial(heads_kernel, order),
        out_shape=jax.ShapeDtypeStruct((rows, columns * ctx_count), jnp.float32),
        name="collect_heads",
    )(dealt)


def over(axis, array, dim=0):
    return lax.all_gather(array, axis, axis=dim, tiled=True)


def reduce_over(axis, array, dim=0):
    return lax.psum_scatter(array, axis, scatter_dimension=dim, tiled=True)


def exchange(array):
    return lax.all_to_all(array, "ctx", split_axis=0, concat_axis=0, tiled=True)


def transposed_dot(left, right):
    return lax.dot_general(
        left, right, (((0,), (0,)), ((), ())), preferred_element_type=jnp.float32
    )


def dot_transposed(left, right):
    return lax.dot_general(
        left, right, (((1,), (1,)), ((), ())), preferred_element_type=jnp.float32
    )


def split_plan(
    hidden_in,
    segments,
    block_pairs,
    routes,
    out_grad,
    norm_gain_attn,
    qkv_weight,
    qkv_bias,
    out_weight,
    norm_gain_ffn,
    router_weight,
    shared_gate_weight,
    shared_in_weight,
    shared_out_weight,
    expert_in_weight,
    expert_out_weight,
):
    low = jnp.bfloat16
    full = jnp.float32
    tokens_dev, width = hidden_in.shape[1:]
    block_len = tokens_dev // 2
    ctx_count = lax.axis_size("ctx")
    fsdp_count = lax.axis_size("fsdp")
    ctx_rank = lax.axis_index("ctx")
    dev_count = ctx_count * fsdp_count
    row_len = ctx_count * tokens_dev
    early = width * 3 // 8
    head_count = width // HD
    shard = qkv_weight.shape[0]
    expert_count = router_weight.shape[1]
    shared_shard = shared_out_weight.shape[0]
    shared_width = fsdp_count * shared_shard
    expert_width = expert_out_weight.shape[1] * fsdp_count
    pair_rank = ctx_rank // 2
    side = ctx_rank % 2
    pairs = ctx_count // 2
    head_order = [j + (p * 2 + t) * pairs for j in range(pairs) for p in range(2) for t in range(2)]

    small = jnp.concatenate(
        [
            norm_gain_attn,
            norm_gain_ffn,
            shared_gate_weight,
            router_weight.T.reshape(-1),
            qkv_bias,
        ]
    )
    small_count = small.shape[0]
    small = jnp.pad(small, (0, 16 * HD - small_count)).reshape(16, HD)
    own_numbers = jnp.concatenate(
        [routes.reshape(tokens_dev, -1).T, segments.reshape(1, tokens_dev)], axis=0
    )
    number_count = own_numbers.shape[0]
    own_numbers = jnp.pad(own_numbers, ((0, 8 - number_count), (0, 0)))
    qkv_parts = (
        qkv_weight.reshape(shard, 3, head_count, HD)[:, :, jnp.array(head_order)]
        .reshape(shard, 3, ctx_count, 2 * HD)
        .transpose(2, 0, 1, 3)
        .reshape(ctx_count, shard, 6 * HD)
    )
    own_inputs = hidden_in.reshape(tokens_dev, width)
    row_inputs, qkv_c, out_pair, small_all, numbers = opening(
        ctx_count, 1, own_inputs, qkv_parts, out_weight, small, own_numbers
    )
    qkv_c = qkv_c.reshape(width, 6 * HD)
    out_c = lax.dynamic_index_in_dim(
        out_pair.reshape(2, 2 * HD, width), side, 0, keepdims=False
    )
    small_all = small_all.reshape(dev_count, 16 * HD)
    gain_attn = small_all[:, :shard].reshape(width).astype(full)
    gain_ffn = small_all[:, shard : 2 * shard].reshape(width).astype(full)
    gate_full = small_all[:, 2 * shard : 3 * shard].reshape(width)
    router_t = (
        small_all[:, 3 * shard : (3 + expert_count) * shard]
        .reshape(dev_count, expert_count, shard)
        .transpose(1, 0, 2)
        .reshape(expert_count, width)
    )
    bias_full = small_all[:, (3 + expert_count) * shard : small_count].reshape(3, head_count, HD)
    router_gate = jnp.concatenate([router_t, gate_full[None, :]], axis=0)
    row_seg = numbers[:, number_count - 1].reshape(row_len)
    routed_here = jnp.any(numbers[:, : number_count - 1] == ctx_rank, axis=1).reshape(row_len)

    shared_in_weight, numbers = lax.optimization_barrier((shared_in_weight, numbers))
    expert_outer = over("fsdp", expert_out_weight[0])
    early_upstream = over("ctx", out_grad.reshape(tokens_dev, width)[:, :early])
    inner_parts = deal_columns(shared_in_weight, ctx_count, 2 * fsdp_count)
    expert_inner = over("fsdp", expert_in_weight[0])
    inner_parts = exchange(inner_parts)
    my_heads = [pair_rank + (side * 2 + t) * pairs for t in range(2)]
    bias_c = jnp.concatenate(
        [lax.dynamic_index_in_dim(bias_full, h, 1, keepdims=False) for h in my_heads], axis=1
    ).reshape(6 * HD)

    offsets = jnp.arange(block_len, dtype=jnp.int32)
    positions = (block_pairs[:, None] * block_len + offsets[None, :]).reshape(row_len)
    inputs = own_inputs.astype(full)
    row_inputs = row_inputs.reshape(row_len, width)
    half_len = HD // 2
    frequency = THETA ** (-jnp.arange(half_len, dtype=full) / half_len)
    places = positions.astype(full)
    angles = places[:, None] * frequency[None, :]
    cosine, sine = jnp.cos(angles), jnp.sin(angles)
    cosine = jnp.concatenate([cosine, cosine], axis=1)
    sine = jnp.concatenate([-sine, sine], axis=1)
    key_seg = row_seg.astype(full)
    query_seg = jnp.where(row_seg >= 0, key_seg, -2.0)
    query_marks = jnp.stack([places, query_seg])
    key_marks = jnp.stack([places, key_seg])
    row_normed, queries, keys, values, attended_row, log_totals, branch_part = attend(
        row_inputs,
        gain_attn[None, :],
        qkv_c,
        bias_c.astype(full)[None, :],
        cosine,
        sine,
        query_marks.T,
        key_marks,
        out_c,
    )
    branch_part, inner_parts, early_upstream, expert_outer = lax.optimization_barrier(
        (branch_part, inner_parts, early_upstream, expert_outer)
    )
    branch = line_scatter(ctx_count, 2, branch_part.reshape(ctx_count, tokens_dev, width))
    middle = inputs + branch
    normed_ffn = rms_scale(middle, gain_ffn).astype(low)

    row_ffn, inner_c, outer_c = line_gather(
        ctx_count,
        4,
        normed_ffn,
        inner_parts.reshape(ctx_count * shard, 2 * shared_width),
        shared_out_weight,
    )
    row_ffn = row_ffn.reshape(row_len, width)
    row_ffn, late_grad = lax.optimization_barrier((row_ffn, out_grad))
    late_upstream = over("ctx", late_grad.reshape(tokens_dev, width)[:, early:])
    inner_c = inner_c.reshape(width, 2 * shared_width)
    outer_c = outer_c.reshape(shared_width, width)
    row_logits = dot_transposed(row_ffn, router_gate)
    row_probs = jax.nn.softmax(row_logits[:, :expert_count], axis=-1)
    expert_ids = jnp.arange(expert_count, dtype=jnp.int32)
    here = jnp.where(
        routed_here, jnp.sum(jnp.where(expert_ids[None, :] == ctx_rank, row_probs, 0.0), axis=1), 0.0
    )
    row_gate = jax.nn.sigmoid(row_logits[:, expert_count])
    expert_gu = matmul_low(row_ffn, expert_inner)
    expert_hidden = swiglu_mix(expert_gu, expert_width).astype(low)
    expert_result = matmul_low(expert_hidden, expert_outer).astype(low).astype(full)
    row_shared, expert_result = lax.optimization_barrier((row_ffn, expert_result))
    shared_gu = matmul_low(row_shared, inner_c)
    shared_hidden = swiglu_mix(shared_gu, shared_width).astype(low)
    shared_out = matmul_low(shared_hidden, outer_c)
    shared_out, late_upstream = lax.optimization_barrier((shared_out, late_upstream))
    row_upstream = lax.optimization_barrier(
        jnp.concatenate([early_upstream, late_upstream], axis=1)
    )
    upstream_row = row_upstream.astype(full)
    out_part = (row_gate[:, None] * shared_out + here[:, None] * expert_result).astype(low)
    gate_dot = jnp.sum(upstream_row * shared_out, axis=1)
    expert_dot = jnp.where(routed_here, jnp.sum(upstream_row * expert_result, axis=1), 0.0)
    out_landed = reduce_over("ctx", out_part)

    row_upstream, out_part = lax.optimization_barrier((row_upstream, out_part))
    grad_expert_gu, grad_buffers = gate_back(row_upstream, here[:, None], expert_gu, expert_outer)
    sum_expert_outer = reduce_over("fsdp", transposed_dot(expert_hidden, grad_buffers).astype(low))
    grad_rows = dot_transposed(grad_expert_gu, expert_inner).astype(low)
    row_upstream, grad_rows = lax.optimization_barrier((row_upstream, grad_rows))
    grad_shared_gu, grad_shared_out = gate_back(
        row_upstream, row_gate[:, None], shared_gu, outer_c
    )
    grad_inner = transposed_dot(row_ffn, grad_shared_gu).astype(low)
    sum_inner_c = reduce_over("fsdp", grad_inner)
    grad_ffn_part = (
        dot_transposed(grad_shared_gu, inner_c) + grad_rows.astype(full)
    ).astype(low)
    dots = jnp.stack([gate_dot, expert_dot]).reshape(2, ctx_count, tokens_dev).transpose(1, 0, 2)
    grad_ffn_part, grad_inner = lax.optimization_barrier((grad_ffn_part, grad_inner))
    grad_normed, own_dots, grad_expert_inner = line_scatter(
        ctx_count,
        6,
        grad_ffn_part.reshape(ctx_count, tokens_dev, width),
        jnp.pad(dots, ((0, 0), (0, 6), (0, 0))),
        row_ffn,
        grad_expert_gu,
    )
    sum_expert_inner = reduce_over("fsdp", grad_expert_inner)
    hidden_out = (middle + out_landed.astype(full)).astype(low).reshape(1, tokens_dev, width)

    own_logits = dot_transposed(normed_ffn, router_gate)
    router_probs = jax.nn.softmax(own_logits[:, :expert_count], axis=-1)
    gate_value = jax.nn.sigmoid(own_logits[:, expert_count])
    grad_gate_logit = gate_value * (1.0 - gate_value) * jnp.sum(own_dots[:, 0], axis=0)
    grad_choice = own_dots[:, 1].T
    grad_logits = router_probs * (
        grad_choice - jnp.sum(router_probs * grad_choice, axis=1, keepdims=True)
    )
    grad_small = jnp.concatenate([grad_logits, grad_gate_logit[:, None]], axis=1).astype(low)
    grad_router_gate = transposed_dot(grad_small, normed_ffn)
    grad_normed = grad_normed + matmul_low(grad_small, router_gate)
    unused_norm, norm_pull = jax.vjp(rms_scale, middle, gain_ffn)
    grad_middle_norm, grad_gain_ffn = norm_pull(grad_normed)
    grad_middle = out_grad.reshape(tokens_dev, width).astype(full) + grad_middle_norm

    grad_branch, sum_expert_outer, hidden_out = lax.optimization_barrier(
        (grad_middle.astype(low), sum_expert_outer, hidden_out)
    )
    row_branch, grad_outer = product_gather(
        ctx_count, 3, grad_branch, shared_hidden, grad_shared_out
    )
    row_branch, sum_inner_c = lax.optimization_barrier(
        (row_branch.reshape(row_len, width), sum_inner_c)
    )
    sum_inner = collect_columns(
        exchange(sum_inner_c.reshape(ctx_count, shard, 2 * shared_width)), 2 * fsdp_count
    )
    grad_attn_part, grad_qkv_c, grad_out_c, grad_bias_c, grad_gain_attn = attend_back(
        row_branch,
        out_c,
        queries,
        keys,
        values,
        attended_row,
        log_totals.T,
        cosine,
        sine,
        key_marks.T,
        query_marks,
        row_inputs,
        row_normed,
        qkv_c,
    )
    grad_out_c = grad_out_c.reshape(2, HD, width)
    padded_out = jnp.concatenate(
        [jnp.where(side == p, grad_out_c, jnp.zeros_like(grad_out_c)) for p in range(2)], axis=0
    )
    grad_attn_part, sum_inner = lax.optimization_barrier((grad_attn_part, sum_inner))
    grad_bias_c = grad_bias_c.reshape(3, 1, 2, HD)
    mine = (jnp.arange(ctx_count) == ctx_rank)[None, :, None, None]
    places_of = [head_order.index(h) for h in range(head_count)]
    grad_bias = (
        jnp.where(mine, grad_bias_c, 0.0)
        .reshape(3, pairs, 2, 2, HD)
        .transpose(0, 2, 3, 1, 4)
        .reshape(dev_count, -1)
    )
    small_grads = jnp.concatenate(
        [
            grad_gain_attn.reshape(dev_count, shard),
            grad_gain_ffn.reshape(dev_count, shard),
            grad_router_gate.reshape(expert_count + 1, dev_count, shard)
            .transpose(1, 0, 2)
            .reshape(dev_count, (expert_count + 1) * shard),
            grad_bias,
        ],
        axis=1,
    )
    small_grads = jnp.pad(small_grads, ((0, 0), (0, 8 * HD - small_count)))
    grad_normed_attn, sum_qkv_c, sum_out, sum_outer, sums = closing(
        ctx_count,
        5,
        grad_attn_part.reshape(ctx_count, tokens_dev, width),
        grad_qkv_c.reshape(fsdp_count, ctx_count * shard, 6 * HD),
        padded_out,
        grad_outer.reshape(fsdp_count, shared_shard, width),
        small_grads.reshape(fsdp_count, ctx_count, 8, HD),
    )
    sums = sums.reshape(8 * HD)[:small_count]
    sum_qkv = collect_heads(sum_qkv_c, head_order)
    unused_norm, first_pull = jax.vjp(lambda v: rms_scale(v, gain_attn), inputs)
    input_grad = grad_middle + first_pull(grad_normed_attn)[0]
    sum_router = sums[2 * shard : (2 + expert_count) * shard].reshape(expert_count, shard).T
    return (
        hidden_out,
        input_grad.reshape(1, tokens_dev, width),
        sums[:shard],
        sum_qkv,
        sums[(3 + expert_count) * shard :],
        sum_out,
        sums[shard : 2 * shard],
        sum_router,
        sums[(2 + expert_count) * shard : (3 + expert_count) * shard],
        sum_inner,
        sum_outer,
        sum_expert_inner.astype(full)[None],
        sum_expert_outer.astype(full)[None],
    )


def local(*arrays):
    width = arrays[0].shape[2]
    ctx_count = lax.axis_size("ctx")
    shard = arrays[6].shape[0]
    fits = (
        width == 2 * ctx_count * HD
        and 2 * shard == HD
        and ctx_count % 2 == 0
        and lax.axis_size("fsdp") * ctx_count * shard == width
        and arrays[14].shape[0] == 1
    )
    return split_plan(*arrays) if fits else gathered_plan(*arrays)


def solution(mesh):
    in_specs = (
        P("fsdp", "ctx", None),
        P("fsdp", "ctx"),
        P(),
        P("fsdp", "ctx", None),
        P("fsdp", "ctx", None),
        P(("fsdp", "ctx")),
        P(("fsdp", "ctx"), None),
        P(("fsdp", "ctx")),
        P(("fsdp", "ctx"), None),
        P(("fsdp", "ctx")),
        P(("fsdp", "ctx"), None),
        P(("fsdp", "ctx")),
        P(("fsdp", "ctx"), None),
        P(("fsdp", "ctx"), None),
        P("ctx", "fsdp", None),
        P("ctx", "fsdp", None),
    )
    out_specs = (
        P("fsdp", "ctx", None),
        P("fsdp", "ctx", None),
        P(("fsdp", "ctx")),
        P(("fsdp", "ctx"), None),
        P(("fsdp", "ctx")),
        P(("fsdp", "ctx"), None),
        P(("fsdp", "ctx")),
        P(("fsdp", "ctx"), None),
        P(("fsdp", "ctx")),
        P(("fsdp", "ctx"), None),
        P(("fsdp", "ctx"), None),
        P("ctx", "fsdp", None),
        P("ctx", "fsdp", None),
    )
    return jax.shard_map(local, mesh=mesh, in_specs=in_specs, out_specs=out_specs, check_vma=False)
```

```python
import functools

import jax
import jax.numpy as jnp
from jax import lax
from jax.experimental import pallas as pl
from jax.experimental.pallas import tpu as pltpu
from jax.sharding import PartitionSpec as P

HD = 128


EPSILON = 1e-06
THETA = 1000000.0
heads_per_group = 4


def rms_scale(values, gain_vec):
    return (
        values * lax.rsqrt(jnp.mean(values * values, axis=-1, keepdims=True) + EPSILON) * gain_vec
    )


def rotate(values, positions):
    half_len = values.shape[-1] // 2
    frequency = THETA ** (-jnp.arange(half_len, dtype=jnp.float32) / half_len)
    angles = positions.astype(jnp.float32)[:, None] * frequency[None, :]
    cosine = jnp.cos(angles)[:, None, :]
    sine_part = jnp.sin(angles)[:, None, :]
    first_half = values[..., :half_len]
    second = values[..., half_len:]
    return jnp.concatenate(
        [first_half * cosine - second * sine_part, second * cosine + first_half * sine_part],
        axis=-1,
    )


def visible(query_pos, query_seg, key_pos, key_seg):
    same_doc = (key_seg[None, :] == query_seg[:, None]) & (query_seg[:, None] >= 0)
    causal = key_pos[None, :] <= query_pos[:, None]
    return same_doc & causal | (key_pos[None, :] == query_pos[:, None])


def swiglu_mix(gate_up, hidden_width):
    return jax.nn.silu(gate_up[..., :hidden_width]) * gate_up[..., hidden_width:]


def matmul_low(left, right):
    return jnp.dot(left, right, preferred_element_type=jnp.float32)


def gathered_plan(
    hidden_in,
    segments,
    block_pairs,
    routes,
    out_grad,
    norm_gain_attn,
    qkv_weight,
    qkv_bias,
    out_weight,
    norm_gain_ffn,
    router_weight,
    shared_gate_weight,
    shared_in_weight,
    shared_out_weight,
    expert_in_weight,
    expert_out_weight,
):
    tokens_dev = hidden_in.shape[1]
    model_width = hidden_in.shape[2]
    block_len = tokens_dev // 2
    inputs = hidden_in.reshape(tokens_dev, model_width).astype(jnp.float32)
    seg_local = segments.reshape(tokens_dev)
    token_routes = routes.reshape(tokens_dev, -1)
    top_count = token_routes.shape[1]
    ctx_count = lax.axis_size("ctx")
    ctx_rank = lax.axis_index("ctx")
    offsets = jnp.arange(block_len, dtype=jnp.int32)
    all_positions = (
        block_pairs.reshape(ctx_count, 2)[:, :, None] * block_len + offsets[None, None, :]
    ).reshape(ctx_count * tokens_dev)
    my_positions = lax.dynamic_slice_in_dim(all_positions, ctx_rank * tokens_dev, tokens_dev, 0)
    gathered = (
        lax.all_gather(norm_gain_attn, ("fsdp", "ctx"), axis=0, tiled=True),
        lax.all_gather(qkv_weight, ("fsdp", "ctx"), axis=0, tiled=True),
        lax.all_gather(qkv_bias, ("fsdp", "ctx"), axis=0, tiled=True),
        lax.all_gather(out_weight, ("fsdp", "ctx"), axis=0, tiled=True),
        lax.all_gather(norm_gain_ffn, ("fsdp", "ctx"), axis=0, tiled=True),
        lax.all_gather(router_weight, ("fsdp", "ctx"), axis=0, tiled=True),
        lax.all_gather(shared_gate_weight, ("fsdp", "ctx"), axis=0, tiled=True),
        lax.all_gather(shared_in_weight, ("fsdp", "ctx"), axis=0, tiled=True),
        lax.all_gather(shared_out_weight, ("fsdp", "ctx"), axis=0, tiled=True),
    )
    (
        gain_attn,
        qkv_full,
        shift_full,
        out_full,
        gain_ffn,
        router_full,
        gate_full,
        inner_full,
        outer_full,
    ) = gathered
    gain_attn = gain_attn.astype(jnp.float32)
    gain_ffn = gain_ffn.astype(jnp.float32)
    heads_width = out_full.shape[0]
    head_count = heads_width // HD
    group_width = heads_per_group * HD
    group_count = head_count // heads_per_group
    normed = rms_scale(inputs, gain_attn).astype(jnp.bfloat16)
    projected = matmul_low(normed, qkv_full) + shift_full.astype(jnp.float32)
    query_pre = projected[:, :heads_width].reshape(tokens_dev, head_count, HD)
    key_pre = projected[:, heads_width : 2 * heads_width].reshape(tokens_dev, head_count, HD)

    def place_heads(query_in, key_in):
        return (rotate(query_in, my_positions) * HD ** (-0.5), rotate(key_in, my_positions))

    query_rot, key_rot = place_heads(query_pre, key_pre)
    query_low = query_rot.reshape(tokens_dev, heads_width).astype(jnp.bfloat16)
    key_low = key_rot.reshape(tokens_dev, heads_width).astype(jnp.bfloat16)
    value_low = projected[:, 2 * heads_width :].astype(jnp.bfloat16)
    keys_all, values_all, segs_all = (
        lax.all_gather(key_low, "ctx", axis=0, tiled=True),
        lax.all_gather(value_low, "ctx", axis=0, tiled=True),
        lax.all_gather(seg_local.astype(jnp.bfloat16), "ctx", axis=0, tiled=True),
    )
    allowed = visible(
        my_positions, seg_local.astype(jnp.float32), all_positions, segs_all.astype(jnp.float32)
    )

    def head_slice(matrix, group_index):
        return lax.dynamic_slice_in_dim(matrix, group_index * group_width, group_width, 1).reshape(
            matrix.shape[0], heads_per_group, HD
        )

    def forward_group(group_index):
        query_part = head_slice(query_low, group_index)
        key_part = head_slice(keys_all, group_index)
        value_part = head_slice(values_all, group_index)
        scores = jnp.einsum(
            "qhd,khd->hqk", query_part, key_part, preferred_element_type=jnp.float32
        )
        scores = jnp.where(allowed[None], scores, -1e30)
        highest = jnp.max(scores, axis=-1, keepdims=True)
        log_total = highest + jnp.log(jnp.sum(jnp.exp(scores - highest), axis=-1, keepdims=True))
        weights = jnp.exp(scores - log_total).astype(jnp.bfloat16)
        mixed = jnp.einsum("hqk,khd->qhd", weights, value_part, preferred_element_type=jnp.float32)
        return (mixed, log_total[..., 0])

    mixed_groups, log_totals = lax.map(forward_group, jnp.arange(group_count, dtype=jnp.int32))
    attended = (
        jnp.moveaxis(mixed_groups, 0, 1).reshape(tokens_dev, heads_width).astype(jnp.bfloat16)
    )
    middle = inputs + matmul_low(attended, out_full)
    normed_ffn = rms_scale(middle, gain_ffn).astype(jnp.bfloat16)
    logits = matmul_low(normed_ffn, router_full)
    router_probs = jax.nn.softmax(logits, axis=-1)
    expert_count = logits.shape[1]
    expert_ids = jnp.arange(expert_count, dtype=jnp.int32)
    chosen = (token_routes[:, :, None] == expert_ids[None, None, :]).astype(jnp.float32)
    gate_weights = jnp.sum(chosen * router_probs[:, None, :], axis=-1)
    capacity = 2 * tokens_dev * top_count // expert_count
    local_experts = expert_in_weight.shape[0]
    assigned = tokens_dev * top_count
    flat_routes = token_routes.reshape(assigned)
    onehot = (flat_routes[:, None] == expert_ids[None, :]).astype(jnp.int32)
    earlier = jnp.cumsum(onehot, axis=0) - onehot
    places = flat_routes * capacity + jnp.sum(earlier * onehot, axis=1)
    slot_source = (
        jnp.full((expert_count * capacity,), assigned, jnp.int32)
        .at[places]
        .set(jnp.arange(assigned, dtype=jnp.int32))
    )
    slot_token = slot_source // top_count
    padded_rows = jnp.concatenate([normed_ffn, jnp.zeros((1, model_width), jnp.bfloat16)], axis=0)
    outgoing = padded_rows[slot_token].reshape(ctx_count, local_experts * capacity, model_width)
    expert_inner, expert_outer = (
        lax.all_gather(expert_in_weight, "fsdp", axis=1, tiled=True),
        lax.all_gather(expert_out_weight, "fsdp", axis=1, tiled=True),
    )
    landed_tokens = lax.all_to_all(outgoing, "ctx", split_axis=0, concat_axis=0, tiled=True)
    incoming = landed_tokens.reshape(ctx_count, local_experts, capacity, model_width)
    expert_gu = jnp.einsum(
        "necd,edf->necf", incoming, expert_inner, preferred_element_type=jnp.float32
    )
    expert_width = expert_outer.shape[1]
    expert_hidden = swiglu_mix(expert_gu, expert_width).astype(jnp.bfloat16)
    expert_result = jnp.einsum(
        "necf,efd->necd", expert_hidden, expert_outer, preferred_element_type=jnp.float32
    ).astype(jnp.bfloat16)
    returned = lax.all_to_all(
        expert_result.reshape(ctx_count, local_experts * capacity, model_width),
        "ctx",
        split_axis=0,
        concat_axis=0,
        tiled=True,
    )
    picked = (
        returned.reshape(expert_count * capacity, model_width)[places]
        .reshape(tokens_dev, top_count, model_width)
        .astype(jnp.float32)
    )
    routed = jnp.sum(gate_weights[:, :, None] * picked, axis=1)
    upstream = out_grad.reshape(tokens_dev, model_width).astype(jnp.float32)
    shared_gu = matmul_low(normed_ffn, inner_full)
    shared_width = outer_full.shape[0]
    shared_hidden = swiglu_mix(shared_gu, shared_width).astype(jnp.bfloat16)
    shared_out = matmul_low(shared_hidden, outer_full)
    gate_value = jax.nn.sigmoid(matmul_low(normed_ffn, gate_full))
    output = middle + gate_value[:, None] * shared_out + routed
    hidden_out = output.astype(jnp.bfloat16).reshape(1, tokens_dev, model_width)
    gain_ffn, router_full, gate_full, inner_full, outer_full = (
        lax.all_gather(norm_gain_ffn, ("fsdp", "ctx"), axis=0, tiled=True),
        lax.all_gather(router_weight, ("fsdp", "ctx"), axis=0, tiled=True),
        lax.all_gather(shared_gate_weight, ("fsdp", "ctx"), axis=0, tiled=True),
        lax.all_gather(shared_in_weight, ("fsdp", "ctx"), axis=0, tiled=True),
        lax.all_gather(shared_out_weight, ("fsdp", "ctx"), axis=0, tiled=True),
    )
    gain_ffn = gain_ffn.astype(jnp.float32)
    grad_shared_out = (gate_value[:, None] * upstream).astype(jnp.bfloat16)
    grad_outer = jnp.einsum(
        "tf,td->fd", shared_hidden, grad_shared_out, preferred_element_type=jnp.float32
    )
    grad_hidden = jnp.einsum(
        "td,fd->tf", grad_shared_out, outer_full, preferred_element_type=jnp.float32
    )
    unused_mix, mix_pull = jax.vjp(functools.partial(swiglu_mix, hidden_width=shared_width), shared_gu)
    grad_shared_gu = mix_pull(grad_hidden)[0].astype(jnp.bfloat16)
    grad_inner = jnp.einsum(
        "td,tf->df", normed_ffn, grad_shared_gu, preferred_element_type=jnp.float32
    )
    grad_normed = jnp.einsum(
        "tf,df->td", grad_shared_gu, inner_full, preferred_element_type=jnp.float32
    )
    grad_gate_logit = (
        gate_value * (1.0 - gate_value) * jnp.sum(upstream * shared_out, axis=1)
    ).astype(jnp.bfloat16)
    grad_gate_vec = jnp.einsum(
        "td,t->d", normed_ffn, grad_gate_logit, preferred_element_type=jnp.float32
    )
    grad_normed = (
        grad_normed
        + grad_gate_logit.astype(jnp.float32)[:, None] * gate_full.astype(jnp.float32)[None, :]
    )
    grad_gates = jnp.sum(upstream[:, None, :] * picked, axis=2)
    grad_choice_probs = jnp.sum(chosen * grad_gates[:, :, None], axis=1)
    grad_logits = (
        router_probs
        * (grad_choice_probs - jnp.sum(router_probs * grad_choice_probs, axis=1, keepdims=True))
    ).astype(jnp.bfloat16)
    grad_router = jnp.einsum(
        "td,te->de", normed_ffn, grad_logits, preferred_element_type=jnp.float32
    )
    grad_normed = grad_normed + jnp.einsum(
        "te,de->td", grad_logits, router_full, preferred_element_type=jnp.float32
    )
    grad_slots = (
        (gate_weights[:, :, None] * upstream[:, None, :])
        .astype(jnp.bfloat16)
        .reshape(assigned, model_width)
    )
    padded_grads = jnp.concatenate([grad_slots, jnp.zeros((1, model_width), jnp.bfloat16)], axis=0)
    grad_outgoing = padded_grads[slot_source].reshape(
        ctx_count, local_experts * capacity, model_width
    )
    grad_incoming = lax.all_to_all(
        grad_outgoing, "ctx", split_axis=0, concat_axis=0, tiled=True
    ).reshape(ctx_count, local_experts, capacity, model_width)
    grad_expert_hidden = jnp.einsum(
        "necd,efd->necf", grad_incoming, expert_outer, preferred_element_type=jnp.float32
    )
    grad_expert_outer = jnp.einsum(
        "necf,necd->efd", expert_hidden, grad_incoming, preferred_element_type=jnp.float32
    )
    unused_mix, expert_pull = jax.vjp(functools.partial(swiglu_mix, hidden_width=expert_width), expert_gu)
    grad_expert_gu = expert_pull(grad_expert_hidden)[0].astype(jnp.bfloat16)
    grad_expert_inner = jnp.einsum(
        "necd,necf->edf", incoming, grad_expert_gu, preferred_element_type=jnp.float32
    )
    grad_expert_rows = jnp.einsum(
        "necf,edf->necd", grad_expert_gu, expert_inner, preferred_element_type=jnp.float32
    ).astype(jnp.bfloat16)
    grad_returned = lax.all_to_all(
        grad_expert_rows.reshape(ctx_count, local_experts * capacity, model_width),
        "ctx",
        split_axis=0,
        concat_axis=0,
        tiled=True,
    )
    grad_picked = grad_returned.reshape(expert_count * capacity, model_width)[places].reshape(
        tokens_dev, top_count, model_width
    )
    grad_normed = grad_normed + jnp.sum(grad_picked.astype(jnp.float32), axis=1)
    sum_expert_inner, sum_expert_outer = (
        lax.psum_scatter(
            grad_expert_inner.astype(jnp.bfloat16), "fsdp", scatter_dimension=1, tiled=True
        ).astype(jnp.float32),
        lax.psum_scatter(
            grad_expert_outer.astype(jnp.bfloat16), "fsdp", scatter_dimension=1, tiled=True
        ).astype(jnp.float32),
    )
    unused_norm, norm_pull = jax.vjp(rms_scale, middle, gain_ffn)
    grad_middle_norm, grad_gain_ffn = norm_pull(grad_normed)
    grad_middle = upstream + grad_middle_norm
    sum_gain_ffn, sum_router, sum_gate_vec, sum_inner, sum_outer = (
        lax.psum_scatter(grad_gain_ffn, ("fsdp", "ctx"), scatter_dimension=0, tiled=True),
        lax.psum_scatter(grad_router, ("fsdp", "ctx"), scatter_dimension=0, tiled=True),
        lax.psum_scatter(grad_gate_vec, ("fsdp", "ctx"), scatter_dimension=0, tiled=True),
        lax.psum_scatter(grad_inner, ("fsdp", "ctx"), scatter_dimension=0, tiled=True),
        lax.psum_scatter(grad_outer, ("fsdp", "ctx"), scatter_dimension=0, tiled=True),
    )
    grad_branch = grad_middle.astype(jnp.bfloat16)
    grad_out_mat = jnp.einsum(
        "tc,td->cd", attended, grad_branch, preferred_element_type=jnp.float32
    )
    grad_attended = jnp.einsum(
        "td,cd->tc", grad_branch, out_full, preferred_element_type=jnp.float32
    ).astype(jnp.bfloat16)
    keys_again, values_again = (
        lax.all_gather(key_low, "ctx", axis=0, tiled=True),
        lax.all_gather(value_low, "ctx", axis=0, tiled=True),
    )

    def backward_group(group_index):
        query_part = head_slice(query_low, group_index)
        key_part = head_slice(keys_again, group_index)
        value_part = head_slice(values_again, group_index)
        grad_part = head_slice(grad_attended, group_index)
        log_total = lax.dynamic_index_in_dim(log_totals, group_index, 0, keepdims=False)
        scores = jnp.einsum(
            "qhd,khd->hqk", query_part, key_part, preferred_element_type=jnp.float32
        )
        scores = jnp.where(allowed[None], scores, -1e30)
        weights = jnp.exp(scores - log_total[..., None])
        grad_weights = jnp.einsum(
            "qhd,khd->hqk", grad_part, value_part, preferred_element_type=jnp.float32
        )
        offset_term = jnp.sum(weights * grad_weights, axis=-1, keepdims=True)
        grad_scores = (weights * (grad_weights - offset_term)).astype(jnp.bfloat16)
        grad_query = jnp.einsum(
            "hqk,khd->qhd", grad_scores, key_part, preferred_element_type=jnp.float32
        )
        grad_key = jnp.einsum(
            "hqk,qhd->khd", grad_scores, query_part, preferred_element_type=jnp.float32
        )
        grad_value = jnp.einsum(
            "hqk,qhd->khd",
            weights.astype(jnp.bfloat16),
            grad_part,
            preferred_element_type=jnp.float32,
        )
        return (grad_query, grad_key, grad_value)

    grad_queries, grad_keys, grad_values = lax.map(
        backward_group, jnp.arange(group_count, dtype=jnp.int32)
    )
    row_total = keys_again.shape[0]
    grad_key_rows = jnp.moveaxis(grad_keys, 0, 1).reshape(row_total, heads_width)
    grad_value_rows = jnp.moveaxis(grad_values, 0, 1).reshape(row_total, heads_width)
    key_share, value_share = (
        lax.psum_scatter(
            grad_key_rows.astype(jnp.bfloat16), "ctx", scatter_dimension=0, tiled=True
        ).astype(jnp.float32),
        lax.psum_scatter(
            grad_value_rows.astype(jnp.bfloat16), "ctx", scatter_dimension=0, tiled=True
        ).astype(jnp.float32),
    )
    grad_query_heads = jnp.moveaxis(grad_queries, 0, 1).reshape(tokens_dev, head_count, HD)
    unused_rot, rotate_pull = jax.vjp(place_heads, query_pre, key_pre)
    grad_query_pre, grad_key_pre = rotate_pull(
        (grad_query_heads, key_share.reshape(tokens_dev, head_count, HD))
    )
    grad_projected = jnp.concatenate(
        [
            grad_query_pre.reshape(tokens_dev, heads_width),
            grad_key_pre.reshape(tokens_dev, heads_width),
            value_share,
        ],
        axis=1,
    ).astype(jnp.bfloat16)
    grad_qkv = jnp.einsum("td,tc->dc", normed, grad_projected, preferred_element_type=jnp.float32)
    grad_shift = jnp.sum(grad_projected.astype(jnp.float32), axis=0)
    grad_normed_attn = jnp.einsum(
        "tc,dc->td", grad_projected, qkv_full, preferred_element_type=jnp.float32
    )
    unused_norm, first_pull = jax.vjp(rms_scale, inputs, gain_attn)
    grad_inputs_norm, grad_gain_attn = first_pull(grad_normed_attn)
    input_grad = grad_middle + grad_inputs_norm
    sum_gain_attn, sum_qkv, sum_shift, sum_out = (
        lax.psum_scatter(grad_gain_attn, ("fsdp", "ctx"), scatter_dimension=0, tiled=True),
        lax.psum_scatter(grad_qkv, ("fsdp", "ctx"), scatter_dimension=0, tiled=True),
        lax.psum_scatter(grad_shift, ("fsdp", "ctx"), scatter_dimension=0, tiled=True),
        lax.psum_scatter(grad_out_mat, ("fsdp", "ctx"), scatter_dimension=0, tiled=True),
    )
    return (
        hidden_out,
        input_grad.reshape(1, tokens_dev, model_width),
        sum_gain_attn,
        sum_qkv,
        sum_shift,
        sum_out,
        sum_gain_ffn,
        sum_router,
        sum_gate_vec,
        sum_inner,
        sum_outer,
        sum_expert_inner,
        sum_expert_outer,
    )


SPAN = 256


def flat_dot(left, right):
    return lax.dot_general(left, right, (((1,), (0,)), ((), ())), preferred_element_type=jnp.float32)


def turned_dot(left, right):
    return lax.dot_general(left, right, (((1,), (1,)), ((), ())), preferred_element_type=jnp.float32)


def span_of(index, size=SPAN):
    return pl.ds(pl.multiple_of(index * size, size), size)


MESH = pl.DeviceIdType.MESH
ANY = pl.BlockSpec(memory_space=pl.ANY)
VMEM = pl.BlockSpec(memory_space=pltpu.VMEM)


def remote(source, target, send_sem, recv_sem, **place):
    return pltpu.make_async_remote_copy(
        src_ref=source,
        dst_ref=target,
        send_sem=send_sem,
        recv_sem=recv_sem,
        device_id=place,
        device_id_type=MESH,
    )


def line_place():
    here = lax.axis_index("ctx")
    line = here % 2
    return here, here // 2, line, here + 1 - 2 * line


def greet_line(last, here, level, side, others=0):
    barrier = pltpu.get_barrier_semaphore()
    pl.semaphore_signal(barrier, inc=1, device_id={"ctx": side}, device_id_type=MESH)

    @pl.when(level < last)
    def up():
        pl.semaphore_signal(barrier, inc=1, device_id={"ctx": here + 2}, device_id_type=MESH)

    @pl.when(level > 0)
    def down():
        pl.semaphore_signal(barrier, inc=1, device_id={"ctx": here - 2}, device_id_type=MESH)

    ends = jnp.where(level < last, 1, 0) + jnp.where(level > 0, 1, 0)
    pl.semaphore_wait(barrier, 1 + others + ends)


def line_copy(rows_ref, block, way, target, sems, source=None):
    send_sem, recv_sem = sems
    return remote(
        rows_ref.at[block] if source is None else source,
        rows_ref.at[block],
        send_sem.at[block, way],
        recv_sem.at[block],
        ctx=target,
    )


def line_start(rows_ref, own_ref, sems, place, last):
    here, level, line, side = place

    @pl.when(level < last)
    def up():
        line_copy(rows_ref, here, 0, here + 2, sems, own_ref).start()

    @pl.when(level > 0)
    def down():
        line_copy(rows_ref, here, 1, here - 2, sems, own_ref).start()

    line_copy(rows_ref, here, 2, side, sems, own_ref).start()


def line_step(rows_ref, sems, place, last, step):
    here, level, line, side = place

    @pl.when(level >= step)
    def from_below():
        block = here - 2 * step
        line_copy(rows_ref, block, 0, side, sems).wait_recv()

        @pl.when(level < last)
        def on():
            line_copy(rows_ref, block, 0, here + 2, sems).start()

        line_copy(rows_ref, block, 2, side, sems).start()

    @pl.when(level + step <= last)
    def from_above():
        block = here + 2 * step
        line_copy(rows_ref, block, 1, side, sems).wait_recv()

        @pl.when(level > 0)
        def on():
            line_copy(rows_ref, block, 1, here - 2, sems).start()

        line_copy(rows_ref, block, 2, side, sems).start()


def line_finish(rows_ref, sems, place, last):
    here, level, line, side = place
    for other in range(last + 1):
        block = 2 * other + line
        line_copy(rows_ref, 2 * other + 1 - line, 2, side, sems).wait_recv()
        line_copy(rows_ref, block, 2, side, sems).wait_send()

        @pl.when((other <= level) & (level < last))
        def up():
            line_copy(rows_ref, block, 0, side, sems).wait_send()

        @pl.when((other >= level) & (level > 0))
        def down():
            line_copy(rows_ref, block, 1, side, sems).wait_send()


ROWS_STEP = 16


def add_rows(target, pieces, row_count):
    def one(index, carry):
        rows = pl.ds(pl.multiple_of(index * ROWS_STEP, ROWS_STEP), ROWS_STEP)
        total = pieces[0][rows, :].astype(jnp.float32)
        for piece in pieces[1:]:
            total = total + piece[rows, :].astype(jnp.float32)
        target[rows, :] = total.astype(target.dtype)
        return carry

    lax.fori_loop(0, row_count // ROWS_STEP, one, 0)


def scatter_turns(last, part, total, crossed, rising, falling, sums, *sems):
    cross_send, cross_recv, move_send, rise_recv, fall_recv = sems
    here, level, line, side = line_place()
    row_count = total.shape[0]

    def turn(k):
        middle = (level > 0) & (level < last)
        swapped = k + jnp.where(middle, (0, 0, 1, -1)[k], 0)
        return jnp.where(level * 2 < last, last - swapped, swapped)

    def cross(goal):
        return remote(
            part.at[2 * goal + 1 - line],
            crossed.at[goal],
            cross_send.at[goal],
            cross_recv.at[goal],
            ctx=side,
        )

    def rise(goal):
        return remote(
            sums.at[goal], rising.at[goal], move_send.at[goal], rise_recv.at[goal], ctx=here + 2
        )

    def fall(goal):
        return remote(
            sums.at[goal], falling.at[goal], move_send.at[goal], fall_recv.at[goal], ctx=here - 2
        )

    for k in range(min(2, last + 1)):
        cross(turn(k)).start()
    for k in range(last + 1):
        yield k
        goal = turn(k)
        mine = part.at[2 * goal + line]
        cross(goal).wait_recv()
        if k + 2 <= last:
            cross(turn(k + 2)).start()

        @pl.when(goal > level)
        def upward():
            @pl.when(level > 0)
            def joined():
                rise(goal).wait_recv()
                add_rows(sums.at[goal], (mine, crossed.at[goal], rising.at[goal]), row_count)

            @pl.when(level == 0)
            def first():
                add_rows(sums.at[goal], (mine, crossed.at[goal]), row_count)

            rise(goal).start()

        @pl.when(goal < level)
        def downward():
            @pl.when(level < last)
            def joined():
                fall(goal).wait_recv()
                add_rows(sums.at[goal], (mine, crossed.at[goal], falling.at[goal]), row_count)

            @pl.when(level == last)
            def first():
                add_rows(sums.at[goal], (mine, crossed.at[goal]), row_count)

            fall(goal).start()

        @pl.when(goal == level)
        def here_at_last():
            @pl.when(level > 0)
            def from_below():
                rise(goal).wait_recv()

            @pl.when(level < last)
            def from_above():
                fall(goal).wait_recv()

            @pl.when(level == 0)
            def bottom():
                add_rows(total, (mine, crossed.at[goal], falling.at[goal]), row_count)

            @pl.when(level == last)
            def top():
                add_rows(total, (mine, crossed.at[goal], rising.at[goal]), row_count)

            @pl.when((level > 0) & (level < last))
            def between():
                add_rows(
                    total,
                    (mine, crossed.at[goal], rising.at[goal], falling.at[goal]),
                    row_count,
                )

    for goal in range(last + 1):
        cross(goal).wait_send()

        @pl.when(goal != level)
        def sent():
            rise(goal).wait_send()


def scatter_kernel(
    ctx_count, part, small, far_tokens, far_grads, total, small_in, weight_grad, *refs
):
    *refs, product, store_sem, tokens, grads, load_sem = refs
    loads = [
        pltpu.make_async_copy(source, target, load_sem.at[i])
        for i, (source, target) in enumerate(((far_tokens, tokens), (far_grads, grads)))
    ]
    for copy in loads:
        copy.start()
    greet_all(ctx_count)
    here = lax.axis_index("ctx")
    starts, waits = spread(
        lambda peer: small.at[peer], lambda source: small_in.at[source], refs[9:11], ctx_count
    )
    for copy in starts:
        copy.start()
    small_in[here] = small[here]
    turns = scatter_turns(ctx_count // 2 - 1, part, total, *refs[:9])
    next(turns)
    pieces = ctx_count // 2
    depth = tokens.shape[1] // pieces
    stores = []
    for copy in loads:
        copy.wait()
    for piece in range(pieces):

        @pl.loop(0, depth // SPAN)
        def multiply(index):
            here = pl.ds(pl.multiple_of(piece * depth + index * SPAN, SPAN), SPAN)
            product[here, :] = flat_dot(tokens[:, here].T, grads[...]).astype(product.dtype)

        rows = pl.ds(piece * depth, depth)
        stores.append(
            pltpu.make_async_copy(product.at[rows], weight_grad.at[rows], store_sem.at[piece])
        )
        stores[-1].start()
        next(turns, None)
    for copy in waits:
        copy.wait_recv()
    for copy in starts:
        copy.wait_send()
    for copy in stores:
        copy.wait()


def line_scatter_kernel(last, part, total, *refs):
    here, level, line, side = line_place()
    greet_line(last, here, level, side)
    for step in scatter_turns(last, part, total, *refs):
        pass


def line_scatter(ctx_count, call_id, part, small=None, tokens=None, grads=None):
    rows, width = part.shape[1:]
    half = ctx_count // 2
    dma = pltpu.SemaphoreType.DMA((half,))
    spread_dma = pltpu.SemaphoreType.DMA((ctx_count,))
    slots = pltpu.VMEM((half, rows, width), part.dtype)
    total = jax.ShapeDtypeStruct((rows, width), jnp.float32)
    params = pltpu.CompilerParams(
        collective_id=call_id, has_side_effects=True, vmem_limit_bytes=40 * 2**20
    )
    if small is None:
        return pl.pallas_call(
            functools.partial(line_scatter_kernel, half - 1),
            out_shape=total,
            in_specs=[VMEM],
            out_specs=VMEM,
            scratch_shapes=[slots] * 4 + [dma] * 5,
            compiler_params=params,
            name="line_scatter",
        )(part)
    product = (tokens.shape[1], grads.shape[1])
    params = pltpu.CompilerParams(
        collective_id=call_id, has_side_effects=True, vmem_limit_bytes=40 * 2**20
    )
    return pl.pallas_call(
        functools.partial(scatter_kernel, ctx_count),
        out_shape=[
            total,
            jax.ShapeDtypeStruct(small.shape, small.dtype),
            jax.ShapeDtypeStruct(product, part.dtype),
        ],
        in_specs=[VMEM] * 2 + [ANY] * 2,
        out_specs=[VMEM] * 2 + [ANY],
        scratch_shapes=[slots] * 4
        + [dma] * 5
        + [spread_dma] * 2
        + [pltpu.VMEM(product, part.dtype), pltpu.SemaphoreType.DMA((half,))]
        + [
            pltpu.VMEM(tokens.shape, tokens.dtype),
            pltpu.VMEM(grads.shape, grads.dtype),
            pltpu.SemaphoreType.DMA((2,)),
        ],
        compiler_params=params,
        name="line_scatter",
    )(part, small, tokens, grads)


def fsdp_place():
    here = lax.axis_index("fsdp")
    beside = here + 1 - 2 * (here % 2)
    return here, beside, (here + 2) % 4, (beside + 2) % 4


def greet_all(ctx_count):
    barrier = pltpu.get_barrier_semaphore()
    here = lax.axis_index("ctx")
    group = lax.axis_index("fsdp")
    for k in range(1, ctx_count):
        pl.semaphore_signal(
            barrier, inc=1, device_id={"ctx": (here + k) % ctx_count}, device_id_type=MESH
        )
    for k in range(1, 4):
        pl.semaphore_signal(barrier, inc=1, device_id={"fsdp": (group + k) % 4}, device_id_type=MESH)
    pl.semaphore_wait(barrier, ctx_count + 2)


def share_start(blocks, sems, own=None):
    send_sem, recv_sem = sems
    here, beside, across, corner = fsdp_place()
    source = blocks.at[here] if own is None else own
    for way, target in ((0, across), (1, beside)):
        remote(source, blocks.at[here], send_sem.at[way], recv_sem.at[here], fsdp=target).start()


def share_step(blocks, sems):
    send_sem, recv_sem = sems
    here, beside, across, corner = fsdp_place()
    copy = remote(
        blocks.at[across], blocks.at[across], send_sem.at[2], recv_sem.at[across], fsdp=beside
    )
    copy.wait_recv()
    copy.start()


def share_finish(blocks, sems):
    send_sem, recv_sem = sems
    here, beside, across, corner = fsdp_place()
    for way, block in ((0, beside), (1, corner)):
        copy = remote(
            blocks.at[block], blocks.at[block], send_sem.at[way], recv_sem.at[block], fsdp=beside
        )
        copy.wait_recv()
        copy.wait_send()
    remote(
        blocks.at[here], blocks.at[here], send_sem.at[2], recv_sem.at[here], fsdp=beside
    ).wait_send()


def spread(pieces, landing, sems, ctx_count):
    send_sem, recv_sem = sems
    here = lax.axis_index("ctx")

    def copy(k, peer, source):
        return remote(pieces(peer), landing(source), send_sem.at[k], recv_sem.at[k], ctx=peer)

    starts = [copy(k, (here + k) % ctx_count, here) for k in range(1, ctx_count)]
    waits = [
        copy(k, (here + k) % ctx_count, (here + ctx_count - k) % ctx_count)
        for k in range(1, ctx_count)
    ]
    return starts, waits


def greet_near(last, here, level, side):
    barrier = pltpu.get_barrier_semaphore()
    group = lax.axis_index("fsdp")
    for k in range(1, 4):
        pl.semaphore_signal(barrier, inc=1, device_id={"fsdp": (group + k) % 4}, device_id_type=MESH)
    greet_line(last, here, level, side, 3)


def gather_kernel(last, shared_count, *refs):
    total = 1 + shared_count
    owns, rows, keep_sem = refs[:total], refs[total : 2 * total], refs[2 * total]
    refs = refs[2 * total + 1 :]
    place = line_place()
    here, level, line, side = place
    sems = [(refs[2 * i], refs[2 * i + 1]) for i in range(total)]
    group = lax.axis_index("fsdp")
    if shared_count:
        greet_near(last, here, level, side)
    else:
        greet_line(last, here, level, side)
    line_start(rows[0], owns[0], sems[0], place, last)
    for i in range(1, total):
        share_start(rows[i], sems[i], owns[i])
    keeps = [
        pltpu.make_async_copy(
            owns[i], rows[i].at[group if i else here], keep_sem.at[i]
        )
        for i in range(total)
    ]
    for copy in keeps:
        copy.start()
    for step in range(1, last + 1):
        line_step(rows[0], sems[0], place, last, step)
    for i in range(1, total):
        share_step(rows[i], sems[i])
    line_finish(rows[0], sems[0], place, last)
    for i in range(1, total):
        share_finish(rows[i], sems[i])
    for copy in keeps:
        copy.wait()


def product_kernel(last, own, units, grads, rows, product, keep_sem, send_sem, recv_sem):
    place = line_place()
    here, level, line, side = place
    sems = (send_sem, recv_sem)
    greet_line(last, here, level, side)
    line_start(rows, own, sems, place, last)
    keep = pltpu.make_async_copy(own, rows.at[here], keep_sem.at[0])
    keep.start()
    turned = units[...].T
    piece = grads.shape[1] // (last + 1)
    for step in range(last + 1):
        columns = pl.ds(step * piece, piece)
        product[:, columns] = flat_dot(turned, grads[:, columns]).astype(product.dtype)
        if step < last:
            line_step(rows, sems, place, last, step + 1)
    line_finish(rows, sems, place, last)
    keep.wait()


def product_gather(ctx_count, call_id, own, units, grads):
    dma = pltpu.SemaphoreType.DMA
    return pl.pallas_call(
        functools.partial(product_kernel, ctx_count // 2 - 1),
        out_shape=[
            jax.ShapeDtypeStruct((ctx_count,) + own.shape, own.dtype),
            jax.ShapeDtypeStruct((units.shape[1], grads.shape[1]), own.dtype),
        ],
        in_specs=[VMEM] * 3,
        out_specs=[ANY, VMEM],
        scratch_shapes=[dma((1,)), dma((ctx_count, 3)), dma((ctx_count,))],
        compiler_params=pltpu.CompilerParams(
            collective_id=call_id, has_side_effects=True, vmem_limit_bytes=32 * 2**20
        ),
        name="product_gather",
    )(own, units, grads)


def line_gather(ctx_count, call_id, own, *shared):
    count = len(shared)
    dma = pltpu.SemaphoreType.DMA
    return pl.pallas_call(
        functools.partial(gather_kernel, ctx_count // 2 - 1, count),
        out_shape=[jax.ShapeDtypeStruct((ctx_count,) + own.shape, own.dtype)]
        + [jax.ShapeDtypeStruct((4,) + a.shape, a.dtype) for a in shared],
        in_specs=[VMEM] * (1 + count),
        out_specs=[ANY] * (1 + count),
        scratch_shapes=[dma((1 + count,)), dma((ctx_count, 3)), dma((ctx_count,))]
        + [dma((3,)), dma((4,))] * count,
        compiler_params=pltpu.CompilerParams(collective_id=call_id, has_side_effects=True),
        name="line_gather",
    )(own, *shared)


def opening_kernel(
    ctx_count,
    own,
    qkv_own,
    out_own,
    small_own,
    number_own,
    rows,
    qkv,
    out_pair,
    small,
    numbers,
    keep_sem,
    pair_send,
    pair_recv,
    row_send,
    row_recv,
    share_send,
    share_recv,
    *sems,
):
    last = ctx_count // 2 - 1
    place = line_place()
    here, level, line, side = place
    group, beside, across, corner = fsdp_place()
    sems = [(sems[2 * i], sems[2 * i + 1]) for i in range(5)]
    qkv_spread, small_spread, number_spread, out_share, small_share = sems
    row_sems = (row_send, row_recv)
    greet_all(ctx_count)
    qkv_start, qkv_wait = spread(
        lambda peer: qkv_own.at[peer], lambda source: qkv.at[group, source], qkv_spread, ctx_count
    )
    small_start, small_wait = spread(
        lambda peer: small_own, lambda source: small.at[group, source], small_spread, ctx_count
    )
    number_start, number_wait = spread(
        lambda peer: number_own, lambda source: numbers.at[source], number_spread, ctx_count
    )

    def piece_copy(way, owner, k, target, first=False):
        source = (here + ctx_count - k) % ctx_count
        return remote(
            qkv_own.at[here] if first else qkv.at[owner, source],
            qkv.at[owner, source],
            share_send.at[way, k],
            share_recv.at[owner, k],
            fsdp=target,
        )

    def piece_on(k):
        piece_copy(0, group, k, across, k == 0).start()
        piece_copy(1, group, k, beside, k == 0).start()

    for copy in small_start + number_start + qkv_start:
        copy.start()
    line_start(rows, own, row_sems, place, last)
    piece_on(0)
    pair = remote(
        out_own, out_pair.at[group, line], pair_send.at[0], pair_recv.at[0], ctx=side
    )
    pair.start()
    keeps = [
        pltpu.make_async_copy(source, target, keep_sem.at[i])
        for i, (source, target) in enumerate(
            (
                (qkv_own.at[here], qkv.at[group, here]),
                (out_own, out_pair.at[group, line]),
                (small_own, small.at[group, here]),
                (number_own, numbers.at[here]),
                (own, rows.at[here]),
            )
        )
    ]
    for copy in keeps:
        copy.start()
    for copy in small_wait:
        copy.wait_recv()
    keeps[2].wait()
    share_start(small, small_share)
    line_step(rows, row_sems, place, last, 1)
    for k in range(1, ctx_count):
        qkv_wait[k - 1].wait_recv()
        piece_on(k)
    remote(
        out_own, out_pair.at[group, 1 - line], pair_send.at[0], pair_recv.at[0], ctx=side
    ).wait_recv()
    keeps[1].wait()
    share_start(out_pair, out_share)
    line_step(rows, row_sems, place, last, 2)
    for k in range(ctx_count):
        piece_copy(0, across, k, across).wait_recv()
        piece_copy(2, across, k, beside).start()
    share_step(small, small_share)
    for step in range(3, last + 1):
        line_step(rows, row_sems, place, last, step)
    share_step(out_pair, out_share)
    line_finish(rows, row_sems, place, last)
    for copy in number_wait:
        copy.wait_recv()
    for copy in qkv_start + small_start + number_start:
        copy.wait_send()
    pair.wait_send()
    for k in range(ctx_count):
        piece_copy(1, beside, k, beside).wait_recv()
        piece_copy(2, corner, k, beside).wait_recv()
        for way in range(3):
            piece_copy(way, group, k, beside).wait_send()
    share_finish(small, small_share)
    share_finish(out_pair, out_share)
    for i in (0, 3, 4):
        keeps[i].wait()


def opening(ctx_count, call_id, own, qkv_own, out_own, small_own, number_own):
    def out(lead, array):
        return jax.ShapeDtypeStruct(lead + array.shape, array.dtype)

    dma = pltpu.SemaphoreType.DMA
    return pl.pallas_call(
        functools.partial(opening_kernel, ctx_count),
        out_shape=[
            out((ctx_count,), own),
            out((4,), qkv_own),
            out((4, 2), out_own),
            out((4, ctx_count), small_own),
            out((ctx_count,), number_own),
        ],
        in_specs=[VMEM] * 5,
        out_specs=[ANY] * 5,
        scratch_shapes=[
            dma((5,)),
            dma((1,)),
            dma((1,)),
            dma((ctx_count, 3)),
            dma((ctx_count,)),
            dma((3, ctx_count)),
            dma((4, ctx_count)),
        ]
        + [dma((ctx_count,))] * 6
        + [dma((3,)), dma((4,))] * 2,
        compiler_params=pltpu.CompilerParams(collective_id=call_id, has_side_effects=True),
        name="opening",
    )(own, qkv_own, out_own, small_own, number_own)


def group_reduce(blocks, beside_in, pair_sums, across_in, settled, sems):
    core_send, core_recv, far_send, far_recv = sems
    group, beside, across, corner = fsdp_place()
    rows = settled.shape[0]

    def core_copy(slot, block):
        return remote(
            blocks.at[block],
            beside_in.at[slot],
            core_send.at[slot],
            core_recv.at[slot],
            fsdp=beside,
        )

    far = remote(pair_sums.at[1], across_in, far_send.at[0], far_recv.at[0], fsdp=across)
    core_copy(1, corner).start()
    core_copy(0, beside).start()
    yield
    core_copy(1, corner).wait_recv()
    add_rows(pair_sums.at[1], (blocks.at[across], beside_in.at[1]), rows)
    far.start()
    core_copy(0, beside).wait_recv()
    add_rows(pair_sums.at[0], (blocks.at[group], beside_in.at[0]), rows)
    yield
    far.wait_recv()
    add_rows(settled, (pair_sums.at[0], across_in), rows)
    yield
    core_copy(1, corner).wait_send()
    core_copy(0, beside).wait_send()
    far.wait_send()
    yield


def closing_kernel(ctx_count, part, weight, pair, plain, small, *refs):
    total, landed, pair_total, plain_total, small_total = refs[:5]
    line_slots, weight_slots, pair_slots, plain_slots = (
        refs[5:9],
        refs[9:13],
        refs[13:17],
        refs[17:20],
    )
    pair_in, small_in, small_sums, small_across = refs[20:24]
    sems = refs[24:]
    line_sems, weight_sems, pair_sems, plain_sems = sems[:5], sems[5:9], sems[9:13], sems[13:17]
    keep_sem, half_send, half_recv = sems[17:20]
    weight_spread, small_spread, (group_send, group_recv) = sems[20:22], sems[22:24], sems[24:26]
    here, level, line, side = line_place()
    group = lax.axis_index("fsdp")
    greet_all(ctx_count)
    turns = scatter_turns(ctx_count // 2 - 1, part, total, *line_slots, *line_sems)
    settled, pair_settled = weight_slots[3], pair_slots[3]
    weight_steps = group_reduce(weight, *weight_slots, weight_sems)
    pair_steps = group_reduce(pair, *pair_slots, pair_sems)
    plain_steps = group_reduce(plain, *plain_slots, plain_total, plain_sems)
    small_start, small_wait = spread(
        lambda peer: small.at[:, peer], lambda source: small_in.at[source], small_spread, ctx_count
    )
    for copy in small_start:
        copy.start()
    next(weight_steps)
    next(turns)
    next(weight_steps)
    next(pair_steps)
    next(turns)
    next(pair_steps)
    next(plain_steps)
    for copy in small_wait:
        copy.wait_recv()
    small_sum = small[:, here]
    for k in range(1, ctx_count):
        small_sum = small_sum + small_in[(here + k) % ctx_count]
    small_sums[...] = small_sum
    group_copies = [
        remote(
            small_sums.at[(group + k) % 4],
            small_across.at[k],
            group_send.at[k],
            group_recv.at[k],
            fsdp=(group + k) % 4,
        )
        for k in range(1, 4)
    ]
    for copy in group_copies:
        copy.start()
    next(weight_steps)
    piece = settled.shape[0] // ctx_count
    weight_start, weight_wait = spread(
        lambda peer: settled.at[pl.ds(pl.multiple_of(peer * piece, piece), piece)],
        lambda source: landed.at[source],
        weight_spread,
        ctx_count,
    )
    for copy in weight_start:
        copy.start()
    keep = pltpu.make_async_copy(
        settled.at[pl.ds(pl.multiple_of(here * piece, piece), piece)],
        landed.at[here],
        keep_sem.at[0],
    )
    keep.start()
    next(plain_steps)
    next(turns)
    next(pair_steps)
    half = pair_total.shape[0]
    half_copy = remote(
        pair_settled.at[pl.ds(pl.multiple_of((1 - line) * half, half), half)],
        pair_in,
        half_send.at[0],
        half_recv.at[0],
        ctx=side,
    )
    half_copy.start()
    for copy in group_copies:
        copy.wait_recv()
    small_total[...] = small_sums[group] + small_across[1] + small_across[2] + small_across[3]
    for step in turns:
        pass
    next(plain_steps)
    half_copy.wait_recv()
    kept = pair_settled.at[pl.ds(pl.multiple_of(line * half, half), half)]
    add_rows(pair_total, (kept, pair_in), half)
    for copy in weight_wait:
        copy.wait_recv()
    for copy in weight_start + small_start + group_copies:
        copy.wait_send()
    half_copy.wait_send()
    next(weight_steps)
    next(pair_steps)
    next(plain_steps)
    keep.wait()


def closing(ctx_count, call_id, part, weight, pair, plain, small):
    rows, width = part.shape[1:]
    half = ctx_count // 2
    dma = pltpu.SemaphoreType.DMA
    slots = pltpu.VMEM((half, rows, width), part.dtype)

    def group_slots(array):
        one = pltpu.VMEM(array.shape[1:], array.dtype)
        two = pltpu.VMEM((2,) + array.shape[1:], array.dtype)
        return [two, two, one, one]

    block, columns = weight.shape[1:]
    pair_half = (pair.shape[1] // 2, pair.shape[2])
    return pl.pallas_call(
        functools.partial(closing_kernel, ctx_count),
        out_shape=[
            jax.ShapeDtypeStruct((rows, width), jnp.float32),
            jax.ShapeDtypeStruct((ctx_count, block // ctx_count, columns), weight.dtype),
            jax.ShapeDtypeStruct(pair_half, jnp.float32),
            jax.ShapeDtypeStruct(plain.shape[1:], jnp.float32),
            jax.ShapeDtypeStruct(small.shape[2:], small.dtype),
        ],
        in_specs=[VMEM] * 5,
        out_specs=[VMEM] * 5,
        scratch_shapes=[slots] * 4
        + group_slots(weight)
        + group_slots(pair)
        + group_slots(plain)[:3]
        + [
            pltpu.VMEM(pair_half, pair.dtype),
            pltpu.VMEM((ctx_count, 4) + small.shape[2:], small.dtype),
            pltpu.VMEM((4,) + small.shape[2:], small.dtype),
            pltpu.VMEM((4,) + small.shape[2:], small.dtype),
        ]
        + [dma((half,))] * 5
        + [dma((2,)), dma((2,)), dma((1,)), dma((1,))] * 3
        + [dma((1,))] * 3
        + [dma((ctx_count,))] * 4
        + [dma((4,))] * 2,
        compiler_params=pltpu.CompilerParams(
            collective_id=call_id, has_side_effects=True, vmem_limit_bytes=36 * 2**20
        ),
        name="closing",
    )(part, weight, pair, plain, small)


def scaled_rows(values):
    return values * lax.rsqrt(jnp.mean(values * values, axis=-1, keepdims=True) + EPSILON)


def attend_kernel(
    inputs,
    gain,
    weight,
    bias,
    cosine,
    sine,
    columns,
    lines,
    out_weight,
    normed,
    queries,
    keys,
    values,
    attended,
    log_totals,
    part,
):
    rows = inputs.shape[0]
    low = jnp.bfloat16
    heads = queries.shape[1] // HD

    @pl.loop(0, rows // SPAN)
    def project(index):
        here = span_of(index)
        unit = scaled_rows(inputs[here, :].astype(jnp.float32)) * gain[...]
        normed[here, :] = unit.astype(low)
        projected = flat_dot(normed[here, :], weight[...]) + bias[...]
        turn, tilt = cosine[here, :], sine[here, :]
        for head in range(heads):
            own = slice(head * HD, (head + 1) * HD)
            query = projected[:, own]
            query = query * turn + pltpu.roll(query, HD // 2, 1) * tilt
            queries[here, own] = (query * HD ** (-0.5)).astype(low)
            key = projected[:, (heads + head) * HD : (heads + head + 1) * HD]
            keys[here, own] = (key * turn + pltpu.roll(key, HD // 2, 1) * tilt).astype(low)
            values[here, own] = projected[
                :, (2 * heads + head) * HD : (2 * heads + head + 1) * HD
            ].astype(low)

    @pl.loop(0, rows // SPAN)
    def attend(index):
        here = span_of(index)
        position, segment = columns[here, 0:1], columns[here, 1:2]
        allowed = (lines[1:2, :] == segment) & (lines[0:1, :] <= position)
        allowed = allowed | (lines[0:1, :] == position)
        for head in range(heads):
            own = slice(head * HD, (head + 1) * HD)
            scores = turned_dot(queries[here, own], keys[:, own])
            scores = jnp.where(allowed, scores, -1e30)
            highest = jnp.max(scores, axis=1, keepdims=True)
            weights = jnp.exp(scores - highest)
            sums = jnp.sum(weights, axis=1, keepdims=True)
            log_totals[here, head : head + 1] = highest + jnp.log(sums)
            probs = (weights * (1.0 / sums)).astype(low)
            attended[here, own] = flat_dot(probs, values[:, own]).astype(low)
        part[here, :] = flat_dot(attended[here, :], out_weight[...]).astype(low)


def attend(inputs, gain, weight, bias, cosine, sine, columns, lines, out_weight):
    rows, width = inputs.shape
    wide = out_weight.shape[0]
    low = jnp.bfloat16
    shape = jax.ShapeDtypeStruct
    return pl.pallas_call(
        attend_kernel,
        out_shape=[shape((rows, width), low)]
        + [shape((rows, wide), low)] * 4
        + [shape((rows, wide // HD), jnp.float32), shape((rows, width), low)],
        in_specs=[VMEM] * 9,
        out_specs=[VMEM] * 7,
        compiler_params=pltpu.CompilerParams(vmem_limit_bytes=40 * 2**20),
        cost_estimate=pl.CostEstimate(
            flops=2 * rows * width * 4 * wide + 4 * rows * rows * wide,
            bytes_accessed=20 * 2**20,
            transcendentals=rows * rows * wide // HD,
        ),
        name="attend",
    )(inputs, gain, weight, bias, cosine, sine, columns, lines, out_weight)


def attend_back_kernel(
    branch,
    out_weight,
    queries,
    keys,
    values,
    attended,
    totals,
    cosine,
    sine,
    columns,
    lines,
    far_inputs,
    far_normed,
    far_weight,
    part,
    grad_weight,
    grad_out,
    grad_bias,
    grad_gain,
    grads,
    grad_attended,
    grad_keys,
    grad_values,
    gain_sum,
    inputs,
    normed,
    weight,
    load_sem,
):
    rows, width = branch.shape
    low = jnp.bfloat16
    full = jnp.float32
    wide = queries.shape[1]
    heads = wide // HD
    loads = [
        pltpu.make_async_copy(source, target, load_sem.at[i])
        for i, (source, target) in enumerate(
            ((far_weight, weight), (far_inputs, inputs), (far_normed, normed))
        )
    ]
    for copy in loads:
        copy.start()

    @pl.loop(0, rows // SPAN)
    def into_heads(index):
        here = span_of(index)
        grad_attended[here, :] = turned_dot(branch[here, :], out_weight[...]).astype(low)

    for head in range(heads):
        own = slice(head * HD, (head + 1) * HD)
        grad_keys[...] = jnp.zeros_like(grad_keys)
        grad_values[...] = jnp.zeros_like(grad_values)

        @pl.loop(0, rows // SPAN)
        def scores_back(index):
            here = span_of(index)
            position, segment = lines[0:1, here], lines[1:2, here]
            allowed = (columns[:, 1:2] == segment) & (columns[:, 0:1] <= position)
            allowed = allowed | (columns[:, 0:1] == position)
            query, grad = queries[here, own], grad_attended[here, own]
            scores = jnp.where(allowed, turned_dot(keys[:, own], query), -1e30)
            probs = jnp.exp(scores - totals[head : head + 1, here])
            grad_probs = turned_dot(values[:, own], grad)
            delta = jnp.sum(probs * grad_probs, axis=0, keepdims=True)
            grad_scores = (probs * (grad_probs - delta)).astype(low)
            grad_keys[...] += flat_dot(grad_scores, query)
            grad_values[...] += flat_dot(probs.astype(low), grad)
            grad_query = flat_dot(grad_scores.T, keys[:, own]) * HD ** (-0.5)
            grads[here, own] = (
                grad_query * cosine[here, :] + pltpu.roll(grad_query * sine[here, :], HD // 2, 1)
            ).astype(low)

        @pl.loop(0, rows // SPAN)
        def keys_back(index):
            here = span_of(index)
            grad_key = grad_keys[here, :]
            grads[here, (heads + head) * HD : (heads + head + 1) * HD] = (
                grad_key * cosine[here, :] + pltpu.roll(grad_key * sine[here, :], HD // 2, 1)
            ).astype(low)
            grads[here, (2 * heads + head) * HD : (2 * heads + head + 1) * HD] = grad_values[
                here, :
            ].astype(low)

    gain_sum[...] = jnp.zeros_like(gain_sum)
    grad_bias[...] = jnp.zeros_like(grad_bias)
    for copy in loads:
        copy.wait()

    @pl.loop(0, rows // SPAN)
    def project_back(index):
        here = span_of(index)
        grad_rows = turned_dot(grads[here, :], weight[...])
        part[here, :] = grad_rows.astype(low)
        unit = scaled_rows(inputs[here, :].astype(full))
        gain_sum[...] += jnp.sum(grad_rows * unit, axis=0, keepdims=True)
        grad_bias[...] += jnp.sum(grads[here, :].astype(full), axis=0, keepdims=True)

    grad_gain[...] = gain_sum[...]

    @pl.loop(0, width // SPAN)
    def weight_back(index):
        here = span_of(index)
        grad_weight[here, :] = flat_dot(normed[:, here].T, grads[...]).astype(low)

    attended_turned = attended[...].T

    @pl.loop(0, width // (2 * SPAN))
    def out_back(index):
        here = span_of(index, 2 * SPAN)
        grad_out[:, here] = flat_dot(attended_turned, branch[:, here]).astype(low)


def attend_back(
    branch,
    out_weight,
    queries,
    keys,
    values,
    attended,
    totals,
    cosine,
    sine,
    columns,
    lines,
    inputs,
    normed,
    weight,
):
    rows, width = branch.shape
    wide = out_weight.shape[0]
    low = jnp.bfloat16
    full = jnp.float32
    shape = jax.ShapeDtypeStruct
    return pl.pallas_call(
        attend_back_kernel,
        out_shape=[
            shape((rows, width), low),
            shape(weight.shape, low),
            shape((wide, width), low),
            shape((1, 3 * wide), full),
            shape((1, width), full),
        ],
        in_specs=[VMEM] * 11 + [ANY] * 3,
        out_specs=[VMEM] * 5,
        scratch_shapes=[
            pltpu.VMEM((rows, 3 * wide), low),
            pltpu.VMEM((rows, wide), low),
            pltpu.VMEM((rows, HD), full),
            pltpu.VMEM((rows, HD), full),
            pltpu.VMEM((1, width), full),
            pltpu.VMEM(inputs.shape, low),
            pltpu.VMEM(normed.shape, low),
            pltpu.VMEM(weight.shape, low),
            pltpu.SemaphoreType.DMA((3,)),
        ],
        compiler_params=pltpu.CompilerParams(vmem_limit_bytes=40 * 2**20),
        cost_estimate=pl.CostEstimate(
            flops=2 * rows * width * 8 * wide + 10 * rows * rows * wide,
            bytes_accessed=35 * 2**20,
            transcendentals=rows * rows * wide // HD,
        ),
        name="attend_back",
    )(
        branch,
        out_weight,
        queries,
        keys,
        values,
        attended,
        totals,
        cosine,
        sine,
        columns,
        lines,
        inputs,
        normed,
        weight,
    )


def gate_back_kernel(upstream, scale, gate_up, weight_out, grads, scaled):
    low = jnp.bfloat16
    half = gate_up.shape[1] // 2
    scaled[...] = (scale[...] * upstream[...].astype(jnp.float32)).astype(low)
    grad_unit = turned_dot(scaled[...], weight_out[...])
    gate, up = gate_up[:, :half], gate_up[:, half:]
    sigmoid = 1.0 / (1.0 + jnp.exp(-gate))
    grad_gate = grad_unit * up * (sigmoid * (1.0 + gate * (1.0 - sigmoid)))
    grad_up = grad_unit * (gate * sigmoid)
    grads[...] = jnp.concatenate([grad_gate.astype(low), grad_up.astype(low)], axis=1)


def gate_back(upstream, scale, gate_up, weight_out):
    rows, width = upstream.shape
    hidden = weight_out.shape[0]
    low = jnp.bfloat16

    def block(columns):
        return pl.BlockSpec((SPAN, columns), lambda i: (i, 0))

    return pl.pallas_call(
        gate_back_kernel,
        grid=(rows // SPAN,),
        out_shape=[
            jax.ShapeDtypeStruct((rows, 2 * hidden), low),
            jax.ShapeDtypeStruct((rows, width), low),
        ],
        in_specs=[
            block(width),
            block(1),
            block(2 * hidden),
            pl.BlockSpec((hidden, width), lambda i: (0, 0)),
        ],
        out_specs=[block(2 * hidden), block(width)],
        compiler_params=pltpu.CompilerParams(vmem_limit_bytes=48 * 2**20),
        cost_estimate=pl.CostEstimate(
            flops=2 * rows * width * hidden,
            bytes_accessed=rows * (12 * hidden + 4 * width) + 2 * hidden * width,
            transcendentals=rows * hidden,
        ),
        name="gate_back",
    )(upstream, scale, gate_up, weight_out)


def deal_kernel(pieces, weight, dealt):
    ctx_count = dealt.shape[0]
    width = dealt.shape[2] // pieces
    for c in range(ctx_count):
        dealt[c] = jnp.concatenate(
            [
                weight[:, (q * ctx_count + c) * width : (q * ctx_count + c + 1) * width]
                for q in range(pieces)
            ],
            axis=1,
        )


def deal_columns(weight, ctx_count, pieces):
    rows, columns = weight.shape
    return pl.pallas_call(
        functools.partial(deal_kernel, pieces),
        out_shape=jax.ShapeDtypeStruct((ctx_count, rows, columns // ctx_count), weight.dtype),
        name="deal_columns",
    )(weight)


def collect_kernel(pieces, dealt, whole):
    ctx_count = dealt.shape[0]
    width = dealt.shape[2] // pieces
    whole[...] = jnp.concatenate(
        [
            dealt[c, :, q * width : (q + 1) * width]
            for q in range(pieces)
            for c in range(ctx_count)
        ],
        axis=1,
    ).astype(whole.dtype)


def collect_columns(dealt, pieces):
    ctx_count, rows, columns = dealt.shape
    return pl.pallas_call(
        functools.partial(collect_kernel, pieces),
        out_shape=jax.ShapeDtypeStruct((rows, columns * ctx_count), jnp.float32),
        name="collect_columns",
    )(dealt)


def heads_kernel(order, dealt, whole):
    pairs = dealt.shape[0] * 2
    for place, head in enumerate(order):
        for which in range(3):
            column = (which * 2 + place % 2) * HD
            target = (which * pairs + head) * HD
            whole[:, target : target + HD] = dealt[
                place // 2, :, column : column + HD
            ].astype(whole.dtype)


def collect_heads(dealt, order):
    ctx_count, rows, columns = dealt.shape
    return pl.pallas_call(
        functools.partial(heads_kernel, order),
        out_shape=jax.ShapeDtypeStruct((rows, columns * ctx_count), jnp.float32),
        name="collect_heads",
    )(dealt)


def over(axis, array, dim=0):
    return lax.all_gather(array, axis, axis=dim, tiled=True)


def reduce_over(axis, array, dim=0):
    return lax.psum_scatter(array, axis, scatter_dimension=dim, tiled=True)


def exchange(array):
    return lax.all_to_all(array, "ctx", split_axis=0, concat_axis=0, tiled=True)


def transposed_dot(left, right):
    return lax.dot_general(
        left, right, (((0,), (0,)), ((), ())), preferred_element_type=jnp.float32
    )


def dot_transposed(left, right):
    return lax.dot_general(
        left, right, (((1,), (1,)), ((), ())), preferred_element_type=jnp.float32
    )


def split_plan(
    hidden_in,
    segments,
    block_pairs,
    routes,
    out_grad,
    norm_gain_attn,
    qkv_weight,
    qkv_bias,
    out_weight,
    norm_gain_ffn,
    router_weight,
    shared_gate_weight,
    shared_in_weight,
    shared_out_weight,
    expert_in_weight,
    expert_out_weight,
):
    low = jnp.bfloat16
    full = jnp.float32
    tokens_dev, width = hidden_in.shape[1:]
    block_len = tokens_dev // 2
    ctx_count = lax.axis_size("ctx")
    fsdp_count = lax.axis_size("fsdp")
    ctx_rank = lax.axis_index("ctx")
    dev_count = ctx_count * fsdp_count
    row_len = ctx_count * tokens_dev
    early = width * 3 // 8
    head_count = width // HD
    shard = qkv_weight.shape[0]
    expert_count = router_weight.shape[1]
    shared_shard = shared_out_weight.shape[0]
    shared_width = fsdp_count * shared_shard
    expert_width = expert_out_weight.shape[1] * fsdp_count
    pair_rank = ctx_rank // 2
    side = ctx_rank % 2
    pairs = ctx_count // 2
    head_order = [j + (p * 2 + t) * pairs for j in range(pairs) for p in range(2) for t in range(2)]

    small = jnp.concatenate(
        [
            norm_gain_attn,
            norm_gain_ffn,
            shared_gate_weight,
            router_weight.T.reshape(-1),
            qkv_bias,
        ]
    )
    small_count = small.shape[0]
    small = jnp.pad(small, (0, 16 * HD - small_count)).reshape(16, HD)
    own_numbers = jnp.concatenate(
        [routes.reshape(tokens_dev, -1).T, segments.reshape(1, tokens_dev)], axis=0
    )
    number_count = own_numbers.shape[0]
    own_numbers = jnp.pad(own_numbers, ((0, 8 - number_count), (0, 0)))
    qkv_parts = (
        qkv_weight.reshape(shard, 3, head_count, HD)[:, :, jnp.array(head_order)]
        .reshape(shard, 3, ctx_count, 2 * HD)
        .transpose(2, 0, 1, 3)
        .reshape(ctx_count, shard, 6 * HD)
    )
    own_inputs = hidden_in.reshape(tokens_dev, width)
    row_inputs, qkv_c, out_pair, small_all, numbers = opening(
        ctx_count, 1, own_inputs, qkv_parts, out_weight, small, own_numbers
    )
    qkv_c = qkv_c.reshape(width, 6 * HD)
    out_c = lax.dynamic_index_in_dim(
        out_pair.reshape(2, 2 * HD, width), side, 0, keepdims=False
    )
    small_all = small_all.reshape(dev_count, 16 * HD)
    gain_attn = small_all[:, :shard].reshape(width).astype(full)
    gain_ffn = small_all[:, shard : 2 * shard].reshape(width).astype(full)
    gate_full = small_all[:, 2 * shard : 3 * shard].reshape(width)
    router_t = (
        small_all[:, 3 * shard : (3 + expert_count) * shard]
        .reshape(dev_count, expert_count, shard)
        .transpose(1, 0, 2)
        .reshape(expert_count, width)
    )
    bias_full = small_all[:, (3 + expert_count) * shard : small_count].reshape(3, head_count, HD)
    router_gate = jnp.concatenate([router_t, gate_full[None, :]], axis=0)
    row_seg = numbers[:, number_count - 1].reshape(row_len)
    routed_here = jnp.any(numbers[:, : number_count - 1] == ctx_rank, axis=1).reshape(row_len)

    shared_in_weight, numbers = lax.optimization_barrier((shared_in_weight, numbers))
    expert_outer = over("fsdp", expert_out_weight[0])
    early_upstream = over("ctx", out_grad.reshape(tokens_dev, width)[:, :early])
    inner_parts = deal_columns(shared_in_weight, ctx_count, 2 * fsdp_count)
    expert_inner = over("fsdp", expert_in_weight[0])
    inner_parts = exchange(inner_parts)
    my_heads = [pair_rank + (side * 2 + t) * pairs for t in range(2)]
    bias_c = jnp.concatenate(
        [lax.dynamic_index_in_dim(bias_full, h, 1, keepdims=False) for h in my_heads], axis=1
    ).reshape(6 * HD)

    offsets = jnp.arange(block_len, dtype=jnp.int32)
    positions = (block_pairs[:, None] * block_len + offsets[None, :]).reshape(row_len)
    inputs = own_inputs.astype(full)
    row_inputs = row_inputs.reshape(row_len, width)
    half_len = HD // 2
    frequency = THETA ** (-jnp.arange(half_len, dtype=full) / half_len)
    places = positions.astype(full)
    angles = places[:, None] * frequency[None, :]
    cosine, sine = jnp.cos(angles), jnp.sin(angles)
    cosine = jnp.concatenate([cosine, cosine], axis=1)
    sine = jnp.concatenate([-sine, sine], axis=1)
    key_seg = row_seg.astype(full)
    query_seg = jnp.where(row_seg >= 0, key_seg, -2.0)
    query_marks = jnp.stack([places, query_seg])
    key_marks = jnp.stack([places, key_seg])
    row_normed, queries, keys, values, attended_row, log_totals, branch_part = attend(
        row_inputs,
        gain_attn[None, :],
        qkv_c,
        bias_c.astype(full)[None, :],
        cosine,
        sine,
        query_marks.T,
        key_marks,
        out_c,
    )
    branch_part, inner_parts, early_upstream, expert_outer = lax.optimization_barrier(
        (branch_part, inner_parts, early_upstream, expert_outer)
    )
    branch = line_scatter(ctx_count, 2, branch_part.reshape(ctx_count, tokens_dev, width))
    middle = inputs + branch
    normed_ffn = rms_scale(middle, gain_ffn).astype(low)

    row_ffn, inner_c, outer_c = line_gather(
        ctx_count,
        4,
        normed_ffn,
        inner_parts.reshape(ctx_count * shard, 2 * shared_width),
        shared_out_weight,
    )
    row_ffn = row_ffn.reshape(row_len, width)
    row_ffn, late_grad = lax.optimization_barrier((row_ffn, out_grad))
    late_upstream = over("ctx", late_grad.reshape(tokens_dev, width)[:, early:])
    inner_c = inner_c.reshape(width, 2 * shared_width)
    outer_c = outer_c.reshape(shared_width, width)
    row_logits = dot_transposed(row_ffn, router_gate)
    row_probs = jax.nn.softmax(row_logits[:, :expert_count], axis=-1)
    expert_ids = jnp.arange(expert_count, dtype=jnp.int32)
    here = jnp.where(
        routed_here, jnp.sum(jnp.where(expert_ids[None, :] == ctx_rank, row_probs, 0.0), axis=1), 0.0
    )
    row_gate = jax.nn.sigmoid(row_logits[:, expert_count])
    expert_gu = matmul_low(row_ffn, expert_inner)
    expert_hidden = swiglu_mix(expert_gu, expert_width).astype(low)
    expert_result = matmul_low(expert_hidden, expert_outer).astype(low).astype(full)
    row_shared, expert_result = lax.optimization_barrier((row_ffn, expert_result))
    shared_gu = matmul_low(row_shared, inner_c)
    shared_hidden = swiglu_mix(shared_gu, shared_width).astype(low)
    shared_out = matmul_low(shared_hidden, outer_c)
    shared_out, late_upstream = lax.optimization_barrier((shared_out, late_upstream))
    row_upstream = lax.optimization_barrier(
        jnp.concatenate([early_upstream, late_upstream], axis=1)
    )
    upstream_row = row_upstream.astype(full)
    out_part = (row_gate[:, None] * shared_out + here[:, None] * expert_result).astype(low)
    gate_dot = jnp.sum(upstream_row * shared_out, axis=1)
    expert_dot = jnp.where(routed_here, jnp.sum(upstream_row * expert_result, axis=1), 0.0)
    out_landed = reduce_over("ctx", out_part)

    row_upstream, out_part = lax.optimization_barrier((row_upstream, out_part))
    grad_expert_gu, grad_buffers = gate_back(row_upstream, here[:, None], expert_gu, expert_outer)
    sum_expert_outer = reduce_over("fsdp", transposed_dot(expert_hidden, grad_buffers).astype(low))
    grad_rows = dot_transposed(grad_expert_gu, expert_inner).astype(low)
    row_upstream, grad_rows = lax.optimization_barrier((row_upstream, grad_rows))
    grad_shared_gu, grad_shared_out = gate_back(
        row_upstream, row_gate[:, None], shared_gu, outer_c
    )
    grad_inner = transposed_dot(row_ffn, grad_shared_gu).astype(low)
    sum_inner_c = reduce_over("fsdp", grad_inner)
    grad_ffn_part = (
        dot_transposed(grad_shared_gu, inner_c) + grad_rows.astype(full)
    ).astype(low)
    dots = jnp.stack([gate_dot, expert_dot]).reshape(2, ctx_count, tokens_dev).transpose(1, 0, 2)
    grad_ffn_part, grad_inner = lax.optimization_barrier((grad_ffn_part, grad_inner))
    grad_normed, own_dots, grad_expert_inner = line_scatter(
        ctx_count,
        6,
        grad_ffn_part.reshape(ctx_count, tokens_dev, width),
        jnp.pad(dots, ((0, 0), (0, 6), (0, 0))),
        row_ffn,
        grad_expert_gu,
    )
    sum_expert_inner = reduce_over("fsdp", grad_expert_inner)
    hidden_out = (middle + out_landed.astype(full)).astype(low).reshape(1, tokens_dev, width)

    own_logits = dot_transposed(normed_ffn, router_gate)
    router_probs = jax.nn.softmax(own_logits[:, :expert_count], axis=-1)
    gate_value = jax.nn.sigmoid(own_logits[:, expert_count])
    grad_gate_logit = gate_value * (1.0 - gate_value) * jnp.sum(own_dots[:, 0], axis=0)
    grad_choice = own_dots[:, 1].T
    grad_logits = router_probs * (
        grad_choice - jnp.sum(router_probs * grad_choice, axis=1, keepdims=True)
    )
    grad_small = jnp.concatenate([grad_logits, grad_gate_logit[:, None]], axis=1).astype(low)
    grad_router_gate = transposed_dot(grad_small, normed_ffn)
    grad_normed = grad_normed + matmul_low(grad_small, router_gate)
    unused_norm, norm_pull = jax.vjp(rms_scale, middle, gain_ffn)
    grad_middle_norm, grad_gain_ffn = norm_pull(grad_normed)
    grad_middle = out_grad.reshape(tokens_dev, width).astype(full) + grad_middle_norm

    grad_branch, sum_expert_outer, hidden_out = lax.optimization_barrier(
        (grad_middle.astype(low), sum_expert_outer, hidden_out)
    )
    row_branch, grad_outer = product_gather(
        ctx_count, 3, grad_branch, shared_hidden, grad_shared_out
    )
    row_branch, sum_inner_c = lax.optimization_barrier(
        (row_branch.reshape(row_len, width), sum_inner_c)
    )
    sum_inner = collect_columns(
        exchange(sum_inner_c.reshape(ctx_count, shard, 2 * shared_width)), 2 * fsdp_count
    )
    grad_attn_part, grad_qkv_c, grad_out_c, grad_bias_c, grad_gain_attn = attend_back(
        row_branch,
        out_c,
        queries,
        keys,
        values,
        attended_row,
        log_totals.T,
        cosine,
        sine,
        key_marks.T,
        query_marks,
        row_inputs,
        row_normed,
        qkv_c,
    )
    grad_out_c = grad_out_c.reshape(2, HD, width)
    padded_out = jnp.concatenate(
        [jnp.where(side == p, grad_out_c, jnp.zeros_like(grad_out_c)) for p in range(2)], axis=0
    )
    grad_attn_part, sum_inner = lax.optimization_barrier((grad_attn_part, sum_inner))
    grad_bias_c = grad_bias_c.reshape(3, 1, 2, HD)
    mine = (jnp.arange(ctx_count) == ctx_rank)[None, :, None, None]
    places_of = [head_order.index(h) for h in range(head_count)]
    grad_bias = (
        jnp.where(mine, grad_bias_c, 0.0)
        .reshape(3, pairs, 2, 2, HD)
        .transpose(0, 2, 3, 1, 4)
        .reshape(dev_count, -1)
    )
    small_grads = jnp.concatenate(
        [
            grad_gain_attn.reshape(dev_count, shard),
            grad_gain_ffn.reshape(dev_count, shard),
            grad_router_gate.reshape(expert_count + 1, dev_count, shard)
            .transpose(1, 0, 2)
            .reshape(dev_count, (expert_count + 1) * shard),
            grad_bias,
        ],
        axis=1,
    )
    small_grads = jnp.pad(small_grads, ((0, 0), (0, 8 * HD - small_count)))
    grad_normed_attn, sum_qkv_c, sum_out, sum_outer, sums = closing(
        ctx_count,
        5,
        grad_attn_part.reshape(ctx_count, tokens_dev, width),
        grad_qkv_c.reshape(fsdp_count, ctx_count * shard, 6 * HD),
        padded_out,
        grad_outer.reshape(fsdp_count, shared_shard, width),
        small_grads.reshape(fsdp_count, ctx_count, 8, HD),
    )
    sums = sums.reshape(8 * HD)[:small_count]
    sum_qkv = collect_heads(sum_qkv_c, head_order)
    unused_norm, first_pull = jax.vjp(lambda v: rms_scale(v, gain_attn), inputs)
    input_grad = grad_middle + first_pull(grad_normed_attn)[0]
    sum_router = sums[2 * shard : (2 + expert_count) * shard].reshape(expert_count, shard).T
    return (
        hidden_out,
        input_grad.reshape(1, tokens_dev, width),
        sums[:shard],
        sum_qkv,
        sums[(3 + expert_count) * shard :],
        sum_out,
        sums[shard : 2 * shard],
        sum_router,
        sums[(2 + expert_count) * shard : (3 + expert_count) * shard],
        sum_inner,
        sum_outer,
        sum_expert_inner.astype(full)[None],
        sum_expert_outer.astype(full)[None],
    )


def local(*arrays):
    width = arrays[0].shape[2]
    ctx_count = lax.axis_size("ctx")
    shard = arrays[6].shape[0]
    fits = (
        width == 2 * ctx_count * HD
        and 2 * shard == HD
        and ctx_count % 2 == 0
        and lax.axis_size("fsdp") * ctx_count * shard == width
        and arrays[14].shape[0] == 1
    )
    return split_plan(*arrays) if fits else gathered_plan(*arrays)


def solution(mesh):
    in_specs = (
        P("fsdp", "ctx", None),
        P("fsdp", "ctx"),
        P(),
        P("fsdp", "ctx", None),
        P("fsdp", "ctx", None),
        P(("fsdp", "ctx")),
        P(("fsdp", "ctx"), None),
        P(("fsdp", "ctx")),
        P(("fsdp", "ctx"), None),
        P(("fsdp", "ctx")),
        P(("fsdp", "ctx"), None),
        P(("fsdp", "ctx")),
        P(("fsdp", "ctx"), None),
        P(("fsdp", "ctx"), None),
        P("ctx", "fsdp", None),
        P("ctx", "fsdp", None),
    )
    out_specs = (
        P("fsdp", "ctx", None),
        P("fsdp", "ctx", None),
        P(("fsdp", "ctx")),
        P(("fsdp", "ctx"), None),
        P(("fsdp", "ctx")),
        P(("fsdp", "ctx"), None),
        P(("fsdp", "ctx")),
        P(("fsdp", "ctx"), None),
        P(("fsdp", "ctx")),
        P(("fsdp", "ctx"), None),
        P(("fsdp", "ctx"), None),
        P("ctx", "fsdp", None),
        P("ctx", "fsdp", None),
    )
    return jax.shard_map(local, mesh=mesh, in_specs=in_specs, out_specs=out_specs, check_vma=False)
```

```python
import functools

import jax
import jax.numpy as jnp
from jax import lax
from jax.experimental import pallas as pl
from jax.experimental.pallas import tpu as pltpu
from jax.sharding import PartitionSpec as P

HD = 128


EPSILON = 1e-06
THETA = 1000000.0
heads_per_group = 4


def rms_scale(values, gain_vec):
    return (
        values * lax.rsqrt(jnp.mean(values * values, axis=-1, keepdims=True) + EPSILON) * gain_vec
    )


def rotate(values, positions):
    half_len = values.shape[-1] // 2
    frequency = THETA ** (-jnp.arange(half_len, dtype=jnp.float32) / half_len)
    angles = positions.astype(jnp.float32)[:, None] * frequency[None, :]
    cosine = jnp.cos(angles)[:, None, :]
    sine_part = jnp.sin(angles)[:, None, :]
    first_half = values[..., :half_len]
    second = values[..., half_len:]
    return jnp.concatenate(
        [first_half * cosine - second * sine_part, second * cosine + first_half * sine_part],
        axis=-1,
    )


def visible(query_pos, query_seg, key_pos, key_seg):
    same_doc = (key_seg[None, :] == query_seg[:, None]) & (query_seg[:, None] >= 0)
    causal = key_pos[None, :] <= query_pos[:, None]
    return same_doc & causal | (key_pos[None, :] == query_pos[:, None])


def swiglu_mix(gate_up, hidden_width):
    return jax.nn.silu(gate_up[..., :hidden_width]) * gate_up[..., hidden_width:]


def matmul_low(left, right):
    return jnp.dot(left, right, preferred_element_type=jnp.float32)


def gathered_plan(
    hidden_in,
    segments,
    block_pairs,
    routes,
    out_grad,
    norm_gain_attn,
    qkv_weight,
    qkv_bias,
    out_weight,
    norm_gain_ffn,
    router_weight,
    shared_gate_weight,
    shared_in_weight,
    shared_out_weight,
    expert_in_weight,
    expert_out_weight,
):
    tokens_dev = hidden_in.shape[1]
    model_width = hidden_in.shape[2]
    block_len = tokens_dev // 2
    inputs = hidden_in.reshape(tokens_dev, model_width).astype(jnp.float32)
    seg_local = segments.reshape(tokens_dev)
    token_routes = routes.reshape(tokens_dev, -1)
    top_count = token_routes.shape[1]
    ctx_count = lax.axis_size("ctx")
    ctx_rank = lax.axis_index("ctx")
    offsets = jnp.arange(block_len, dtype=jnp.int32)
    all_positions = (
        block_pairs.reshape(ctx_count, 2)[:, :, None] * block_len + offsets[None, None, :]
    ).reshape(ctx_count * tokens_dev)
    my_positions = lax.dynamic_slice_in_dim(all_positions, ctx_rank * tokens_dev, tokens_dev, 0)
    gathered = (
        lax.all_gather(norm_gain_attn, ("fsdp", "ctx"), axis=0, tiled=True),
        lax.all_gather(qkv_weight, ("fsdp", "ctx"), axis=0, tiled=True),
        lax.all_gather(qkv_bias, ("fsdp", "ctx"), axis=0, tiled=True),
        lax.all_gather(out_weight, ("fsdp", "ctx"), axis=0, tiled=True),
        lax.all_gather(norm_gain_ffn, ("fsdp", "ctx"), axis=0, tiled=True),
        lax.all_gather(router_weight, ("fsdp", "ctx"), axis=0, tiled=True),
        lax.all_gather(shared_gate_weight, ("fsdp", "ctx"), axis=0, tiled=True),
        lax.all_gather(shared_in_weight, ("fsdp", "ctx"), axis=0, tiled=True),
        lax.all_gather(shared_out_weight, ("fsdp", "ctx"), axis=0, tiled=True),
    )
    (
        gain_attn,
        qkv_full,
        shift_full,
        out_full,
        gain_ffn,
        router_full,
        gate_full,
        inner_full,
        outer_full,
    ) = gathered
    gain_attn = gain_attn.astype(jnp.float32)
    gain_ffn = gain_ffn.astype(jnp.float32)
    heads_width = out_full.shape[0]
    head_count = heads_width // HD
    group_width = heads_per_group * HD
    group_count = head_count // heads_per_group
    normed = rms_scale(inputs, gain_attn).astype(jnp.bfloat16)
    projected = matmul_low(normed, qkv_full) + shift_full.astype(jnp.float32)
    query_pre = projected[:, :heads_width].reshape(tokens_dev, head_count, HD)
    key_pre = projected[:, heads_width : 2 * heads_width].reshape(tokens_dev, head_count, HD)

    def place_heads(query_in, key_in):
        return (rotate(query_in, my_positions) * HD ** (-0.5), rotate(key_in, my_positions))

    query_rot, key_rot = place_heads(query_pre, key_pre)
    query_low = query_rot.reshape(tokens_dev, heads_width).astype(jnp.bfloat16)
    key_low = key_rot.reshape(tokens_dev, heads_width).astype(jnp.bfloat16)
    value_low = projected[:, 2 * heads_width :].astype(jnp.bfloat16)
    keys_all, values_all, segs_all = (
        lax.all_gather(key_low, "ctx", axis=0, tiled=True),
        lax.all_gather(value_low, "ctx", axis=0, tiled=True),
        lax.all_gather(seg_local.astype(jnp.bfloat16), "ctx", axis=0, tiled=True),
    )
    allowed = visible(
        my_positions, seg_local.astype(jnp.float32), all_positions, segs_all.astype(jnp.float32)
    )

    def head_slice(matrix, group_index):
        return lax.dynamic_slice_in_dim(matrix, group_index * group_width, group_width, 1).reshape(
            matrix.shape[0], heads_per_group, HD
        )

    def forward_group(group_index):
        query_part = head_slice(query_low, group_index)
        key_part = head_slice(keys_all, group_index)
        value_part = head_slice(values_all, group_index)
        scores = jnp.einsum(
            "qhd,khd->hqk", query_part, key_part, preferred_element_type=jnp.float32
        )
        scores = jnp.where(allowed[None], scores, -1e30)
        highest = jnp.max(scores, axis=-1, keepdims=True)
        log_total = highest + jnp.log(jnp.sum(jnp.exp(scores - highest), axis=-1, keepdims=True))
        weights = jnp.exp(scores - log_total).astype(jnp.bfloat16)
        mixed = jnp.einsum("hqk,khd->qhd", weights, value_part, preferred_element_type=jnp.float32)
        return (mixed, log_total[..., 0])

    mixed_groups, log_totals = lax.map(forward_group, jnp.arange(group_count, dtype=jnp.int32))
    attended = (
        jnp.moveaxis(mixed_groups, 0, 1).reshape(tokens_dev, heads_width).astype(jnp.bfloat16)
    )
    middle = inputs + matmul_low(attended, out_full)
    normed_ffn = rms_scale(middle, gain_ffn).astype(jnp.bfloat16)
    logits = matmul_low(normed_ffn, router_full)
    router_probs = jax.nn.softmax(logits, axis=-1)
    expert_count = logits.shape[1]
    expert_ids = jnp.arange(expert_count, dtype=jnp.int32)
    chosen = (token_routes[:, :, None] == expert_ids[None, None, :]).astype(jnp.float32)
    gate_weights = jnp.sum(chosen * router_probs[:, None, :], axis=-1)
    capacity = 2 * tokens_dev * top_count // expert_count
    local_experts = expert_in_weight.shape[0]
    assigned = tokens_dev * top_count
    flat_routes = token_routes.reshape(assigned)
    onehot = (flat_routes[:, None] == expert_ids[None, :]).astype(jnp.int32)
    earlier = jnp.cumsum(onehot, axis=0) - onehot
    places = flat_routes * capacity + jnp.sum(earlier * onehot, axis=1)
    slot_source = (
        jnp.full((expert_count * capacity,), assigned, jnp.int32)
        .at[places]
        .set(jnp.arange(assigned, dtype=jnp.int32))
    )
    slot_token = slot_source // top_count
    padded_rows = jnp.concatenate([normed_ffn, jnp.zeros((1, model_width), jnp.bfloat16)], axis=0)
    outgoing = padded_rows[slot_token].reshape(ctx_count, local_experts * capacity, model_width)
    expert_inner, expert_outer = (
        lax.all_gather(expert_in_weight, "fsdp", axis=1, tiled=True),
        lax.all_gather(expert_out_weight, "fsdp", axis=1, tiled=True),
    )
    landed_tokens = lax.all_to_all(outgoing, "ctx", split_axis=0, concat_axis=0, tiled=True)
    incoming = landed_tokens.reshape(ctx_count, local_experts, capacity, model_width)
    expert_gu = jnp.einsum(
        "necd,edf->necf", incoming, expert_inner, preferred_element_type=jnp.float32
    )
    expert_width = expert_outer.shape[1]
    expert_hidden = swiglu_mix(expert_gu, expert_width).astype(jnp.bfloat16)
    expert_result = jnp.einsum(
        "necf,efd->necd", expert_hidden, expert_outer, preferred_element_type=jnp.float32
    ).astype(jnp.bfloat16)
    returned = lax.all_to_all(
        expert_result.reshape(ctx_count, local_experts * capacity, model_width),
        "ctx",
        split_axis=0,
        concat_axis=0,
        tiled=True,
    )
    picked = (
        returned.reshape(expert_count * capacity, model_width)[places]
        .reshape(tokens_dev, top_count, model_width)
        .astype(jnp.float32)
    )
    routed = jnp.sum(gate_weights[:, :, None] * picked, axis=1)
    upstream = out_grad.reshape(tokens_dev, model_width).astype(jnp.float32)
    shared_gu = matmul_low(normed_ffn, inner_full)
    shared_width = outer_full.shape[0]
    shared_hidden = swiglu_mix(shared_gu, shared_width).astype(jnp.bfloat16)
    shared_out = matmul_low(shared_hidden, outer_full)
    gate_value = jax.nn.sigmoid(matmul_low(normed_ffn, gate_full))
    output = middle + gate_value[:, None] * shared_out + routed
    hidden_out = output.astype(jnp.bfloat16).reshape(1, tokens_dev, model_width)
    gain_ffn, router_full, gate_full, inner_full, outer_full = (
        lax.all_gather(norm_gain_ffn, ("fsdp", "ctx"), axis=0, tiled=True),
        lax.all_gather(router_weight, ("fsdp", "ctx"), axis=0, tiled=True),
        lax.all_gather(shared_gate_weight, ("fsdp", "ctx"), axis=0, tiled=True),
        lax.all_gather(shared_in_weight, ("fsdp", "ctx"), axis=0, tiled=True),
        lax.all_gather(shared_out_weight, ("fsdp", "ctx"), axis=0, tiled=True),
    )
    gain_ffn = gain_ffn.astype(jnp.float32)
    grad_shared_out = (gate_value[:, None] * upstream).astype(jnp.bfloat16)
    grad_outer = jnp.einsum(
        "tf,td->fd", shared_hidden, grad_shared_out, preferred_element_type=jnp.float32
    )
    grad_hidden = jnp.einsum(
        "td,fd->tf", grad_shared_out, outer_full, preferred_element_type=jnp.float32
    )
    unused_mix, mix_pull = jax.vjp(functools.partial(swiglu_mix, hidden_width=shared_width), shared_gu)
    grad_shared_gu = mix_pull(grad_hidden)[0].astype(jnp.bfloat16)
    grad_inner = jnp.einsum(
        "td,tf->df", normed_ffn, grad_shared_gu, preferred_element_type=jnp.float32
    )
    grad_normed = jnp.einsum(
        "tf,df->td", grad_shared_gu, inner_full, preferred_element_type=jnp.float32
    )
    grad_gate_logit = (
        gate_value * (1.0 - gate_value) * jnp.sum(upstream * shared_out, axis=1)
    ).astype(jnp.bfloat16)
    grad_gate_vec = jnp.einsum(
        "td,t->d", normed_ffn, grad_gate_logit, preferred_element_type=jnp.float32
    )
    grad_normed = (
        grad_normed
        + grad_gate_logit.astype(jnp.float32)[:, None] * gate_full.astype(jnp.float32)[None, :]
    )
    grad_gates = jnp.sum(upstream[:, None, :] * picked, axis=2)
    grad_choice_probs = jnp.sum(chosen * grad_gates[:, :, None], axis=1)
    grad_logits = (
        router_probs
        * (grad_choice_probs - jnp.sum(router_probs * grad_choice_probs, axis=1, keepdims=True))
    ).astype(jnp.bfloat16)
    grad_router = jnp.einsum(
        "td,te->de", normed_ffn, grad_logits, preferred_element_type=jnp.float32
    )
    grad_normed = grad_normed + jnp.einsum(
        "te,de->td", grad_logits, router_full, preferred_element_type=jnp.float32
    )
    grad_slots = (
        (gate_weights[:, :, None] * upstream[:, None, :])
        .astype(jnp.bfloat16)
        .reshape(assigned, model_width)
    )
    padded_grads = jnp.concatenate([grad_slots, jnp.zeros((1, model_width), jnp.bfloat16)], axis=0)
    grad_outgoing = padded_grads[slot_source].reshape(
        ctx_count, local_experts * capacity, model_width
    )
    grad_incoming = lax.all_to_all(
        grad_outgoing, "ctx", split_axis=0, concat_axis=0, tiled=True
    ).reshape(ctx_count, local_experts, capacity, model_width)
    grad_expert_hidden = jnp.einsum(
        "necd,efd->necf", grad_incoming, expert_outer, preferred_element_type=jnp.float32
    )
    grad_expert_outer = jnp.einsum(
        "necf,necd->efd", expert_hidden, grad_incoming, preferred_element_type=jnp.float32
    )
    unused_mix, expert_pull = jax.vjp(functools.partial(swiglu_mix, hidden_width=expert_width), expert_gu)
    grad_expert_gu = expert_pull(grad_expert_hidden)[0].astype(jnp.bfloat16)
    grad_expert_inner = jnp.einsum(
        "necd,necf->edf", incoming, grad_expert_gu, preferred_element_type=jnp.float32
    )
    grad_expert_rows = jnp.einsum(
        "necf,edf->necd", grad_expert_gu, expert_inner, preferred_element_type=jnp.float32
    ).astype(jnp.bfloat16)
    grad_returned = lax.all_to_all(
        grad_expert_rows.reshape(ctx_count, local_experts * capacity, model_width),
        "ctx",
        split_axis=0,
        concat_axis=0,
        tiled=True,
    )
    grad_picked = grad_returned.reshape(expert_count * capacity, model_width)[places].reshape(
        tokens_dev, top_count, model_width
    )
    grad_normed = grad_normed + jnp.sum(grad_picked.astype(jnp.float32), axis=1)
    sum_expert_inner, sum_expert_outer = (
        lax.psum_scatter(
            grad_expert_inner.astype(jnp.bfloat16), "fsdp", scatter_dimension=1, tiled=True
        ).astype(jnp.float32),
        lax.psum_scatter(
            grad_expert_outer.astype(jnp.bfloat16), "fsdp", scatter_dimension=1, tiled=True
        ).astype(jnp.float32),
    )
    unused_norm, norm_pull = jax.vjp(rms_scale, middle, gain_ffn)
    grad_middle_norm, grad_gain_ffn = norm_pull(grad_normed)
    grad_middle = upstream + grad_middle_norm
    sum_gain_ffn, sum_router, sum_gate_vec, sum_inner, sum_outer = (
        lax.psum_scatter(grad_gain_ffn, ("fsdp", "ctx"), scatter_dimension=0, tiled=True),
        lax.psum_scatter(grad_router, ("fsdp", "ctx"), scatter_dimension=0, tiled=True),
        lax.psum_scatter(grad_gate_vec, ("fsdp", "ctx"), scatter_dimension=0, tiled=True),
        lax.psum_scatter(grad_inner, ("fsdp", "ctx"), scatter_dimension=0, tiled=True),
        lax.psum_scatter(grad_outer, ("fsdp", "ctx"), scatter_dimension=0, tiled=True),
    )
    grad_branch = grad_middle.astype(jnp.bfloat16)
    grad_out_mat = jnp.einsum(
        "tc,td->cd", attended, grad_branch, preferred_element_type=jnp.float32
    )
    grad_attended = jnp.einsum(
        "td,cd->tc", grad_branch, out_full, preferred_element_type=jnp.float32
    ).astype(jnp.bfloat16)
    keys_again, values_again = (
        lax.all_gather(key_low, "ctx", axis=0, tiled=True),
        lax.all_gather(value_low, "ctx", axis=0, tiled=True),
    )

    def backward_group(group_index):
        query_part = head_slice(query_low, group_index)
        key_part = head_slice(keys_again, group_index)
        value_part = head_slice(values_again, group_index)
        grad_part = head_slice(grad_attended, group_index)
        log_total = lax.dynamic_index_in_dim(log_totals, group_index, 0, keepdims=False)
        scores = jnp.einsum(
            "qhd,khd->hqk", query_part, key_part, preferred_element_type=jnp.float32
        )
        scores = jnp.where(allowed[None], scores, -1e30)
        weights = jnp.exp(scores - log_total[..., None])
        grad_weights = jnp.einsum(
            "qhd,khd->hqk", grad_part, value_part, preferred_element_type=jnp.float32
        )
        offset_term = jnp.sum(weights * grad_weights, axis=-1, keepdims=True)
        grad_scores = (weights * (grad_weights - offset_term)).astype(jnp.bfloat16)
        grad_query = jnp.einsum(
            "hqk,khd->qhd", grad_scores, key_part, preferred_element_type=jnp.float32
        )
        grad_key = jnp.einsum(
            "hqk,qhd->khd", grad_scores, query_part, preferred_element_type=jnp.float32
        )
        grad_value = jnp.einsum(
            "hqk,qhd->khd",
            weights.astype(jnp.bfloat16),
            grad_part,
            preferred_element_type=jnp.float32,
        )
        return (grad_query, grad_key, grad_value)

    grad_queries, grad_keys, grad_values = lax.map(
        backward_group, jnp.arange(group_count, dtype=jnp.int32)
    )
    row_total = keys_again.shape[0]
    grad_key_rows = jnp.moveaxis(grad_keys, 0, 1).reshape(row_total, heads_width)
    grad_value_rows = jnp.moveaxis(grad_values, 0, 1).reshape(row_total, heads_width)
    key_share, value_share = (
        lax.psum_scatter(
            grad_key_rows.astype(jnp.bfloat16), "ctx", scatter_dimension=0, tiled=True
        ).astype(jnp.float32),
        lax.psum_scatter(
            grad_value_rows.astype(jnp.bfloat16), "ctx", scatter_dimension=0, tiled=True
        ).astype(jnp.float32),
    )
    grad_query_heads = jnp.moveaxis(grad_queries, 0, 1).reshape(tokens_dev, head_count, HD)
    unused_rot, rotate_pull = jax.vjp(place_heads, query_pre, key_pre)
    grad_query_pre, grad_key_pre = rotate_pull(
        (grad_query_heads, key_share.reshape(tokens_dev, head_count, HD))
    )
    grad_projected = jnp.concatenate(
        [
            grad_query_pre.reshape(tokens_dev, heads_width),
            grad_key_pre.reshape(tokens_dev, heads_width),
            value_share,
        ],
        axis=1,
    ).astype(jnp.bfloat16)
    grad_qkv = jnp.einsum("td,tc->dc", normed, grad_projected, preferred_element_type=jnp.float32)
    grad_shift = jnp.sum(grad_projected.astype(jnp.float32), axis=0)
    grad_normed_attn = jnp.einsum(
        "tc,dc->td", grad_projected, qkv_full, preferred_element_type=jnp.float32
    )
    unused_norm, first_pull = jax.vjp(rms_scale, inputs, gain_attn)
    grad_inputs_norm, grad_gain_attn = first_pull(grad_normed_attn)
    input_grad = grad_middle + grad_inputs_norm
    sum_gain_attn, sum_qkv, sum_shift, sum_out = (
        lax.psum_scatter(grad_gain_attn, ("fsdp", "ctx"), scatter_dimension=0, tiled=True),
        lax.psum_scatter(grad_qkv, ("fsdp", "ctx"), scatter_dimension=0, tiled=True),
        lax.psum_scatter(grad_shift, ("fsdp", "ctx"), scatter_dimension=0, tiled=True),
        lax.psum_scatter(grad_out_mat, ("fsdp", "ctx"), scatter_dimension=0, tiled=True),
    )
    return (
        hidden_out,
        input_grad.reshape(1, tokens_dev, model_width),
        sum_gain_attn,
        sum_qkv,
        sum_shift,
        sum_out,
        sum_gain_ffn,
        sum_router,
        sum_gate_vec,
        sum_inner,
        sum_outer,
        sum_expert_inner,
        sum_expert_outer,
    )


SPAN = 256


def flat_dot(left, right):
    return lax.dot_general(left, right, (((1,), (0,)), ((), ())), preferred_element_type=jnp.float32)


def turned_dot(left, right):
    return lax.dot_general(left, right, (((1,), (1,)), ((), ())), preferred_element_type=jnp.float32)


def span_of(index, size=SPAN):
    return pl.ds(pl.multiple_of(index * size, size), size)


MESH = pl.DeviceIdType.MESH
ANY = pl.BlockSpec(memory_space=pl.ANY)
VMEM = pl.BlockSpec(memory_space=pltpu.VMEM)


def remote(source, target, send_sem, recv_sem, **place):
    return pltpu.make_async_remote_copy(
        src_ref=source,
        dst_ref=target,
        send_sem=send_sem,
        recv_sem=recv_sem,
        device_id=place,
        device_id_type=MESH,
    )


def line_place():
    here = lax.axis_index("ctx")
    line = here % 2
    return here, here // 2, line, here + 1 - 2 * line


def greet_line(last, here, level, side, others=0):
    barrier = pltpu.get_barrier_semaphore()
    pl.semaphore_signal(barrier, inc=1, device_id={"ctx": side}, device_id_type=MESH)

    @pl.when(level < last)
    def up():
        pl.semaphore_signal(barrier, inc=1, device_id={"ctx": here + 2}, device_id_type=MESH)

    @pl.when(level > 0)
    def down():
        pl.semaphore_signal(barrier, inc=1, device_id={"ctx": here - 2}, device_id_type=MESH)

    ends = jnp.where(level < last, 1, 0) + jnp.where(level > 0, 1, 0)
    pl.semaphore_wait(barrier, 1 + others + ends)


def line_copy(rows_ref, block, way, target, sems, source=None):
    send_sem, recv_sem = sems
    return remote(
        rows_ref.at[block] if source is None else source,
        rows_ref.at[block],
        send_sem.at[block, way],
        recv_sem.at[block],
        ctx=target,
    )


def line_start(rows_ref, own_ref, sems, place, last):
    here, level, line, side = place

    @pl.when(level < last)
    def up():
        line_copy(rows_ref, here, 0, here + 2, sems, own_ref).start()

    @pl.when(level > 0)
    def down():
        line_copy(rows_ref, here, 1, here - 2, sems, own_ref).start()

    line_copy(rows_ref, here, 2, side, sems, own_ref).start()


def line_step(rows_ref, sems, place, last, step):
    here, level, line, side = place

    @pl.when(level >= step)
    def from_below():
        block = here - 2 * step
        line_copy(rows_ref, block, 0, side, sems).wait_recv()

        @pl.when(level < last)
        def on():
            line_copy(rows_ref, block, 0, here + 2, sems).start()

        line_copy(rows_ref, block, 2, side, sems).start()

    @pl.when(level + step <= last)
    def from_above():
        block = here + 2 * step
        line_copy(rows_ref, block, 1, side, sems).wait_recv()

        @pl.when(level > 0)
        def on():
            line_copy(rows_ref, block, 1, here - 2, sems).start()

        line_copy(rows_ref, block, 2, side, sems).start()


def line_finish(rows_ref, sems, place, last):
    here, level, line, side = place
    for other in range(last + 1):
        block = 2 * other + line
        line_copy(rows_ref, 2 * other + 1 - line, 2, side, sems).wait_recv()
        line_copy(rows_ref, block, 2, side, sems).wait_send()

        @pl.when((other <= level) & (level < last))
        def up():
            line_copy(rows_ref, block, 0, side, sems).wait_send()

        @pl.when((other >= level) & (level > 0))
        def down():
            line_copy(rows_ref, block, 1, side, sems).wait_send()


ROWS_STEP = 16


def add_rows(target, pieces, row_count):
    def one(index, carry):
        rows = pl.ds(pl.multiple_of(index * ROWS_STEP, ROWS_STEP), ROWS_STEP)
        total = pieces[0][rows, :].astype(jnp.float32)
        for piece in pieces[1:]:
            total = total + piece[rows, :].astype(jnp.float32)
        target[rows, :] = total.astype(target.dtype)
        return carry

    lax.fori_loop(0, row_count // ROWS_STEP, one, 0)


def scatter_turns(last, part, total, crossed, rising, falling, sums, *sems):
    cross_send, cross_recv, move_send, rise_recv, fall_recv = sems
    here, level, line, side = line_place()
    row_count = total.shape[0]

    def turn(k):
        middle = (level > 0) & (level < last)
        swapped = k + jnp.where(middle, (0, 0, 1, -1)[k], 0)
        return jnp.where(level * 2 < last, last - swapped, swapped)

    def cross(goal):
        return remote(
            part.at[2 * goal + 1 - line],
            crossed.at[goal],
            cross_send.at[goal],
            cross_recv.at[goal],
            ctx=side,
        )

    def rise(goal):
        return remote(
            sums.at[goal], rising.at[goal], move_send.at[goal], rise_recv.at[goal], ctx=here + 2
        )

    def fall(goal):
        return remote(
            sums.at[goal], falling.at[goal], move_send.at[goal], fall_recv.at[goal], ctx=here - 2
        )

    for k in range(min(2, last + 1)):
        cross(turn(k)).start()
    for k in range(last + 1):
        yield k
        goal = turn(k)
        mine = part.at[2 * goal + line]
        cross(goal).wait_recv()
        if k + 2 <= last:
            cross(turn(k + 2)).start()

        @pl.when(goal > level)
        def upward():
            @pl.when(level > 0)
            def joined():
                rise(goal).wait_recv()
                add_rows(sums.at[goal], (mine, crossed.at[goal], rising.at[goal]), row_count)

            @pl.when(level == 0)
            def first():
                add_rows(sums.at[goal], (mine, crossed.at[goal]), row_count)

            rise(goal).start()

        @pl.when(goal < level)
        def downward():
            @pl.when(level < last)
            def joined():
                fall(goal).wait_recv()
                add_rows(sums.at[goal], (mine, crossed.at[goal], falling.at[goal]), row_count)

            @pl.when(level == last)
            def first():
                add_rows(sums.at[goal], (mine, crossed.at[goal]), row_count)

            fall(goal).start()

        @pl.when(goal == level)
        def here_at_last():
            @pl.when(level > 0)
            def from_below():
                rise(goal).wait_recv()

            @pl.when(level < last)
            def from_above():
                fall(goal).wait_recv()

            @pl.when(level == 0)
            def bottom():
                add_rows(total, (mine, crossed.at[goal], falling.at[goal]), row_count)

            @pl.when(level == last)
            def top():
                add_rows(total, (mine, crossed.at[goal], rising.at[goal]), row_count)

            @pl.when((level > 0) & (level < last))
            def between():
                add_rows(
                    total,
                    (mine, crossed.at[goal], rising.at[goal], falling.at[goal]),
                    row_count,
                )

    for goal in range(last + 1):
        cross(goal).wait_send()

        @pl.when(goal != level)
        def sent():
            rise(goal).wait_send()


def scatter_kernel(
    ctx_count, part, small, far_tokens, far_grads, total, small_in, weight_grad, *refs
):
    *refs, product, store_sem, tokens, grads, load_sem = refs
    loads = [
        pltpu.make_async_copy(source, target, load_sem.at[i])
        for i, (source, target) in enumerate(((far_tokens, tokens), (far_grads, grads)))
    ]
    for copy in loads:
        copy.start()
    greet_all(ctx_count)
    here = lax.axis_index("ctx")
    starts, waits = spread(
        lambda peer: small.at[peer], lambda source: small_in.at[source], refs[9:11], ctx_count
    )
    for copy in starts:
        copy.start()
    small_in[here] = small[here]
    turns = scatter_turns(ctx_count // 2 - 1, part, total, *refs[:9])
    next(turns)
    pieces = ctx_count // 2
    depth = tokens.shape[1] // pieces
    stores = []
    for copy in loads:
        copy.wait()
    for piece in range(pieces):

        @pl.loop(0, depth // SPAN)
        def multiply(index):
            here = pl.ds(pl.multiple_of(piece * depth + index * SPAN, SPAN), SPAN)
            product[here, :] = flat_dot(tokens[:, here].T, grads[...]).astype(product.dtype)

        rows = pl.ds(piece * depth, depth)
        stores.append(
            pltpu.make_async_copy(product.at[rows], weight_grad.at[rows], store_sem.at[piece])
        )
        stores[-1].start()
        next(turns, None)
    for copy in waits:
        copy.wait_recv()
    for copy in starts:
        copy.wait_send()
    for copy in stores:
        copy.wait()


def line_scatter_kernel(last, part, total, *refs):
    here, level, line, side = line_place()
    greet_line(last, here, level, side)
    for step in scatter_turns(last, part, total, *refs):
        pass


def line_scatter(ctx_count, call_id, part, small=None, tokens=None, grads=None):
    rows, width = part.shape[1:]
    half = ctx_count // 2
    dma = pltpu.SemaphoreType.DMA((half,))
    spread_dma = pltpu.SemaphoreType.DMA((ctx_count,))
    slots = pltpu.VMEM((half, rows, width), part.dtype)
    total = jax.ShapeDtypeStruct((rows, width), jnp.float32)
    params = pltpu.CompilerParams(
        collective_id=call_id, has_side_effects=True, vmem_limit_bytes=40 * 2**20
    )
    if small is None:
        return pl.pallas_call(
            functools.partial(line_scatter_kernel, half - 1),
            out_shape=total,
            in_specs=[VMEM],
            out_specs=VMEM,
            scratch_shapes=[slots] * 4 + [dma] * 5,
            compiler_params=params,
            name="line_scatter",
        )(part)
    product = (tokens.shape[1], grads.shape[1])
    params = pltpu.CompilerParams(
        collective_id=call_id, has_side_effects=True, vmem_limit_bytes=56 * 2**20
    )
    return pl.pallas_call(
        functools.partial(scatter_kernel, ctx_count),
        out_shape=[
            total,
            jax.ShapeDtypeStruct(small.shape, small.dtype),
            jax.ShapeDtypeStruct(product, part.dtype),
        ],
        in_specs=[VMEM] * 2 + [ANY] * 2,
        out_specs=[VMEM] * 2 + [ANY],
        scratch_shapes=[slots] * 4
        + [dma] * 5
        + [spread_dma] * 2
        + [pltpu.VMEM(product, part.dtype), pltpu.SemaphoreType.DMA((half,))]
        + [
            pltpu.VMEM(tokens.shape, tokens.dtype),
            pltpu.VMEM(grads.shape, grads.dtype),
            pltpu.SemaphoreType.DMA((2,)),
        ],
        compiler_params=params,
        name="line_scatter",
    )(part, small, tokens, grads)


def fsdp_place():
    here = lax.axis_index("fsdp")
    beside = here + 1 - 2 * (here % 2)
    return here, beside, (here + 2) % 4, (beside + 2) % 4


def greet_all(ctx_count):
    barrier = pltpu.get_barrier_semaphore()
    here = lax.axis_index("ctx")
    group = lax.axis_index("fsdp")
    for k in range(1, ctx_count):
        pl.semaphore_signal(
            barrier, inc=1, device_id={"ctx": (here + k) % ctx_count}, device_id_type=MESH
        )
    for k in range(1, 4):
        pl.semaphore_signal(barrier, inc=1, device_id={"fsdp": (group + k) % 4}, device_id_type=MESH)
    pl.semaphore_wait(barrier, ctx_count + 2)


def share_start(blocks, sems, own=None):
    send_sem, recv_sem = sems
    here, beside, across, corner = fsdp_place()
    source = blocks.at[here] if own is None else own
    for way, target in ((0, across), (1, beside)):
        remote(source, blocks.at[here], send_sem.at[way], recv_sem.at[here], fsdp=target).start()


def share_step(blocks, sems):
    send_sem, recv_sem = sems
    here, beside, across, corner = fsdp_place()
    copy = remote(
        blocks.at[across], blocks.at[across], send_sem.at[2], recv_sem.at[across], fsdp=beside
    )
    copy.wait_recv()
    copy.start()


def share_finish(blocks, sems):
    send_sem, recv_sem = sems
    here, beside, across, corner = fsdp_place()
    for way, block in ((0, beside), (1, corner)):
        copy = remote(
            blocks.at[block], blocks.at[block], send_sem.at[way], recv_sem.at[block], fsdp=beside
        )
        copy.wait_recv()
        copy.wait_send()
    remote(
        blocks.at[here], blocks.at[here], send_sem.at[2], recv_sem.at[here], fsdp=beside
    ).wait_send()


def spread(pieces, landing, sems, ctx_count):
    send_sem, recv_sem = sems
    here = lax.axis_index("ctx")

    def copy(k, peer, source):
        return remote(pieces(peer), landing(source), send_sem.at[k], recv_sem.at[k], ctx=peer)

    starts = [copy(k, (here + k) % ctx_count, here) for k in range(1, ctx_count)]
    waits = [
        copy(k, (here + k) % ctx_count, (here + ctx_count - k) % ctx_count)
        for k in range(1, ctx_count)
    ]
    return starts, waits


def greet_near(last, here, level, side):
    barrier = pltpu.get_barrier_semaphore()
    group = lax.axis_index("fsdp")
    for k in range(1, 4):
        pl.semaphore_signal(barrier, inc=1, device_id={"fsdp": (group + k) % 4}, device_id_type=MESH)
    greet_line(last, here, level, side, 3)


def gather_kernel(last, shared_count, *refs):
    total = 1 + shared_count
    owns, rows, keep_sem = refs[:total], refs[total : 2 * total], refs[2 * total]
    refs = refs[2 * total + 1 :]
    place = line_place()
    here, level, line, side = place
    sems = [(refs[2 * i], refs[2 * i + 1]) for i in range(total)]
    group = lax.axis_index("fsdp")
    if shared_count:
        greet_near(last, here, level, side)
    else:
        greet_line(last, here, level, side)
    line_start(rows[0], owns[0], sems[0], place, last)
    for i in range(1, total):
        share_start(rows[i], sems[i], owns[i])
    keeps = [
        pltpu.make_async_copy(
            owns[i], rows[i].at[group if i else here], keep_sem.at[i]
        )
        for i in range(total)
    ]
    for copy in keeps:
        copy.start()
    for step in range(1, last + 1):
        line_step(rows[0], sems[0], place, last, step)
    for i in range(1, total):
        share_step(rows[i], sems[i])
    line_finish(rows[0], sems[0], place, last)
    for i in range(1, total):
        share_finish(rows[i], sems[i])
    for copy in keeps:
        copy.wait()


def product_kernel(last, own, units, grads, rows, product, keep_sem, send_sem, recv_sem):
    place = line_place()
    here, level, line, side = place
    sems = (send_sem, recv_sem)
    greet_line(last, here, level, side)
    line_start(rows, own, sems, place, last)
    keep = pltpu.make_async_copy(own, rows.at[here], keep_sem.at[0])
    keep.start()
    turned = units[...].T
    piece = grads.shape[1] // (last + 1)
    for step in range(last + 1):
        columns = pl.ds(step * piece, piece)
        product[:, columns] = flat_dot(turned, grads[:, columns]).astype(product.dtype)
        if step < last:
            line_step(rows, sems, place, last, step + 1)
    line_finish(rows, sems, place, last)
    keep.wait()


def product_gather(ctx_count, call_id, own, units, grads):
    dma = pltpu.SemaphoreType.DMA
    return pl.pallas_call(
        functools.partial(product_kernel, ctx_count // 2 - 1),
        out_shape=[
            jax.ShapeDtypeStruct((ctx_count,) + own.shape, own.dtype),
            jax.ShapeDtypeStruct((units.shape[1], grads.shape[1]), own.dtype),
        ],
        in_specs=[VMEM] * 3,
        out_specs=[ANY, VMEM],
        scratch_shapes=[dma((1,)), dma((ctx_count, 3)), dma((ctx_count,))],
        compiler_params=pltpu.CompilerParams(
            collective_id=call_id, has_side_effects=True, vmem_limit_bytes=32 * 2**20
        ),
        name="product_gather",
    )(own, units, grads)


def line_gather(ctx_count, call_id, own, *shared):
    count = len(shared)
    dma = pltpu.SemaphoreType.DMA
    return pl.pallas_call(
        functools.partial(gather_kernel, ctx_count // 2 - 1, count),
        out_shape=[jax.ShapeDtypeStruct((ctx_count,) + own.shape, own.dtype)]
        + [jax.ShapeDtypeStruct((4,) + a.shape, a.dtype) for a in shared],
        in_specs=[VMEM] * (1 + count),
        out_specs=[ANY] * (1 + count),
        scratch_shapes=[dma((1 + count,)), dma((ctx_count, 3)), dma((ctx_count,))]
        + [dma((3,)), dma((4,))] * count,
        compiler_params=pltpu.CompilerParams(collective_id=call_id, has_side_effects=True),
        name="line_gather",
    )(own, *shared)


def opening_kernel(
    ctx_count,
    own,
    qkv_own,
    out_own,
    small_own,
    number_own,
    rows,
    qkv,
    out_pair,
    small,
    numbers,
    keep_sem,
    pair_send,
    pair_recv,
    row_send,
    row_recv,
    share_send,
    share_recv,
    *sems,
):
    last = ctx_count // 2 - 1
    place = line_place()
    here, level, line, side = place
    group, beside, across, corner = fsdp_place()
    sems = [(sems[2 * i], sems[2 * i + 1]) for i in range(5)]
    qkv_spread, small_spread, number_spread, out_share, small_share = sems
    row_sems = (row_send, row_recv)
    greet_all(ctx_count)
    qkv_start, qkv_wait = spread(
        lambda peer: qkv_own.at[peer], lambda source: qkv.at[group, source], qkv_spread, ctx_count
    )
    small_start, small_wait = spread(
        lambda peer: small_own, lambda source: small.at[group, source], small_spread, ctx_count
    )
    number_start, number_wait = spread(
        lambda peer: number_own, lambda source: numbers.at[source], number_spread, ctx_count
    )

    def piece_copy(way, owner, k, target, first=False):
        source = (here + ctx_count - k) % ctx_count
        return remote(
            qkv_own.at[here] if first else qkv.at[owner, source],
            qkv.at[owner, source],
            share_send.at[way, k],
            share_recv.at[owner, k],
            fsdp=target,
        )

    def piece_on(k):
        piece_copy(0, group, k, across, k == 0).start()
        piece_copy(1, group, k, beside, k == 0).start()

    for copy in small_start + number_start + qkv_start:
        copy.start()
    line_start(rows, own, row_sems, place, last)
    piece_on(0)
    pair = remote(
        out_own, out_pair.at[group, line], pair_send.at[0], pair_recv.at[0], ctx=side
    )
    pair.start()
    keeps = [
        pltpu.make_async_copy(source, target, keep_sem.at[i])
        for i, (source, target) in enumerate(
            (
                (qkv_own.at[here], qkv.at[group, here]),
                (out_own, out_pair.at[group, line]),
                (small_own, small.at[group, here]),
                (number_own, numbers.at[here]),
                (own, rows.at[here]),
            )
        )
    ]
    for copy in keeps:
        copy.start()
    for copy in small_wait:
        copy.wait_recv()
    keeps[2].wait()
    share_start(small, small_share)
    line_step(rows, row_sems, place, last, 1)
    for k in range(1, ctx_count):
        qkv_wait[k - 1].wait_recv()
        piece_on(k)
    remote(
        out_own, out_pair.at[group, 1 - line], pair_send.at[0], pair_recv.at[0], ctx=side
    ).wait_recv()
    keeps[1].wait()
    share_start(out_pair, out_share)
    line_step(rows, row_sems, place, last, 2)
    for k in range(ctx_count):
        piece_copy(0, across, k, across).wait_recv()
        piece_copy(2, across, k, beside).start()
    share_step(small, small_share)
    for step in range(3, last + 1):
        line_step(rows, row_sems, place, last, step)
    share_step(out_pair, out_share)
    line_finish(rows, row_sems, place, last)
    for copy in number_wait:
        copy.wait_recv()
    for copy in qkv_start + small_start + number_start:
        copy.wait_send()
    pair.wait_send()
    for k in range(ctx_count):
        piece_copy(1, beside, k, beside).wait_recv()
        piece_copy(2, corner, k, beside).wait_recv()
        for way in range(3):
            piece_copy(way, group, k, beside).wait_send()
    share_finish(small, small_share)
    share_finish(out_pair, out_share)
    for i in (0, 3, 4):
        keeps[i].wait()


def opening(ctx_count, call_id, own, qkv_own, out_own, small_own, number_own):
    def out(lead, array):
        return jax.ShapeDtypeStruct(lead + array.shape, array.dtype)

    dma = pltpu.SemaphoreType.DMA
    return pl.pallas_call(
        functools.partial(opening_kernel, ctx_count),
        out_shape=[
            out((ctx_count,), own),
            out((4,), qkv_own),
            out((4, 2), out_own),
            out((4, ctx_count), small_own),
            out((ctx_count,), number_own),
        ],
        in_specs=[VMEM] * 5,
        out_specs=[ANY] * 5,
        scratch_shapes=[
            dma((5,)),
            dma((1,)),
            dma((1,)),
            dma((ctx_count, 3)),
            dma((ctx_count,)),
            dma((3, ctx_count)),
            dma((4, ctx_count)),
        ]
        + [dma((ctx_count,))] * 6
        + [dma((3,)), dma((4,))] * 2,
        compiler_params=pltpu.CompilerParams(collective_id=call_id, has_side_effects=True),
        name="opening",
    )(own, qkv_own, out_own, small_own, number_own)


def group_reduce(blocks, beside_in, pair_sums, across_in, settled, sems):
    core_send, core_recv, far_send, far_recv = sems
    group, beside, across, corner = fsdp_place()
    rows = settled.shape[0]

    def core_copy(slot, block):
        return remote(
            blocks.at[block],
            beside_in.at[slot],
            core_send.at[slot],
            core_recv.at[slot],
            fsdp=beside,
        )

    far = remote(pair_sums.at[1], across_in, far_send.at[0], far_recv.at[0], fsdp=across)
    core_copy(1, corner).start()
    core_copy(0, beside).start()
    yield
    core_copy(1, corner).wait_recv()
    add_rows(pair_sums.at[1], (blocks.at[across], beside_in.at[1]), rows)
    far.start()
    core_copy(0, beside).wait_recv()
    add_rows(pair_sums.at[0], (blocks.at[group], beside_in.at[0]), rows)
    yield
    far.wait_recv()
    add_rows(settled, (pair_sums.at[0], across_in), rows)
    yield
    core_copy(1, corner).wait_send()
    core_copy(0, beside).wait_send()
    far.wait_send()
    yield


def closing_kernel(ctx_count, part, weight, pair, plain, small, *refs):
    total, landed, pair_total, plain_total, small_total = refs[:5]
    line_slots, weight_slots, pair_slots, plain_slots = (
        refs[5:9],
        refs[9:13],
        refs[13:17],
        refs[17:20],
    )
    pair_in, small_in, small_sums, small_across = refs[20:24]
    sems = refs[24:]
    line_sems, weight_sems, pair_sems, plain_sems = sems[:5], sems[5:9], sems[9:13], sems[13:17]
    keep_sem, half_send, half_recv = sems[17:20]
    weight_spread, small_spread, (group_send, group_recv) = sems[20:22], sems[22:24], sems[24:26]
    here, level, line, side = line_place()
    group = lax.axis_index("fsdp")
    greet_all(ctx_count)
    turns = scatter_turns(ctx_count // 2 - 1, part, total, *line_slots, *line_sems)
    settled, pair_settled = weight_slots[3], pair_slots[3]
    weight_steps = group_reduce(weight, *weight_slots, weight_sems)
    pair_steps = group_reduce(pair, *pair_slots, pair_sems)
    plain_steps = group_reduce(plain, *plain_slots, plain_total, plain_sems)
    small_start, small_wait = spread(
        lambda peer: small.at[:, peer], lambda source: small_in.at[source], small_spread, ctx_count
    )
    for copy in small_start:
        copy.start()
    next(weight_steps)
    next(turns)
    next(weight_steps)
    next(pair_steps)
    next(turns)
    next(pair_steps)
    next(plain_steps)
    for copy in small_wait:
        copy.wait_recv()
    small_sum = small[:, here]
    for k in range(1, ctx_count):
        small_sum = small_sum + small_in[(here + k) % ctx_count]
    small_sums[...] = small_sum
    group_copies = [
        remote(
            small_sums.at[(group + k) % 4],
            small_across.at[k],
            group_send.at[k],
            group_recv.at[k],
            fsdp=(group + k) % 4,
        )
        for k in range(1, 4)
    ]
    for copy in group_copies:
        copy.start()
    next(weight_steps)
    piece = settled.shape[0] // ctx_count
    weight_start, weight_wait = spread(
        lambda peer: settled.at[pl.ds(pl.multiple_of(peer * piece, piece), piece)],
        lambda source: landed.at[source],
        weight_spread,
        ctx_count,
    )
    for copy in weight_start:
        copy.start()
    keep = pltpu.make_async_copy(
        settled.at[pl.ds(pl.multiple_of(here * piece, piece), piece)],
        landed.at[here],
        keep_sem.at[0],
    )
    keep.start()
    next(plain_steps)
    next(turns)
    next(pair_steps)
    half = pair_total.shape[0]
    half_copy = remote(
        pair_settled.at[pl.ds(pl.multiple_of((1 - line) * half, half), half)],
        pair_in,
        half_send.at[0],
        half_recv.at[0],
        ctx=side,
    )
    half_copy.start()
    for copy in group_copies:
        copy.wait_recv()
    small_total[...] = small_sums[group] + small_across[1] + small_across[2] + small_across[3]
    for step in turns:
        pass
    next(plain_steps)
    half_copy.wait_recv()
    kept = pair_settled.at[pl.ds(pl.multiple_of(line * half, half), half)]
    add_rows(pair_total, (kept, pair_in), half)
    for copy in weight_wait:
        copy.wait_recv()
    for copy in weight_start + small_start + group_copies:
        copy.wait_send()
    half_copy.wait_send()
    next(weight_steps)
    next(pair_steps)
    next(plain_steps)
    keep.wait()


def closing(ctx_count, call_id, part, weight, pair, plain, small):
    rows, width = part.shape[1:]
    half = ctx_count // 2
    dma = pltpu.SemaphoreType.DMA
    slots = pltpu.VMEM((half, rows, width), part.dtype)

    def group_slots(array):
        one = pltpu.VMEM(array.shape[1:], array.dtype)
        two = pltpu.VMEM((2,) + array.shape[1:], array.dtype)
        return [two, two, one, one]

    block, columns = weight.shape[1:]
    pair_half = (pair.shape[1] // 2, pair.shape[2])
    return pl.pallas_call(
        functools.partial(closing_kernel, ctx_count),
        out_shape=[
            jax.ShapeDtypeStruct((rows, width), jnp.float32),
            jax.ShapeDtypeStruct((ctx_count, block // ctx_count, columns), weight.dtype),
            jax.ShapeDtypeStruct(pair_half, jnp.float32),
            jax.ShapeDtypeStruct(plain.shape[1:], jnp.float32),
            jax.ShapeDtypeStruct(small.shape[2:], small.dtype),
        ],
        in_specs=[VMEM] * 5,
        out_specs=[VMEM] * 5,
        scratch_shapes=[slots] * 4
        + group_slots(weight)
        + group_slots(pair)
        + group_slots(plain)[:3]
        + [
            pltpu.VMEM(pair_half, pair.dtype),
            pltpu.VMEM((ctx_count, 4) + small.shape[2:], small.dtype),
            pltpu.VMEM((4,) + small.shape[2:], small.dtype),
            pltpu.VMEM((4,) + small.shape[2:], small.dtype),
        ]
        + [dma((half,))] * 5
        + [dma((2,)), dma((2,)), dma((1,)), dma((1,))] * 3
        + [dma((1,))] * 3
        + [dma((ctx_count,))] * 4
        + [dma((4,))] * 2,
        compiler_params=pltpu.CompilerParams(
            collective_id=call_id, has_side_effects=True, vmem_limit_bytes=56 * 2**20
        ),
        name="closing",
    )(part, weight, pair, plain, small)


def scaled_rows(values):
    return values * lax.rsqrt(jnp.mean(values * values, axis=-1, keepdims=True) + EPSILON)


def attend_kernel(
    inputs,
    gain,
    weight,
    bias,
    cosine,
    sine,
    columns,
    lines,
    out_weight,
    normed,
    queries,
    keys,
    values,
    attended,
    log_totals,
    part,
):
    rows = inputs.shape[0]
    low = jnp.bfloat16
    heads = queries.shape[1] // HD

    @pl.loop(0, rows // SPAN)
    def project(index):
        here = span_of(index)
        unit = scaled_rows(inputs[here, :].astype(jnp.float32)) * gain[...]
        normed[here, :] = unit.astype(low)
        projected = flat_dot(normed[here, :], weight[...]) + bias[...]
        turn, tilt = cosine[here, :], sine[here, :]
        for head in range(heads):
            own = slice(head * HD, (head + 1) * HD)
            query = projected[:, own]
            query = query * turn + pltpu.roll(query, HD // 2, 1) * tilt
            queries[here, own] = (query * HD ** (-0.5)).astype(low)
            key = projected[:, (heads + head) * HD : (heads + head + 1) * HD]
            keys[here, own] = (key * turn + pltpu.roll(key, HD // 2, 1) * tilt).astype(low)
            values[here, own] = projected[
                :, (2 * heads + head) * HD : (2 * heads + head + 1) * HD
            ].astype(low)

    @pl.loop(0, rows // SPAN)
    def attend(index):
        here = span_of(index)
        position, segment = columns[here, 0:1], columns[here, 1:2]
        allowed = (lines[1:2, :] == segment) & (lines[0:1, :] <= position)
        allowed = allowed | (lines[0:1, :] == position)
        for head in range(heads):
            own = slice(head * HD, (head + 1) * HD)
            scores = turned_dot(queries[here, own], keys[:, own])
            scores = jnp.where(allowed, scores, -1e30)
            highest = jnp.max(scores, axis=1, keepdims=True)
            weights = jnp.exp(scores - highest)
            sums = jnp.sum(weights, axis=1, keepdims=True)
            log_totals[here, head : head + 1] = highest + jnp.log(sums)
            probs = (weights * (1.0 / sums)).astype(low)
            attended[here, own] = flat_dot(probs, values[:, own]).astype(low)
        part[here, :] = flat_dot(attended[here, :], out_weight[...]).astype(low)


def attend(inputs, gain, weight, bias, cosine, sine, columns, lines, out_weight):
    rows, width = inputs.shape
    wide = out_weight.shape[0]
    low = jnp.bfloat16
    shape = jax.ShapeDtypeStruct
    return pl.pallas_call(
        attend_kernel,
        out_shape=[shape((rows, width), low)]
        + [shape((rows, wide), low)] * 4
        + [shape((rows, wide // HD), jnp.float32), shape((rows, width), low)],
        in_specs=[VMEM] * 9,
        out_specs=[VMEM] * 7,
        compiler_params=pltpu.CompilerParams(vmem_limit_bytes=40 * 2**20),
        cost_estimate=pl.CostEstimate(
            flops=2 * rows * width * 4 * wide + 4 * rows * rows * wide,
            bytes_accessed=20 * 2**20,
            transcendentals=rows * rows * wide // HD,
        ),
        name="attend",
    )(inputs, gain, weight, bias, cosine, sine, columns, lines, out_weight)


def attend_back_kernel(
    branch,
    out_weight,
    queries,
    keys,
    values,
    attended,
    totals,
    cosine,
    sine,
    columns,
    lines,
    far_inputs,
    far_normed,
    far_weight,
    part,
    grad_weight,
    grad_out,
    grad_bias,
    grad_gain,
    grads,
    grad_attended,
    grad_keys,
    grad_values,
    gain_sum,
    inputs,
    normed,
    weight,
    load_sem,
):
    rows, width = branch.shape
    low = jnp.bfloat16
    full = jnp.float32
    wide = queries.shape[1]
    heads = wide // HD
    loads = [
        pltpu.make_async_copy(source, target, load_sem.at[i])
        for i, (source, target) in enumerate(
            ((far_weight, weight), (far_inputs, inputs), (far_normed, normed))
        )
    ]
    for copy in loads:
        copy.start()

    @pl.loop(0, rows // SPAN)
    def into_heads(index):
        here = span_of(index)
        grad_attended[here, :] = turned_dot(branch[here, :], out_weight[...]).astype(low)

    for head in range(heads):
        own = slice(head * HD, (head + 1) * HD)
        grad_keys[...] = jnp.zeros_like(grad_keys)
        grad_values[...] = jnp.zeros_like(grad_values)

        @pl.loop(0, rows // SPAN)
        def scores_back(index):
            here = span_of(index)
            position, segment = lines[0:1, here], lines[1:2, here]
            allowed = (columns[:, 1:2] == segment) & (columns[:, 0:1] <= position)
            allowed = allowed | (columns[:, 0:1] == position)
            query, grad = queries[here, own], grad_attended[here, own]
            scores = jnp.where(allowed, turned_dot(keys[:, own], query), -1e30)
            probs = jnp.exp(scores - totals[head : head + 1, here])
            grad_probs = turned_dot(values[:, own], grad)
            delta = jnp.sum(probs * grad_probs, axis=0, keepdims=True)
            grad_scores = (probs * (grad_probs - delta)).astype(low)
            grad_keys[...] += flat_dot(grad_scores, query)
            grad_values[...] += flat_dot(probs.astype(low), grad)
            grad_query = flat_dot(grad_scores.T, keys[:, own]) * HD ** (-0.5)
            grads[here, own] = (
                grad_query * cosine[here, :] + pltpu.roll(grad_query * sine[here, :], HD // 2, 1)
            ).astype(low)

        @pl.loop(0, rows // SPAN)
        def keys_back(index):
            here = span_of(index)
            grad_key = grad_keys[here, :]
            grads[here, (heads + head) * HD : (heads + head + 1) * HD] = (
                grad_key * cosine[here, :] + pltpu.roll(grad_key * sine[here, :], HD // 2, 1)
            ).astype(low)
            grads[here, (2 * heads + head) * HD : (2 * heads + head + 1) * HD] = grad_values[
                here, :
            ].astype(low)

    gain_sum[...] = jnp.zeros_like(gain_sum)
    grad_bias[...] = jnp.zeros_like(grad_bias)
    for copy in loads:
        copy.wait()

    @pl.loop(0, rows // SPAN)
    def project_back(index):
        here = span_of(index)
        grad_rows = turned_dot(grads[here, :], weight[...])
        part[here, :] = grad_rows.astype(low)
        unit = scaled_rows(inputs[here, :].astype(full))
        gain_sum[...] += jnp.sum(grad_rows * unit, axis=0, keepdims=True)
        grad_bias[...] += jnp.sum(grads[here, :].astype(full), axis=0, keepdims=True)

    grad_gain[...] = gain_sum[...]

    @pl.loop(0, width // SPAN)
    def weight_back(index):
        here = span_of(index)
        grad_weight[here, :] = flat_dot(normed[:, here].T, grads[...]).astype(low)

    attended_turned = attended[...].T

    @pl.loop(0, width // (2 * SPAN))
    def out_back(index):
        here = span_of(index, 2 * SPAN)
        grad_out[:, here] = flat_dot(attended_turned, branch[:, here]).astype(low)


def attend_back(
    branch,
    out_weight,
    queries,
    keys,
    values,
    attended,
    totals,
    cosine,
    sine,
    columns,
    lines,
    inputs,
    normed,
    weight,
):
    rows, width = branch.shape
    wide = out_weight.shape[0]
    low = jnp.bfloat16
    full = jnp.float32
    shape = jax.ShapeDtypeStruct
    return pl.pallas_call(
        attend_back_kernel,
        out_shape=[
            shape((rows, width), low),
            shape(weight.shape, low),
            shape((wide, width), low),
            shape((1, 3 * wide), full),
            shape((1, width), full),
        ],
        in_specs=[VMEM] * 11 + [ANY] * 3,
        out_specs=[VMEM] * 5,
        scratch_shapes=[
            pltpu.VMEM((rows, 3 * wide), low),
            pltpu.VMEM((rows, wide), low),
            pltpu.VMEM((rows, HD), full),
            pltpu.VMEM((rows, HD), full),
            pltpu.VMEM((1, width), full),
            pltpu.VMEM(inputs.shape, low),
            pltpu.VMEM(normed.shape, low),
            pltpu.VMEM(weight.shape, low),
            pltpu.SemaphoreType.DMA((3,)),
        ],
        compiler_params=pltpu.CompilerParams(vmem_limit_bytes=56 * 2**20),
        cost_estimate=pl.CostEstimate(
            flops=2 * rows * width * 8 * wide + 10 * rows * rows * wide,
            bytes_accessed=35 * 2**20,
            transcendentals=rows * rows * wide // HD,
        ),
        name="attend_back",
    )(
        branch,
        out_weight,
        queries,
        keys,
        values,
        attended,
        totals,
        cosine,
        sine,
        columns,
        lines,
        inputs,
        normed,
        weight,
    )


def gate_back_kernel(upstream, scale, gate_up, weight_out, grads, scaled):
    low = jnp.bfloat16
    half = gate_up.shape[1] // 2
    scaled[...] = (scale[...] * upstream[...].astype(jnp.float32)).astype(low)
    grad_unit = turned_dot(scaled[...], weight_out[...])
    gate, up = gate_up[:, :half], gate_up[:, half:]
    sigmoid = 1.0 / (1.0 + jnp.exp(-gate))
    grad_gate = grad_unit * up * (sigmoid * (1.0 + gate * (1.0 - sigmoid)))
    grad_up = grad_unit * (gate * sigmoid)
    grads[...] = jnp.concatenate([grad_gate.astype(low), grad_up.astype(low)], axis=1)


def gate_back(upstream, scale, gate_up, weight_out):
    rows, width = upstream.shape
    hidden = weight_out.shape[0]
    low = jnp.bfloat16

    def block(columns):
        return pl.BlockSpec((SPAN, columns), lambda i: (i, 0))

    return pl.pallas_call(
        gate_back_kernel,
        grid=(rows // SPAN,),
        out_shape=[
            jax.ShapeDtypeStruct((rows, 2 * hidden), low),
            jax.ShapeDtypeStruct((rows, width), low),
        ],
        in_specs=[
            block(width),
            block(1),
            block(2 * hidden),
            pl.BlockSpec((hidden, width), lambda i: (0, 0)),
        ],
        out_specs=[block(2 * hidden), block(width)],
        compiler_params=pltpu.CompilerParams(vmem_limit_bytes=48 * 2**20),
        cost_estimate=pl.CostEstimate(
            flops=2 * rows * width * hidden,
            bytes_accessed=rows * (12 * hidden + 4 * width) + 2 * hidden * width,
            transcendentals=rows * hidden,
        ),
        name="gate_back",
    )(upstream, scale, gate_up, weight_out)


def deal_kernel(pieces, weight, dealt):
    ctx_count = dealt.shape[0]
    width = dealt.shape[2] // pieces
    for c in range(ctx_count):
        dealt[c] = jnp.concatenate(
            [
                weight[:, (q * ctx_count + c) * width : (q * ctx_count + c + 1) * width]
                for q in range(pieces)
            ],
            axis=1,
        )


def deal_columns(weight, ctx_count, pieces):
    rows, columns = weight.shape
    return pl.pallas_call(
        functools.partial(deal_kernel, pieces),
        out_shape=jax.ShapeDtypeStruct((ctx_count, rows, columns // ctx_count), weight.dtype),
        name="deal_columns",
    )(weight)


def collect_kernel(pieces, dealt, whole):
    ctx_count = dealt.shape[0]
    width = dealt.shape[2] // pieces
    whole[...] = jnp.concatenate(
        [
            dealt[c, :, q * width : (q + 1) * width]
            for q in range(pieces)
            for c in range(ctx_count)
        ],
        axis=1,
    ).astype(whole.dtype)


def collect_columns(dealt, pieces):
    ctx_count, rows, columns = dealt.shape
    return pl.pallas_call(
        functools.partial(collect_kernel, pieces),
        out_shape=jax.ShapeDtypeStruct((rows, columns * ctx_count), jnp.float32),
        name="collect_columns",
    )(dealt)


def heads_kernel(order, dealt, whole):
    pairs = dealt.shape[0] * 2
    for place, head in enumerate(order):
        for which in range(3):
            column = (which * 2 + place % 2) * HD
            target = (which * pairs + head) * HD
            whole[:, target : target + HD] = dealt[
                place // 2, :, column : column + HD
            ].astype(whole.dtype)


def collect_heads(dealt, order):
    ctx_count, rows, columns = dealt.shape
    return pl.pallas_call(
        functools.partial(heads_kernel, order),
        out_shape=jax.ShapeDtypeStruct((rows, columns * ctx_count), jnp.float32),
        name="collect_heads",
    )(dealt)


def over(axis, array, dim=0):
    return lax.all_gather(array, axis, axis=dim, tiled=True)


def reduce_over(axis, array, dim=0):
    return lax.psum_scatter(array, axis, scatter_dimension=dim, tiled=True)


def exchange(array):
    return lax.all_to_all(array, "ctx", split_axis=0, concat_axis=0, tiled=True)


def transposed_dot(left, right):
    return lax.dot_general(
        left, right, (((0,), (0,)), ((), ())), preferred_element_type=jnp.float32
    )


def dot_transposed(left, right):
    return lax.dot_general(
        left, right, (((1,), (1,)), ((), ())), preferred_element_type=jnp.float32
    )


def split_plan(
    hidden_in,
    segments,
    block_pairs,
    routes,
    out_grad,
    norm_gain_attn,
    qkv_weight,
    qkv_bias,
    out_weight,
    norm_gain_ffn,
    router_weight,
    shared_gate_weight,
    shared_in_weight,
    shared_out_weight,
    expert_in_weight,
    expert_out_weight,
):
    low = jnp.bfloat16
    full = jnp.float32
    tokens_dev, width = hidden_in.shape[1:]
    block_len = tokens_dev // 2
    ctx_count = lax.axis_size("ctx")
    fsdp_count = lax.axis_size("fsdp")
    ctx_rank = lax.axis_index("ctx")
    dev_count = ctx_count * fsdp_count
    row_len = ctx_count * tokens_dev
    early = width * 3 // 8
    head_count = width // HD
    shard = qkv_weight.shape[0]
    expert_count = router_weight.shape[1]
    shared_shard = shared_out_weight.shape[0]
    shared_width = fsdp_count * shared_shard
    expert_width = expert_out_weight.shape[1] * fsdp_count
    pair_rank = ctx_rank // 2
    side = ctx_rank % 2
    pairs = ctx_count // 2
    head_order = [j + (p * 2 + t) * pairs for j in range(pairs) for p in range(2) for t in range(2)]

    small = jnp.concatenate(
        [
            norm_gain_attn,
            norm_gain_ffn,
            shared_gate_weight,
            router_weight.T.reshape(-1),
            qkv_bias,
        ]
    )
    small_count = small.shape[0]
    small = jnp.pad(small, (0, 16 * HD - small_count)).reshape(16, HD)
    own_numbers = jnp.concatenate(
        [routes.reshape(tokens_dev, -1).T, segments.reshape(1, tokens_dev)], axis=0
    )
    number_count = own_numbers.shape[0]
    own_numbers = jnp.pad(own_numbers, ((0, 8 - number_count), (0, 0)))
    qkv_parts = (
        qkv_weight.reshape(shard, 3, head_count, HD)[:, :, jnp.array(head_order)]
        .reshape(shard, 3, ctx_count, 2 * HD)
        .transpose(2, 0, 1, 3)
        .reshape(ctx_count, shard, 6 * HD)
    )
    own_inputs = hidden_in.reshape(tokens_dev, width)
    row_inputs, qkv_c, out_pair, small_all, numbers = opening(
        ctx_count, 1, own_inputs, qkv_parts, out_weight, small, own_numbers
    )
    qkv_c = qkv_c.reshape(width, 6 * HD)
    out_c = lax.dynamic_index_in_dim(
        out_pair.reshape(2, 2 * HD, width), side, 0, keepdims=False
    )
    small_all = small_all.reshape(dev_count, 16 * HD)
    gain_attn = small_all[:, :shard].reshape(width).astype(full)
    gain_ffn = small_all[:, shard : 2 * shard].reshape(width).astype(full)
    gate_full = small_all[:, 2 * shard : 3 * shard].reshape(width)
    router_t = (
        small_all[:, 3 * shard : (3 + expert_count) * shard]
        .reshape(dev_count, expert_count, shard)
        .transpose(1, 0, 2)
        .reshape(expert_count, width)
    )
    bias_full = small_all[:, (3 + expert_count) * shard : small_count].reshape(3, head_count, HD)
    router_gate = jnp.concatenate([router_t, gate_full[None, :]], axis=0)
    row_seg = numbers[:, number_count - 1].reshape(row_len)
    routed_here = jnp.any(numbers[:, : number_count - 1] == ctx_rank, axis=1).reshape(row_len)

    expert_outer = over("fsdp", expert_out_weight[0])
    shared_in_weight, numbers, expert_outer = lax.optimization_barrier(
        (shared_in_weight, numbers, expert_outer)
    )
    inner_parts = deal_columns(shared_in_weight, ctx_count, 2 * fsdp_count)
    expert_inner = over("fsdp", expert_in_weight[0])
    inner_parts = exchange(inner_parts)
    my_heads = [pair_rank + (side * 2 + t) * pairs for t in range(2)]
    bias_c = jnp.concatenate(
        [lax.dynamic_index_in_dim(bias_full, h, 1, keepdims=False) for h in my_heads], axis=1
    ).reshape(6 * HD)

    offsets = jnp.arange(block_len, dtype=jnp.int32)
    positions = (block_pairs[:, None] * block_len + offsets[None, :]).reshape(row_len)
    inputs = own_inputs.astype(full)
    row_inputs = row_inputs.reshape(row_len, width)
    half_len = HD // 2
    frequency = THETA ** (-jnp.arange(half_len, dtype=full) / half_len)
    places = positions.astype(full)
    angles = places[:, None] * frequency[None, :]
    cosine, sine = jnp.cos(angles), jnp.sin(angles)
    cosine = jnp.concatenate([cosine, cosine], axis=1)
    sine = jnp.concatenate([-sine, sine], axis=1)
    key_seg = row_seg.astype(full)
    query_seg = jnp.where(row_seg >= 0, key_seg, -2.0)
    query_marks = jnp.stack([places, query_seg])
    key_marks = jnp.stack([places, key_seg])
    row_normed, queries, keys, values, attended_row, log_totals, branch_part = attend(
        row_inputs,
        gain_attn[None, :],
        qkv_c,
        bias_c.astype(full)[None, :],
        cosine,
        sine,
        query_marks.T,
        key_marks,
        out_c,
    )
    branch_part, inner_parts = lax.optimization_barrier((branch_part, inner_parts))
    branch = line_scatter(ctx_count, 2, branch_part.reshape(ctx_count, tokens_dev, width))
    middle = inputs + branch
    normed_ffn = rms_scale(middle, gain_ffn).astype(low)
    normed_ffn, early_grad, expert_inner = lax.optimization_barrier(
        (normed_ffn, out_grad, expert_inner)
    )
    early_upstream = over("ctx", early_grad.reshape(tokens_dev, width)[:, :early])

    row_ffn, inner_c, outer_c = line_gather(
        ctx_count,
        4,
        normed_ffn,
        inner_parts.reshape(ctx_count * shard, 2 * shared_width),
        shared_out_weight,
    )
    row_ffn = row_ffn.reshape(row_len, width)
    row_ffn, late_grad, early_upstream = lax.optimization_barrier(
        (row_ffn, out_grad, early_upstream)
    )
    late_upstream = over("ctx", late_grad.reshape(tokens_dev, width)[:, early:])
    inner_c = inner_c.reshape(width, 2 * shared_width)
    outer_c = outer_c.reshape(shared_width, width)
    row_logits = dot_transposed(row_ffn, router_gate)
    row_probs = jax.nn.softmax(row_logits[:, :expert_count], axis=-1)
    expert_ids = jnp.arange(expert_count, dtype=jnp.int32)
    here = jnp.where(
        routed_here, jnp.sum(jnp.where(expert_ids[None, :] == ctx_rank, row_probs, 0.0), axis=1), 0.0
    )
    row_gate = jax.nn.sigmoid(row_logits[:, expert_count])
    expert_gu = matmul_low(row_ffn, expert_inner)
    expert_hidden = swiglu_mix(expert_gu, expert_width).astype(low)
    expert_result = matmul_low(expert_hidden, expert_outer).astype(low).astype(full)
    row_shared, expert_result = lax.optimization_barrier((row_ffn, expert_result))
    shared_gu = matmul_low(row_shared, inner_c)
    shared_hidden = swiglu_mix(shared_gu, shared_width).astype(low)
    shared_out = matmul_low(shared_hidden, outer_c)
    shared_out, late_upstream = lax.optimization_barrier((shared_out, late_upstream))
    row_upstream = lax.optimization_barrier(
        jnp.concatenate([early_upstream, late_upstream], axis=1)
    )
    upstream_row = row_upstream.astype(full)
    out_part = (row_gate[:, None] * shared_out + here[:, None] * expert_result).astype(low)
    gate_dot = jnp.sum(upstream_row * shared_out, axis=1)
    expert_dot = jnp.where(routed_here, jnp.sum(upstream_row * expert_result, axis=1), 0.0)
    out_landed = reduce_over("ctx", out_part)

    row_upstream, out_part = lax.optimization_barrier((row_upstream, out_part))
    grad_expert_gu, grad_buffers = gate_back(row_upstream, here[:, None], expert_gu, expert_outer)
    sum_expert_outer = reduce_over("fsdp", transposed_dot(expert_hidden, grad_buffers).astype(low))
    grad_rows = dot_transposed(grad_expert_gu, expert_inner).astype(low)
    row_upstream, grad_rows = lax.optimization_barrier((row_upstream, grad_rows))
    grad_shared_gu, grad_shared_out = gate_back(
        row_upstream, row_gate[:, None], shared_gu, outer_c
    )
    grad_inner = transposed_dot(row_ffn, grad_shared_gu).astype(low)
    sum_inner_c = reduce_over("fsdp", grad_inner)
    grad_ffn_part = (
        dot_transposed(grad_shared_gu, inner_c) + grad_rows.astype(full)
    ).astype(low)
    dots = jnp.stack([gate_dot, expert_dot]).reshape(2, ctx_count, tokens_dev).transpose(1, 0, 2)
    grad_ffn_part, grad_inner = lax.optimization_barrier((grad_ffn_part, grad_inner))
    grad_normed, own_dots, grad_expert_inner = line_scatter(
        ctx_count,
        6,
        grad_ffn_part.reshape(ctx_count, tokens_dev, width),
        jnp.pad(dots, ((0, 0), (0, 6), (0, 0))),
        row_ffn,
        grad_expert_gu,
    )
    sum_expert_inner = reduce_over("fsdp", grad_expert_inner)
    hidden_out = (middle + out_landed.astype(full)).astype(low).reshape(1, tokens_dev, width)

    own_logits = dot_transposed(normed_ffn, router_gate)
    router_probs = jax.nn.softmax(own_logits[:, :expert_count], axis=-1)
    gate_value = jax.nn.sigmoid(own_logits[:, expert_count])
    grad_gate_logit = gate_value * (1.0 - gate_value) * jnp.sum(own_dots[:, 0], axis=0)
    grad_choice = own_dots[:, 1].T
    grad_logits = router_probs * (
        grad_choice - jnp.sum(router_probs * grad_choice, axis=1, keepdims=True)
    )
    grad_small = jnp.concatenate([grad_logits, grad_gate_logit[:, None]], axis=1).astype(low)
    grad_router_gate = transposed_dot(grad_small, normed_ffn)
    grad_normed = grad_normed + matmul_low(grad_small, router_gate)
    unused_norm, norm_pull = jax.vjp(rms_scale, middle, gain_ffn)
    grad_middle_norm, grad_gain_ffn = norm_pull(grad_normed)
    grad_middle = out_grad.reshape(tokens_dev, width).astype(full) + grad_middle_norm

    grad_branch, hidden_out = lax.optimization_barrier((grad_middle.astype(low), hidden_out))
    row_branch, grad_outer = product_gather(
        ctx_count, 3, grad_branch, shared_hidden, grad_shared_out
    )
    row_branch, sum_inner_c = lax.optimization_barrier(
        (row_branch.reshape(row_len, width), sum_inner_c)
    )
    sum_inner = collect_columns(
        exchange(sum_inner_c.reshape(ctx_count, shard, 2 * shared_width)), 2 * fsdp_count
    )
    grad_attn_part, grad_qkv_c, grad_out_c, grad_bias_c, grad_gain_attn = attend_back(
        row_branch,
        out_c,
        queries,
        keys,
        values,
        attended_row,
        log_totals.T,
        cosine,
        sine,
        key_marks.T,
        query_marks,
        row_inputs,
        row_normed,
        qkv_c,
    )
    grad_out_c = grad_out_c.reshape(2, HD, width)
    padded_out = jnp.concatenate(
        [jnp.where(side == p, grad_out_c, jnp.zeros_like(grad_out_c)) for p in range(2)], axis=0
    )
    grad_attn_part, sum_inner, sum_expert_outer = lax.optimization_barrier(
        (grad_attn_part, sum_inner, sum_expert_outer)
    )
    grad_bias_c = grad_bias_c.reshape(3, 1, 2, HD)
    mine = (jnp.arange(ctx_count) == ctx_rank)[None, :, None, None]
    places_of = [head_order.index(h) for h in range(head_count)]
    grad_bias = (
        jnp.where(mine, grad_bias_c, 0.0)
        .reshape(3, pairs, 2, 2, HD)
        .transpose(0, 2, 3, 1, 4)
        .reshape(dev_count, -1)
    )
    small_grads = jnp.concatenate(
        [
            grad_gain_attn.reshape(dev_count, shard),
            grad_gain_ffn.reshape(dev_count, shard),
            grad_router_gate.reshape(expert_count + 1, dev_count, shard)
            .transpose(1, 0, 2)
            .reshape(dev_count, (expert_count + 1) * shard),
            grad_bias,
        ],
        axis=1,
    )
    small_grads = jnp.pad(small_grads, ((0, 0), (0, 8 * HD - small_count)))
    grad_normed_attn, sum_qkv_c, sum_out, sum_outer, sums = closing(
        ctx_count,
        5,
        grad_attn_part.reshape(ctx_count, tokens_dev, width),
        grad_qkv_c.reshape(fsdp_count, ctx_count * shard, 6 * HD),
        padded_out,
        grad_outer.reshape(fsdp_count, shared_shard, width),
        small_grads.reshape(fsdp_count, ctx_count, 8, HD),
    )
    sums = sums.reshape(8 * HD)[:small_count]
    sum_qkv = collect_heads(sum_qkv_c, head_order)
    unused_norm, first_pull = jax.vjp(lambda v: rms_scale(v, gain_attn), inputs)
    input_grad = grad_middle + first_pull(grad_normed_attn)[0]
    sum_router = sums[2 * shard : (2 + expert_count) * shard].reshape(expert_count, shard).T
    return (
        hidden_out,
        input_grad.reshape(1, tokens_dev, width),
        sums[:shard],
        sum_qkv,
        sums[(3 + expert_count) * shard :],
        sum_out,
        sums[shard : 2 * shard],
        sum_router,
        sums[(2 + expert_count) * shard : (3 + expert_count) * shard],
        sum_inner,
        sum_outer,
        sum_expert_inner.astype(full)[None],
        sum_expert_outer.astype(full)[None],
    )


def local(*arrays):
    width = arrays[0].shape[2]
    ctx_count = lax.axis_size("ctx")
    shard = arrays[6].shape[0]
    fits = (
        width == 2 * ctx_count * HD
        and 2 * shard == HD
        and ctx_count % 2 == 0
        and lax.axis_size("fsdp") * ctx_count * shard == width
        and arrays[14].shape[0] == 1
    )
    return split_plan(*arrays) if fits else gathered_plan(*arrays)


def solution(mesh):
    in_specs = (
        P("fsdp", "ctx", None),
        P("fsdp", "ctx"),
        P(),
        P("fsdp", "ctx", None),
        P("fsdp", "ctx", None),
        P(("fsdp", "ctx")),
        P(("fsdp", "ctx"), None),
        P(("fsdp", "ctx")),
        P(("fsdp", "ctx"), None),
        P(("fsdp", "ctx")),
        P(("fsdp", "ctx"), None),
        P(("fsdp", "ctx")),
        P(("fsdp", "ctx"), None),
        P(("fsdp", "ctx"), None),
        P("ctx", "fsdp", None),
        P("ctx", "fsdp", None),
    )
    out_specs = (
        P("fsdp", "ctx", None),
        P("fsdp", "ctx", None),
        P(("fsdp", "ctx")),
        P(("fsdp", "ctx"), None),
        P(("fsdp", "ctx")),
        P(("fsdp", "ctx"), None),
        P(("fsdp", "ctx")),
        P(("fsdp", "ctx"), None),
        P(("fsdp", "ctx")),
        P(("fsdp", "ctx"), None),
        P(("fsdp", "ctx"), None),
        P("ctx", "fsdp", None),
        P("ctx", "fsdp", None),
    )
    return jax.shard_map(local, mesh=mesh, in_specs=in_specs, out_specs=out_specs, check_vma=False)
```

```python
import functools

import jax
import jax.numpy as jnp
from jax import lax
from jax.experimental import pallas as pl
from jax.experimental.pallas import tpu as pltpu
from jax.sharding import PartitionSpec as P

HD = 128


EPSILON = 1e-06
THETA = 1000000.0
heads_per_group = 4


def rms_scale(values, gain_vec):
    return (
        values * lax.rsqrt(jnp.mean(values * values, axis=-1, keepdims=True) + EPSILON) * gain_vec
    )


def rotate(values, positions):
    half_len = values.shape[-1] // 2
    frequency = THETA ** (-jnp.arange(half_len, dtype=jnp.float32) / half_len)
    angles = positions.astype(jnp.float32)[:, None] * frequency[None, :]
    cosine = jnp.cos(angles)[:, None, :]
    sine_part = jnp.sin(angles)[:, None, :]
    first_half = values[..., :half_len]
    second = values[..., half_len:]
    return jnp.concatenate(
        [first_half * cosine - second * sine_part, second * cosine + first_half * sine_part],
        axis=-1,
    )


def visible(query_pos, query_seg, key_pos, key_seg):
    same_doc = (key_seg[None, :] == query_seg[:, None]) & (query_seg[:, None] >= 0)
    causal = key_pos[None, :] <= query_pos[:, None]
    return same_doc & causal | (key_pos[None, :] == query_pos[:, None])


def swiglu_mix(gate_up, hidden_width):
    return jax.nn.silu(gate_up[..., :hidden_width]) * gate_up[..., hidden_width:]


def matmul_low(left, right):
    return jnp.dot(left, right, preferred_element_type=jnp.float32)


def gathered_plan(
    hidden_in,
    segments,
    block_pairs,
    routes,
    out_grad,
    norm_gain_attn,
    qkv_weight,
    qkv_bias,
    out_weight,
    norm_gain_ffn,
    router_weight,
    shared_gate_weight,
    shared_in_weight,
    shared_out_weight,
    expert_in_weight,
    expert_out_weight,
):
    tokens_dev = hidden_in.shape[1]
    model_width = hidden_in.shape[2]
    block_len = tokens_dev // 2
    inputs = hidden_in.reshape(tokens_dev, model_width).astype(jnp.float32)
    seg_local = segments.reshape(tokens_dev)
    token_routes = routes.reshape(tokens_dev, -1)
    top_count = token_routes.shape[1]
    ctx_count = lax.axis_size("ctx")
    ctx_rank = lax.axis_index("ctx")
    offsets = jnp.arange(block_len, dtype=jnp.int32)
    all_positions = (
        block_pairs.reshape(ctx_count, 2)[:, :, None] * block_len + offsets[None, None, :]
    ).reshape(ctx_count * tokens_dev)
    my_positions = lax.dynamic_slice_in_dim(all_positions, ctx_rank * tokens_dev, tokens_dev, 0)
    gathered = (
        lax.all_gather(norm_gain_attn, ("fsdp", "ctx"), axis=0, tiled=True),
        lax.all_gather(qkv_weight, ("fsdp", "ctx"), axis=0, tiled=True),
        lax.all_gather(qkv_bias, ("fsdp", "ctx"), axis=0, tiled=True),
        lax.all_gather(out_weight, ("fsdp", "ctx"), axis=0, tiled=True),
        lax.all_gather(norm_gain_ffn, ("fsdp", "ctx"), axis=0, tiled=True),
        lax.all_gather(router_weight, ("fsdp", "ctx"), axis=0, tiled=True),
        lax.all_gather(shared_gate_weight, ("fsdp", "ctx"), axis=0, tiled=True),
        lax.all_gather(shared_in_weight, ("fsdp", "ctx"), axis=0, tiled=True),
        lax.all_gather(shared_out_weight, ("fsdp", "ctx"), axis=0, tiled=True),
    )
    (
        gain_attn,
        qkv_full,
        shift_full,
        out_full,
        gain_ffn,
        router_full,
        gate_full,
        inner_full,
        outer_full,
    ) = gathered
    gain_attn = gain_attn.astype(jnp.float32)
    gain_ffn = gain_ffn.astype(jnp.float32)
    heads_width = out_full.shape[0]
    head_count = heads_width // HD
    group_width = heads_per_group * HD
    group_count = head_count // heads_per_group
    normed = rms_scale(inputs, gain_attn).astype(jnp.bfloat16)
    projected = matmul_low(normed, qkv_full) + shift_full.astype(jnp.float32)
    query_pre = projected[:, :heads_width].reshape(tokens_dev, head_count, HD)
    key_pre = projected[:, heads_width : 2 * heads_width].reshape(tokens_dev, head_count, HD)

    def place_heads(query_in, key_in):
        return (rotate(query_in, my_positions) * HD ** (-0.5), rotate(key_in, my_positions))

    query_rot, key_rot = place_heads(query_pre, key_pre)
    query_low = query_rot.reshape(tokens_dev, heads_width).astype(jnp.bfloat16)
    key_low = key_rot.reshape(tokens_dev, heads_width).astype(jnp.bfloat16)
    value_low = projected[:, 2 * heads_width :].astype(jnp.bfloat16)
    keys_all, values_all, segs_all = (
        lax.all_gather(key_low, "ctx", axis=0, tiled=True),
        lax.all_gather(value_low, "ctx", axis=0, tiled=True),
        lax.all_gather(seg_local.astype(jnp.bfloat16), "ctx", axis=0, tiled=True),
    )
    allowed = visible(
        my_positions, seg_local.astype(jnp.float32), all_positions, segs_all.astype(jnp.float32)
    )

    def head_slice(matrix, group_index):
        return lax.dynamic_slice_in_dim(matrix, group_index * group_width, group_width, 1).reshape(
            matrix.shape[0], heads_per_group, HD
        )

    def forward_group(group_index):
        query_part = head_slice(query_low, group_index)
        key_part = head_slice(keys_all, group_index)
        value_part = head_slice(values_all, group_index)
        scores = jnp.einsum(
            "qhd,khd->hqk", query_part, key_part, preferred_element_type=jnp.float32
        )
        scores = jnp.where(allowed[None], scores, -1e30)
        highest = jnp.max(scores, axis=-1, keepdims=True)
        log_total = highest + jnp.log(jnp.sum(jnp.exp(scores - highest), axis=-1, keepdims=True))
        weights = jnp.exp(scores - log_total).astype(jnp.bfloat16)
        mixed = jnp.einsum("hqk,khd->qhd", weights, value_part, preferred_element_type=jnp.float32)
        return (mixed, log_total[..., 0])

    mixed_groups, log_totals = lax.map(forward_group, jnp.arange(group_count, dtype=jnp.int32))
    attended = (
        jnp.moveaxis(mixed_groups, 0, 1).reshape(tokens_dev, heads_width).astype(jnp.bfloat16)
    )
    middle = inputs + matmul_low(attended, out_full)
    normed_ffn = rms_scale(middle, gain_ffn).astype(jnp.bfloat16)
    logits = matmul_low(normed_ffn, router_full)
    router_probs = jax.nn.softmax(logits, axis=-1)
    expert_count = logits.shape[1]
    expert_ids = jnp.arange(expert_count, dtype=jnp.int32)
    chosen = (token_routes[:, :, None] == expert_ids[None, None, :]).astype(jnp.float32)
    gate_weights = jnp.sum(chosen * router_probs[:, None, :], axis=-1)
    capacity = 2 * tokens_dev * top_count // expert_count
    local_experts = expert_in_weight.shape[0]
    assigned = tokens_dev * top_count
    flat_routes = token_routes.reshape(assigned)
    onehot = (flat_routes[:, None] == expert_ids[None, :]).astype(jnp.int32)
    earlier = jnp.cumsum(onehot, axis=0) - onehot
    places = flat_routes * capacity + jnp.sum(earlier * onehot, axis=1)
    slot_source = (
        jnp.full((expert_count * capacity,), assigned, jnp.int32)
        .at[places]
        .set(jnp.arange(assigned, dtype=jnp.int32))
    )
    slot_token = slot_source // top_count
    padded_rows = jnp.concatenate([normed_ffn, jnp.zeros((1, model_width), jnp.bfloat16)], axis=0)
    outgoing = padded_rows[slot_token].reshape(ctx_count, local_experts * capacity, model_width)
    expert_inner, expert_outer = (
        lax.all_gather(expert_in_weight, "fsdp", axis=1, tiled=True),
        lax.all_gather(expert_out_weight, "fsdp", axis=1, tiled=True),
    )
    landed_tokens = lax.all_to_all(outgoing, "ctx", split_axis=0, concat_axis=0, tiled=True)
    incoming = landed_tokens.reshape(ctx_count, local_experts, capacity, model_width)
    expert_gu = jnp.einsum(
        "necd,edf->necf", incoming, expert_inner, preferred_element_type=jnp.float32
    )
    expert_width = expert_outer.shape[1]
    expert_hidden = swiglu_mix(expert_gu, expert_width).astype(jnp.bfloat16)
    expert_result = jnp.einsum(
        "necf,efd->necd", expert_hidden, expert_outer, preferred_element_type=jnp.float32
    ).astype(jnp.bfloat16)
    returned = lax.all_to_all(
        expert_result.reshape(ctx_count, local_experts * capacity, model_width),
        "ctx",
        split_axis=0,
        concat_axis=0,
        tiled=True,
    )
    picked = (
        returned.reshape(expert_count * capacity, model_width)[places]
        .reshape(tokens_dev, top_count, model_width)
        .astype(jnp.float32)
    )
    routed = jnp.sum(gate_weights[:, :, None] * picked, axis=1)
    upstream = out_grad.reshape(tokens_dev, model_width).astype(jnp.float32)
    shared_gu = matmul_low(normed_ffn, inner_full)
    shared_width = outer_full.shape[0]
    shared_hidden = swiglu_mix(shared_gu, shared_width).astype(jnp.bfloat16)
    shared_out = matmul_low(shared_hidden, outer_full)
    gate_value = jax.nn.sigmoid(matmul_low(normed_ffn, gate_full))
    output = middle + gate_value[:, None] * shared_out + routed
    hidden_out = output.astype(jnp.bfloat16).reshape(1, tokens_dev, model_width)
    gain_ffn, router_full, gate_full, inner_full, outer_full = (
        lax.all_gather(norm_gain_ffn, ("fsdp", "ctx"), axis=0, tiled=True),
        lax.all_gather(router_weight, ("fsdp", "ctx"), axis=0, tiled=True),
        lax.all_gather(shared_gate_weight, ("fsdp", "ctx"), axis=0, tiled=True),
        lax.all_gather(shared_in_weight, ("fsdp", "ctx"), axis=0, tiled=True),
        lax.all_gather(shared_out_weight, ("fsdp", "ctx"), axis=0, tiled=True),
    )
    gain_ffn = gain_ffn.astype(jnp.float32)
    grad_shared_out = (gate_value[:, None] * upstream).astype(jnp.bfloat16)
    grad_outer = jnp.einsum(
        "tf,td->fd", shared_hidden, grad_shared_out, preferred_element_type=jnp.float32
    )
    grad_hidden = jnp.einsum(
        "td,fd->tf", grad_shared_out, outer_full, preferred_element_type=jnp.float32
    )
    unused_mix, mix_pull = jax.vjp(functools.partial(swiglu_mix, hidden_width=shared_width), shared_gu)
    grad_shared_gu = mix_pull(grad_hidden)[0].astype(jnp.bfloat16)
    grad_inner = jnp.einsum(
        "td,tf->df", normed_ffn, grad_shared_gu, preferred_element_type=jnp.float32
    )
    grad_normed = jnp.einsum(
        "tf,df->td", grad_shared_gu, inner_full, preferred_element_type=jnp.float32
    )
    grad_gate_logit = (
        gate_value * (1.0 - gate_value) * jnp.sum(upstream * shared_out, axis=1)
    ).astype(jnp.bfloat16)
    grad_gate_vec = jnp.einsum(
        "td,t->d", normed_ffn, grad_gate_logit, preferred_element_type=jnp.float32
    )
    grad_normed = (
        grad_normed
        + grad_gate_logit.astype(jnp.float32)[:, None] * gate_full.astype(jnp.float32)[None, :]
    )
    grad_gates = jnp.sum(upstream[:, None, :] * picked, axis=2)
    grad_choice_probs = jnp.sum(chosen * grad_gates[:, :, None], axis=1)
    grad_logits = (
        router_probs
        * (grad_choice_probs - jnp.sum(router_probs * grad_choice_probs, axis=1, keepdims=True))
    ).astype(jnp.bfloat16)
    grad_router = jnp.einsum(
        "td,te->de", normed_ffn, grad_logits, preferred_element_type=jnp.float32
    )
    grad_normed = grad_normed + jnp.einsum(
        "te,de->td", grad_logits, router_full, preferred_element_type=jnp.float32
    )
    grad_slots = (
        (gate_weights[:, :, None] * upstream[:, None, :])
        .astype(jnp.bfloat16)
        .reshape(assigned, model_width)
    )
    padded_grads = jnp.concatenate([grad_slots, jnp.zeros((1, model_width), jnp.bfloat16)], axis=0)
    grad_outgoing = padded_grads[slot_source].reshape(
        ctx_count, local_experts * capacity, model_width
    )
    grad_incoming = lax.all_to_all(
        grad_outgoing, "ctx", split_axis=0, concat_axis=0, tiled=True
    ).reshape(ctx_count, local_experts, capacity, model_width)
    grad_expert_hidden = jnp.einsum(
        "necd,efd->necf", grad_incoming, expert_outer, preferred_element_type=jnp.float32
    )
    grad_expert_outer = jnp.einsum(
        "necf,necd->efd", expert_hidden, grad_incoming, preferred_element_type=jnp.float32
    )
    unused_mix, expert_pull = jax.vjp(functools.partial(swiglu_mix, hidden_width=expert_width), expert_gu)
    grad_expert_gu = expert_pull(grad_expert_hidden)[0].astype(jnp.bfloat16)
    grad_expert_inner = jnp.einsum(
        "necd,necf->edf", incoming, grad_expert_gu, preferred_element_type=jnp.float32
    )
    grad_expert_rows = jnp.einsum(
        "necf,edf->necd", grad_expert_gu, expert_inner, preferred_element_type=jnp.float32
    ).astype(jnp.bfloat16)
    grad_returned = lax.all_to_all(
        grad_expert_rows.reshape(ctx_count, local_experts * capacity, model_width),
        "ctx",
        split_axis=0,
        concat_axis=0,
        tiled=True,
    )
    grad_picked = grad_returned.reshape(expert_count * capacity, model_width)[places].reshape(
        tokens_dev, top_count, model_width
    )
    grad_normed = grad_normed + jnp.sum(grad_picked.astype(jnp.float32), axis=1)
    sum_expert_inner, sum_expert_outer = (
        lax.psum_scatter(
            grad_expert_inner.astype(jnp.bfloat16), "fsdp", scatter_dimension=1, tiled=True
        ).astype(jnp.float32),
        lax.psum_scatter(
            grad_expert_outer.astype(jnp.bfloat16), "fsdp", scatter_dimension=1, tiled=True
        ).astype(jnp.float32),
    )
    unused_norm, norm_pull = jax.vjp(rms_scale, middle, gain_ffn)
    grad_middle_norm, grad_gain_ffn = norm_pull(grad_normed)
    grad_middle = upstream + grad_middle_norm
    sum_gain_ffn, sum_router, sum_gate_vec, sum_inner, sum_outer = (
        lax.psum_scatter(grad_gain_ffn, ("fsdp", "ctx"), scatter_dimension=0, tiled=True),
        lax.psum_scatter(grad_router, ("fsdp", "ctx"), scatter_dimension=0, tiled=True),
        lax.psum_scatter(grad_gate_vec, ("fsdp", "ctx"), scatter_dimension=0, tiled=True),
        lax.psum_scatter(grad_inner, ("fsdp", "ctx"), scatter_dimension=0, tiled=True),
        lax.psum_scatter(grad_outer, ("fsdp", "ctx"), scatter_dimension=0, tiled=True),
    )
    grad_branch = grad_middle.astype(jnp.bfloat16)
    grad_out_mat = jnp.einsum(
        "tc,td->cd", attended, grad_branch, preferred_element_type=jnp.float32
    )
    grad_attended = jnp.einsum(
        "td,cd->tc", grad_branch, out_full, preferred_element_type=jnp.float32
    ).astype(jnp.bfloat16)
    keys_again, values_again = (
        lax.all_gather(key_low, "ctx", axis=0, tiled=True),
        lax.all_gather(value_low, "ctx", axis=0, tiled=True),
    )

    def backward_group(group_index):
        query_part = head_slice(query_low, group_index)
        key_part = head_slice(keys_again, group_index)
        value_part = head_slice(values_again, group_index)
        grad_part = head_slice(grad_attended, group_index)
        log_total = lax.dynamic_index_in_dim(log_totals, group_index, 0, keepdims=False)
        scores = jnp.einsum(
            "qhd,khd->hqk", query_part, key_part, preferred_element_type=jnp.float32
        )
        scores = jnp.where(allowed[None], scores, -1e30)
        weights = jnp.exp(scores - log_total[..., None])
        grad_weights = jnp.einsum(
            "qhd,khd->hqk", grad_part, value_part, preferred_element_type=jnp.float32
        )
        offset_term = jnp.sum(weights * grad_weights, axis=-1, keepdims=True)
        grad_scores = (weights * (grad_weights - offset_term)).astype(jnp.bfloat16)
        grad_query = jnp.einsum(
            "hqk,khd->qhd", grad_scores, key_part, preferred_element_type=jnp.float32
        )
        grad_key = jnp.einsum(
            "hqk,qhd->khd", grad_scores, query_part, preferred_element_type=jnp.float32
        )
        grad_value = jnp.einsum(
            "hqk,qhd->khd",
            weights.astype(jnp.bfloat16),
            grad_part,
            preferred_element_type=jnp.float32,
        )
        return (grad_query, grad_key, grad_value)

    grad_queries, grad_keys, grad_values = lax.map(
        backward_group, jnp.arange(group_count, dtype=jnp.int32)
    )
    row_total = keys_again.shape[0]
    grad_key_rows = jnp.moveaxis(grad_keys, 0, 1).reshape(row_total, heads_width)
    grad_value_rows = jnp.moveaxis(grad_values, 0, 1).reshape(row_total, heads_width)
    key_share, value_share = (
        lax.psum_scatter(
            grad_key_rows.astype(jnp.bfloat16), "ctx", scatter_dimension=0, tiled=True
        ).astype(jnp.float32),
        lax.psum_scatter(
            grad_value_rows.astype(jnp.bfloat16), "ctx", scatter_dimension=0, tiled=True
        ).astype(jnp.float32),
    )
    grad_query_heads = jnp.moveaxis(grad_queries, 0, 1).reshape(tokens_dev, head_count, HD)
    unused_rot, rotate_pull = jax.vjp(place_heads, query_pre, key_pre)
    grad_query_pre, grad_key_pre = rotate_pull(
        (grad_query_heads, key_share.reshape(tokens_dev, head_count, HD))
    )
    grad_projected = jnp.concatenate(
        [
            grad_query_pre.reshape(tokens_dev, heads_width),
            grad_key_pre.reshape(tokens_dev, heads_width),
            value_share,
        ],
        axis=1,
    ).astype(jnp.bfloat16)
    grad_qkv = jnp.einsum("td,tc->dc", normed, grad_projected, preferred_element_type=jnp.float32)
    grad_shift = jnp.sum(grad_projected.astype(jnp.float32), axis=0)
    grad_normed_attn = jnp.einsum(
        "tc,dc->td", grad_projected, qkv_full, preferred_element_type=jnp.float32
    )
    unused_norm, first_pull = jax.vjp(rms_scale, inputs, gain_attn)
    grad_inputs_norm, grad_gain_attn = first_pull(grad_normed_attn)
    input_grad = grad_middle + grad_inputs_norm
    sum_gain_attn, sum_qkv, sum_shift, sum_out = (
        lax.psum_scatter(grad_gain_attn, ("fsdp", "ctx"), scatter_dimension=0, tiled=True),
        lax.psum_scatter(grad_qkv, ("fsdp", "ctx"), scatter_dimension=0, tiled=True),
        lax.psum_scatter(grad_shift, ("fsdp", "ctx"), scatter_dimension=0, tiled=True),
        lax.psum_scatter(grad_out_mat, ("fsdp", "ctx"), scatter_dimension=0, tiled=True),
    )
    return (
        hidden_out,
        input_grad.reshape(1, tokens_dev, model_width),
        sum_gain_attn,
        sum_qkv,
        sum_shift,
        sum_out,
        sum_gain_ffn,
        sum_router,
        sum_gate_vec,
        sum_inner,
        sum_outer,
        sum_expert_inner,
        sum_expert_outer,
    )


SPAN = 256


def flat_dot(left, right):
    return lax.dot_general(left, right, (((1,), (0,)), ((), ())), preferred_element_type=jnp.float32)


def turned_dot(left, right):
    return lax.dot_general(left, right, (((1,), (1,)), ((), ())), preferred_element_type=jnp.float32)


def span_of(index, size=SPAN):
    return pl.ds(pl.multiple_of(index * size, size), size)


MESH = pl.DeviceIdType.MESH
ANY = pl.BlockSpec(memory_space=pl.ANY)
VMEM = pl.BlockSpec(memory_space=pltpu.VMEM)


def remote(source, target, send_sem, recv_sem, **place):
    return pltpu.make_async_remote_copy(
        src_ref=source,
        dst_ref=target,
        send_sem=send_sem,
        recv_sem=recv_sem,
        device_id=place,
        device_id_type=MESH,
    )


def line_place():
    here = lax.axis_index("ctx")
    line = here % 2
    return here, here // 2, line, here + 1 - 2 * line


def greet_line(last, here, level, side, others=0):
    barrier = pltpu.get_barrier_semaphore()
    pl.semaphore_signal(barrier, inc=1, device_id={"ctx": side}, device_id_type=MESH)

    @pl.when(level < last)
    def up():
        pl.semaphore_signal(barrier, inc=1, device_id={"ctx": here + 2}, device_id_type=MESH)

    @pl.when(level > 0)
    def down():
        pl.semaphore_signal(barrier, inc=1, device_id={"ctx": here - 2}, device_id_type=MESH)

    ends = jnp.where(level < last, 1, 0) + jnp.where(level > 0, 1, 0)
    pl.semaphore_wait(barrier, 1 + others + ends)


def line_copy(rows_ref, block, way, target, sems, source=None):
    send_sem, recv_sem = sems
    return remote(
        rows_ref.at[block] if source is None else source,
        rows_ref.at[block],
        send_sem.at[block, way],
        recv_sem.at[block],
        ctx=target,
    )


def line_start(rows_ref, own_ref, sems, place, last):
    here, level, line, side = place

    @pl.when(level < last)
    def up():
        line_copy(rows_ref, here, 0, here + 2, sems, own_ref).start()

    @pl.when(level > 0)
    def down():
        line_copy(rows_ref, here, 1, here - 2, sems, own_ref).start()

    line_copy(rows_ref, here, 2, side, sems, own_ref).start()


def line_step(rows_ref, sems, place, last, step):
    here, level, line, side = place

    @pl.when(level >= step)
    def from_below():
        block = here - 2 * step
        line_copy(rows_ref, block, 0, side, sems).wait_recv()

        @pl.when(level < last)
        def on():
            line_copy(rows_ref, block, 0, here + 2, sems).start()

        line_copy(rows_ref, block, 2, side, sems).start()

    @pl.when(level + step <= last)
    def from_above():
        block = here + 2 * step
        line_copy(rows_ref, block, 1, side, sems).wait_recv()

        @pl.when(level > 0)
        def on():
            line_copy(rows_ref, block, 1, here - 2, sems).start()

        line_copy(rows_ref, block, 2, side, sems).start()


def line_finish(rows_ref, sems, place, last):
    here, level, line, side = place
    for other in range(last + 1):
        block = 2 * other + line
        line_copy(rows_ref, 2 * other + 1 - line, 2, side, sems).wait_recv()
        line_copy(rows_ref, block, 2, side, sems).wait_send()

        @pl.when((other <= level) & (level < last))
        def up():
            line_copy(rows_ref, block, 0, side, sems).wait_send()

        @pl.when((other >= level) & (level > 0))
        def down():
            line_copy(rows_ref, block, 1, side, sems).wait_send()


ROWS_STEP = 16


def add_rows(target, pieces, row_count):
    def one(index, carry):
        rows = pl.ds(pl.multiple_of(index * ROWS_STEP, ROWS_STEP), ROWS_STEP)
        total = pieces[0][rows, :].astype(jnp.float32)
        for piece in pieces[1:]:
            total = total + piece[rows, :].astype(jnp.float32)
        target[rows, :] = total.astype(target.dtype)
        return carry

    lax.fori_loop(0, row_count // ROWS_STEP, one, 0)


def scatter_turns(last, part, total, crossed, rising, falling, sums, *sems):
    cross_send, cross_recv, move_send, rise_recv, fall_recv = sems
    here, level, line, side = line_place()
    row_count = total.shape[0]

    def turn(k):
        middle = (level > 0) & (level < last)
        swapped = k + jnp.where(middle, (0, 0, 1, -1)[k], 0)
        return jnp.where(level * 2 < last, last - swapped, swapped)

    def cross(goal):
        return remote(
            part.at[2 * goal + 1 - line],
            crossed.at[goal],
            cross_send.at[goal],
            cross_recv.at[goal],
            ctx=side,
        )

    def rise(goal):
        return remote(
            sums.at[goal], rising.at[goal], move_send.at[goal], rise_recv.at[goal], ctx=here + 2
        )

    def fall(goal):
        return remote(
            sums.at[goal], falling.at[goal], move_send.at[goal], fall_recv.at[goal], ctx=here - 2
        )

    for k in range(min(2, last + 1)):
        cross(turn(k)).start()
    for k in range(last + 1):
        yield k
        goal = turn(k)
        mine = part.at[2 * goal + line]
        cross(goal).wait_recv()
        if k + 2 <= last:
            cross(turn(k + 2)).start()

        @pl.when(goal > level)
        def upward():
            @pl.when(level > 0)
            def joined():
                rise(goal).wait_recv()
                add_rows(sums.at[goal], (mine, crossed.at[goal], rising.at[goal]), row_count)

            @pl.when(level == 0)
            def first():
                add_rows(sums.at[goal], (mine, crossed.at[goal]), row_count)

            rise(goal).start()

        @pl.when(goal < level)
        def downward():
            @pl.when(level < last)
            def joined():
                fall(goal).wait_recv()
                add_rows(sums.at[goal], (mine, crossed.at[goal], falling.at[goal]), row_count)

            @pl.when(level == last)
            def first():
                add_rows(sums.at[goal], (mine, crossed.at[goal]), row_count)

            fall(goal).start()

        @pl.when(goal == level)
        def here_at_last():
            @pl.when(level > 0)
            def from_below():
                rise(goal).wait_recv()

            @pl.when(level < last)
            def from_above():
                fall(goal).wait_recv()

            @pl.when(level == 0)
            def bottom():
                add_rows(total, (mine, crossed.at[goal], falling.at[goal]), row_count)

            @pl.when(level == last)
            def top():
                add_rows(total, (mine, crossed.at[goal], rising.at[goal]), row_count)

            @pl.when((level > 0) & (level < last))
            def between():
                add_rows(
                    total,
                    (mine, crossed.at[goal], rising.at[goal], falling.at[goal]),
                    row_count,
                )

    for goal in range(last + 1):
        cross(goal).wait_send()

        @pl.when(goal != level)
        def sent():
            rise(goal).wait_send()


def scatter_kernel(
    ctx_count, part, small, far_tokens, far_grads, total, small_in, weight_grad, *refs
):
    *refs, product, store_sem, tokens, grads, load_sem = refs
    loads = [
        pltpu.make_async_copy(source, target, load_sem.at[i])
        for i, (source, target) in enumerate(((far_tokens, tokens), (far_grads, grads)))
    ]
    for copy in loads:
        copy.start()
    greet_all(ctx_count)
    here = lax.axis_index("ctx")
    starts, waits = spread(
        lambda peer: small.at[peer], lambda source: small_in.at[source], refs[9:11], ctx_count
    )
    for copy in starts:
        copy.start()
    small_in[here] = small[here]
    turns = scatter_turns(ctx_count // 2 - 1, part, total, *refs[:9])
    next(turns)
    pieces = ctx_count // 2
    depth = tokens.shape[1] // pieces
    stores = []
    for copy in loads:
        copy.wait()
    for piece in range(pieces):

        @pl.loop(0, depth // SPAN)
        def multiply(index):
            here = pl.ds(pl.multiple_of(piece * depth + index * SPAN, SPAN), SPAN)
            product[here, :] = flat_dot(tokens[:, here].T, grads[...]).astype(product.dtype)

        rows = pl.ds(piece * depth, depth)
        stores.append(
            pltpu.make_async_copy(product.at[rows], weight_grad.at[rows], store_sem.at[piece])
        )
        stores[-1].start()
        next(turns, None)
    for copy in waits:
        copy.wait_recv()
    for copy in starts:
        copy.wait_send()
    for copy in stores:
        copy.wait()


def line_scatter_kernel(last, part, total, *refs):
    here, level, line, side = line_place()
    greet_line(last, here, level, side)
    for step in scatter_turns(last, part, total, *refs):
        pass


def line_scatter(ctx_count, call_id, part, small=None, tokens=None, grads=None):
    rows, width = part.shape[1:]
    half = ctx_count // 2
    dma = pltpu.SemaphoreType.DMA((half,))
    spread_dma = pltpu.SemaphoreType.DMA((ctx_count,))
    slots = pltpu.VMEM((half, rows, width), part.dtype)
    total = jax.ShapeDtypeStruct((rows, width), jnp.float32)
    params = pltpu.CompilerParams(
        collective_id=call_id, has_side_effects=True, vmem_limit_bytes=40 * 2**20
    )
    if small is None:
        return pl.pallas_call(
            functools.partial(line_scatter_kernel, half - 1),
            out_shape=total,
            in_specs=[VMEM],
            out_specs=VMEM,
            scratch_shapes=[slots] * 4 + [dma] * 5,
            compiler_params=params,
            name="line_scatter",
        )(part)
    product = (tokens.shape[1], grads.shape[1])
    params = pltpu.CompilerParams(
        collective_id=call_id, has_side_effects=True, vmem_limit_bytes=56 * 2**20
    )
    return pl.pallas_call(
        functools.partial(scatter_kernel, ctx_count),
        out_shape=[
            total,
            jax.ShapeDtypeStruct(small.shape, small.dtype),
            jax.ShapeDtypeStruct(product, part.dtype),
        ],
        in_specs=[VMEM] * 2 + [ANY] * 2,
        out_specs=[VMEM] * 2 + [ANY],
        scratch_shapes=[slots] * 4
        + [dma] * 5
        + [spread_dma] * 2
        + [pltpu.VMEM(product, part.dtype), pltpu.SemaphoreType.DMA((half,))]
        + [
            pltpu.VMEM(tokens.shape, tokens.dtype),
            pltpu.VMEM(grads.shape, grads.dtype),
            pltpu.SemaphoreType.DMA((2,)),
        ],
        compiler_params=params,
        name="line_scatter",
    )(part, small, tokens, grads)


def fsdp_place():
    here = lax.axis_index("fsdp")
    beside = here + 1 - 2 * (here % 2)
    return here, beside, (here + 2) % 4, (beside + 2) % 4


def greet_all(ctx_count):
    barrier = pltpu.get_barrier_semaphore()
    here = lax.axis_index("ctx")
    group = lax.axis_index("fsdp")
    for k in range(1, ctx_count):
        pl.semaphore_signal(
            barrier, inc=1, device_id={"ctx": (here + k) % ctx_count}, device_id_type=MESH
        )
    for k in range(1, 4):
        pl.semaphore_signal(barrier, inc=1, device_id={"fsdp": (group + k) % 4}, device_id_type=MESH)
    pl.semaphore_wait(barrier, ctx_count + 2)


def share_start(blocks, sems, own=None):
    send_sem, recv_sem = sems
    here, beside, across, corner = fsdp_place()
    source = blocks.at[here] if own is None else own
    for way, target in ((0, across), (1, beside)):
        remote(source, blocks.at[here], send_sem.at[way], recv_sem.at[here], fsdp=target).start()


def share_step(blocks, sems):
    send_sem, recv_sem = sems
    here, beside, across, corner = fsdp_place()
    copy = remote(
        blocks.at[across], blocks.at[across], send_sem.at[2], recv_sem.at[across], fsdp=beside
    )
    copy.wait_recv()
    copy.start()


def share_finish(blocks, sems):
    send_sem, recv_sem = sems
    here, beside, across, corner = fsdp_place()
    for way, block in ((0, beside), (1, corner)):
        copy = remote(
            blocks.at[block], blocks.at[block], send_sem.at[way], recv_sem.at[block], fsdp=beside
        )
        copy.wait_recv()
        copy.wait_send()
    remote(
        blocks.at[here], blocks.at[here], send_sem.at[2], recv_sem.at[here], fsdp=beside
    ).wait_send()


def spread(pieces, landing, sems, ctx_count):
    send_sem, recv_sem = sems
    here = lax.axis_index("ctx")

    def copy(k, peer, source):
        return remote(pieces(peer), landing(source), send_sem.at[k], recv_sem.at[k], ctx=peer)

    starts = [copy(k, (here + k) % ctx_count, here) for k in range(1, ctx_count)]
    waits = [
        copy(k, (here + k) % ctx_count, (here + ctx_count - k) % ctx_count)
        for k in range(1, ctx_count)
    ]
    return starts, waits


def greet_near(last, here, level, side):
    barrier = pltpu.get_barrier_semaphore()
    group = lax.axis_index("fsdp")
    for k in range(1, 4):
        pl.semaphore_signal(barrier, inc=1, device_id={"fsdp": (group + k) % 4}, device_id_type=MESH)
    greet_line(last, here, level, side, 3)


def gather_kernel(last, shared_count, *refs):
    total = 1 + shared_count
    owns, rows, keep_sem = refs[:total], refs[total : 2 * total], refs[2 * total]
    refs = refs[2 * total + 1 :]
    place = line_place()
    here, level, line, side = place
    sems = [(refs[2 * i], refs[2 * i + 1]) for i in range(total)]
    group = lax.axis_index("fsdp")
    if shared_count:
        greet_near(last, here, level, side)
    else:
        greet_line(last, here, level, side)
    line_start(rows[0], owns[0], sems[0], place, last)
    for i in range(1, total):
        share_start(rows[i], sems[i], owns[i])
    keeps = [
        pltpu.make_async_copy(
            owns[i], rows[i].at[group if i else here], keep_sem.at[i]
        )
        for i in range(total)
    ]
    for copy in keeps:
        copy.start()
    for step in range(1, last + 1):
        line_step(rows[0], sems[0], place, last, step)
    for i in range(1, total):
        share_step(rows[i], sems[i])
    line_finish(rows[0], sems[0], place, last)
    for i in range(1, total):
        share_finish(rows[i], sems[i])
    for copy in keeps:
        copy.wait()


def product_kernel(last, own, units, grads, rows, product, keep_sem, send_sem, recv_sem):
    place = line_place()
    here, level, line, side = place
    sems = (send_sem, recv_sem)
    greet_line(last, here, level, side)
    line_start(rows, own, sems, place, last)
    keep = pltpu.make_async_copy(own, rows.at[here], keep_sem.at[0])
    keep.start()
    turned = units[...].T
    piece = grads.shape[1] // (last + 1)
    for step in range(last + 1):
        columns = pl.ds(step * piece, piece)
        product[:, columns] = flat_dot(turned, grads[:, columns]).astype(product.dtype)
        if step < last:
            line_step(rows, sems, place, last, step + 1)
    line_finish(rows, sems, place, last)
    keep.wait()


def product_gather(ctx_count, call_id, own, units, grads):
    dma = pltpu.SemaphoreType.DMA
    return pl.pallas_call(
        functools.partial(product_kernel, ctx_count // 2 - 1),
        out_shape=[
            jax.ShapeDtypeStruct((ctx_count,) + own.shape, own.dtype),
            jax.ShapeDtypeStruct((units.shape[1], grads.shape[1]), own.dtype),
        ],
        in_specs=[VMEM] * 3,
        out_specs=[ANY, VMEM],
        scratch_shapes=[dma((1,)), dma((ctx_count, 3)), dma((ctx_count,))],
        compiler_params=pltpu.CompilerParams(
            collective_id=call_id, has_side_effects=True, vmem_limit_bytes=32 * 2**20
        ),
        name="product_gather",
    )(own, units, grads)


def line_gather(ctx_count, call_id, own, *shared):
    count = len(shared)
    dma = pltpu.SemaphoreType.DMA
    return pl.pallas_call(
        functools.partial(gather_kernel, ctx_count // 2 - 1, count),
        out_shape=[jax.ShapeDtypeStruct((ctx_count,) + own.shape, own.dtype)]
        + [jax.ShapeDtypeStruct((4,) + a.shape, a.dtype) for a in shared],
        in_specs=[VMEM] * (1 + count),
        out_specs=[ANY] * (1 + count),
        scratch_shapes=[dma((1 + count,)), dma((ctx_count, 3)), dma((ctx_count,))]
        + [dma((3,)), dma((4,))] * count,
        compiler_params=pltpu.CompilerParams(collective_id=call_id, has_side_effects=True),
        name="line_gather",
    )(own, *shared)


def opening_kernel(
    ctx_count,
    own,
    qkv_own,
    out_own,
    small_own,
    number_own,
    rows,
    qkv,
    out_pair,
    small,
    numbers,
    keep_sem,
    pair_send,
    pair_recv,
    row_send,
    row_recv,
    share_send,
    share_recv,
    *sems,
):
    last = ctx_count // 2 - 1
    place = line_place()
    here, level, line, side = place
    group, beside, across, corner = fsdp_place()
    sems = [(sems[2 * i], sems[2 * i + 1]) for i in range(5)]
    qkv_spread, small_spread, number_spread, out_share, small_share = sems
    row_sems = (row_send, row_recv)
    greet_all(ctx_count)
    qkv_start, qkv_wait = spread(
        lambda peer: qkv_own.at[peer], lambda source: qkv.at[group, source], qkv_spread, ctx_count
    )
    small_start, small_wait = spread(
        lambda peer: small_own, lambda source: small.at[group, source], small_spread, ctx_count
    )
    number_start, number_wait = spread(
        lambda peer: number_own, lambda source: numbers.at[source], number_spread, ctx_count
    )

    def piece_copy(way, owner, k, target, first=False):
        source = (here + ctx_count - k) % ctx_count
        return remote(
            qkv_own.at[here] if first else qkv.at[owner, source],
            qkv.at[owner, source],
            share_send.at[way, k],
            share_recv.at[owner, k],
            fsdp=target,
        )

    def piece_on(k):
        piece_copy(0, group, k, across, k == 0).start()
        piece_copy(1, group, k, beside, k == 0).start()

    for copy in small_start + number_start + qkv_start:
        copy.start()
    line_start(rows, own, row_sems, place, last)
    piece_on(0)
    pair = remote(
        out_own, out_pair.at[group, line], pair_send.at[0], pair_recv.at[0], ctx=side
    )
    pair.start()
    keeps = [
        pltpu.make_async_copy(source, target, keep_sem.at[i])
        for i, (source, target) in enumerate(
            (
                (qkv_own.at[here], qkv.at[group, here]),
                (out_own, out_pair.at[group, line]),
                (small_own, small.at[group, here]),
                (number_own, numbers.at[here]),
                (own, rows.at[here]),
            )
        )
    ]
    for copy in keeps:
        copy.start()
    for copy in small_wait:
        copy.wait_recv()
    keeps[2].wait()
    share_start(small, small_share)
    line_step(rows, row_sems, place, last, 1)
    for k in range(1, ctx_count):
        qkv_wait[k - 1].wait_recv()
        piece_on(k)
    remote(
        out_own, out_pair.at[group, 1 - line], pair_send.at[0], pair_recv.at[0], ctx=side
    ).wait_recv()
    keeps[1].wait()
    share_start(out_pair, out_share)
    line_step(rows, row_sems, place, last, 2)
    for k in range(ctx_count):
        piece_copy(0, across, k, across).wait_recv()
        piece_copy(2, across, k, beside).start()
    share_step(small, small_share)
    for step in range(3, last + 1):
        line_step(rows, row_sems, place, last, step)
    share_step(out_pair, out_share)
    line_finish(rows, row_sems, place, last)
    for copy in number_wait:
        copy.wait_recv()
    for copy in qkv_start + small_start + number_start:
        copy.wait_send()
    pair.wait_send()
    for k in range(ctx_count):
        piece_copy(1, beside, k, beside).wait_recv()
        piece_copy(2, corner, k, beside).wait_recv()
        for way in range(3):
            piece_copy(way, group, k, beside).wait_send()
    share_finish(small, small_share)
    share_finish(out_pair, out_share)
    for i in (0, 3, 4):
        keeps[i].wait()


def opening(ctx_count, call_id, own, qkv_own, out_own, small_own, number_own):
    def out(lead, array):
        return jax.ShapeDtypeStruct(lead + array.shape, array.dtype)

    dma = pltpu.SemaphoreType.DMA
    return pl.pallas_call(
        functools.partial(opening_kernel, ctx_count),
        out_shape=[
            out((ctx_count,), own),
            out((4,), qkv_own),
            out((4, 2), out_own),
            out((4, ctx_count), small_own),
            out((ctx_count,), number_own),
        ],
        in_specs=[VMEM] * 5,
        out_specs=[ANY] * 5,
        scratch_shapes=[
            dma((5,)),
            dma((1,)),
            dma((1,)),
            dma((ctx_count, 3)),
            dma((ctx_count,)),
            dma((3, ctx_count)),
            dma((4, ctx_count)),
        ]
        + [dma((ctx_count,))] * 6
        + [dma((3,)), dma((4,))] * 2,
        compiler_params=pltpu.CompilerParams(collective_id=call_id, has_side_effects=True),
        name="opening",
    )(own, qkv_own, out_own, small_own, number_own)


def group_reduce(blocks, beside_in, pair_sums, across_in, settled, sems):
    core_send, core_recv, far_send, far_recv = sems
    group, beside, across, corner = fsdp_place()
    rows = settled.shape[0]

    def core_copy(slot, block):
        return remote(
            blocks.at[block],
            beside_in.at[slot],
            core_send.at[slot],
            core_recv.at[slot],
            fsdp=beside,
        )

    far = remote(pair_sums.at[1], across_in, far_send.at[0], far_recv.at[0], fsdp=across)
    core_copy(1, corner).start()
    core_copy(0, beside).start()
    yield
    core_copy(1, corner).wait_recv()
    add_rows(pair_sums.at[1], (blocks.at[across], beside_in.at[1]), rows)
    far.start()
    core_copy(0, beside).wait_recv()
    add_rows(pair_sums.at[0], (blocks.at[group], beside_in.at[0]), rows)
    yield
    far.wait_recv()
    add_rows(settled, (pair_sums.at[0], across_in), rows)
    yield
    core_copy(1, corner).wait_send()
    core_copy(0, beside).wait_send()
    far.wait_send()
    yield


def closing_kernel(ctx_count, part, weight, pair, plain, small, *refs):
    total, landed, pair_total, plain_total, small_total = refs[:5]
    line_slots, weight_slots, pair_slots, plain_slots = (
        refs[5:9],
        refs[9:13],
        refs[13:17],
        refs[17:20],
    )
    pair_in, small_in, small_sums, small_across = refs[20:24]
    sems = refs[24:]
    line_sems, weight_sems, pair_sems, plain_sems = sems[:5], sems[5:9], sems[9:13], sems[13:17]
    keep_sem, half_send, half_recv = sems[17:20]
    weight_spread, small_spread, (group_send, group_recv) = sems[20:22], sems[22:24], sems[24:26]
    here, level, line, side = line_place()
    group = lax.axis_index("fsdp")
    greet_all(ctx_count)
    turns = scatter_turns(ctx_count // 2 - 1, part, total, *line_slots, *line_sems)
    settled, pair_settled = weight_slots[3], pair_slots[3]
    weight_steps = group_reduce(weight, *weight_slots, weight_sems)
    pair_steps = group_reduce(pair, *pair_slots, pair_sems)
    plain_steps = group_reduce(plain, *plain_slots, plain_total, plain_sems)
    small_start, small_wait = spread(
        lambda peer: small.at[:, peer], lambda source: small_in.at[source], small_spread, ctx_count
    )
    for copy in small_start:
        copy.start()
    next(weight_steps)
    next(turns)
    next(weight_steps)
    next(pair_steps)
    next(turns)
    next(pair_steps)
    next(plain_steps)
    for copy in small_wait:
        copy.wait_recv()
    small_sum = small[:, here]
    for k in range(1, ctx_count):
        small_sum = small_sum + small_in[(here + k) % ctx_count]
    small_sums[...] = small_sum
    group_copies = [
        remote(
            small_sums.at[(group + k) % 4],
            small_across.at[k],
            group_send.at[k],
            group_recv.at[k],
            fsdp=(group + k) % 4,
        )
        for k in range(1, 4)
    ]
    for copy in group_copies:
        copy.start()
    next(weight_steps)
    piece = settled.shape[0] // ctx_count
    weight_start, weight_wait = spread(
        lambda peer: settled.at[pl.ds(pl.multiple_of(peer * piece, piece), piece)],
        lambda source: landed.at[source],
        weight_spread,
        ctx_count,
    )
    for copy in weight_start:
        copy.start()
    keep = pltpu.make_async_copy(
        settled.at[pl.ds(pl.multiple_of(here * piece, piece), piece)],
        landed.at[here],
        keep_sem.at[0],
    )
    keep.start()
    next(plain_steps)
    next(turns)
    next(pair_steps)
    half = pair_total.shape[0]
    half_copy = remote(
        pair_settled.at[pl.ds(pl.multiple_of((1 - line) * half, half), half)],
        pair_in,
        half_send.at[0],
        half_recv.at[0],
        ctx=side,
    )
    half_copy.start()
    for copy in group_copies:
        copy.wait_recv()
    small_total[...] = small_sums[group] + small_across[1] + small_across[2] + small_across[3]
    for step in turns:
        pass
    next(plain_steps)
    half_copy.wait_recv()
    kept = pair_settled.at[pl.ds(pl.multiple_of(line * half, half), half)]
    add_rows(pair_total, (kept, pair_in), half)
    for copy in weight_wait:
        copy.wait_recv()
    for copy in weight_start + small_start + group_copies:
        copy.wait_send()
    half_copy.wait_send()
    next(weight_steps)
    next(pair_steps)
    next(plain_steps)
    keep.wait()


def closing(ctx_count, call_id, part, weight, pair, plain, small):
    rows, width = part.shape[1:]
    half = ctx_count // 2
    dma = pltpu.SemaphoreType.DMA
    slots = pltpu.VMEM((half, rows, width), part.dtype)

    def group_slots(array):
        one = pltpu.VMEM(array.shape[1:], array.dtype)
        two = pltpu.VMEM((2,) + array.shape[1:], array.dtype)
        return [two, two, one, one]

    block, columns = weight.shape[1:]
    pair_half = (pair.shape[1] // 2, pair.shape[2])
    return pl.pallas_call(
        functools.partial(closing_kernel, ctx_count),
        out_shape=[
            jax.ShapeDtypeStruct((rows, width), jnp.float32),
            jax.ShapeDtypeStruct((ctx_count, block // ctx_count, columns), weight.dtype),
            jax.ShapeDtypeStruct(pair_half, jnp.float32),
            jax.ShapeDtypeStruct(plain.shape[1:], jnp.float32),
            jax.ShapeDtypeStruct(small.shape[2:], small.dtype),
        ],
        in_specs=[VMEM] * 5,
        out_specs=[VMEM] * 5,
        scratch_shapes=[slots] * 4
        + group_slots(weight)
        + group_slots(pair)
        + group_slots(plain)[:3]
        + [
            pltpu.VMEM(pair_half, pair.dtype),
            pltpu.VMEM((ctx_count, 4) + small.shape[2:], small.dtype),
            pltpu.VMEM((4,) + small.shape[2:], small.dtype),
            pltpu.VMEM((4,) + small.shape[2:], small.dtype),
        ]
        + [dma((half,))] * 5
        + [dma((2,)), dma((2,)), dma((1,)), dma((1,))] * 3
        + [dma((1,))] * 3
        + [dma((ctx_count,))] * 4
        + [dma((4,))] * 2,
        compiler_params=pltpu.CompilerParams(
            collective_id=call_id, has_side_effects=True, vmem_limit_bytes=56 * 2**20
        ),
        name="closing",
    )(part, weight, pair, plain, small)


def scaled_rows(values):
    return values * lax.rsqrt(jnp.mean(values * values, axis=-1, keepdims=True) + EPSILON)


def attend_kernel(
    inputs,
    gain,
    weight,
    bias,
    cosine,
    sine,
    columns,
    lines,
    out_weight,
    normed,
    queries,
    keys,
    values,
    attended,
    log_totals,
    part,
):
    rows = inputs.shape[0]
    low = jnp.bfloat16
    heads = queries.shape[1] // HD

    @pl.loop(0, rows // SPAN)
    def project(index):
        here = span_of(index)
        unit = scaled_rows(inputs[here, :].astype(jnp.float32)) * gain[...]
        normed[here, :] = unit.astype(low)
        projected = flat_dot(normed[here, :], weight[...]) + bias[...]
        turn, tilt = cosine[here, :], sine[here, :]
        for head in range(heads):
            own = slice(head * HD, (head + 1) * HD)
            query = projected[:, own]
            query = query * turn + pltpu.roll(query, HD // 2, 1) * tilt
            queries[here, own] = (query * HD ** (-0.5)).astype(low)
            key = projected[:, (heads + head) * HD : (heads + head + 1) * HD]
            keys[here, own] = (key * turn + pltpu.roll(key, HD // 2, 1) * tilt).astype(low)
            values[here, own] = projected[
                :, (2 * heads + head) * HD : (2 * heads + head + 1) * HD
            ].astype(low)

    @pl.loop(0, rows // SPAN)
    def attend(index):
        here = span_of(index)
        position, segment = columns[here, 0:1], columns[here, 1:2]
        allowed = (lines[1:2, :] == segment) & (lines[0:1, :] <= position)
        allowed = allowed | (lines[0:1, :] == position)
        for head in range(heads):
            own = slice(head * HD, (head + 1) * HD)
            scores = turned_dot(queries[here, own], keys[:, own])
            scores = jnp.where(allowed, scores, -1e30)
            highest = jnp.max(scores, axis=1, keepdims=True)
            weights = jnp.exp(scores - highest)
            sums = jnp.sum(weights, axis=1, keepdims=True)
            log_totals[here, head : head + 1] = highest + jnp.log(sums)
            probs = (weights * (1.0 / sums)).astype(low)
            attended[here, own] = flat_dot(probs, values[:, own]).astype(low)
        part[here, :] = flat_dot(attended[here, :], out_weight[...]).astype(low)


def attend(inputs, gain, weight, bias, cosine, sine, columns, lines, out_weight):
    rows, width = inputs.shape
    wide = out_weight.shape[0]
    low = jnp.bfloat16
    shape = jax.ShapeDtypeStruct
    return pl.pallas_call(
        attend_kernel,
        out_shape=[shape((rows, width), low)]
        + [shape((rows, wide), low)] * 4
        + [shape((rows, wide // HD), jnp.float32), shape((rows, width), low)],
        in_specs=[VMEM] * 9,
        out_specs=[VMEM] * 7,
        compiler_params=pltpu.CompilerParams(vmem_limit_bytes=40 * 2**20),
        cost_estimate=pl.CostEstimate(
            flops=2 * rows * width * 4 * wide + 4 * rows * rows * wide,
            bytes_accessed=20 * 2**20,
            transcendentals=rows * rows * wide // HD,
        ),
        name="attend",
    )(inputs, gain, weight, bias, cosine, sine, columns, lines, out_weight)


def attend_back_kernel(
    branch,
    out_weight,
    queries,
    keys,
    values,
    attended,
    totals,
    cosine,
    sine,
    columns,
    lines,
    far_inputs,
    far_normed,
    far_weight,
    part,
    grad_weight,
    grad_out,
    grad_bias,
    grad_gain,
    grads,
    grad_attended,
    grad_keys,
    grad_values,
    gain_sum,
    inputs,
    normed,
    weight,
    load_sem,
):
    rows, width = branch.shape
    low = jnp.bfloat16
    full = jnp.float32
    wide = queries.shape[1]
    heads = wide // HD
    loads = [
        pltpu.make_async_copy(source, target, load_sem.at[i])
        for i, (source, target) in enumerate(
            ((far_weight, weight), (far_inputs, inputs), (far_normed, normed))
        )
    ]
    for copy in loads:
        copy.start()

    @pl.loop(0, rows // SPAN)
    def into_heads(index):
        here = span_of(index)
        grad_attended[here, :] = turned_dot(branch[here, :], out_weight[...]).astype(low)

    for head in range(heads):
        own = slice(head * HD, (head + 1) * HD)
        grad_keys[...] = jnp.zeros_like(grad_keys)
        grad_values[...] = jnp.zeros_like(grad_values)

        @pl.loop(0, rows // SPAN)
        def scores_back(index):
            here = span_of(index)
            position, segment = lines[0:1, here], lines[1:2, here]
            allowed = (columns[:, 1:2] == segment) & (columns[:, 0:1] <= position)
            allowed = allowed | (columns[:, 0:1] == position)
            query, grad = queries[here, own], grad_attended[here, own]
            scores = jnp.where(allowed, turned_dot(keys[:, own], query), -1e30)
            probs = jnp.exp(scores - totals[head : head + 1, here])
            grad_probs = turned_dot(values[:, own], grad)
            delta = jnp.sum(probs * grad_probs, axis=0, keepdims=True)
            grad_scores = (probs * (grad_probs - delta)).astype(low)
            grad_keys[...] += flat_dot(grad_scores, query)
            grad_values[...] += flat_dot(probs.astype(low), grad)
            grad_query = flat_dot(grad_scores.T, keys[:, own]) * HD ** (-0.5)
            grads[here, own] = (
                grad_query * cosine[here, :] + pltpu.roll(grad_query * sine[here, :], HD // 2, 1)
            ).astype(low)

        @pl.loop(0, rows // SPAN)
        def keys_back(index):
            here = span_of(index)
            grad_key = grad_keys[here, :]
            grads[here, (heads + head) * HD : (heads + head + 1) * HD] = (
                grad_key * cosine[here, :] + pltpu.roll(grad_key * sine[here, :], HD // 2, 1)
            ).astype(low)
            grads[here, (2 * heads + head) * HD : (2 * heads + head + 1) * HD] = grad_values[
                here, :
            ].astype(low)

    gain_sum[...] = jnp.zeros_like(gain_sum)
    grad_bias[...] = jnp.zeros_like(grad_bias)
    for copy in loads:
        copy.wait()

    @pl.loop(0, rows // SPAN)
    def project_back(index):
        here = span_of(index)
        grad_rows = turned_dot(grads[here, :], weight[...])
        part[here, :] = grad_rows.astype(low)
        unit = scaled_rows(inputs[here, :].astype(full))
        gain_sum[...] += jnp.sum(grad_rows * unit, axis=0, keepdims=True)
        grad_bias[...] += jnp.sum(grads[here, :].astype(full), axis=0, keepdims=True)

    grad_gain[...] = gain_sum[...]

    @pl.loop(0, width // SPAN)
    def weight_back(index):
        here = span_of(index)
        grad_weight[here, :] = flat_dot(normed[:, here].T, grads[...]).astype(low)

    attended_turned = attended[...].T

    @pl.loop(0, width // (2 * SPAN))
    def out_back(index):
        here = span_of(index, 2 * SPAN)
        grad_out[:, here] = flat_dot(attended_turned, branch[:, here]).astype(low)


def attend_back(
    branch,
    out_weight,
    queries,
    keys,
    values,
    attended,
    totals,
    cosine,
    sine,
    columns,
    lines,
    inputs,
    normed,
    weight,
):
    rows, width = branch.shape
    wide = out_weight.shape[0]
    low = jnp.bfloat16
    full = jnp.float32
    shape = jax.ShapeDtypeStruct
    return pl.pallas_call(
        attend_back_kernel,
        out_shape=[
            shape((rows, width), low),
            shape(weight.shape, low),
            shape((wide, width), low),
            shape((1, 3 * wide), full),
            shape((1, width), full),
        ],
        in_specs=[VMEM] * 11 + [ANY] * 3,
        out_specs=[VMEM] * 5,
        scratch_shapes=[
            pltpu.VMEM((rows, 3 * wide), low),
            pltpu.VMEM((rows, wide), low),
            pltpu.VMEM((rows, HD), full),
            pltpu.VMEM((rows, HD), full),
            pltpu.VMEM((1, width), full),
            pltpu.VMEM(inputs.shape, low),
            pltpu.VMEM(normed.shape, low),
            pltpu.VMEM(weight.shape, low),
            pltpu.SemaphoreType.DMA((3,)),
        ],
        compiler_params=pltpu.CompilerParams(vmem_limit_bytes=56 * 2**20),
        cost_estimate=pl.CostEstimate(
            flops=2 * rows * width * 8 * wide + 10 * rows * rows * wide,
            bytes_accessed=35 * 2**20,
            transcendentals=rows * rows * wide // HD,
        ),
        name="attend_back",
    )(
        branch,
        out_weight,
        queries,
        keys,
        values,
        attended,
        totals,
        cosine,
        sine,
        columns,
        lines,
        inputs,
        normed,
        weight,
    )


def gate_back_kernel(upstream, scale, gate_up, weight_out, grads, scaled):
    low = jnp.bfloat16
    half = gate_up.shape[1] // 2
    scaled[...] = (scale[...] * upstream[...].astype(jnp.float32)).astype(low)
    grad_unit = turned_dot(scaled[...], weight_out[...])
    gate, up = gate_up[:, :half], gate_up[:, half:]
    sigmoid = 1.0 / (1.0 + jnp.exp(-gate))
    grad_gate = grad_unit * up * (sigmoid * (1.0 + gate * (1.0 - sigmoid)))
    grad_up = grad_unit * (gate * sigmoid)
    grads[...] = jnp.concatenate([grad_gate.astype(low), grad_up.astype(low)], axis=1)


def gate_back(upstream, scale, gate_up, weight_out):
    rows, width = upstream.shape
    hidden = weight_out.shape[0]
    low = jnp.bfloat16

    def block(columns):
        return pl.BlockSpec((SPAN, columns), lambda i: (i, 0))

    return pl.pallas_call(
        gate_back_kernel,
        grid=(rows // SPAN,),
        out_shape=[
            jax.ShapeDtypeStruct((rows, 2 * hidden), low),
            jax.ShapeDtypeStruct((rows, width), low),
        ],
        in_specs=[
            block(width),
            block(1),
            block(2 * hidden),
            pl.BlockSpec((hidden, width), lambda i: (0, 0)),
        ],
        out_specs=[block(2 * hidden), block(width)],
        compiler_params=pltpu.CompilerParams(vmem_limit_bytes=48 * 2**20),
        cost_estimate=pl.CostEstimate(
            flops=2 * rows * width * hidden,
            bytes_accessed=rows * (12 * hidden + 4 * width) + 2 * hidden * width,
            transcendentals=rows * hidden,
        ),
        name="gate_back",
    )(upstream, scale, gate_up, weight_out)


def deal_kernel(pieces, weight, dealt):
    ctx_count = dealt.shape[0]
    width = dealt.shape[2] // pieces
    for c in range(ctx_count):
        dealt[c] = jnp.concatenate(
            [
                weight[:, (q * ctx_count + c) * width : (q * ctx_count + c + 1) * width]
                for q in range(pieces)
            ],
            axis=1,
        )


def deal_columns(weight, ctx_count, pieces):
    rows, columns = weight.shape
    return pl.pallas_call(
        functools.partial(deal_kernel, pieces),
        out_shape=jax.ShapeDtypeStruct((ctx_count, rows, columns // ctx_count), weight.dtype),
        name="deal_columns",
    )(weight)


def collect_kernel(pieces, dealt, whole):
    ctx_count = dealt.shape[0]
    width = dealt.shape[2] // pieces
    whole[...] = jnp.concatenate(
        [
            dealt[c, :, q * width : (q + 1) * width]
            for q in range(pieces)
            for c in range(ctx_count)
        ],
        axis=1,
    ).astype(whole.dtype)


def collect_columns(dealt, pieces):
    ctx_count, rows, columns = dealt.shape
    return pl.pallas_call(
        functools.partial(collect_kernel, pieces),
        out_shape=jax.ShapeDtypeStruct((rows, columns * ctx_count), jnp.float32),
        name="collect_columns",
    )(dealt)


def heads_kernel(order, dealt, whole):
    pairs = dealt.shape[0] * 2
    for place, head in enumerate(order):
        for which in range(3):
            column = (which * 2 + place % 2) * HD
            target = (which * pairs + head) * HD
            whole[:, target : target + HD] = dealt[
                place // 2, :, column : column + HD
            ].astype(whole.dtype)


def collect_heads(dealt, order):
    ctx_count, rows, columns = dealt.shape
    return pl.pallas_call(
        functools.partial(heads_kernel, order),
        out_shape=jax.ShapeDtypeStruct((rows, columns * ctx_count), jnp.float32),
        name="collect_heads",
    )(dealt)


def over(axis, array, dim=0):
    return lax.all_gather(array, axis, axis=dim, tiled=True)


def reduce_over(axis, array, dim=0):
    return lax.psum_scatter(array, axis, scatter_dimension=dim, tiled=True)


def exchange(array):
    return lax.all_to_all(array, "ctx", split_axis=0, concat_axis=0, tiled=True)


def transposed_dot(left, right):
    return lax.dot_general(
        left, right, (((0,), (0,)), ((), ())), preferred_element_type=jnp.float32
    )


def dot_transposed(left, right):
    return lax.dot_general(
        left, right, (((1,), (1,)), ((), ())), preferred_element_type=jnp.float32
    )


def split_plan(
    hidden_in,
    segments,
    block_pairs,
    routes,
    out_grad,
    norm_gain_attn,
    qkv_weight,
    qkv_bias,
    out_weight,
    norm_gain_ffn,
    router_weight,
    shared_gate_weight,
    shared_in_weight,
    shared_out_weight,
    expert_in_weight,
    expert_out_weight,
):
    low = jnp.bfloat16
    full = jnp.float32
    tokens_dev, width = hidden_in.shape[1:]
    block_len = tokens_dev // 2
    ctx_count = lax.axis_size("ctx")
    fsdp_count = lax.axis_size("fsdp")
    ctx_rank = lax.axis_index("ctx")
    dev_count = ctx_count * fsdp_count
    row_len = ctx_count * tokens_dev
    early = width // 2
    head_count = width // HD
    shard = qkv_weight.shape[0]
    expert_count = router_weight.shape[1]
    shared_shard = shared_out_weight.shape[0]
    shared_width = fsdp_count * shared_shard
    expert_width = expert_out_weight.shape[1] * fsdp_count
    pair_rank = ctx_rank // 2
    side = ctx_rank % 2
    pairs = ctx_count // 2
    head_order = [j + (p * 2 + t) * pairs for j in range(pairs) for p in range(2) for t in range(2)]

    small = jnp.concatenate(
        [
            norm_gain_attn,
            norm_gain_ffn,
            shared_gate_weight,
            router_weight.T.reshape(-1),
            qkv_bias,
        ]
    )
    small_count = small.shape[0]
    small = jnp.pad(small, (0, 16 * HD - small_count)).reshape(16, HD)
    own_numbers = jnp.concatenate(
        [routes.reshape(tokens_dev, -1).T, segments.reshape(1, tokens_dev)], axis=0
    )
    number_count = own_numbers.shape[0]
    own_numbers = jnp.pad(own_numbers, ((0, 8 - number_count), (0, 0)))
    qkv_parts = (
        qkv_weight.reshape(shard, 3, head_count, HD)[:, :, jnp.array(head_order)]
        .reshape(shard, 3, ctx_count, 2 * HD)
        .transpose(2, 0, 1, 3)
        .reshape(ctx_count, shard, 6 * HD)
    )
    own_inputs = hidden_in.reshape(tokens_dev, width)
    row_inputs, qkv_c, out_pair, small_all, numbers = opening(
        ctx_count, 1, own_inputs, qkv_parts, out_weight, small, own_numbers
    )
    qkv_c = qkv_c.reshape(width, 6 * HD)
    out_c = lax.dynamic_index_in_dim(
        out_pair.reshape(2, 2 * HD, width), side, 0, keepdims=False
    )
    small_all = small_all.reshape(dev_count, 16 * HD)
    gain_attn = small_all[:, :shard].reshape(width).astype(full)
    gain_ffn = small_all[:, shard : 2 * shard].reshape(width).astype(full)
    gate_full = small_all[:, 2 * shard : 3 * shard].reshape(width)
    router_t = (
        small_all[:, 3 * shard : (3 + expert_count) * shard]
        .reshape(dev_count, expert_count, shard)
        .transpose(1, 0, 2)
        .reshape(expert_count, width)
    )
    bias_full = small_all[:, (3 + expert_count) * shard : small_count].reshape(3, head_count, HD)
    router_gate = jnp.concatenate([router_t, gate_full[None, :]], axis=0)
    row_seg = numbers[:, number_count - 1].reshape(row_len)
    routed_here = jnp.any(numbers[:, : number_count - 1] == ctx_rank, axis=1).reshape(row_len)

    shared_in_weight, numbers = lax.optimization_barrier((shared_in_weight, numbers))
    expert_outer = over("fsdp", expert_out_weight[0])
    early_upstream = over("ctx", out_grad.reshape(tokens_dev, width)[:, :early])
    inner_parts = deal_columns(shared_in_weight, ctx_count, 2 * fsdp_count)
    expert_inner = over("fsdp", expert_in_weight[0])
    inner_parts = exchange(inner_parts)
    my_heads = [pair_rank + (side * 2 + t) * pairs for t in range(2)]
    bias_c = jnp.concatenate(
        [lax.dynamic_index_in_dim(bias_full, h, 1, keepdims=False) for h in my_heads], axis=1
    ).reshape(6 * HD)

    offsets = jnp.arange(block_len, dtype=jnp.int32)
    positions = (block_pairs[:, None] * block_len + offsets[None, :]).reshape(row_len)
    inputs = own_inputs.astype(full)
    row_inputs = row_inputs.reshape(row_len, width)
    half_len = HD // 2
    frequency = THETA ** (-jnp.arange(half_len, dtype=full) / half_len)
    places = positions.astype(full)
    angles = places[:, None] * frequency[None, :]
    cosine, sine = jnp.cos(angles), jnp.sin(angles)
    cosine = jnp.concatenate([cosine, cosine], axis=1)
    sine = jnp.concatenate([-sine, sine], axis=1)
    key_seg = row_seg.astype(full)
    query_seg = jnp.where(row_seg >= 0, key_seg, -2.0)
    query_marks = jnp.stack([places, query_seg])
    key_marks = jnp.stack([places, key_seg])
    row_normed, queries, keys, values, attended_row, log_totals, branch_part = attend(
        row_inputs,
        gain_attn[None, :],
        qkv_c,
        bias_c.astype(full)[None, :],
        cosine,
        sine,
        query_marks.T,
        key_marks,
        out_c,
    )
    branch_part, inner_parts, early_upstream, expert_outer = lax.optimization_barrier(
        (branch_part, inner_parts, early_upstream, expert_outer)
    )
    branch = line_scatter(ctx_count, 2, branch_part.reshape(ctx_count, tokens_dev, width))
    middle = inputs + branch
    normed_ffn = rms_scale(middle, gain_ffn).astype(low)

    row_ffn, inner_c, outer_c = line_gather(
        ctx_count,
        4,
        normed_ffn,
        inner_parts.reshape(ctx_count * shard, 2 * shared_width),
        shared_out_weight,
    )
    row_ffn = row_ffn.reshape(row_len, width)
    row_ffn, late_grad = lax.optimization_barrier((row_ffn, out_grad))
    late_upstream = over("ctx", late_grad.reshape(tokens_dev, width)[:, early:])
    inner_c = inner_c.reshape(width, 2 * shared_width)
    outer_c = outer_c.reshape(shared_width, width)
    row_logits = dot_transposed(row_ffn, router_gate)
    row_probs = jax.nn.softmax(row_logits[:, :expert_count], axis=-1)
    expert_ids = jnp.arange(expert_count, dtype=jnp.int32)
    here = jnp.where(
        routed_here, jnp.sum(jnp.where(expert_ids[None, :] == ctx_rank, row_probs, 0.0), axis=1), 0.0
    )
    row_gate = jax.nn.sigmoid(row_logits[:, expert_count])
    expert_gu = matmul_low(row_ffn, expert_inner)
    expert_hidden = swiglu_mix(expert_gu, expert_width).astype(low)
    expert_result = matmul_low(expert_hidden, expert_outer).astype(low).astype(full)
    row_shared, expert_result = lax.optimization_barrier((row_ffn, expert_result))
    shared_gu = matmul_low(row_shared, inner_c)
    shared_hidden = swiglu_mix(shared_gu, shared_width).astype(low)
    shared_out = matmul_low(shared_hidden, outer_c)
    shared_out, late_upstream = lax.optimization_barrier((shared_out, late_upstream))
    row_upstream = lax.optimization_barrier(
        jnp.concatenate([early_upstream, late_upstream], axis=1)
    )
    upstream_row = row_upstream.astype(full)
    out_part = (row_gate[:, None] * shared_out + here[:, None] * expert_result).astype(low)
    gate_dot = jnp.sum(upstream_row * shared_out, axis=1)
    expert_dot = jnp.where(routed_here, jnp.sum(upstream_row * expert_result, axis=1), 0.0)
    out_landed = reduce_over("ctx", out_part)

    row_upstream, out_part = lax.optimization_barrier((row_upstream, out_part))
    grad_expert_gu, grad_buffers = gate_back(row_upstream, here[:, None], expert_gu, expert_outer)
    sum_expert_outer = reduce_over("fsdp", transposed_dot(expert_hidden, grad_buffers).astype(low))
    grad_rows = dot_transposed(grad_expert_gu, expert_inner).astype(low)
    row_upstream, grad_rows = lax.optimization_barrier((row_upstream, grad_rows))
    grad_shared_gu, grad_shared_out = gate_back(
        row_upstream, row_gate[:, None], shared_gu, outer_c
    )
    grad_inner = transposed_dot(row_ffn, grad_shared_gu).astype(low)
    sum_inner_c = reduce_over("fsdp", grad_inner)
    grad_ffn_part = (
        dot_transposed(grad_shared_gu, inner_c) + grad_rows.astype(full)
    ).astype(low)
    dots = jnp.stack([gate_dot, expert_dot]).reshape(2, ctx_count, tokens_dev).transpose(1, 0, 2)
    grad_ffn_part, grad_inner = lax.optimization_barrier((grad_ffn_part, grad_inner))
    grad_normed, own_dots, grad_expert_inner = line_scatter(
        ctx_count,
        6,
        grad_ffn_part.reshape(ctx_count, tokens_dev, width),
        jnp.pad(dots, ((0, 0), (0, 6), (0, 0))),
        row_ffn,
        grad_expert_gu,
    )
    sum_expert_inner = reduce_over("fsdp", grad_expert_inner)
    hidden_out = (middle + out_landed.astype(full)).astype(low).reshape(1, tokens_dev, width)

    own_logits = dot_transposed(normed_ffn, router_gate)
    router_probs = jax.nn.softmax(own_logits[:, :expert_count], axis=-1)
    gate_value = jax.nn.sigmoid(own_logits[:, expert_count])
    grad_gate_logit = gate_value * (1.0 - gate_value) * jnp.sum(own_dots[:, 0], axis=0)
    grad_choice = own_dots[:, 1].T
    grad_logits = router_probs * (
        grad_choice - jnp.sum(router_probs * grad_choice, axis=1, keepdims=True)
    )
    grad_small = jnp.concatenate([grad_logits, grad_gate_logit[:, None]], axis=1).astype(low)
    grad_router_gate = transposed_dot(grad_small, normed_ffn)
    grad_normed = grad_normed + matmul_low(grad_small, router_gate)
    unused_norm, norm_pull = jax.vjp(rms_scale, middle, gain_ffn)
    grad_middle_norm, grad_gain_ffn = norm_pull(grad_normed)
    grad_middle = out_grad.reshape(tokens_dev, width).astype(full) + grad_middle_norm

    grad_branch, hidden_out = lax.optimization_barrier((grad_middle.astype(low), hidden_out))
    row_branch, grad_outer = product_gather(
        ctx_count, 3, grad_branch, shared_hidden, grad_shared_out
    )
    row_branch, sum_inner_c = lax.optimization_barrier(
        (row_branch.reshape(row_len, width), sum_inner_c)
    )
    sum_inner = collect_columns(
        exchange(sum_inner_c.reshape(ctx_count, shard, 2 * shared_width)), 2 * fsdp_count
    )
    grad_attn_part, grad_qkv_c, grad_out_c, grad_bias_c, grad_gain_attn = attend_back(
        row_branch,
        out_c,
        queries,
        keys,
        values,
        attended_row,
        log_totals.T,
        cosine,
        sine,
        key_marks.T,
        query_marks,
        row_inputs,
        row_normed,
        qkv_c,
    )
    grad_out_c = grad_out_c.reshape(2, HD, width)
    padded_out = jnp.concatenate(
        [jnp.where(side == p, grad_out_c, jnp.zeros_like(grad_out_c)) for p in range(2)], axis=0
    )
    grad_attn_part, sum_inner, sum_expert_outer = lax.optimization_barrier(
        (grad_attn_part, sum_inner, sum_expert_outer)
    )
    grad_bias_c = grad_bias_c.reshape(3, 1, 2, HD)
    mine = (jnp.arange(ctx_count) == ctx_rank)[None, :, None, None]
    places_of = [head_order.index(h) for h in range(head_count)]
    grad_bias = (
        jnp.where(mine, grad_bias_c, 0.0)
        .reshape(3, pairs, 2, 2, HD)
        .transpose(0, 2, 3, 1, 4)
        .reshape(dev_count, -1)
    )
    small_grads = jnp.concatenate(
        [
            grad_gain_attn.reshape(dev_count, shard),
            grad_gain_ffn.reshape(dev_count, shard),
            grad_router_gate.reshape(expert_count + 1, dev_count, shard)
            .transpose(1, 0, 2)
            .reshape(dev_count, (expert_count + 1) * shard),
            grad_bias,
        ],
        axis=1,
    )
    small_grads = jnp.pad(small_grads, ((0, 0), (0, 8 * HD - small_count)))
    grad_normed_attn, sum_qkv_c, sum_out, sum_outer, sums = closing(
        ctx_count,
        5,
        grad_attn_part.reshape(ctx_count, tokens_dev, width),
        grad_qkv_c.reshape(fsdp_count, ctx_count * shard, 6 * HD),
        padded_out,
        grad_outer.reshape(fsdp_count, shared_shard, width),
        small_grads.reshape(fsdp_count, ctx_count, 8, HD),
    )
    sums = sums.reshape(8 * HD)[:small_count]
    sum_qkv = collect_heads(sum_qkv_c, head_order)
    unused_norm, first_pull = jax.vjp(lambda v: rms_scale(v, gain_attn), inputs)
    input_grad = grad_middle + first_pull(grad_normed_attn)[0]
    sum_router = sums[2 * shard : (2 + expert_count) * shard].reshape(expert_count, shard).T
    return (
        hidden_out,
        input_grad.reshape(1, tokens_dev, width),
        sums[:shard],
        sum_qkv,
        sums[(3 + expert_count) * shard :],
        sum_out,
        sums[shard : 2 * shard],
        sum_router,
        sums[(2 + expert_count) * shard : (3 + expert_count) * shard],
        sum_inner,
        sum_outer,
        sum_expert_inner.astype(full)[None],
        sum_expert_outer.astype(full)[None],
    )


def local(*arrays):
    width = arrays[0].shape[2]
    ctx_count = lax.axis_size("ctx")
    shard = arrays[6].shape[0]
    fits = (
        width == 2 * ctx_count * HD
        and 2 * shard == HD
        and ctx_count % 2 == 0
        and lax.axis_size("fsdp") * ctx_count * shard == width
        and arrays[14].shape[0] == 1
    )
    return split_plan(*arrays) if fits else gathered_plan(*arrays)


def solution(mesh):
    in_specs = (
        P("fsdp", "ctx", None),
        P("fsdp", "ctx"),
        P(),
        P("fsdp", "ctx", None),
        P("fsdp", "ctx", None),
        P(("fsdp", "ctx")),
        P(("fsdp", "ctx"), None),
        P(("fsdp", "ctx")),
        P(("fsdp", "ctx"), None),
        P(("fsdp", "ctx")),
        P(("fsdp", "ctx"), None),
        P(("fsdp", "ctx")),
        P(("fsdp", "ctx"), None),
        P(("fsdp", "ctx"), None),
        P("ctx", "fsdp", None),
        P("ctx", "fsdp", None),
    )
    out_specs = (
        P("fsdp", "ctx", None),
        P("fsdp", "ctx", None),
        P(("fsdp", "ctx")),
        P(("fsdp", "ctx"), None),
        P(("fsdp", "ctx")),
        P(("fsdp", "ctx"), None),
        P(("fsdp", "ctx")),
        P(("fsdp", "ctx"), None),
        P(("fsdp", "ctx")),
        P(("fsdp", "ctx"), None),
        P(("fsdp", "ctx"), None),
        P("ctx", "fsdp", None),
        P("ctx", "fsdp", None),
    )
    return jax.shard_map(local, mesh=mesh, in_specs=in_specs, out_specs=out_specs, check_vma=False)
```

```python
import functools

import jax
import jax.numpy as jnp
from jax import lax
from jax.experimental import pallas as pl
from jax.experimental.pallas import tpu as pltpu
from jax.sharding import PartitionSpec as P

HD = 128


EPSILON = 1e-06
THETA = 1000000.0
heads_per_group = 4


def rms_scale(values, gain_vec):
    return (
        values * lax.rsqrt(jnp.mean(values * values, axis=-1, keepdims=True) + EPSILON) * gain_vec
    )


def rotate(values, positions):
    half_len = values.shape[-1] // 2
    frequency = THETA ** (-jnp.arange(half_len, dtype=jnp.float32) / half_len)
    angles = positions.astype(jnp.float32)[:, None] * frequency[None, :]
    cosine = jnp.cos(angles)[:, None, :]
    sine_part = jnp.sin(angles)[:, None, :]
    first_half = values[..., :half_len]
    second = values[..., half_len:]
    return jnp.concatenate(
        [first_half * cosine - second * sine_part, second * cosine + first_half * sine_part],
        axis=-1,
    )


def visible(query_pos, query_seg, key_pos, key_seg):
    same_doc = (key_seg[None, :] == query_seg[:, None]) & (query_seg[:, None] >= 0)
    causal = key_pos[None, :] <= query_pos[:, None]
    return same_doc & causal | (key_pos[None, :] == query_pos[:, None])


def swiglu_mix(gate_up, hidden_width):
    return jax.nn.silu(gate_up[..., :hidden_width]) * gate_up[..., hidden_width:]


def matmul_low(left, right):
    return jnp.dot(left, right, preferred_element_type=jnp.float32)


def gathered_plan(
    hidden_in,
    segments,
    block_pairs,
    routes,
    out_grad,
    norm_gain_attn,
    qkv_weight,
    qkv_bias,
    out_weight,
    norm_gain_ffn,
    router_weight,
    shared_gate_weight,
    shared_in_weight,
    shared_out_weight,
    expert_in_weight,
    expert_out_weight,
):
    tokens_dev = hidden_in.shape[1]
    model_width = hidden_in.shape[2]
    block_len = tokens_dev // 2
    inputs = hidden_in.reshape(tokens_dev, model_width).astype(jnp.float32)
    seg_local = segments.reshape(tokens_dev)
    token_routes = routes.reshape(tokens_dev, -1)
    top_count = token_routes.shape[1]
    ctx_count = lax.axis_size("ctx")
    ctx_rank = lax.axis_index("ctx")
    offsets = jnp.arange(block_len, dtype=jnp.int32)
    all_positions = (
        block_pairs.reshape(ctx_count, 2)[:, :, None] * block_len + offsets[None, None, :]
    ).reshape(ctx_count * tokens_dev)
    my_positions = lax.dynamic_slice_in_dim(all_positions, ctx_rank * tokens_dev, tokens_dev, 0)
    gathered = (
        lax.all_gather(norm_gain_attn, ("fsdp", "ctx"), axis=0, tiled=True),
        lax.all_gather(qkv_weight, ("fsdp", "ctx"), axis=0, tiled=True),
        lax.all_gather(qkv_bias, ("fsdp", "ctx"), axis=0, tiled=True),
        lax.all_gather(out_weight, ("fsdp", "ctx"), axis=0, tiled=True),
        lax.all_gather(norm_gain_ffn, ("fsdp", "ctx"), axis=0, tiled=True),
        lax.all_gather(router_weight, ("fsdp", "ctx"), axis=0, tiled=True),
        lax.all_gather(shared_gate_weight, ("fsdp", "ctx"), axis=0, tiled=True),
        lax.all_gather(shared_in_weight, ("fsdp", "ctx"), axis=0, tiled=True),
        lax.all_gather(shared_out_weight, ("fsdp", "ctx"), axis=0, tiled=True),
    )
    (
        gain_attn,
        qkv_full,
        shift_full,
        out_full,
        gain_ffn,
        router_full,
        gate_full,
        inner_full,
        outer_full,
    ) = gathered
    gain_attn = gain_attn.astype(jnp.float32)
    gain_ffn = gain_ffn.astype(jnp.float32)
    heads_width = out_full.shape[0]
    head_count = heads_width // HD
    group_width = heads_per_group * HD
    group_count = head_count // heads_per_group
    normed = rms_scale(inputs, gain_attn).astype(jnp.bfloat16)
    projected = matmul_low(normed, qkv_full) + shift_full.astype(jnp.float32)
    query_pre = projected[:, :heads_width].reshape(tokens_dev, head_count, HD)
    key_pre = projected[:, heads_width : 2 * heads_width].reshape(tokens_dev, head_count, HD)

    def place_heads(query_in, key_in):
        return (rotate(query_in, my_positions) * HD ** (-0.5), rotate(key_in, my_positions))

    query_rot, key_rot = place_heads(query_pre, key_pre)
    query_low = query_rot.reshape(tokens_dev, heads_width).astype(jnp.bfloat16)
    key_low = key_rot.reshape(tokens_dev, heads_width).astype(jnp.bfloat16)
    value_low = projected[:, 2 * heads_width :].astype(jnp.bfloat16)
    keys_all, values_all, segs_all = (
        lax.all_gather(key_low, "ctx", axis=0, tiled=True),
        lax.all_gather(value_low, "ctx", axis=0, tiled=True),
        lax.all_gather(seg_local.astype(jnp.bfloat16), "ctx", axis=0, tiled=True),
    )
    allowed = visible(
        my_positions, seg_local.astype(jnp.float32), all_positions, segs_all.astype(jnp.float32)
    )

    def head_slice(matrix, group_index):
        return lax.dynamic_slice_in_dim(matrix, group_index * group_width, group_width, 1).reshape(
            matrix.shape[0], heads_per_group, HD
        )

    def forward_group(group_index):
        query_part = head_slice(query_low, group_index)
        key_part = head_slice(keys_all, group_index)
        value_part = head_slice(values_all, group_index)
        scores = jnp.einsum(
            "qhd,khd->hqk", query_part, key_part, preferred_element_type=jnp.float32
        )
        scores = jnp.where(allowed[None], scores, -1e30)
        highest = jnp.max(scores, axis=-1, keepdims=True)
        log_total = highest + jnp.log(jnp.sum(jnp.exp(scores - highest), axis=-1, keepdims=True))
        weights = jnp.exp(scores - log_total).astype(jnp.bfloat16)
        mixed = jnp.einsum("hqk,khd->qhd", weights, value_part, preferred_element_type=jnp.float32)
        return (mixed, log_total[..., 0])

    mixed_groups, log_totals = lax.map(forward_group, jnp.arange(group_count, dtype=jnp.int32))
    attended = (
        jnp.moveaxis(mixed_groups, 0, 1).reshape(tokens_dev, heads_width).astype(jnp.bfloat16)
    )
    middle = inputs + matmul_low(attended, out_full)
    normed_ffn = rms_scale(middle, gain_ffn).astype(jnp.bfloat16)
    logits = matmul_low(normed_ffn, router_full)
    router_probs = jax.nn.softmax(logits, axis=-1)
    expert_count = logits.shape[1]
    expert_ids = jnp.arange(expert_count, dtype=jnp.int32)
    chosen = (token_routes[:, :, None] == expert_ids[None, None, :]).astype(jnp.float32)
    gate_weights = jnp.sum(chosen * router_probs[:, None, :], axis=-1)
    capacity = 2 * tokens_dev * top_count // expert_count
    local_experts = expert_in_weight.shape[0]
    assigned = tokens_dev * top_count
    flat_routes = token_routes.reshape(assigned)
    onehot = (flat_routes[:, None] == expert_ids[None, :]).astype(jnp.int32)
    earlier = jnp.cumsum(onehot, axis=0) - onehot
    places = flat_routes * capacity + jnp.sum(earlier * onehot, axis=1)
    slot_source = (
        jnp.full((expert_count * capacity,), assigned, jnp.int32)
        .at[places]
        .set(jnp.arange(assigned, dtype=jnp.int32))
    )
    slot_token = slot_source // top_count
    padded_rows = jnp.concatenate([normed_ffn, jnp.zeros((1, model_width), jnp.bfloat16)], axis=0)
    outgoing = padded_rows[slot_token].reshape(ctx_count, local_experts * capacity, model_width)
    expert_inner, expert_outer = (
        lax.all_gather(expert_in_weight, "fsdp", axis=1, tiled=True),
        lax.all_gather(expert_out_weight, "fsdp", axis=1, tiled=True),
    )
    landed_tokens = lax.all_to_all(outgoing, "ctx", split_axis=0, concat_axis=0, tiled=True)
    incoming = landed_tokens.reshape(ctx_count, local_experts, capacity, model_width)
    expert_gu = jnp.einsum(
        "necd,edf->necf", incoming, expert_inner, preferred_element_type=jnp.float32
    )
    expert_width = expert_outer.shape[1]
    expert_hidden = swiglu_mix(expert_gu, expert_width).astype(jnp.bfloat16)
    expert_result = jnp.einsum(
        "necf,efd->necd", expert_hidden, expert_outer, preferred_element_type=jnp.float32
    ).astype(jnp.bfloat16)
    returned = lax.all_to_all(
        expert_result.reshape(ctx_count, local_experts * capacity, model_width),
        "ctx",
        split_axis=0,
        concat_axis=0,
        tiled=True,
    )
    picked = (
        returned.reshape(expert_count * capacity, model_width)[places]
        .reshape(tokens_dev, top_count, model_width)
        .astype(jnp.float32)
    )
    routed = jnp.sum(gate_weights[:, :, None] * picked, axis=1)
    upstream = out_grad.reshape(tokens_dev, model_width).astype(jnp.float32)
    shared_gu = matmul_low(normed_ffn, inner_full)
    shared_width = outer_full.shape[0]
    shared_hidden = swiglu_mix(shared_gu, shared_width).astype(jnp.bfloat16)
    shared_out = matmul_low(shared_hidden, outer_full)
    gate_value = jax.nn.sigmoid(matmul_low(normed_ffn, gate_full))
    output = middle + gate_value[:, None] * shared_out + routed
    hidden_out = output.astype(jnp.bfloat16).reshape(1, tokens_dev, model_width)
    gain_ffn, router_full, gate_full, inner_full, outer_full = (
        lax.all_gather(norm_gain_ffn, ("fsdp", "ctx"), axis=0, tiled=True),
        lax.all_gather(router_weight, ("fsdp", "ctx"), axis=0, tiled=True),
        lax.all_gather(shared_gate_weight, ("fsdp", "ctx"), axis=0, tiled=True),
        lax.all_gather(shared_in_weight, ("fsdp", "ctx"), axis=0, tiled=True),
        lax.all_gather(shared_out_weight, ("fsdp", "ctx"), axis=0, tiled=True),
    )
    gain_ffn = gain_ffn.astype(jnp.float32)
    grad_shared_out = (gate_value[:, None] * upstream).astype(jnp.bfloat16)
    grad_outer = jnp.einsum(
        "tf,td->fd", shared_hidden, grad_shared_out, preferred_element_type=jnp.float32
    )
    grad_hidden = jnp.einsum(
        "td,fd->tf", grad_shared_out, outer_full, preferred_element_type=jnp.float32
    )
    unused_mix, mix_pull = jax.vjp(functools.partial(swiglu_mix, hidden_width=shared_width), shared_gu)
    grad_shared_gu = mix_pull(grad_hidden)[0].astype(jnp.bfloat16)
    grad_inner = jnp.einsum(
        "td,tf->df", normed_ffn, grad_shared_gu, preferred_element_type=jnp.float32
    )
    grad_normed = jnp.einsum(
        "tf,df->td", grad_shared_gu, inner_full, preferred_element_type=jnp.float32
    )
    grad_gate_logit = (
        gate_value * (1.0 - gate_value) * jnp.sum(upstream * shared_out, axis=1)
    ).astype(jnp.bfloat16)
    grad_gate_vec = jnp.einsum(
        "td,t->d", normed_ffn, grad_gate_logit, preferred_element_type=jnp.float32
    )
    grad_normed = (
        grad_normed
        + grad_gate_logit.astype(jnp.float32)[:, None] * gate_full.astype(jnp.float32)[None, :]
    )
    grad_gates = jnp.sum(upstream[:, None, :] * picked, axis=2)
    grad_choice_probs = jnp.sum(chosen * grad_gates[:, :, None], axis=1)
    grad_logits = (
        router_probs
        * (grad_choice_probs - jnp.sum(router_probs * grad_choice_probs, axis=1, keepdims=True))
    ).astype(jnp.bfloat16)
    grad_router = jnp.einsum(
        "td,te->de", normed_ffn, grad_logits, preferred_element_type=jnp.float32
    )
    grad_normed = grad_normed + jnp.einsum(
        "te,de->td", grad_logits, router_full, preferred_element_type=jnp.float32
    )
    grad_slots = (
        (gate_weights[:, :, None] * upstream[:, None, :])
        .astype(jnp.bfloat16)
        .reshape(assigned, model_width)
    )
    padded_grads = jnp.concatenate([grad_slots, jnp.zeros((1, model_width), jnp.bfloat16)], axis=0)
    grad_outgoing = padded_grads[slot_source].reshape(
        ctx_count, local_experts * capacity, model_width
    )
    grad_incoming = lax.all_to_all(
        grad_outgoing, "ctx", split_axis=0, concat_axis=0, tiled=True
    ).reshape(ctx_count, local_experts, capacity, model_width)
    grad_expert_hidden = jnp.einsum(
        "necd,efd->necf", grad_incoming, expert_outer, preferred_element_type=jnp.float32
    )
    grad_expert_outer = jnp.einsum(
        "necf,necd->efd", expert_hidden, grad_incoming, preferred_element_type=jnp.float32
    )
    unused_mix, expert_pull = jax.vjp(functools.partial(swiglu_mix, hidden_width=expert_width), expert_gu)
    grad_expert_gu = expert_pull(grad_expert_hidden)[0].astype(jnp.bfloat16)
    grad_expert_inner = jnp.einsum(
        "necd,necf->edf", incoming, grad_expert_gu, preferred_element_type=jnp.float32
    )
    grad_expert_rows = jnp.einsum(
        "necf,edf->necd", grad_expert_gu, expert_inner, preferred_element_type=jnp.float32
    ).astype(jnp.bfloat16)
    grad_returned = lax.all_to_all(
        grad_expert_rows.reshape(ctx_count, local_experts * capacity, model_width),
        "ctx",
        split_axis=0,
        concat_axis=0,
        tiled=True,
    )
    grad_picked = grad_returned.reshape(expert_count * capacity, model_width)[places].reshape(
        tokens_dev, top_count, model_width
    )
    grad_normed = grad_normed + jnp.sum(grad_picked.astype(jnp.float32), axis=1)
    sum_expert_inner, sum_expert_outer = (
        lax.psum_scatter(
            grad_expert_inner.astype(jnp.bfloat16), "fsdp", scatter_dimension=1, tiled=True
        ).astype(jnp.float32),
        lax.psum_scatter(
            grad_expert_outer.astype(jnp.bfloat16), "fsdp", scatter_dimension=1, tiled=True
        ).astype(jnp.float32),
    )
    unused_norm, norm_pull = jax.vjp(rms_scale, middle, gain_ffn)
    grad_middle_norm, grad_gain_ffn = norm_pull(grad_normed)
    grad_middle = upstream + grad_middle_norm
    sum_gain_ffn, sum_router, sum_gate_vec, sum_inner, sum_outer = (
        lax.psum_scatter(grad_gain_ffn, ("fsdp", "ctx"), scatter_dimension=0, tiled=True),
        lax.psum_scatter(grad_router, ("fsdp", "ctx"), scatter_dimension=0, tiled=True),
        lax.psum_scatter(grad_gate_vec, ("fsdp", "ctx"), scatter_dimension=0, tiled=True),
        lax.psum_scatter(grad_inner, ("fsdp", "ctx"), scatter_dimension=0, tiled=True),
        lax.psum_scatter(grad_outer, ("fsdp", "ctx"), scatter_dimension=0, tiled=True),
    )
    grad_branch = grad_middle.astype(jnp.bfloat16)
    grad_out_mat = jnp.einsum(
        "tc,td->cd", attended, grad_branch, preferred_element_type=jnp.float32
    )
    grad_attended = jnp.einsum(
        "td,cd->tc", grad_branch, out_full, preferred_element_type=jnp.float32
    ).astype(jnp.bfloat16)
    keys_again, values_again = (
        lax.all_gather(key_low, "ctx", axis=0, tiled=True),
        lax.all_gather(value_low, "ctx", axis=0, tiled=True),
    )

    def backward_group(group_index):
        query_part = head_slice(query_low, group_index)
        key_part = head_slice(keys_again, group_index)
        value_part = head_slice(values_again, group_index)
        grad_part = head_slice(grad_attended, group_index)
        log_total = lax.dynamic_index_in_dim(log_totals, group_index, 0, keepdims=False)
        scores = jnp.einsum(
            "qhd,khd->hqk", query_part, key_part, preferred_element_type=jnp.float32
        )
        scores = jnp.where(allowed[None], scores, -1e30)
        weights = jnp.exp(scores - log_total[..., None])
        grad_weights = jnp.einsum(
            "qhd,khd->hqk", grad_part, value_part, preferred_element_type=jnp.float32
        )
        offset_term = jnp.sum(weights * grad_weights, axis=-1, keepdims=True)
        grad_scores = (weights * (grad_weights - offset_term)).astype(jnp.bfloat16)
        grad_query = jnp.einsum(
            "hqk,khd->qhd", grad_scores, key_part, preferred_element_type=jnp.float32
        )
        grad_key = jnp.einsum(
            "hqk,qhd->khd", grad_scores, query_part, preferred_element_type=jnp.float32
        )
        grad_value = jnp.einsum(
            "hqk,qhd->khd",
            weights.astype(jnp.bfloat16),
            grad_part,
            preferred_element_type=jnp.float32,
        )
        return (grad_query, grad_key, grad_value)

    grad_queries, grad_keys, grad_values = lax.map(
        backward_group, jnp.arange(group_count, dtype=jnp.int32)
    )
    row_total = keys_again.shape[0]
    grad_key_rows = jnp.moveaxis(grad_keys, 0, 1).reshape(row_total, heads_width)
    grad_value_rows = jnp.moveaxis(grad_values, 0, 1).reshape(row_total, heads_width)
    key_share, value_share = (
        lax.psum_scatter(
            grad_key_rows.astype(jnp.bfloat16), "ctx", scatter_dimension=0, tiled=True
        ).astype(jnp.float32),
        lax.psum_scatter(
            grad_value_rows.astype(jnp.bfloat16), "ctx", scatter_dimension=0, tiled=True
        ).astype(jnp.float32),
    )
    grad_query_heads = jnp.moveaxis(grad_queries, 0, 1).reshape(tokens_dev, head_count, HD)
    unused_rot, rotate_pull = jax.vjp(place_heads, query_pre, key_pre)
    grad_query_pre, grad_key_pre = rotate_pull(
        (grad_query_heads, key_share.reshape(tokens_dev, head_count, HD))
    )
    grad_projected = jnp.concatenate(
        [
            grad_query_pre.reshape(tokens_dev, heads_width),
            grad_key_pre.reshape(tokens_dev, heads_width),
            value_share,
        ],
        axis=1,
    ).astype(jnp.bfloat16)
    grad_qkv = jnp.einsum("td,tc->dc", normed, grad_projected, preferred_element_type=jnp.float32)
    grad_shift = jnp.sum(grad_projected.astype(jnp.float32), axis=0)
    grad_normed_attn = jnp.einsum(
        "tc,dc->td", grad_projected, qkv_full, preferred_element_type=jnp.float32
    )
    unused_norm, first_pull = jax.vjp(rms_scale, inputs, gain_attn)
    grad_inputs_norm, grad_gain_attn = first_pull(grad_normed_attn)
    input_grad = grad_middle + grad_inputs_norm
    sum_gain_attn, sum_qkv, sum_shift, sum_out = (
        lax.psum_scatter(grad_gain_attn, ("fsdp", "ctx"), scatter_dimension=0, tiled=True),
        lax.psum_scatter(grad_qkv, ("fsdp", "ctx"), scatter_dimension=0, tiled=True),
        lax.psum_scatter(grad_shift, ("fsdp", "ctx"), scatter_dimension=0, tiled=True),
        lax.psum_scatter(grad_out_mat, ("fsdp", "ctx"), scatter_dimension=0, tiled=True),
    )
    return (
        hidden_out,
        input_grad.reshape(1, tokens_dev, model_width),
        sum_gain_attn,
        sum_qkv,
        sum_shift,
        sum_out,
        sum_gain_ffn,
        sum_router,
        sum_gate_vec,
        sum_inner,
        sum_outer,
        sum_expert_inner,
        sum_expert_outer,
    )


SPAN = 256


def flat_dot(left, right):
    return lax.dot_general(left, right, (((1,), (0,)), ((), ())), preferred_element_type=jnp.float32)


def turned_dot(left, right):
    return lax.dot_general(left, right, (((1,), (1,)), ((), ())), preferred_element_type=jnp.float32)


def span_of(index, size=SPAN):
    return pl.ds(pl.multiple_of(index * size, size), size)


MESH = pl.DeviceIdType.MESH
ANY = pl.BlockSpec(memory_space=pl.ANY)
VMEM = pl.BlockSpec(memory_space=pltpu.VMEM)


def remote(source, target, send_sem, recv_sem, **place):
    return pltpu.make_async_remote_copy(
        src_ref=source,
        dst_ref=target,
        send_sem=send_sem,
        recv_sem=recv_sem,
        device_id=place,
        device_id_type=MESH,
    )


def line_place():
    here = lax.axis_index("ctx")
    line = here % 2
    return here, here // 2, line, here + 1 - 2 * line


def greet_line(last, here, level, side, others=0):
    barrier = pltpu.get_barrier_semaphore()
    pl.semaphore_signal(barrier, inc=1, device_id={"ctx": side}, device_id_type=MESH)

    @pl.when(level < last)
    def up():
        pl.semaphore_signal(barrier, inc=1, device_id={"ctx": here + 2}, device_id_type=MESH)

    @pl.when(level > 0)
    def down():
        pl.semaphore_signal(barrier, inc=1, device_id={"ctx": here - 2}, device_id_type=MESH)

    ends = jnp.where(level < last, 1, 0) + jnp.where(level > 0, 1, 0)
    pl.semaphore_wait(barrier, 1 + others + ends)


def line_copy(rows_ref, block, way, target, sems, source=None):
    send_sem, recv_sem = sems
    return remote(
        rows_ref.at[block] if source is None else source,
        rows_ref.at[block],
        send_sem.at[block, way],
        recv_sem.at[block],
        ctx=target,
    )


def line_start(rows_ref, own_ref, sems, place, last):
    here, level, line, side = place

    @pl.when(level < last)
    def up():
        line_copy(rows_ref, here, 0, here + 2, sems, own_ref).start()

    @pl.when(level > 0)
    def down():
        line_copy(rows_ref, here, 1, here - 2, sems, own_ref).start()

    line_copy(rows_ref, here, 2, side, sems, own_ref).start()


def line_step(rows_ref, sems, place, last, step):
    here, level, line, side = place

    @pl.when(level >= step)
    def from_below():
        block = here - 2 * step
        line_copy(rows_ref, block, 0, side, sems).wait_recv()

        @pl.when(level < last)
        def on():
            line_copy(rows_ref, block, 0, here + 2, sems).start()

        line_copy(rows_ref, block, 2, side, sems).start()

    @pl.when(level + step <= last)
    def from_above():
        block = here + 2 * step
        line_copy(rows_ref, block, 1, side, sems).wait_recv()

        @pl.when(level > 0)
        def on():
            line_copy(rows_ref, block, 1, here - 2, sems).start()

        line_copy(rows_ref, block, 2, side, sems).start()


def line_finish(rows_ref, sems, place, last):
    here, level, line, side = place
    for other in range(last + 1):
        block = 2 * other + line
        line_copy(rows_ref, 2 * other + 1 - line, 2, side, sems).wait_recv()
        line_copy(rows_ref, block, 2, side, sems).wait_send()

        @pl.when((other <= level) & (level < last))
        def up():
            line_copy(rows_ref, block, 0, side, sems).wait_send()

        @pl.when((other >= level) & (level > 0))
        def down():
            line_copy(rows_ref, block, 1, side, sems).wait_send()


ROWS_STEP = 16


def add_rows(target, pieces, row_count):
    def one(index, carry):
        rows = pl.ds(pl.multiple_of(index * ROWS_STEP, ROWS_STEP), ROWS_STEP)
        total = pieces[0][rows, :].astype(jnp.float32)
        for piece in pieces[1:]:
            total = total + piece[rows, :].astype(jnp.float32)
        target[rows, :] = total.astype(target.dtype)
        return carry

    lax.fori_loop(0, row_count // ROWS_STEP, one, 0)


def scatter_turns(last, part, total, crossed, rising, falling, sums, *sems):
    cross_send, cross_recv, move_send, rise_recv, fall_recv = sems
    here, level, line, side = line_place()
    row_count = total.shape[0]

    def turn(k):
        middle = (level > 0) & (level < last)
        swapped = k + jnp.where(middle, (0, 0, 1, -1)[k], 0)
        return jnp.where(level * 2 < last, last - swapped, swapped)

    def cross(goal):
        return remote(
            part.at[2 * goal + 1 - line],
            crossed.at[goal],
            cross_send.at[goal],
            cross_recv.at[goal],
            ctx=side,
        )

    def rise(goal, target=side):
        return remote(
            sums.at[goal], rising.at[goal], move_send.at[goal], rise_recv.at[goal], ctx=target
        )

    def fall(goal, target=side):
        return remote(
            sums.at[goal], falling.at[goal], move_send.at[goal], fall_recv.at[goal], ctx=target
        )

    for k in range(min(2, last + 1)):
        cross(turn(k)).start()
    for k in range(last + 1):
        yield k
        goal = turn(k)
        mine = part.at[2 * goal + line]
        cross(goal).wait_recv()
        if k + 2 <= last:
            cross(turn(k + 2)).start()

        @pl.when(goal > level)
        def upward():
            @pl.when(level > 0)
            def joined():
                rise(goal).wait_recv()
                add_rows(sums.at[goal], (mine, crossed.at[goal], rising.at[goal]), row_count)

            @pl.when(level == 0)
            def first():
                add_rows(sums.at[goal], (mine, crossed.at[goal]), row_count)

            rise(goal, here + 2).start()

        @pl.when(goal < level)
        def downward():
            @pl.when(level < last)
            def joined():
                fall(goal).wait_recv()
                add_rows(sums.at[goal], (mine, crossed.at[goal], falling.at[goal]), row_count)

            @pl.when(level == last)
            def first():
                add_rows(sums.at[goal], (mine, crossed.at[goal]), row_count)

            fall(goal, here - 2).start()

        @pl.when(goal == level)
        def here_at_last():
            @pl.when(level > 0)
            def from_below():
                rise(goal).wait_recv()

            @pl.when(level < last)
            def from_above():
                fall(goal).wait_recv()

            @pl.when(level == 0)
            def bottom():
                add_rows(total, (mine, crossed.at[goal], falling.at[goal]), row_count)

            @pl.when(level == last)
            def top():
                add_rows(total, (mine, crossed.at[goal], rising.at[goal]), row_count)

            @pl.when((level > 0) & (level < last))
            def between():
                add_rows(
                    total,
                    (mine, crossed.at[goal], rising.at[goal], falling.at[goal]),
                    row_count,
                )

    for goal in range(last + 1):
        cross(goal).wait_send()

        @pl.when(goal != level)
        def sent():
            rise(goal).wait_send()


def scatter_kernel(
    ctx_count, part, small, far_tokens, far_grads, total, small_in, weight_grad, *refs
):
    *refs, product, store_sem, tokens, grads, load_sem = refs
    loads = [
        pltpu.make_async_copy(source, target, load_sem.at[i])
        for i, (source, target) in enumerate(((far_tokens, tokens), (far_grads, grads)))
    ]
    for copy in loads:
        copy.start()
    greet_all(ctx_count)
    here = lax.axis_index("ctx")
    starts, waits = spread(
        lambda peer: small.at[peer], lambda source: small_in.at[source], refs[9:11], ctx_count
    )
    for copy in starts:
        copy.start()
    small_in[here] = small[here]
    turns = scatter_turns(ctx_count // 2 - 1, part, total, *refs[:9])
    next(turns)
    pieces = ctx_count // 2
    depth = tokens.shape[1] // pieces
    stores = []
    for copy in loads:
        copy.wait()
    for piece in range(pieces):

        @pl.loop(0, depth // SPAN)
        def multiply(index):
            here = pl.ds(pl.multiple_of(piece * depth + index * SPAN, SPAN), SPAN)
            product[here, :] = flat_dot(tokens[:, here].T, grads[...]).astype(product.dtype)

        rows = pl.ds(piece * depth, depth)
        stores.append(
            pltpu.make_async_copy(product.at[rows], weight_grad.at[rows], store_sem.at[piece])
        )
        stores[-1].start()
        next(turns, None)
    for copy in waits:
        copy.wait_recv()
    for copy in starts:
        copy.wait_send()
    for copy in stores:
        copy.wait()


def line_scatter_kernel(last, part, total, *refs):
    here, level, line, side = line_place()
    greet_line(last, here, level, side)
    for step in scatter_turns(last, part, total, *refs):
        pass


def line_scatter(ctx_count, call_id, part, small=None, tokens=None, grads=None):
    rows, width = part.shape[1:]
    half = ctx_count // 2
    dma = pltpu.SemaphoreType.DMA((half,))
    spread_dma = pltpu.SemaphoreType.DMA((ctx_count,))
    slots = pltpu.VMEM((half, rows, width), part.dtype)
    total = jax.ShapeDtypeStruct((rows, width), jnp.float32)
    params = pltpu.CompilerParams(
        collective_id=call_id, has_side_effects=True, vmem_limit_bytes=40 * 2**20
    )
    if small is None:
        return pl.pallas_call(
            functools.partial(line_scatter_kernel, half - 1),
            out_shape=total,
            in_specs=[VMEM],
            out_specs=VMEM,
            scratch_shapes=[slots] * 4 + [dma] * 5,
            compiler_params=params,
            name="line_scatter",
        )(part)
    product = (tokens.shape[1], grads.shape[1])
    params = pltpu.CompilerParams(
        collective_id=call_id, has_side_effects=True, vmem_limit_bytes=56 * 2**20
    )
    return pl.pallas_call(
        functools.partial(scatter_kernel, ctx_count),
        out_shape=[
            total,
            jax.ShapeDtypeStruct(small.shape, small.dtype),
            jax.ShapeDtypeStruct(product, part.dtype),
        ],
        in_specs=[VMEM] * 2 + [ANY] * 2,
        out_specs=[VMEM] * 2 + [ANY],
        scratch_shapes=[slots] * 4
        + [dma] * 5
        + [spread_dma] * 2
        + [pltpu.VMEM(product, part.dtype), pltpu.SemaphoreType.DMA((half,))]
        + [
            pltpu.VMEM(tokens.shape, tokens.dtype),
            pltpu.VMEM(grads.shape, grads.dtype),
            pltpu.SemaphoreType.DMA((2,)),
        ],
        compiler_params=params,
        name="line_scatter",
    )(part, small, tokens, grads)


def fsdp_place():
    here = lax.axis_index("fsdp")
    beside = here + 1 - 2 * (here % 2)
    return here, beside, (here + 2) % 4, (beside + 2) % 4


def greet_all(ctx_count):
    barrier = pltpu.get_barrier_semaphore()
    here = lax.axis_index("ctx")
    group = lax.axis_index("fsdp")
    for k in range(1, ctx_count):
        pl.semaphore_signal(
            barrier, inc=1, device_id={"ctx": (here + k) % ctx_count}, device_id_type=MESH
        )
    for k in range(1, 4):
        pl.semaphore_signal(barrier, inc=1, device_id={"fsdp": (group + k) % 4}, device_id_type=MESH)
    pl.semaphore_wait(barrier, ctx_count + 2)


def share_start(blocks, sems, own=None):
    send_sem, recv_sem = sems
    here, beside, across, corner = fsdp_place()
    source = blocks.at[here] if own is None else own
    for way, target in ((0, across), (1, beside)):
        remote(source, blocks.at[here], send_sem.at[way], recv_sem.at[here], fsdp=target).start()


def share_step(blocks, sems):
    send_sem, recv_sem = sems
    here, beside, across, corner = fsdp_place()
    copy = remote(
        blocks.at[across], blocks.at[across], send_sem.at[2], recv_sem.at[across], fsdp=beside
    )
    copy.wait_recv()
    copy.start()


def share_finish(blocks, sems):
    send_sem, recv_sem = sems
    here, beside, across, corner = fsdp_place()
    for way, block in ((0, beside), (1, corner)):
        copy = remote(
            blocks.at[block], blocks.at[block], send_sem.at[way], recv_sem.at[block], fsdp=beside
        )
        copy.wait_recv()
        copy.wait_send()
    remote(
        blocks.at[here], blocks.at[here], send_sem.at[2], recv_sem.at[here], fsdp=beside
    ).wait_send()


def spread(pieces, landing, sems, ctx_count):
    send_sem, recv_sem = sems
    here = lax.axis_index("ctx")

    def copy(k, peer, source):
        return remote(pieces(peer), landing(source), send_sem.at[k], recv_sem.at[k], ctx=peer)

    starts = [copy(k, (here + k) % ctx_count, here) for k in range(1, ctx_count)]
    waits = [
        copy(k, (here + k) % ctx_count, (here + ctx_count - k) % ctx_count)
        for k in range(1, ctx_count)
    ]
    return starts, waits


def greet_near(last, here, level, side):
    barrier = pltpu.get_barrier_semaphore()
    group = lax.axis_index("fsdp")
    for k in range(1, 4):
        pl.semaphore_signal(barrier, inc=1, device_id={"fsdp": (group + k) % 4}, device_id_type=MESH)
    greet_line(last, here, level, side, 3)


def gather_kernel(last, shared_count, *refs):
    total = 1 + shared_count
    owns, rows, keep_sem = refs[:total], refs[total : 2 * total], refs[2 * total]
    refs = refs[2 * total + 1 :]
    place = line_place()
    here, level, line, side = place
    sems = [(refs[2 * i], refs[2 * i + 1]) for i in range(total)]
    group = lax.axis_index("fsdp")
    if shared_count:
        greet_near(last, here, level, side)
    else:
        greet_line(last, here, level, side)
    line_start(rows[0], owns[0], sems[0], place, last)
    for i in range(1, total):
        share_start(rows[i], sems[i], owns[i])
    keeps = [
        pltpu.make_async_copy(
            owns[i], rows[i].at[group if i else here], keep_sem.at[i]
        )
        for i in range(total)
    ]
    for copy in keeps:
        copy.start()
    for step in range(1, last + 1):
        line_step(rows[0], sems[0], place, last, step)
    for i in range(1, total):
        share_step(rows[i], sems[i])
    line_finish(rows[0], sems[0], place, last)
    for i in range(1, total):
        share_finish(rows[i], sems[i])
    for copy in keeps:
        copy.wait()


def product_kernel(last, own, units, grads, rows, product, keep_sem, send_sem, recv_sem):
    place = line_place()
    here, level, line, side = place
    sems = (send_sem, recv_sem)
    greet_line(last, here, level, side)
    line_start(rows, own, sems, place, last)
    keep = pltpu.make_async_copy(own, rows.at[here], keep_sem.at[0])
    keep.start()
    turned = units[...].T
    piece = grads.shape[1] // (last + 1)
    for step in range(last + 1):
        columns = pl.ds(step * piece, piece)
        product[:, columns] = flat_dot(turned, grads[:, columns]).astype(product.dtype)
        if step < last:
            line_step(rows, sems, place, last, step + 1)
    line_finish(rows, sems, place, last)
    keep.wait()


def product_gather(ctx_count, call_id, own, units, grads):
    dma = pltpu.SemaphoreType.DMA
    return pl.pallas_call(
        functools.partial(product_kernel, ctx_count // 2 - 1),
        out_shape=[
            jax.ShapeDtypeStruct((ctx_count,) + own.shape, own.dtype),
            jax.ShapeDtypeStruct((units.shape[1], grads.shape[1]), own.dtype),
        ],
        in_specs=[VMEM] * 3,
        out_specs=[ANY, VMEM],
        scratch_shapes=[dma((1,)), dma((ctx_count, 3)), dma((ctx_count,))],
        compiler_params=pltpu.CompilerParams(
            collective_id=call_id, has_side_effects=True, vmem_limit_bytes=32 * 2**20
        ),
        name="product_gather",
    )(own, units, grads)


def line_gather(ctx_count, call_id, own, *shared):
    count = len(shared)
    dma = pltpu.SemaphoreType.DMA
    return pl.pallas_call(
        functools.partial(gather_kernel, ctx_count // 2 - 1, count),
        out_shape=[jax.ShapeDtypeStruct((ctx_count,) + own.shape, own.dtype)]
        + [jax.ShapeDtypeStruct((4,) + a.shape, a.dtype) for a in shared],
        in_specs=[VMEM] * (1 + count),
        out_specs=[ANY] * (1 + count),
        scratch_shapes=[dma((1 + count,)), dma((ctx_count, 3)), dma((ctx_count,))]
        + [dma((3,)), dma((4,))] * count,
        compiler_params=pltpu.CompilerParams(collective_id=call_id, has_side_effects=True),
        name="line_gather",
    )(own, *shared)


def opening_kernel(
    ctx_count,
    own,
    qkv_own,
    out_own,
    small_own,
    number_own,
    rows,
    qkv,
    out_pair,
    small,
    numbers,
    keep_sem,
    pair_send,
    pair_recv,
    row_send,
    row_recv,
    share_send,
    share_recv,
    *sems,
):
    last = ctx_count // 2 - 1
    place = line_place()
    here, level, line, side = place
    group, beside, across, corner = fsdp_place()
    sems = [(sems[2 * i], sems[2 * i + 1]) for i in range(5)]
    qkv_spread, small_spread, number_spread, out_share, small_share = sems
    row_sems = (row_send, row_recv)
    greet_all(ctx_count)
    qkv_start, qkv_wait = spread(
        lambda peer: qkv_own.at[peer], lambda source: qkv.at[group, source], qkv_spread, ctx_count
    )
    small_start, small_wait = spread(
        lambda peer: small_own, lambda source: small.at[group, source], small_spread, ctx_count
    )
    number_start, number_wait = spread(
        lambda peer: number_own, lambda source: numbers.at[source], number_spread, ctx_count
    )

    def piece_copy(way, owner, k, target, first=False):
        source = (here + ctx_count - k) % ctx_count
        return remote(
            qkv_own.at[here] if first else qkv.at[owner, source],
            qkv.at[owner, source],
            share_send.at[way, k],
            share_recv.at[owner, k],
            fsdp=target,
        )

    def piece_on(k):
        piece_copy(0, group, k, across, k == 0).start()
        piece_copy(1, group, k, beside, k == 0).start()

    for copy in small_start + number_start + qkv_start:
        copy.start()
    line_start(rows, own, row_sems, place, last)
    piece_on(0)
    pair = remote(
        out_own, out_pair.at[group, line], pair_send.at[0], pair_recv.at[0], ctx=side
    )
    pair.start()
    keeps = [
        pltpu.make_async_copy(source, target, keep_sem.at[i])
        for i, (source, target) in enumerate(
            (
                (qkv_own.at[here], qkv.at[group, here]),
                (out_own, out_pair.at[group, line]),
                (small_own, small.at[group, here]),
                (number_own, numbers.at[here]),
                (own, rows.at[here]),
            )
        )
    ]
    for copy in keeps:
        copy.start()
    for copy in small_wait:
        copy.wait_recv()
    keeps[2].wait()
    share_start(small, small_share)
    line_step(rows, row_sems, place, last, 1)
    for k in range(1, ctx_count):
        qkv_wait[k - 1].wait_recv()
        piece_on(k)
    remote(
        out_own, out_pair.at[group, 1 - line], pair_send.at[0], pair_recv.at[0], ctx=side
    ).wait_recv()
    keeps[1].wait()
    share_start(out_pair, out_share)
    line_step(rows, row_sems, place, last, 2)
    for k in range(ctx_count):
        piece_copy(0, across, k, across).wait_recv()
        piece_copy(2, across, k, beside).start()
    share_step(small, small_share)
    for step in range(3, last + 1):
        line_step(rows, row_sems, place, last, step)
    share_step(out_pair, out_share)
    line_finish(rows, row_sems, place, last)
    for copy in number_wait:
        copy.wait_recv()
    for copy in qkv_start + small_start + number_start:
        copy.wait_send()
    pair.wait_send()
    for k in range(ctx_count):
        piece_copy(1, beside, k, beside).wait_recv()
        piece_copy(2, corner, k, beside).wait_recv()
        for way in range(3):
            piece_copy(way, group, k, beside).wait_send()
    share_finish(small, small_share)
    share_finish(out_pair, out_share)
    for i in (0, 3, 4):
        keeps[i].wait()


def opening(ctx_count, call_id, own, qkv_own, out_own, small_own, number_own):
    def out(lead, array):
        return jax.ShapeDtypeStruct(lead + array.shape, array.dtype)

    dma = pltpu.SemaphoreType.DMA
    return pl.pallas_call(
        functools.partial(opening_kernel, ctx_count),
        out_shape=[
            out((ctx_count,), own),
            out((4,), qkv_own),
            out((4, 2), out_own),
            out((4, ctx_count), small_own),
            out((ctx_count,), number_own),
        ],
        in_specs=[VMEM] * 5,
        out_specs=[ANY] * 5,
        scratch_shapes=[
            dma((5,)),
            dma((1,)),
            dma((1,)),
            dma((ctx_count, 3)),
            dma((ctx_count,)),
            dma((3, ctx_count)),
            dma((4, ctx_count)),
        ]
        + [dma((ctx_count,))] * 6
        + [dma((3,)), dma((4,))] * 2,
        compiler_params=pltpu.CompilerParams(collective_id=call_id, has_side_effects=True),
        name="opening",
    )(own, qkv_own, out_own, small_own, number_own)


def group_reduce(blocks, beside_in, pair_sums, across_in, settled, sems):
    core_send, core_recv, far_send, far_recv = sems
    group, beside, across, corner = fsdp_place()
    rows = settled.shape[0]

    def core_copy(slot, block):
        return remote(
            blocks.at[block],
            beside_in.at[slot],
            core_send.at[slot],
            core_recv.at[slot],
            fsdp=beside,
        )

    far = remote(pair_sums.at[1], across_in, far_send.at[0], far_recv.at[0], fsdp=across)
    core_copy(1, corner).start()
    core_copy(0, beside).start()
    yield
    core_copy(1, corner).wait_recv()
    add_rows(pair_sums.at[1], (blocks.at[across], beside_in.at[1]), rows)
    far.start()
    core_copy(0, beside).wait_recv()
    add_rows(pair_sums.at[0], (blocks.at[group], beside_in.at[0]), rows)
    yield
    far.wait_recv()
    add_rows(settled, (pair_sums.at[0], across_in), rows)
    yield
    core_copy(1, corner).wait_send()
    core_copy(0, beside).wait_send()
    far.wait_send()
    yield


def closing_kernel(ctx_count, part, weight, pair, plain, small, *refs):
    total, landed, pair_total, plain_total, small_total = refs[:5]
    line_slots, weight_slots, pair_slots, plain_slots = (
        refs[5:9],
        refs[9:13],
        refs[13:17],
        refs[17:20],
    )
    pair_in, small_in, small_sums, small_across = refs[20:24]
    sems = refs[24:]
    line_sems, weight_sems, pair_sems, plain_sems = sems[:5], sems[5:9], sems[9:13], sems[13:17]
    keep_sem, half_send, half_recv = sems[17:20]
    weight_spread, small_spread, (group_send, group_recv) = sems[20:22], sems[22:24], sems[24:26]
    here, level, line, side = line_place()
    group = lax.axis_index("fsdp")
    greet_all(ctx_count)
    turns = scatter_turns(ctx_count // 2 - 1, part, total, *line_slots, *line_sems)
    settled, pair_settled = weight_slots[3], pair_slots[3]
    weight_steps = group_reduce(weight, *weight_slots, weight_sems)
    pair_steps = group_reduce(pair, *pair_slots, pair_sems)
    plain_steps = group_reduce(plain, *plain_slots, plain_total, plain_sems)
    small_start, small_wait = spread(
        lambda peer: small.at[:, peer], lambda source: small_in.at[source], small_spread, ctx_count
    )
    for copy in small_start:
        copy.start()
    next(weight_steps)
    next(turns)
    next(weight_steps)
    next(pair_steps)
    next(turns)
    next(pair_steps)
    next(plain_steps)
    for copy in small_wait:
        copy.wait_recv()
    small_sum = small[:, here]
    for k in range(1, ctx_count):
        small_sum = small_sum + small_in[(here + k) % ctx_count]
    small_sums[...] = small_sum
    group_copies = [
        remote(
            small_sums.at[(group + k) % 4],
            small_across.at[k],
            group_send.at[k],
            group_recv.at[k],
            fsdp=(group + k) % 4,
        )
        for k in range(1, 4)
    ]
    for copy in group_copies:
        copy.start()
    next(weight_steps)
    piece = settled.shape[0] // ctx_count
    weight_start, weight_wait = spread(
        lambda peer: settled.at[pl.ds(pl.multiple_of(peer * piece, piece), piece)],
        lambda source: landed.at[source],
        weight_spread,
        ctx_count,
    )
    for copy in weight_start:
        copy.start()
    keep = pltpu.make_async_copy(
        settled.at[pl.ds(pl.multiple_of(here * piece, piece), piece)],
        landed.at[here],
        keep_sem.at[0],
    )
    keep.start()
    next(plain_steps)
    next(turns)
    next(pair_steps)
    half = pair_total.shape[0]
    half_copy = remote(
        pair_settled.at[pl.ds(pl.multiple_of((1 - line) * half, half), half)],
        pair_in,
        half_send.at[0],
        half_recv.at[0],
        ctx=side,
    )
    half_copy.start()
    for copy in group_copies:
        copy.wait_recv()
    small_total[...] = small_sums[group] + small_across[1] + small_across[2] + small_across[3]
    for step in turns:
        pass
    next(plain_steps)
    half_copy.wait_recv()
    kept = pair_settled.at[pl.ds(pl.multiple_of(line * half, half), half)]
    add_rows(pair_total, (kept, pair_in), half)
    for copy in weight_wait:
        copy.wait_recv()
    for copy in weight_start + small_start + group_copies:
        copy.wait_send()
    half_copy.wait_send()
    next(weight_steps)
    next(pair_steps)
    next(plain_steps)
    keep.wait()


def closing(ctx_count, call_id, part, weight, pair, plain, small):
    rows, width = part.shape[1:]
    half = ctx_count // 2
    dma = pltpu.SemaphoreType.DMA
    slots = pltpu.VMEM((half, rows, width), part.dtype)

    def group_slots(array):
        one = pltpu.VMEM(array.shape[1:], array.dtype)
        two = pltpu.VMEM((2,) + array.shape[1:], array.dtype)
        return [two, two, one, one]

    block, columns = weight.shape[1:]
    pair_half = (pair.shape[1] // 2, pair.shape[2])
    return pl.pallas_call(
        functools.partial(closing_kernel, ctx_count),
        out_shape=[
            jax.ShapeDtypeStruct((rows, width), jnp.float32),
            jax.ShapeDtypeStruct((ctx_count, block // ctx_count, columns), weight.dtype),
            jax.ShapeDtypeStruct(pair_half, jnp.float32),
            jax.ShapeDtypeStruct(plain.shape[1:], jnp.float32),
            jax.ShapeDtypeStruct(small.shape[2:], small.dtype),
        ],
        in_specs=[VMEM] * 5,
        out_specs=[VMEM] * 5,
        scratch_shapes=[slots] * 4
        + group_slots(weight)
        + group_slots(pair)
        + group_slots(plain)[:3]
        + [
            pltpu.VMEM(pair_half, pair.dtype),
            pltpu.VMEM((ctx_count, 4) + small.shape[2:], small.dtype),
            pltpu.VMEM((4,) + small.shape[2:], small.dtype),
            pltpu.VMEM((4,) + small.shape[2:], small.dtype),
        ]
        + [dma((half,))] * 5
        + [dma((2,)), dma((2,)), dma((1,)), dma((1,))] * 3
        + [dma((1,))] * 3
        + [dma((ctx_count,))] * 4
        + [dma((4,))] * 2,
        compiler_params=pltpu.CompilerParams(
            collective_id=call_id, has_side_effects=True, vmem_limit_bytes=56 * 2**20
        ),
        name="closing",
    )(part, weight, pair, plain, small)


def scaled_rows(values):
    return values * lax.rsqrt(jnp.mean(values * values, axis=-1, keepdims=True) + EPSILON)


def attend_kernel(
    inputs,
    gain,
    weight,
    bias,
    cosine,
    sine,
    columns,
    lines,
    out_weight,
    normed,
    queries,
    keys,
    values,
    attended,
    log_totals,
    part,
):
    rows = inputs.shape[0]
    low = jnp.bfloat16
    heads = queries.shape[1] // HD

    @pl.loop(0, rows // SPAN)
    def project(index):
        here = span_of(index)
        unit = scaled_rows(inputs[here, :].astype(jnp.float32)) * gain[...]
        normed[here, :] = unit.astype(low)
        projected = flat_dot(normed[here, :], weight[...]) + bias[...]
        turn, tilt = cosine[here, :], sine[here, :]
        for head in range(heads):
            own = slice(head * HD, (head + 1) * HD)
            query = projected[:, own]
            query = query * turn + pltpu.roll(query, HD // 2, 1) * tilt
            queries[here, own] = (query * HD ** (-0.5)).astype(low)
            key = projected[:, (heads + head) * HD : (heads + head + 1) * HD]
            keys[here, own] = (key * turn + pltpu.roll(key, HD // 2, 1) * tilt).astype(low)
            values[here, own] = projected[
                :, (2 * heads + head) * HD : (2 * heads + head + 1) * HD
            ].astype(low)

    @pl.loop(0, rows // SPAN)
    def attend(index):
        here = span_of(index)
        position, segment = columns[here, 0:1], columns[here, 1:2]
        allowed = (lines[1:2, :] == segment) & (lines[0:1, :] <= position)
        allowed = allowed | (lines[0:1, :] == position)
        for head in range(heads):
            own = slice(head * HD, (head + 1) * HD)
            scores = turned_dot(queries[here, own], keys[:, own])
            scores = jnp.where(allowed, scores, -1e30)
            highest = jnp.max(scores, axis=1, keepdims=True)
            weights = jnp.exp(scores - highest)
            sums = jnp.sum(weights, axis=1, keepdims=True)
            log_totals[here, head : head + 1] = highest + jnp.log(sums)
            probs = (weights * (1.0 / sums)).astype(low)
            attended[here, own] = flat_dot(probs, values[:, own]).astype(low)
        part[here, :] = flat_dot(attended[here, :], out_weight[...]).astype(low)


def attend(inputs, gain, weight, bias, cosine, sine, columns, lines, out_weight):
    rows, width = inputs.shape
    wide = out_weight.shape[0]
    low = jnp.bfloat16
    shape = jax.ShapeDtypeStruct
    return pl.pallas_call(
        attend_kernel,
        out_shape=[shape((rows, width), low)]
        + [shape((rows, wide), low)] * 4
        + [shape((rows, wide // HD), jnp.float32), shape((rows, width), low)],
        in_specs=[VMEM] * 9,
        out_specs=[VMEM] * 7,
        compiler_params=pltpu.CompilerParams(vmem_limit_bytes=40 * 2**20),
        cost_estimate=pl.CostEstimate(
            flops=2 * rows * width * 4 * wide + 4 * rows * rows * wide,
            bytes_accessed=20 * 2**20,
            transcendentals=rows * rows * wide // HD,
        ),
        name="attend",
    )(inputs, gain, weight, bias, cosine, sine, columns, lines, out_weight)


def attend_back_kernel(
    branch,
    out_weight,
    queries,
    keys,
    values,
    attended,
    totals,
    cosine,
    sine,
    columns,
    lines,
    far_inputs,
    far_normed,
    far_weight,
    part,
    grad_weight,
    grad_out,
    grad_bias,
    grad_gain,
    grads,
    grad_attended,
    grad_keys,
    grad_values,
    gain_sum,
    inputs,
    normed,
    weight,
    load_sem,
):
    rows, width = branch.shape
    low = jnp.bfloat16
    full = jnp.float32
    wide = queries.shape[1]
    heads = wide // HD
    loads = [
        pltpu.make_async_copy(source, target, load_sem.at[i])
        for i, (source, target) in enumerate(
            ((far_weight, weight), (far_inputs, inputs), (far_normed, normed))
        )
    ]
    for copy in loads:
        copy.start()

    @pl.loop(0, rows // SPAN)
    def into_heads(index):
        here = span_of(index)
        grad_attended[here, :] = turned_dot(branch[here, :], out_weight[...]).astype(low)

    for head in range(heads):
        own = slice(head * HD, (head + 1) * HD)
        grad_keys[...] = jnp.zeros_like(grad_keys)
        grad_values[...] = jnp.zeros_like(grad_values)

        @pl.loop(0, rows // SPAN)
        def scores_back(index):
            here = span_of(index)
            position, segment = lines[0:1, here], lines[1:2, here]
            allowed = (columns[:, 1:2] == segment) & (columns[:, 0:1] <= position)
            allowed = allowed | (columns[:, 0:1] == position)
            query, grad = queries[here, own], grad_attended[here, own]
            scores = jnp.where(allowed, turned_dot(keys[:, own], query), -1e30)
            probs = jnp.exp(scores - totals[head : head + 1, here])
            grad_probs = turned_dot(values[:, own], grad)
            delta = jnp.sum(probs * grad_probs, axis=0, keepdims=True)
            grad_scores = (probs * (grad_probs - delta)).astype(low)
            grad_keys[...] += flat_dot(grad_scores, query)
            grad_values[...] += flat_dot(probs.astype(low), grad)
            grad_query = flat_dot(grad_scores.T, keys[:, own]) * HD ** (-0.5)
            grads[here, own] = (
                grad_query * cosine[here, :] + pltpu.roll(grad_query * sine[here, :], HD // 2, 1)
            ).astype(low)

        @pl.loop(0, rows // SPAN)
        def keys_back(index):
            here = span_of(index)
            grad_key = grad_keys[here, :]
            grads[here, (heads + head) * HD : (heads + head + 1) * HD] = (
                grad_key * cosine[here, :] + pltpu.roll(grad_key * sine[here, :], HD // 2, 1)
            ).astype(low)
            grads[here, (2 * heads + head) * HD : (2 * heads + head + 1) * HD] = grad_values[
                here, :
            ].astype(low)

    gain_sum[...] = jnp.zeros_like(gain_sum)
    grad_bias[...] = jnp.zeros_like(grad_bias)
    for copy in loads:
        copy.wait()

    @pl.loop(0, rows // SPAN)
    def project_back(index):
        here = span_of(index)
        grad_rows = turned_dot(grads[here, :], weight[...])
        part[here, :] = grad_rows.astype(low)
        unit = scaled_rows(inputs[here, :].astype(full))
        gain_sum[...] += jnp.sum(grad_rows * unit, axis=0, keepdims=True)
        grad_bias[...] += jnp.sum(grads[here, :].astype(full), axis=0, keepdims=True)

    grad_gain[...] = gain_sum[...]

    @pl.loop(0, width // SPAN)
    def weight_back(index):
        here = span_of(index)
        grad_weight[here, :] = flat_dot(normed[:, here].T, grads[...]).astype(low)

    attended_turned = attended[...].T

    @pl.loop(0, width // (2 * SPAN))
    def out_back(index):
        here = span_of(index, 2 * SPAN)
        grad_out[:, here] = flat_dot(attended_turned, branch[:, here]).astype(low)


def attend_back(
    branch,
    out_weight,
    queries,
    keys,
    values,
    attended,
    totals,
    cosine,
    sine,
    columns,
    lines,
    inputs,
    normed,
    weight,
):
    rows, width = branch.shape
    wide = out_weight.shape[0]
    low = jnp.bfloat16
    full = jnp.float32
    shape = jax.ShapeDtypeStruct
    return pl.pallas_call(
        attend_back_kernel,
        out_shape=[
            shape((rows, width), low),
            shape(weight.shape, low),
            shape((wide, width), low),
            shape((1, 3 * wide), full),
            shape((1, width), full),
        ],
        in_specs=[VMEM] * 11 + [ANY] * 3,
        out_specs=[VMEM] * 5,
        scratch_shapes=[
            pltpu.VMEM((rows, 3 * wide), low),
            pltpu.VMEM((rows, wide), low),
            pltpu.VMEM((rows, HD), full),
            pltpu.VMEM((rows, HD), full),
            pltpu.VMEM((1, width), full),
            pltpu.VMEM(inputs.shape, low),
            pltpu.VMEM(normed.shape, low),
            pltpu.VMEM(weight.shape, low),
            pltpu.SemaphoreType.DMA((3,)),
        ],
        compiler_params=pltpu.CompilerParams(vmem_limit_bytes=56 * 2**20),
        cost_estimate=pl.CostEstimate(
            flops=2 * rows * width * 8 * wide + 10 * rows * rows * wide,
            bytes_accessed=35 * 2**20,
            transcendentals=rows * rows * wide // HD,
        ),
        name="attend_back",
    )(
        branch,
        out_weight,
        queries,
        keys,
        values,
        attended,
        totals,
        cosine,
        sine,
        columns,
        lines,
        inputs,
        normed,
        weight,
    )


def gate_back_kernel(upstream, scale, gate_up, weight_out, grads, scaled):
    low = jnp.bfloat16
    half = gate_up.shape[1] // 2
    scaled[...] = (scale[...] * upstream[...].astype(jnp.float32)).astype(low)
    grad_unit = turned_dot(scaled[...], weight_out[...])
    gate, up = gate_up[:, :half], gate_up[:, half:]
    sigmoid = 1.0 / (1.0 + jnp.exp(-gate))
    grad_gate = grad_unit * up * (sigmoid * (1.0 + gate * (1.0 - sigmoid)))
    grad_up = grad_unit * (gate * sigmoid)
    grads[...] = jnp.concatenate([grad_gate.astype(low), grad_up.astype(low)], axis=1)


def gate_back(upstream, scale, gate_up, weight_out):
    rows, width = upstream.shape
    hidden = weight_out.shape[0]
    low = jnp.bfloat16

    def block(columns):
        return pl.BlockSpec((SPAN, columns), lambda i: (i, 0))

    return pl.pallas_call(
        gate_back_kernel,
        grid=(rows // SPAN,),
        out_shape=[
            jax.ShapeDtypeStruct((rows, 2 * hidden), low),
            jax.ShapeDtypeStruct((rows, width), low),
        ],
        in_specs=[
            block(width),
            block(1),
            block(2 * hidden),
            pl.BlockSpec((hidden, width), lambda i: (0, 0)),
        ],
        out_specs=[block(2 * hidden), block(width)],
        compiler_params=pltpu.CompilerParams(vmem_limit_bytes=48 * 2**20),
        cost_estimate=pl.CostEstimate(
            flops=2 * rows * width * hidden,
            bytes_accessed=rows * (12 * hidden + 4 * width) + 2 * hidden * width,
            transcendentals=rows * hidden,
        ),
        name="gate_back",
    )(upstream, scale, gate_up, weight_out)


def deal_kernel(pieces, weight, dealt):
    ctx_count = dealt.shape[0]
    width = dealt.shape[2] // pieces
    for c in range(ctx_count):
        dealt[c] = jnp.concatenate(
            [
                weight[:, (q * ctx_count + c) * width : (q * ctx_count + c + 1) * width]
                for q in range(pieces)
            ],
            axis=1,
        )


def deal_columns(weight, ctx_count, pieces):
    rows, columns = weight.shape
    return pl.pallas_call(
        functools.partial(deal_kernel, pieces),
        out_shape=jax.ShapeDtypeStruct((ctx_count, rows, columns // ctx_count), weight.dtype),
        name="deal_columns",
    )(weight)


def collect_kernel(pieces, dealt, whole):
    ctx_count = dealt.shape[0]
    width = dealt.shape[2] // pieces
    whole[...] = jnp.concatenate(
        [
            dealt[c, :, q * width : (q + 1) * width]
            for q in range(pieces)
            for c in range(ctx_count)
        ],
        axis=1,
    ).astype(whole.dtype)


def collect_columns(dealt, pieces):
    ctx_count, rows, columns = dealt.shape
    return pl.pallas_call(
        functools.partial(collect_kernel, pieces),
        out_shape=jax.ShapeDtypeStruct((rows, columns * ctx_count), jnp.float32),
        name="collect_columns",
    )(dealt)


def heads_kernel(order, dealt, whole):
    pairs = dealt.shape[0] * 2
    for place, head in enumerate(order):
        for which in range(3):
            column = (which * 2 + place % 2) * HD
            target = (which * pairs + head) * HD
            whole[:, target : target + HD] = dealt[
                place // 2, :, column : column + HD
            ].astype(whole.dtype)


def collect_heads(dealt, order):
    ctx_count, rows, columns = dealt.shape
    return pl.pallas_call(
        functools.partial(heads_kernel, order),
        out_shape=jax.ShapeDtypeStruct((rows, columns * ctx_count), jnp.float32),
        name="collect_heads",
    )(dealt)


def over(axis, array, dim=0):
    return lax.all_gather(array, axis, axis=dim, tiled=True)


def reduce_over(axis, array, dim=0):
    return lax.psum_scatter(array, axis, scatter_dimension=dim, tiled=True)


def exchange(array):
    return lax.all_to_all(array, "ctx", split_axis=0, concat_axis=0, tiled=True)


def transposed_dot(left, right):
    return lax.dot_general(
        left, right, (((0,), (0,)), ((), ())), preferred_element_type=jnp.float32
    )


def dot_transposed(left, right):
    return lax.dot_general(
        left, right, (((1,), (1,)), ((), ())), preferred_element_type=jnp.float32
    )


def split_plan(
    hidden_in,
    segments,
    block_pairs,
    routes,
    out_grad,
    norm_gain_attn,
    qkv_weight,
    qkv_bias,
    out_weight,
    norm_gain_ffn,
    router_weight,
    shared_gate_weight,
    shared_in_weight,
    shared_out_weight,
    expert_in_weight,
    expert_out_weight,
):
    low = jnp.bfloat16
    full = jnp.float32
    tokens_dev, width = hidden_in.shape[1:]
    block_len = tokens_dev // 2
    ctx_count = lax.axis_size("ctx")
    fsdp_count = lax.axis_size("fsdp")
    ctx_rank = lax.axis_index("ctx")
    dev_count = ctx_count * fsdp_count
    row_len = ctx_count * tokens_dev
    early = width // 2
    head_count = width // HD
    shard = qkv_weight.shape[0]
    expert_count = router_weight.shape[1]
    shared_shard = shared_out_weight.shape[0]
    shared_width = fsdp_count * shared_shard
    expert_width = expert_out_weight.shape[1] * fsdp_count
    pair_rank = ctx_rank // 2
    side = ctx_rank % 2
    pairs = ctx_count // 2
    head_order = [j + (p * 2 + t) * pairs for j in range(pairs) for p in range(2) for t in range(2)]

    small = jnp.concatenate(
        [
            norm_gain_attn,
            norm_gain_ffn,
            shared_gate_weight,
            router_weight.T.reshape(-1),
            qkv_bias,
        ]
    )
    small_count = small.shape[0]
    small = jnp.pad(small, (0, 16 * HD - small_count)).reshape(16, HD)
    own_numbers = jnp.concatenate(
        [routes.reshape(tokens_dev, -1).T, segments.reshape(1, tokens_dev)], axis=0
    )
    number_count = own_numbers.shape[0]
    own_numbers = jnp.pad(own_numbers, ((0, 8 - number_count), (0, 0)))
    qkv_parts = (
        qkv_weight.reshape(shard, 3, head_count, HD)[:, :, jnp.array(head_order)]
        .reshape(shard, 3, ctx_count, 2 * HD)
        .transpose(2, 0, 1, 3)
        .reshape(ctx_count, shard, 6 * HD)
    )
    own_inputs = hidden_in.reshape(tokens_dev, width)
    row_inputs, qkv_c, out_pair, small_all, numbers = opening(
        ctx_count, 1, own_inputs, qkv_parts, out_weight, small, own_numbers
    )
    qkv_c = qkv_c.reshape(width, 6 * HD)
    out_c = lax.dynamic_index_in_dim(
        out_pair.reshape(2, 2 * HD, width), side, 0, keepdims=False
    )
    small_all = small_all.reshape(dev_count, 16 * HD)
    gain_attn = small_all[:, :shard].reshape(width).astype(full)
    gain_ffn = small_all[:, shard : 2 * shard].reshape(width).astype(full)
    gate_full = small_all[:, 2 * shard : 3 * shard].reshape(width)
    router_t = (
        small_all[:, 3 * shard : (3 + expert_count) * shard]
        .reshape(dev_count, expert_count, shard)
        .transpose(1, 0, 2)
        .reshape(expert_count, width)
    )
    bias_full = small_all[:, (3 + expert_count) * shard : small_count].reshape(3, head_count, HD)
    router_gate = jnp.concatenate([router_t, gate_full[None, :]], axis=0)
    row_seg = numbers[:, number_count - 1].reshape(row_len)
    routed_here = jnp.any(numbers[:, : number_count - 1] == ctx_rank, axis=1).reshape(row_len)

    shared_in_weight, numbers = lax.optimization_barrier((shared_in_weight, numbers))
    expert_outer = over("fsdp", expert_out_weight[0])
    early_upstream = over("ctx", out_grad.reshape(tokens_dev, width)[:, :early])
    inner_parts = deal_columns(shared_in_weight, ctx_count, 2 * fsdp_count)
    expert_inner = over("fsdp", expert_in_weight[0])
    inner_parts = exchange(inner_parts)
    my_heads = [pair_rank + (side * 2 + t) * pairs for t in range(2)]
    bias_c = jnp.concatenate(
        [lax.dynamic_index_in_dim(bias_full, h, 1, keepdims=False) for h in my_heads], axis=1
    ).reshape(6 * HD)

    offsets = jnp.arange(block_len, dtype=jnp.int32)
    positions = (block_pairs[:, None] * block_len + offsets[None, :]).reshape(row_len)
    inputs = own_inputs.astype(full)
    row_inputs = row_inputs.reshape(row_len, width)
    half_len = HD // 2
    frequency = THETA ** (-jnp.arange(half_len, dtype=full) / half_len)
    places = positions.astype(full)
    angles = places[:, None] * frequency[None, :]
    cosine, sine = jnp.cos(angles), jnp.sin(angles)
    cosine = jnp.concatenate([cosine, cosine], axis=1)
    sine = jnp.concatenate([-sine, sine], axis=1)
    key_seg = row_seg.astype(full)
    query_seg = jnp.where(row_seg >= 0, key_seg, -2.0)
    query_marks = jnp.stack([places, query_seg])
    key_marks = jnp.stack([places, key_seg])
    row_normed, queries, keys, values, attended_row, log_totals, branch_part = attend(
        row_inputs,
        gain_attn[None, :],
        qkv_c,
        bias_c.astype(full)[None, :],
        cosine,
        sine,
        query_marks.T,
        key_marks,
        out_c,
    )
    branch_part, inner_parts, early_upstream, expert_outer = lax.optimization_barrier(
        (branch_part, inner_parts, early_upstream, expert_outer)
    )
    branch = line_scatter(ctx_count, 2, branch_part.reshape(ctx_count, tokens_dev, width))
    middle = inputs + branch
    normed_ffn = rms_scale(middle, gain_ffn).astype(low)

    row_ffn, inner_c, outer_c = line_gather(
        ctx_count,
        4,
        normed_ffn,
        inner_parts.reshape(ctx_count * shard, 2 * shared_width),
        shared_out_weight,
    )
    row_ffn = row_ffn.reshape(row_len, width)
    row_ffn, late_grad = lax.optimization_barrier((row_ffn, out_grad))
    late_upstream = over("ctx", late_grad.reshape(tokens_dev, width)[:, early:])
    inner_c = inner_c.reshape(width, 2 * shared_width)
    outer_c = outer_c.reshape(shared_width, width)
    row_logits = dot_transposed(row_ffn, router_gate)
    row_probs = jax.nn.softmax(row_logits[:, :expert_count], axis=-1)
    expert_ids = jnp.arange(expert_count, dtype=jnp.int32)
    here = jnp.where(
        routed_here, jnp.sum(jnp.where(expert_ids[None, :] == ctx_rank, row_probs, 0.0), axis=1), 0.0
    )
    row_gate = jax.nn.sigmoid(row_logits[:, expert_count])
    expert_gu = matmul_low(row_ffn, expert_inner)
    expert_hidden = swiglu_mix(expert_gu, expert_width).astype(low)
    expert_result = matmul_low(expert_hidden, expert_outer).astype(low).astype(full)
    row_shared, expert_result = lax.optimization_barrier((row_ffn, expert_result))
    shared_gu = matmul_low(row_shared, inner_c)
    shared_hidden = swiglu_mix(shared_gu, shared_width).astype(low)
    shared_out = matmul_low(shared_hidden, outer_c)
    shared_out, late_upstream = lax.optimization_barrier((shared_out, late_upstream))
    row_upstream = lax.optimization_barrier(
        jnp.concatenate([early_upstream, late_upstream], axis=1)
    )
    upstream_row = row_upstream.astype(full)
    out_part = (row_gate[:, None] * shared_out + here[:, None] * expert_result).astype(low)
    gate_dot = jnp.sum(upstream_row * shared_out, axis=1)
    expert_dot = jnp.where(routed_here, jnp.sum(upstream_row * expert_result, axis=1), 0.0)
    out_landed = reduce_over("ctx", out_part)

    row_upstream, out_part = lax.optimization_barrier((row_upstream, out_part))
    grad_expert_gu, grad_buffers = gate_back(row_upstream, here[:, None], expert_gu, expert_outer)
    sum_expert_outer = reduce_over("fsdp", transposed_dot(expert_hidden, grad_buffers).astype(low))
    grad_rows = dot_transposed(grad_expert_gu, expert_inner).astype(low)
    row_upstream, grad_rows = lax.optimization_barrier((row_upstream, grad_rows))
    grad_shared_gu, grad_shared_out = gate_back(
        row_upstream, row_gate[:, None], shared_gu, outer_c
    )
    grad_inner = transposed_dot(row_ffn, grad_shared_gu).astype(low)
    sum_inner_c = reduce_over("fsdp", grad_inner)
    grad_ffn_part = (
        dot_transposed(grad_shared_gu, inner_c) + grad_rows.astype(full)
    ).astype(low)
    dots = jnp.stack([gate_dot, expert_dot]).reshape(2, ctx_count, tokens_dev).transpose(1, 0, 2)
    grad_ffn_part, grad_inner = lax.optimization_barrier((grad_ffn_part, grad_inner))
    grad_normed, own_dots, grad_expert_inner = line_scatter(
        ctx_count,
        6,
        grad_ffn_part.reshape(ctx_count, tokens_dev, width),
        jnp.pad(dots, ((0, 0), (0, 6), (0, 0))),
        row_ffn,
        grad_expert_gu,
    )
    sum_expert_inner = reduce_over("fsdp", grad_expert_inner)
    hidden_out = (middle + out_landed.astype(full)).astype(low).reshape(1, tokens_dev, width)

    own_logits = dot_transposed(normed_ffn, router_gate)
    router_probs = jax.nn.softmax(own_logits[:, :expert_count], axis=-1)
    gate_value = jax.nn.sigmoid(own_logits[:, expert_count])
    grad_gate_logit = gate_value * (1.0 - gate_value) * jnp.sum(own_dots[:, 0], axis=0)
    grad_choice = own_dots[:, 1].T
    grad_logits = router_probs * (
        grad_choice - jnp.sum(router_probs * grad_choice, axis=1, keepdims=True)
    )
    grad_small = jnp.concatenate([grad_logits, grad_gate_logit[:, None]], axis=1).astype(low)
    grad_router_gate = transposed_dot(grad_small, normed_ffn)
    grad_normed = grad_normed + matmul_low(grad_small, router_gate)
    unused_norm, norm_pull = jax.vjp(rms_scale, middle, gain_ffn)
    grad_middle_norm, grad_gain_ffn = norm_pull(grad_normed)
    grad_middle = out_grad.reshape(tokens_dev, width).astype(full) + grad_middle_norm

    grad_branch, hidden_out = lax.optimization_barrier((grad_middle.astype(low), hidden_out))
    row_branch, grad_outer = product_gather(
        ctx_count, 3, grad_branch, shared_hidden, grad_shared_out
    )
    row_branch, sum_inner_c = lax.optimization_barrier(
        (row_branch.reshape(row_len, width), sum_inner_c)
    )
    sum_inner = collect_columns(
        exchange(sum_inner_c.reshape(ctx_count, shard, 2 * shared_width)), 2 * fsdp_count
    )
    grad_attn_part, grad_qkv_c, grad_out_c, grad_bias_c, grad_gain_attn = attend_back(
        row_branch,
        out_c,
        queries,
        keys,
        values,
        attended_row,
        log_totals.T,
        cosine,
        sine,
        key_marks.T,
        query_marks,
        row_inputs,
        row_normed,
        qkv_c,
    )
    grad_out_c = grad_out_c.reshape(2, HD, width)
    padded_out = jnp.concatenate(
        [jnp.where(side == p, grad_out_c, jnp.zeros_like(grad_out_c)) for p in range(2)], axis=0
    )
    grad_attn_part, sum_inner, sum_expert_outer = lax.optimization_barrier(
        (grad_attn_part, sum_inner, sum_expert_outer)
    )
    grad_bias_c = grad_bias_c.reshape(3, 1, 2, HD)
    mine = (jnp.arange(ctx_count) == ctx_rank)[None, :, None, None]
    places_of = [head_order.index(h) for h in range(head_count)]
    grad_bias = (
        jnp.where(mine, grad_bias_c, 0.0)
        .reshape(3, pairs, 2, 2, HD)
        .transpose(0, 2, 3, 1, 4)
        .reshape(dev_count, -1)
    )
    small_grads = jnp.concatenate(
        [
            grad_gain_attn.reshape(dev_count, shard),
            grad_gain_ffn.reshape(dev_count, shard),
            grad_router_gate.reshape(expert_count + 1, dev_count, shard)
            .transpose(1, 0, 2)
            .reshape(dev_count, (expert_count + 1) * shard),
            grad_bias,
        ],
        axis=1,
    )
    small_grads = jnp.pad(small_grads, ((0, 0), (0, 8 * HD - small_count)))
    grad_normed_attn, sum_qkv_c, sum_out, sum_outer, sums = closing(
        ctx_count,
        5,
        grad_attn_part.reshape(ctx_count, tokens_dev, width),
        grad_qkv_c.reshape(fsdp_count, ctx_count * shard, 6 * HD),
        padded_out,
        grad_outer.reshape(fsdp_count, shared_shard, width),
        small_grads.reshape(fsdp_count, ctx_count, 8, HD),
    )
    sums = sums.reshape(8 * HD)[:small_count]
    sum_qkv = collect_heads(sum_qkv_c, head_order)
    unused_norm, first_pull = jax.vjp(lambda v: rms_scale(v, gain_attn), inputs)
    input_grad = grad_middle + first_pull(grad_normed_attn)[0]
    sum_router = sums[2 * shard : (2 + expert_count) * shard].reshape(expert_count, shard).T
    return (
        hidden_out,
        input_grad.reshape(1, tokens_dev, width),
        sums[:shard],
        sum_qkv,
        sums[(3 + expert_count) * shard :],
        sum_out,
        sums[shard : 2 * shard],
        sum_router,
        sums[(2 + expert_count) * shard : (3 + expert_count) * shard],
        sum_inner,
        sum_outer,
        sum_expert_inner.astype(full)[None],
        sum_expert_outer.astype(full)[None],
    )


def local(*arrays):
    width = arrays[0].shape[2]
    ctx_count = lax.axis_size("ctx")
    shard = arrays[6].shape[0]
    fits = (
        width == 2 * ctx_count * HD
        and 2 * shard == HD
        and ctx_count % 2 == 0
        and lax.axis_size("fsdp") * ctx_count * shard == width
        and arrays[14].shape[0] == 1
    )
    return split_plan(*arrays) if fits else gathered_plan(*arrays)


def solution(mesh):
    in_specs = (
        P("fsdp", "ctx", None),
        P("fsdp", "ctx"),
        P(),
        P("fsdp", "ctx", None),
        P("fsdp", "ctx", None),
        P(("fsdp", "ctx")),
        P(("fsdp", "ctx"), None),
        P(("fsdp", "ctx")),
        P(("fsdp", "ctx"), None),
        P(("fsdp", "ctx")),
        P(("fsdp", "ctx"), None),
        P(("fsdp", "ctx")),
        P(("fsdp", "ctx"), None),
        P(("fsdp", "ctx"), None),
        P("ctx", "fsdp", None),
        P("ctx", "fsdp", None),
    )
    out_specs = (
        P("fsdp", "ctx", None),
        P("fsdp", "ctx", None),
        P(("fsdp", "ctx")),
        P(("fsdp", "ctx"), None),
        P(("fsdp", "ctx")),
        P(("fsdp", "ctx"), None),
        P(("fsdp", "ctx")),
        P(("fsdp", "ctx"), None),
        P(("fsdp", "ctx")),
        P(("fsdp", "ctx"), None),
        P(("fsdp", "ctx"), None),
        P("ctx", "fsdp", None),
        P("ctx", "fsdp", None),
    )
    return jax.shard_map(local, mesh=mesh, in_specs=in_specs, out_specs=out_specs, check_vma=False)
```
